32 devices in a mesh: dp: 8 (over z, x), cores: 4 (over y, core).
Axes of the slice: x: 2, y: 2, z: 4, core: 2. Of those that a mesh axis runs over, the one named last changes fastest.
Arguments:
- features: bfloat16 [65536, 1027], P(('dp', 'cores')), may hold values from -6 to 6
- labels: int32 [65536], P(('dp', 'cores')), may hold values 0 or 1
- days: int32 [65536], P(('dp', 'cores')), may hold values from 0 to 23, as said below
- master: float32 [4214944], P(('dp', 'cores'))
- moment_one: float32 [4214944], P(('dp', 'cores'))
- moment_two: float32 [4214944], P(('dp', 'cores')), as said below
Outputs:
- logits: float32 [65536], P(('dp', 'cores'))
- loss: float32 [], replicated
- feature_grad: float32 [65536, 1027], P(('dp', 'cores'))
- flat_grad: float32 [4214944], P(('dp', 'cores'))
- new_moment_one: float32 [4214944], P(('dp', 'cores'))
- new_moment_two: float32 [4214944], P(('dp', 'cores'))
- new_master: float32 [4214944], P(('dp', 'cores'))
- new_bias: float32 [4192], P(('dp', 'cores'))
The draws below stay inside these ranges and needn't reach their ends.
Inputs may be any that keep to these rules, and one draw needn't show every extreme that they name: Each of the 24 days holds at least one example; day numbers mostly grow with the example's index. `moment_two`: Positive.
All inputs are finite; a program needn't handle non-finite values. No bound on the sum of `labels` on one device may be relied on, other than what follows from the above.
Results may differ from the reference program's by a relative error of at most 0.012.
The reference program's roundings to bfloat16 on the way count: a program that leaves them out, or rounds other values in their place, can miss the bound.
Values may be sent and summed in bfloat16 or wider, within the bound.
No kernel may reach another device: no remote copies, remote signals or barrier semaphores. Data moves between devices by JAX's collectives and lax.ppermute only.
A program may use at most 256 MiB of HBM per device.

```python
import math
import jax
import jax.numpy as jnp
from jax import lax

D = 1027
H = 1024
DAYS = 24
STEP = 10
B_DEV = 2048
TOKENS = 65536
CROSS_PIECE = 32961
WIDE_PIECE = 33
DEEP_PIECE = 32864
UNIT_PIECE = 32
SQUARE_PIECE = 32768
SHARD = 131717
PFLAT = 4214944


def layout_values(values):
    count = PFLAT // SHARD
    lengths = [CROSS_PIECE, WIDE_PIECE, CROSS_PIECE, WIDE_PIECE, DEEP_PIECE, UNIT_PIECE, SQUARE_PIECE, UNIT_PIECE, UNIT_PIECE, 1]
    columns = [jnp.full((count, length), value, jnp.float32) for length, value in zip(lengths, values)]
    return jnp.concatenate(columns, axis=1).reshape(-1)


def master_scales():
    return [D ** (-0.5), 0.03, D ** (-0.5), 0.03, (0.25 / D) ** 0.5, 0.03, 1.7 * H ** (-0.5), 0.03, 1.67 * H ** (-0.5), 0.3]


def master_centers():
    return [0.0, 0.0, 0.0, 0.0, 0.0, 0.0, 0.0, 0.0, 0.0, -1.2]


def grad_scales():
    base = DAYS / math.sqrt(TOKENS)
    joint = 0.05 * DAYS
    head_unit = 1.67 / math.sqrt(H)
    spread = 1.56 / math.sqrt(H)
    return [0.27 * base / math.sqrt(D), 0.27 * base / math.sqrt(D), 0.27 * base / math.sqrt(D), 0.19 * base / math.sqrt(D), 0.77 * base / math.sqrt(H), spread * math.sqrt((0.25 * base) ** 2 + (0.5 * joint) ** 2), head_unit * math.sqrt((0.16 * base) ** 2 + (0.14 * joint) ** 2), head_unit * math.sqrt((0.25 * base) ** 2 + (0.5 * joint) ** 2), math.sqrt((0.3 * base) ** 2 + (0.37 * joint) ** 2), math.sqrt((0.45 * base) ** 2 + joint ** 2)]


def draw_days(key, part):
    key = jax.random.fold_in(key, 7)
    rows = jnp.arange(TOKENS, dtype=jnp.int32)
    base = rows * DAYS // TOKENS
    starts = rows * DAYS % TOKENS < DAYS
    offset = jax.random.randint(key, (TOKENS,), 0, 2, dtype=jnp.int32)
    return ((base + jnp.where(starts, 0, offset)) % DAYS).astype(jnp.int32)


def draw_master(key, part):
    key = jax.random.fold_in(key, 11)
    scale = layout_values(master_scales())
    center = layout_values(master_centers())
    values = jax.random.truncated_normal(key, -4.0, 4.0, (PFLAT,), jnp.float32)
    return values * scale + center


def draw_moment_one(key, part):
    key = jax.random.fold_in(key, 12)
    scale = layout_values(grad_scales())
    values = jax.random.truncated_normal(key, -4.0, 4.0, (PFLAT,), jnp.float32)
    return values * scale / 9.0


def draw_moment_two(key, part):
    key = jax.random.fold_in(key, 13)
    scale = layout_values(grad_scales())
    factor = jax.random.uniform(key, (PFLAT,), jnp.float32, 1.0, 4.0)
    return scale * scale * 0.001 * factor


def place_ends(drawn, own_key, low, high):
    place = [jax.random.randint(jax.random.fold_in(own_key, axis), (), 0, length) for axis, length in enumerate(drawn.shape)]
    widest = drawn.shape.index(max(drawn.shape))
    beside = place[:widest] + [(place[widest] + 1) % drawn.shape[widest]] + place[widest + 1:]
    return drawn.at[tuple(place)].set(low).at[tuple(beside)].set(high)


def shard_levels(key, extent, shards, smallest, high):
    gain = 1.0
    for axis_at, parts in shards:
        draws = jax.random.uniform(jax.random.fold_in(jax.random.fold_in(key, 6), axis_at), (parts,), jnp.float32, smallest / len(shards), high / len(shards))
        gain = gain * jnp.repeat(jnp.exp(draws), extent[axis_at] // parts).reshape((-1,) + (1,) * (len(extent) - 1 - axis_at))
    return gain


def normal_values(rng, extent, deviation, reach, shards=(), kind=jnp.bfloat16):
    entries = jax.random.normal(rng, extent, jnp.float32) * deviation
    if len(shards) > 0:
        entries = shard_levels(rng, extent, shards, -0.22, 0.18) * entries
    return jnp.clip(entries, min=-reach, max=reach).astype(kind)


def setup_inputs(seed: int = 0) -> dict:
    arg_keys = jax.random.split(jax.random.key(seed), 7)
    features = normal_values(arg_keys[0], (TOKENS, D), 1.0, 6.0, ((0, 32),))
    labels = place_ends((jax.random.randint(arg_keys[1], (TOKENS,), 0, 4) < 1).astype(jnp.int32), jax.random.fold_in(arg_keys[1], 1), 0, 1)
    days = draw_days(jax.random.fold_in(arg_keys[6], 71), 0)
    master = draw_master(jax.random.fold_in(arg_keys[6], 71), 0)
    moment_one = draw_moment_one(jax.random.fold_in(arg_keys[6], 71), 0)
    moment_two = draw_moment_two(jax.random.fold_in(arg_keys[6], 71), 0)
    return {"features": features, "labels": labels, "days": days, "master": master, "moment_one": moment_one, "moment_two": moment_two}


@jax.custom_vjp
def low(v):
    return lax.optimization_barrier(v.astype(jnp.bfloat16)).astype(jnp.float32)

@jax.custom_vjp
def low_back(v):
    return v

def low_keep(v):
    return (low(v), None)

def low_pass(kept, grad):
    return (grad,)

def back_keep(v):
    return (v, None)

def back_low(kept, grad):
    return (low(grad),)
low.defvjp(low_keep, low_pass)
low_back.defvjp(back_keep, back_low)

def shapes():
    return [(D, D), (D,), (D, D), (D,), (D, H), (H,), (H, H), (H,), (H,), (1,)]

def pieces():
    return [CROSS_PIECE, WIDE_PIECE, CROSS_PIECE, WIDE_PIECE, DEEP_PIECE, UNIT_PIECE, SQUARE_PIECE, UNIT_PIECE, UNIT_PIECE, 1]

def starts_of():
    starts = []
    position = 0
    for piece in pieces():
        starts.append(position)
        position += piece
    return starts

def unpack(flat):
    table = flat.reshape(PFLAT // SHARD, SHARD)
    result = []
    for shape, piece, start in zip(shapes(), pieces(), starts_of()):
        length = math.prod(shape)
        result.append(table[:, start:start + piece].reshape(-1)[:length].reshape(shape))
    return result

def pack(values):
    count = PFLAT // SHARD
    columns = []
    for value, piece in zip(values, pieces()):
        line = value.reshape(-1)
        line = jnp.concatenate([line, jnp.zeros((count * piece - line.shape[0],), line.dtype)])
        columns.append(line.reshape(count, piece))
    return jnp.concatenate(columns, axis=1).reshape(-1)

def bias_part(flat):
    table = flat.reshape(PFLAT // SHARD, SHARD)
    starts = starts_of()
    lengths = pieces()
    return jnp.concatenate([table[:, starts[index]:starts[index] + lengths[index]] for index in (1, 3, 5, 7, 9)], axis=1).reshape(-1)

def forward(params, features, label_rows, weight_rows):
    cross_one, bias_one, cross_two, bias_two, deep_one, deep_bias_one, deep_two, deep_bias_two, head, head_bias = params
    highest = lax.Precision.HIGHEST
    mixer_one = low_back(jnp.dot(features, cross_one, precision=highest) + bias_one)
    layer_one = features * mixer_one + features
    mixer_two = low_back(jnp.dot(low(layer_one), cross_two, precision=highest) + bias_two)
    layer_two = features * mixer_two + layer_one
    deep_pre_one = low_back(jnp.dot(low(layer_two), deep_one, precision=highest) + deep_bias_one)
    hidden_one = jax.nn.gelu(deep_pre_one)
    deep_pre_two = low_back(jnp.dot(low(hidden_one), deep_two, precision=highest) + deep_bias_two)
    hidden_two = jax.nn.gelu(deep_pre_two)
    logits = jnp.dot(low(hidden_two), head, precision=highest) + head_bias[0]
    entropy = jax.nn.softplus(logits) - label_rows * logits
    return (jnp.sum(weight_rows * entropy), (logits, entropy))

def reference(features, labels, days, master, moment_one, moment_two):
    weights = master.astype(jnp.bfloat16).astype(jnp.float32)
    params = unpack(weights)
    day_hot = (days[:, None] == jnp.arange(DAYS, dtype=jnp.int32)[None, :]).astype(jnp.float32)
    counts = lax.optimization_barrier(jnp.sum(day_hot, axis=0))
    row_weight = jnp.take(1.0 / counts, days)
    label_float = labels.astype(jnp.float32)
    blocks = TOKENS // B_DEV
    inputs = (features.reshape(blocks, B_DEV, D), label_float.reshape(blocks, B_DEV), row_weight.reshape(blocks, B_DEV))

    def accumulate(totals, block):
        block_features, block_labels, block_weight = block

        def local(param_list, feature_rows):
            return forward(param_list, feature_rows, block_labels, block_weight)
        value, backward, extras = jax.vjp(local, params, block_features.astype(jnp.float32), has_aux=True)
        grads, block_grad = backward(jnp.ones_like(value))
        totals = jax.tree.map(lambda left, right: left + right, totals, grads)
        return (totals, (extras[0], extras[1], block_grad))
    zeros = jax.tree.map(jnp.zeros_like, params)
    grads, (logits, entropy, feature_grad) = lax.scan(accumulate, zeros, inputs)
    logits = logits.reshape(TOKENS)
    entropy = entropy.reshape(TOKENS)
    feature_grad = feature_grad.reshape(TOKENS, D)
    day_loss = jnp.dot(entropy, day_hot, precision=lax.Precision.HIGHEST)
    loss = jnp.sum(day_loss / counts)
    flat_grad = pack(list(grads))
    new_moment_one = 0.9 * moment_one + 0.1 * flat_grad
    new_moment_two = 0.999 * moment_two + 0.001 * flat_grad * flat_grad
    corrected_one = new_moment_one / (1.0 - 0.9 ** STEP)
    corrected_two = new_moment_two / (1.0 - 0.999 ** STEP)
    new_master = master - 0.03 * (corrected_one / (jnp.sqrt(corrected_two) + 1e-08) + 0.01 * master)
    new_bias = bias_part(new_master)
    return (logits, loss, feature_grad, flat_grad, new_moment_one, new_moment_two, new_master, new_bias)
```

```python
import math

import jax
import jax.numpy as jnp
from jax import lax
from jax.sharding import PartitionSpec as P

D = 1027
H = 1024
DAYS = 24
STEP = 10


def shapes():
    return [(D, D), (D,), (D, D), (D,), (D, H), (H,), (H, H), (H,), (H,), (1,)]


def piece_sizes(count):
    return [(math.prod(shape) + count - 1) // count for shape in shapes()[:-1]] + [1]


def starts_of(count):
    starts = []
    position = 0
    for piece in piece_sizes(count):
        starts.append(position)
        position += piece
    return starts


def bias_part(shard, count):
    starts = starts_of(count)
    lengths = piece_sizes(count)
    return jnp.concatenate(
        [shard[starts[index] : starts[index] + lengths[index]] for index in (1, 3, 5, 7, 9)]
    )


def rows_product(left, right):
    return lax.dot_general(
        left, right, (((0,), (0,)), ((), ())), preferred_element_type=jnp.float32
    )


def back_product(grad_rows, matrix):
    return lax.dot_general(
        grad_rows, matrix, (((1,), (1,)), ((), ())), preferred_element_type=jnp.float32
    )


def column_sums(rounded):
    return jnp.sum(rounded, axis=0, dtype=jnp.float32)


AXES = ("dp", "cores")
EXTRA = D - H


def spill_rows(piece, width, rows, count):
    excess = piece - rows * width
    return max(EXTRA, -(-((count - 1) * excess) // width))


def to_block(piece, index, width, rows, count):
    excess = piece.shape[0] - rows * width
    spill = spill_rows(piece.shape[0], width, rows, count)
    size = (rows + spill) * width
    lead = (count - 1) * excess
    padded = jnp.pad(piece, (lead, max(0, size - piece.shape[0])))
    return lax.dynamic_slice(padded, (lead - index * excess,), (size,)).reshape(rows + spill, width)


def from_block(block, index, piece, rows, count):
    width = block.shape[1]
    excess = piece - rows * width
    last = (count - 1) * excess
    line = jnp.pad(block.reshape(-1), (0, max(0, last + piece - block.size)))
    return lax.dynamic_slice(line, (index * excess,), (piece,))


def aux_pack(parts):
    line = jnp.concatenate([part.reshape(-1) for part in parts])
    size = -(-line.shape[0] // (16 * H)) * 16 * H
    return jnp.pad(line, (0, size - line.shape[0])).reshape(-1, H)


def with_spill(main, spill, rows, count):
    width = main.shape[1]
    shifted = jnp.concatenate([jnp.zeros_like(spill[:1]), spill[:-1]], axis=0)
    full = jnp.pad(shifted, ((0, 0), (0, rows - spill.shape[1]), (0, 0)))
    body = main + full.reshape(count * rows, width)
    return jnp.concatenate([body, spill[count - 1, :EXTRA]], axis=0)


def overlap_rows(matrix, rows, spill, count):
    width = matrix.shape[1]
    body = matrix[: count * rows].reshape(count, rows, width)[1:, :spill]
    last = jnp.pad(matrix[count * rows :], ((0, spill - EXTRA), (0, 0)))[None]
    return jnp.concatenate([body, last], axis=0)


def local(features, labels, days, master, moment_one, moment_two):
    devices = lax.axis_size(AXES)
    index = lax.axis_index(AXES)
    rows = H // devices
    starts = starts_of(devices)
    sizes = piece_sizes(devices)
    piece = [master[a : a + l] for a, l in zip(starts, sizes)]
    wide_spill = spill_rows(sizes[0], D, rows, devices)
    deep_spill = spill_rows(sizes[4], H, rows, devices)
    block_one = to_block(piece[0], index, D, rows, devices)
    block_two = to_block(piece[2], index, D, rows, devices)
    block_deep = to_block(piece[4], index, H, rows, devices)
    aux = aux_pack(
        [
            block_one[rows:, :H],
            block_two[rows:, :H],
            block_deep[rows:],
            block_one[:, H:],
            block_two[:, H:],
        ]
        + [piece[i] for i in (1, 3, 5, 7, 8, 9)]
    )
    aux_rows = aux.shape[0]
    low = jnp.bfloat16
    aux_all = lax.all_gather(aux.astype(low), AXES, axis=0, tiled=True)
    main_one = lax.all_gather(block_one[:rows, :H].astype(low), AXES, axis=0, tiled=True)
    main_two = lax.all_gather(block_two[:rows, :H].astype(low), AXES, axis=0, tiled=True)
    main_deep = lax.all_gather(block_deep[:rows].astype(low), AXES, axis=0, tiled=True)
    deep_two = lax.all_gather(
        piece[6].reshape(rows, H).astype(low), AXES, axis=0, tiled=True
    )
    aux_all = aux_all.reshape(devices, aux_rows * H)
    position = 0
    aux_shapes = [
        (wide_spill, H),
        (wide_spill, H),
        (deep_spill, H),
        (rows + wide_spill, EXTRA),
        (rows + wide_spill, EXTRA),
    ] + [(sizes[i],) for i in (1, 3, 5, 7, 8, 9)]
    got = []
    for shape in aux_shapes:
        length = math.prod(shape)
        got.append(aux_all[:, position : position + length].reshape((devices,) + shape))
        position += length

    def wide(main, spill, side):
        body = with_spill(main, spill, rows, devices)
        edge = with_spill(
            side[:, :rows].reshape(devices * rows, EXTRA), side[:, rows:], rows, devices
        )
        return jnp.concatenate([body, edge], axis=1)

    cross_one = wide(main_one, got[0], got[3])
    cross_two = wide(main_two, got[1], got[4])
    deep_one = with_spill(main_deep, got[2], rows, devices)
    bias_one = got[5].reshape(-1)[:D]
    bias_two = got[6].reshape(-1)[:D]
    deep_bias_one = got[7].reshape(-1)[:H]
    deep_bias_two = got[8].reshape(-1)[:H]
    head = got[9].reshape(-1)[:H]
    head_bias = got[10].reshape(-1)[:1]
    highest = lax.Precision.HIGHEST
    day_hot = (days[:, None] == jnp.arange(DAYS, dtype=jnp.int32)[None, :]).astype(jnp.float32)
    local_counts = jnp.sum(day_hot, axis=0)
    counts = lax.psum(local_counts, ("dp", "cores"))
    feature_float = features.astype(jnp.float32)
    mixer_one = jnp.dot(features, cross_one, preferred_element_type=jnp.float32) + bias_one.astype(
        jnp.float32
    )
    layer_one = feature_float * mixer_one + feature_float
    layer_one_low = layer_one.astype(jnp.bfloat16)
    mixer_two = jnp.dot(
        layer_one_low, cross_two, preferred_element_type=jnp.float32
    ) + bias_two.astype(jnp.float32)
    layer_two = feature_float * mixer_two + layer_one
    layer_two_low = layer_two.astype(jnp.bfloat16)
    deep_pre_one = jnp.dot(
        layer_two_low, deep_one, preferred_element_type=jnp.float32
    ) + deep_bias_one.astype(jnp.float32)
    hidden_one, gelu_back_one = jax.vjp(jax.nn.gelu, deep_pre_one)
    hidden_one_low = hidden_one.astype(jnp.bfloat16)
    deep_pre_two = jnp.dot(
        hidden_one_low, deep_two, preferred_element_type=jnp.float32
    ) + deep_bias_two.astype(jnp.float32)
    hidden_two, gelu_back_two = jax.vjp(jax.nn.gelu, deep_pre_two)
    hidden_two_low = hidden_two.astype(jnp.bfloat16)
    logits = (
        jnp.dot(hidden_two_low, head, preferred_element_type=jnp.float32)
        + head_bias.astype(jnp.float32)[0]
    )
    label_float = labels.astype(jnp.float32)
    entropy = jax.nn.softplus(logits) - label_float * logits
    local_loss = jnp.dot(entropy, day_hot, precision=highest)
    day_loss = lax.psum(local_loss, ("dp", "cores"))
    loss = jnp.sum(day_loss / counts)
    row_weight = jnp.dot(day_hot, 1.0 / counts, precision=highest)
    logit_grad = (jax.nn.sigmoid(logits) - label_float) * row_weight
    head_grad = jnp.dot(logit_grad, hidden_two_low, preferred_element_type=jnp.float32)
    head_bias_grad = jnp.sum(logit_grad)[None]
    hidden_two_grad = logit_grad[:, None] * head.astype(jnp.float32)[None, :]
    pre_two_grad = gelu_back_two(hidden_two_grad)[0].astype(jnp.bfloat16)
    deep_two_grad = rows_product(hidden_one_low, pre_two_grad)
    deep_bias_two_grad = column_sums(pre_two_grad)
    hidden_one_grad = back_product(pre_two_grad, deep_two)
    pre_one_grad = gelu_back_one(hidden_one_grad)[0].astype(jnp.bfloat16)
    deep_one_grad = rows_product(layer_two_low, pre_one_grad)
    deep_bias_one_grad = column_sums(pre_one_grad)
    layer_two_grad = back_product(pre_one_grad, deep_one)
    mixer_two_grad = (layer_two_grad * feature_float).astype(jnp.bfloat16)
    cross_two_grad = rows_product(layer_one_low, mixer_two_grad)
    bias_two_grad = column_sums(mixer_two_grad)
    layer_one_grad = layer_two_grad + back_product(mixer_two_grad, cross_two)
    mixer_one_grad = (layer_one_grad * feature_float).astype(jnp.bfloat16)
    cross_one_grad = rows_product(features, mixer_one_grad)
    bias_one_grad = column_sums(mixer_one_grad)
    feature_grad = (
        layer_two_grad * mixer_two
        + layer_one_grad * (mixer_one + 1.0)
        + back_product(mixer_one_grad, cross_one)
    )
    def scatter(value):
        return lax.psum_scatter(value.astype(low), AXES, scatter_dimension=0, tiled=True).astype(
            jnp.float32
        )

    own_deep_two = scatter(deep_two_grad)
    own_deep_one = scatter(deep_one_grad[:H])
    own_cross_two = scatter(cross_two_grad[:H, :H])
    own_cross_one = scatter(cross_one_grad[:H, :H])

    def edge(matrix):
        side = matrix[:, H:]
        return jnp.concatenate(
            [
                side[:H].reshape(devices, rows, EXTRA),
                overlap_rows(side, rows, wide_spill, devices),
            ],
            axis=1,
        )

    def cut(vector, size):
        return jnp.pad(vector, (0, devices * size - vector.shape[0])).reshape(devices, size)

    aux_parts = [
        overlap_rows(cross_one_grad[:, :H], rows, wide_spill, devices),
        overlap_rows(cross_two_grad[:, :H], rows, wide_spill, devices),
        overlap_rows(deep_one_grad, rows, deep_spill, devices),
        edge(cross_one_grad),
        edge(cross_two_grad),
    ] + [
        cut(value, sizes[i])
        for value, i in zip(
            (bias_one_grad, bias_two_grad, deep_bias_one_grad, deep_bias_two_grad, head_grad),
            (1, 3, 5, 7, 8),
        )
    ] + [cut(head_bias_grad, 1)]
    line = jnp.concatenate([part.reshape(devices, -1) for part in aux_parts], axis=1)
    line = jnp.pad(line, ((0, 0), (0, aux_rows * H - line.shape[1])))
    own_aux = lax.psum_scatter(
        line.reshape(devices * aux_rows, H), AXES, scatter_dimension=0, tiled=True
    ).reshape(-1)
    mine = []
    position = 0
    for shape in aux_shapes:
        length = math.prod(shape)
        mine.append(own_aux[position : position + length].reshape(shape))
        position += length

    def own_wide(main, spill, side):
        return jnp.concatenate([jnp.concatenate([main, spill], axis=0), side], axis=1)

    flat_grad = jnp.concatenate(
        [
            from_block(own_wide(own_cross_one, mine[0], mine[3]), index, sizes[0], rows, devices),
            mine[5],
            from_block(own_wide(own_cross_two, mine[1], mine[4]), index, sizes[2], rows, devices),
            mine[6],
            from_block(
                jnp.concatenate([own_deep_one, mine[2]], axis=0), index, sizes[4], rows, devices
            ),
            mine[7],
            own_deep_two.reshape(-1),
            mine[8],
            mine[9],
            mine[10],
        ]
    )
    new_moment_one = 0.9 * moment_one + 0.1 * flat_grad
    new_moment_two = 0.999 * moment_two + 0.001 * flat_grad * flat_grad
    corrected_one = new_moment_one / (1.0 - 0.9**STEP)
    corrected_two = new_moment_two / (1.0 - 0.999**STEP)
    new_master = master - 0.03 * (corrected_one / (jnp.sqrt(corrected_two) + 1e-08) + 0.01 * master)
    new_bias = bias_part(new_master, devices)
    return (
        logits,
        loss,
        feature_grad,
        flat_grad,
        new_moment_one,
        new_moment_two,
        new_master,
        new_bias,
    )


def solution(mesh):
    in_specs = (
        P(("dp", "cores"), None),
        P(("dp", "cores")),
        P(("dp", "cores")),
        P(("dp", "cores")),
        P(("dp", "cores")),
        P(("dp", "cores")),
    )
    out_specs = (
        P(("dp", "cores")),
        P(),
        P(("dp", "cores"), None),
        P(("dp", "cores")),
        P(("dp", "cores")),
        P(("dp", "cores")),
        P(("dp", "cores")),
        P(("dp", "cores")),
    )
    return jax.shard_map(local, mesh=mesh, in_specs=in_specs, out_specs=out_specs, check_vma=False)
```

```python
import functools
import math

import jax
import jax.numpy as jnp
from jax import lax
from jax.experimental import pallas as pl
from jax.experimental.pallas import tpu as pltpu
from jax.sharding import PartitionSpec as P

D = 1027
H = 1024
DAYS = 24
STEP = 10


def shapes():
    return [(D, D), (D,), (D, D), (D,), (D, H), (H,), (H, H), (H,), (H,), (1,)]


def piece_sizes(count):
    return [(math.prod(shape) + count - 1) // count for shape in shapes()[:-1]] + [1]


def starts_of(count):
    starts = []
    position = 0
    for piece in piece_sizes(count):
        starts.append(position)
        position += piece
    return starts


def bias_part(shard, count):
    starts = starts_of(count)
    lengths = piece_sizes(count)
    return jnp.concatenate(
        [shard[starts[index] : starts[index] + lengths[index]] for index in (1, 3, 5, 7, 9)]
    )


def rows_product(left, right):
    return lax.dot_general(
        left, right, (((0,), (0,)), ((), ())), preferred_element_type=jnp.float32
    )


def back_product(grad_rows, matrix):
    return lax.dot_general(
        grad_rows, matrix, (((1,), (1,)), ((), ())), preferred_element_type=jnp.float32
    )


def column_sums(rounded):
    return jnp.sum(rounded, axis=0, dtype=jnp.float32)


AXES = ("dp", "cores")
EXTRA = D - H


def spill_rows(piece, width, rows, count):
    excess = piece - rows * width
    return max(EXTRA, -(-((count - 1) * excess) // width))


def to_block(piece, index, width, rows, count):
    excess = piece.shape[0] - rows * width
    spill = spill_rows(piece.shape[0], width, rows, count)
    size = (rows + spill) * width
    lead = (count - 1) * excess
    padded = jnp.pad(piece, (lead, max(0, size - piece.shape[0])))
    return lax.dynamic_slice(padded, (lead - index * excess,), (size,)).reshape(rows + spill, width)


def from_block(block, index, piece, rows, count):
    width = block.shape[1]
    excess = piece - rows * width
    last = (count - 1) * excess
    line = jnp.pad(block.reshape(-1), (0, max(0, last + piece - block.size)))
    return lax.dynamic_slice(line, (index * excess,), (piece,))


def aux_pack(parts):
    line = jnp.concatenate([part.reshape(-1) for part in parts])
    size = -(-line.shape[0] // (16 * H)) * 16 * H
    return jnp.pad(line, (0, size - line.shape[0])).reshape(-1, H)


def with_spill(main, spill, rows, count):
    width = main.shape[1]
    shifted = jnp.concatenate([jnp.zeros_like(spill[:1]), spill[:-1]], axis=0)
    full = jnp.pad(shifted, ((0, 0), (0, rows - spill.shape[1]), (0, 0)))
    body = main + full.reshape(count * rows, width)
    return jnp.concatenate([body, spill[count - 1, :EXTRA]], axis=0)


def overlap_rows(matrix, rows, spill, count):
    width = matrix.shape[1]
    body = matrix[: count * rows].reshape(count, rows, width)[1:, :spill]
    last = jnp.pad(matrix[count * rows :], ((0, spill - EXTRA), (0, 0)))[None]
    return jnp.concatenate([body, last], axis=0)


def bit_groups(mesh):
    devices = mesh.devices.reshape(-1)
    groups = {"z": [], "plane": [], "core": []}
    bit = 1
    while bit < devices.size:
        here = getattr(devices[0], "coords", None)
        there = getattr(devices[bit], "coords", None)
        if here is None or there is None:
            name = "core" if bit == 1 else "plane" if bit <= 4 else "z"
        elif tuple(here) == tuple(there):
            name = "core"
        elif here[2] != there[2]:
            name = "z"
        else:
            name = "plane"
        groups[name].append(bit)
        bit *= 2
    return groups


def masks_of(bits):
    masks = [0]
    for bit in bits:
        masks = masks + [mask | bit for mask in masks]
    return masks


def swap(value, mask, count):
    return lax.ppermute(value, AXES, [(k, k ^ mask) for k in range(count)])


PARAMS = pltpu.CompilerParams(vmem_limit_bytes=48 * 1024 * 1024)
SMEM = pl.BlockSpec(memory_space=pltpu.SMEM)
VMEM = pl.BlockSpec(memory_space=pltpu.VMEM)


def place(index, sources, masks, count):
    def kernel(index_ref, *refs):
        out_ref = refs[-1]
        for ref, row in zip(refs[:-1], masks):
            for j, mask in enumerate(row):
                out_ref[jnp.bitwise_xor(index_ref[0], mask)] = ref[j]

    shape = sources[0].shape[1:]
    return pl.pallas_call(
        kernel,
        out_shape=jax.ShapeDtypeStruct((count,) + shape, sources[0].dtype),
        in_specs=[SMEM] + [VMEM] * len(sources),
        out_specs=VMEM,
        compiler_params=PARAMS,
    )(index, *sources)


def gather(block, index, groups, count):
    z_masks, plane_masks, core_masks = (masks_of(groups[g]) for g in ("z", "plane", "core"))
    line = jnp.stack([block] + [swap(block, mask, count) for mask in z_masks[1:]])
    plane = [line] + [swap(line, mask, count) for mask in plane_masks[1:]]
    sources, masks = list(plane), [[p ^ z for z in z_masks] for p in plane_masks]
    for core in core_masks[1:]:
        sources += [swap(value, core, count) for value in plane]
        masks += [[core ^ p ^ z for z in z_masks] for p in plane_masks]
    return place(index, sources, masks, count)


def split(index, value, masks, kinds):
    def kernel(index_ref, value_ref, *out_refs):
        for ref, row, kind in zip(out_refs, masks, kinds):
            for j, mask in enumerate(row):
                ref[j] = value_ref[jnp.bitwise_xor(index_ref[0], mask)].astype(kind)

    shape = value.shape[1:]
    return pl.pallas_call(
        kernel,
        out_shape=[
            jax.ShapeDtypeStruct((len(row),) + shape, kind) for row, kind in zip(masks, kinds)
        ],
        in_specs=[SMEM, VMEM],
        out_specs=[VMEM] * len(masks),
        compiler_params=PARAMS,
    )(index, value)


def scatter(value, index, groups, count):
    low = jnp.bfloat16
    z_masks, plane_masks, core_masks = (masks_of(groups[g]) for g in ("z", "plane", "core"))
    inner = [p ^ z for p in plane_masks for z in z_masks]
    stacks = split(
        index,
        value,
        [[core ^ m for m in inner] for core in core_masks],
        [jnp.float32] + [low] * (len(core_masks) - 1),
    )
    kept = stacks[0]
    for core, stack in zip(core_masks[1:], stacks[1:]):
        kept = kept + swap(stack, core, count).astype(jnp.float32)
    kept = kept.reshape((len(plane_masks), len(z_masks)) + value.shape[1:])
    total = kept[0]
    for j in range(1, len(plane_masks)):
        total = total + swap(kept[j].astype(low), plane_masks[j], count).astype(jnp.float32)
    own = total[0]
    for j in range(1, len(z_masks)):
        own = own + swap(total[j].astype(low), z_masks[j], count).astype(jnp.float32)
    return own


def total_of(value, count):
    bit = 1
    while bit < count:
        value = value + swap(value, bit, count)
        bit *= 2
    return value


def local(groups, features, labels, days, master, moment_one, moment_two):
    devices = lax.axis_size(AXES)
    index = lax.axis_index(AXES)
    rows = H // devices
    slot = index[None].astype(jnp.int32)
    starts = starts_of(devices)
    sizes = piece_sizes(devices)
    piece = [master[a : a + l] for a, l in zip(starts, sizes)]
    wide_spill = spill_rows(sizes[0], D, rows, devices)
    deep_spill = spill_rows(sizes[4], H, rows, devices)
    block_one = to_block(piece[0], index, D, rows, devices)
    block_two = to_block(piece[2], index, D, rows, devices)
    block_deep = to_block(piece[4], index, H, rows, devices)
    day_hot = (days[:, None] == jnp.arange(DAYS, dtype=jnp.int32)[None, :]).astype(jnp.float32)
    local_counts = jnp.sum(day_hot, axis=0)
    counts_high = jnp.floor(local_counts / 64.0)
    counts_low = local_counts - 64.0 * counts_high
    aux = aux_pack(
        [
            block_one[rows:, :H],
            block_two[rows:, :H],
            block_deep[rows:],
            block_one[:, H:],
            block_two[:, H:],
        ]
        + [piece[i] for i in (1, 3, 5, 7, 8, 9)]
        + [counts_high, counts_low]
    )
    aux_rows = aux.shape[0]
    low = jnp.bfloat16
    first = jnp.concatenate([block_one[:rows, :H], aux], axis=0).astype(low)
    first_all = gather(first, slot, groups, devices)
    main_two = gather(block_two[:rows, :H].astype(low), slot, groups, devices).reshape(H, H)
    main_deep = gather(block_deep[:rows].astype(low), slot, groups, devices).reshape(H, H)
    deep_two = gather(piece[6].reshape(rows, H).astype(low), slot, groups, devices).reshape(H, H)
    main_one = first_all[:, :rows].reshape(H, H)
    aux_all = first_all[:, rows:]
    aux_all = aux_all.reshape(devices, aux_rows * H)
    position = 0
    aux_shapes = [
        (wide_spill, H),
        (wide_spill, H),
        (deep_spill, H),
        (rows + wide_spill, EXTRA),
        (rows + wide_spill, EXTRA),
    ] + [(sizes[i],) for i in (1, 3, 5, 7, 8, 9)] + [(DAYS,), (DAYS,)]
    got = []
    for shape in aux_shapes:
        length = math.prod(shape)
        got.append(aux_all[:, position : position + length].reshape((devices,) + shape))
        position += length

    def wide(main, spill, side):
        body = with_spill(main, spill, rows, devices)
        edge = with_spill(
            side[:, :rows].reshape(devices * rows, EXTRA), side[:, rows:], rows, devices
        )
        return jnp.concatenate([body, edge], axis=1)

    cross_one = wide(main_one, got[0], got[3])
    cross_two = wide(main_two, got[1], got[4])
    deep_one = with_spill(main_deep, got[2], rows, devices)
    bias_one = got[5].reshape(-1)[:D]
    bias_two = got[6].reshape(-1)[:D]
    deep_bias_one = got[7].reshape(-1)[:H]
    deep_bias_two = got[8].reshape(-1)[:H]
    head = got[9].reshape(-1)[:H]
    head_bias = got[10].reshape(-1)[:1]
    highest = lax.Precision.HIGHEST
    counts = jnp.sum(got[11].astype(jnp.float32), axis=0) * 64.0 + jnp.sum(
        got[12].astype(jnp.float32), axis=0
    )
    feature_float = features.astype(jnp.float32)
    mixer_one = jnp.dot(features, cross_one, preferred_element_type=jnp.float32) + bias_one.astype(
        jnp.float32
    )
    layer_one = feature_float * mixer_one + feature_float
    layer_one_low = layer_one.astype(jnp.bfloat16)
    mixer_two = jnp.dot(
        layer_one_low, cross_two, preferred_element_type=jnp.float32
    ) + bias_two.astype(jnp.float32)
    layer_two = feature_float * mixer_two + layer_one
    layer_two_low = layer_two.astype(jnp.bfloat16)
    deep_pre_one = jnp.dot(
        layer_two_low, deep_one, preferred_element_type=jnp.float32
    ) + deep_bias_one.astype(jnp.float32)
    hidden_one, gelu_back_one = jax.vjp(jax.nn.gelu, deep_pre_one)
    hidden_one_low = hidden_one.astype(jnp.bfloat16)
    deep_pre_two = jnp.dot(
        hidden_one_low, deep_two, preferred_element_type=jnp.float32
    ) + deep_bias_two.astype(jnp.float32)
    hidden_two, gelu_back_two = jax.vjp(jax.nn.gelu, deep_pre_two)
    hidden_two_low = hidden_two.astype(jnp.bfloat16)
    logits = (
        jnp.dot(hidden_two_low, head, preferred_element_type=jnp.float32)
        + head_bias.astype(jnp.float32)[0]
    )
    label_float = labels.astype(jnp.float32)
    entropy = jax.nn.softplus(logits) - label_float * logits
    row_weight = jnp.dot(day_hot, 1.0 / counts, precision=highest)
    loss = total_of(jnp.sum(entropy * row_weight), devices)
    logit_grad = (jax.nn.sigmoid(logits) - label_float) * row_weight
    head_grad = jnp.dot(logit_grad, hidden_two_low, preferred_element_type=jnp.float32)
    head_bias_grad = jnp.sum(logit_grad)[None]
    hidden_two_grad = logit_grad[:, None] * head.astype(jnp.float32)[None, :]
    pre_two_grad = gelu_back_two(hidden_two_grad)[0].astype(jnp.bfloat16)
    deep_two_grad = rows_product(hidden_one_low, pre_two_grad)
    deep_bias_two_grad = column_sums(pre_two_grad)
    hidden_one_grad = back_product(pre_two_grad, deep_two)
    pre_one_grad = gelu_back_one(hidden_one_grad)[0].astype(jnp.bfloat16)
    deep_one_grad = rows_product(layer_two_low, pre_one_grad)
    deep_bias_one_grad = column_sums(pre_one_grad)
    layer_two_grad = back_product(pre_one_grad, deep_one)
    mixer_two_grad = (layer_two_grad * feature_float).astype(jnp.bfloat16)
    cross_two_grad = rows_product(layer_one_low, mixer_two_grad)
    bias_two_grad = column_sums(mixer_two_grad)
    layer_one_grad = layer_two_grad + back_product(mixer_two_grad, cross_two)
    mixer_one_grad = (layer_one_grad * feature_float).astype(jnp.bfloat16)
    cross_one_grad = rows_product(features, mixer_one_grad)
    bias_one_grad = column_sums(mixer_one_grad)
    feature_grad = (
        layer_two_grad * mixer_two
        + layer_one_grad * (mixer_one + 1.0)
        + back_product(mixer_one_grad, cross_one)
    )
    def scatter_main(matrix):
        return scatter(matrix[:H, :H].reshape(devices, rows, H), slot, groups, devices)

    own_deep_two = scatter_main(deep_two_grad)
    own_deep_one = scatter_main(deep_one_grad)
    own_cross_two = scatter_main(cross_two_grad)

    def edge(matrix):
        side = matrix[:, H:]
        return jnp.concatenate(
            [
                side[:H].reshape(devices, rows, EXTRA),
                overlap_rows(side, rows, wide_spill, devices),
            ],
            axis=1,
        )

    def cut(vector, size):
        return jnp.pad(vector, (0, devices * size - vector.shape[0])).reshape(devices, size)

    aux_parts = [
        overlap_rows(cross_one_grad[:, :H], rows, wide_spill, devices),
        overlap_rows(cross_two_grad[:, :H], rows, wide_spill, devices),
        overlap_rows(deep_one_grad, rows, deep_spill, devices),
        edge(cross_one_grad),
        edge(cross_two_grad),
    ] + [
        cut(value, sizes[i])
        for value, i in zip(
            (bias_one_grad, bias_two_grad, deep_bias_one_grad, deep_bias_two_grad, head_grad),
            (1, 3, 5, 7, 8),
        )
    ] + [cut(head_bias_grad, 1)]
    line = jnp.concatenate([part.reshape(devices, -1) for part in aux_parts], axis=1)
    line = jnp.pad(line, ((0, 0), (0, aux_rows * H - line.shape[1])))
    last = jnp.concatenate(
        [cross_one_grad[:H, :H].reshape(devices, rows, H), line.reshape(devices, aux_rows, H)],
        axis=1,
    )
    own_last = scatter(last, slot, groups, devices)
    own_cross_one = own_last[:rows]
    own_aux = own_last[rows:].reshape(-1)
    mine = []
    position = 0
    for shape in aux_shapes[:11]:
        length = math.prod(shape)
        mine.append(own_aux[position : position + length].reshape(shape))
        position += length

    def own_wide(main, spill, side):
        return jnp.concatenate([jnp.concatenate([main, spill], axis=0), side], axis=1)

    flat_grad = jnp.concatenate(
        [
            from_block(own_wide(own_cross_one, mine[0], mine[3]), index, sizes[0], rows, devices),
            mine[5],
            from_block(own_wide(own_cross_two, mine[1], mine[4]), index, sizes[2], rows, devices),
            mine[6],
            from_block(
                jnp.concatenate([own_deep_one, mine[2]], axis=0), index, sizes[4], rows, devices
            ),
            mine[7],
            own_deep_two.reshape(-1),
            mine[8],
            mine[9],
            mine[10],
        ]
    )
    new_moment_one = 0.9 * moment_one + 0.1 * flat_grad
    new_moment_two = 0.999 * moment_two + 0.001 * flat_grad * flat_grad
    corrected_one = new_moment_one / (1.0 - 0.9**STEP)
    corrected_two = new_moment_two / (1.0 - 0.999**STEP)
    new_master = master - 0.03 * (corrected_one / (jnp.sqrt(corrected_two) + 1e-08) + 0.01 * master)
    new_bias = bias_part(new_master, devices)
    return (
        logits,
        loss,
        feature_grad,
        flat_grad,
        new_moment_one,
        new_moment_two,
        new_master,
        new_bias,
    )


def solution(mesh):
    in_specs = (
        P(("dp", "cores"), None),
        P(("dp", "cores")),
        P(("dp", "cores")),
        P(("dp", "cores")),
        P(("dp", "cores")),
        P(("dp", "cores")),
    )
    out_specs = (
        P(("dp", "cores")),
        P(),
        P(("dp", "cores"), None),
        P(("dp", "cores")),
        P(("dp", "cores")),
        P(("dp", "cores")),
        P(("dp", "cores")),
        P(("dp", "cores")),
    )
    groups = bit_groups(mesh)
    step = functools.partial(local, groups)
    return jax.shard_map(step, mesh=mesh, in_specs=in_specs, out_specs=out_specs, check_vma=False)
```

```python
import functools
import math

import jax
import jax.numpy as jnp
from jax import lax
from jax.experimental import pallas as pl
from jax.experimental.pallas import tpu as pltpu
from jax.sharding import PartitionSpec as P

D = 1027
H = 1024
DAYS = 24
STEP = 10
AXES = ("dp", "cores")
EXTRA = D - H
LANES = 128
WIDE = H + LANES
AUX_ROWS = 16
SPILL_ROWS = 4
MISC_ROW = 12
UNIT_LINES = 15
TILE = 256
MIB = 1024 * 1024
F32 = jnp.float32
LOW = jnp.bfloat16
SMEM = pl.BlockSpec(memory_space=pltpu.SMEM)
VMEM = pl.BlockSpec(memory_space=pltpu.VMEM)
PARAMS = pltpu.CompilerParams(vmem_limit_bytes=56 * MIB)


def shapes():
    return [(D, D), (D,), (D, D), (D,), (D, H), (H,), (H, H), (H,), (H,), (1,)]


def piece_sizes(count):
    return [(math.prod(shape) + count - 1) // count for shape in shapes()[:-1]] + [1]


def starts_of(count):
    starts = []
    position = 0
    for piece in piece_sizes(count):
        starts.append(position)
        position += piece
    return starts


def to_block(piece, index, width, rows, count):
    excess = piece.shape[0] - rows * width
    size = (rows + SPILL_ROWS) * width
    lead = (count - 1) * excess
    padded = jnp.pad(piece, (lead, max(0, size - piece.shape[0])))
    line = lax.dynamic_slice(padded, (lead - index * excess,), (size,))
    return line.reshape(rows + SPILL_ROWS, width)


def from_block(block, index, piece, rows, count):
    width = block.shape[1]
    excess = piece - rows * width
    last = (count - 1) * excess
    line = jnp.pad(block.reshape(-1), (0, max(0, last + piece - block.size)))
    return lax.dynamic_slice(line, (index * excess,), (piece,))


def bit_groups(mesh):
    devices = mesh.devices.reshape(-1)
    groups = {"z": [], "plane": [], "core": []}
    bit = 1
    while bit < devices.size:
        here = getattr(devices[0], "coords", None)
        there = getattr(devices[bit], "coords", None)
        if here is None or there is None:
            name = "core" if bit == 1 else "plane" if bit <= 4 else "z"
        elif tuple(here) == tuple(there):
            name = "core"
        elif here[2] != there[2]:
            name = "z"
        else:
            name = "plane"
        groups[name].append(bit)
        bit *= 2
    return groups


def masks_of(bits):
    masks = [0]
    for bit in bits:
        masks = masks + [mask | bit for mask in masks]
    return masks


def swap(value, mask, count):
    return lax.ppermute(value, AXES, [(k, k ^ mask) for k in range(count)])


def gather(block, groups, count):
    z_masks = masks_of(groups["z"])
    core_masks = masks_of(groups["core"])
    line = jnp.stack([block] + [swap(block, mask, count) for mask in z_masks[1:]])
    plane = [(line, z_masks)]
    if len(groups["plane"]) == 2 and len(z_masks) > 1:
        one, two = groups["plane"]
        half = len(z_masks) // 2
        by_one = swap(line, one, count)
        by_two = swap(line, two, count)
        plane.append((by_one, [one ^ z for z in z_masks]))
        plane.append((by_two, [two ^ z for z in z_masks]))
        both = one ^ two
        plane.append((swap(by_one[:half], two, count), [both ^ z for z in z_masks[:half]]))
        plane.append((swap(by_two[half:], one, count), [both ^ z for z in z_masks[half:]]))
    else:
        for mask in masks_of(groups["plane"])[1:]:
            plane.append((swap(line, mask, count), [mask ^ z for z in z_masks]))
    result = list(plane)
    for core in core_masks[1:]:
        result += [(swap(value, core, count), [core ^ m for m in row]) for value, row in plane]
    return result


def place(index, stacks, rows, count, spill_at=None, aux=None):
    sources = [value for value, _ in stacks]
    masks = [row for _, row in stacks]
    carries = sources[0].shape[1] > rows
    top = min(16, rows)

    def kernel(index_ref, *refs):
        refs = list(refs)
        aux_ref = refs.pop() if carries else refs.pop(0) if aux is not None else None
        out_ref = refs.pop()
        for ref, row in zip(refs, masks):
            for j, mask in enumerate(row):
                at = jnp.bitwise_xor(index_ref[0], mask)
                out_ref[at] = ref[j, :rows]
                if carries:
                    aux_ref[at] = ref[j, rows:]
        if spill_at is not None:
            for k in range(1, count):
                spill = aux_ref[k - 1].astype(F32)[spill_at : spill_at + SPILL_ROWS]
                old = out_ref[k, :top].astype(F32)
                new = old[:SPILL_ROWS] + spill
                if top > SPILL_ROWS:
                    new = jnp.concatenate([new, old[SPILL_ROWS:]], axis=0)
                out_ref[k, :top] = new.astype(LOW)

    out_shape = [jax.ShapeDtypeStruct((count, rows, H), LOW)]
    if carries:
        out_shape.append(jax.ShapeDtypeStruct((count, AUX_ROWS, H), LOW))
    extra = [aux] if aux is not None and not carries else []
    result = pl.pallas_call(
        kernel,
        out_shape=out_shape,
        in_specs=[SMEM] + [VMEM] * (len(extra) + len(sources)),
        out_specs=[VMEM] * len(out_shape),
        compiler_params=PARAMS,
        name="place",
    )(index, *extra, *sources)
    matrix = result[0].reshape(H, H)
    return (matrix, result[1]) if carries else matrix


def split(index, value, masks, kinds):
    def kernel(index_ref, value_ref, *out_refs):
        for ref, row, kind in zip(out_refs, masks, kinds):
            for j, mask in enumerate(row):
                ref[j] = value_ref[jnp.bitwise_xor(index_ref[0], mask)].astype(kind)

    shape = value.shape[1:]
    return pl.pallas_call(
        kernel,
        out_shape=[
            jax.ShapeDtypeStruct((len(row),) + shape, kind) for row, kind in zip(masks, kinds)
        ],
        in_specs=[SMEM, VMEM],
        out_specs=[VMEM] * len(masks),
        compiler_params=PARAMS,
        name="split",
    )(index, value)


def scatter(value, index, groups, count):
    z_masks, plane_masks, core_masks = (masks_of(groups[g]) for g in ("z", "plane", "core"))
    inner = [p ^ z for p in plane_masks for z in z_masks]
    stacks = split(
        index,
        value,
        [[core ^ m for m in inner] for core in core_masks],
        [F32] + [LOW] * (len(core_masks) - 1),
    )
    kept = stacks[0]
    for core, stack in zip(core_masks[1:], stacks[1:]):
        kept = kept + swap(stack, core, count).astype(F32)
    kept = kept.reshape((len(plane_masks), len(z_masks)) + value.shape[1:])
    total = kept[0]
    if len(groups["plane"]) == 2 and len(z_masks) > 1:
        one, two = groups["plane"]
        half = len(z_masks) // 2
        from_two = swap(kept[3, :half].astype(LOW), two, count).astype(F32)
        from_one = swap(kept[3, half:].astype(LOW), one, count).astype(F32)
        send_one = jnp.concatenate([kept[1, :half] + from_two, kept[1, half:]]).astype(LOW)
        send_two = jnp.concatenate([kept[2, :half], kept[2, half:] + from_one]).astype(LOW)
        total = total + swap(send_one, one, count).astype(F32)
        total = total + swap(send_two, two, count).astype(F32)
    else:
        for j in range(1, len(plane_masks)):
            total = total + swap(kept[j].astype(LOW), plane_masks[j], count).astype(F32)
    own = total[0]
    for j in range(1, len(z_masks)):
        own = own + swap(total[j].astype(LOW), z_masks[j], count).astype(F32)
    return own


def total_of(value, count):
    bit = 1
    while bit < count:
        value = value + swap(value, bit, count)
        bit *= 2
    return value


def product(left, right):
    return lax.dot_general(left, right, (((1,), (0,)), ((), ())), preferred_element_type=F32)


def back(left, right):
    return lax.dot_general(left, right, (((1,), (1,)), ((), ())), preferred_element_type=F32)


def rows_product(left, right):
    return lax.dot_general(left, right, (((0,), (0,)), ((), ())), preferred_element_type=F32)


def keep_extra(value):
    lane = lax.broadcasted_iota(jnp.int32, value.shape, 1)
    return jnp.where(lane < EXTRA, value, 0.0)


def gelu_both(value):
    scale = math.sqrt(2.0 / math.pi)
    square = value * value
    curve = jnp.tanh(value * (scale + scale * 0.044715 * square))
    half = 0.5 * (1.0 + curve)
    slope = half + (0.5 * value) * (1.0 - curve * curve) * (scale + 3.0 * scale * 0.044715 * square)
    return value * half, slope


def by_rows(width):
    return pl.BlockSpec((TILE, width), lambda i: (i, 0))


def whole(*shape):
    return pl.BlockSpec(shape, lambda i: (0,) * len(shape))


CHUNKS = [(a, a + 256) for a in range(0, H, 256)]


def run(name, kernel, out_specs, out_shape, in_specs, flops, *args):
    moved = sum(a.size * a.dtype.itemsize for a in args)
    moved += sum(math.prod(o.shape) * o.dtype.itemsize for o in out_shape)
    return pl.pallas_call(
        kernel,
        grid=(args[0].shape[0] // TILE,),
        in_specs=in_specs,
        out_specs=out_specs,
        out_shape=out_shape,
        compiler_params=PARAMS,
        cost_estimate=pl.CostEstimate(flops=flops, bytes_accessed=moved, transcendentals=0),
        name=name,
    )(*args)


def shaped(kind, *shape):
    return jax.ShapeDtypeStruct(shape, kind)


def forward_one(features, matrix, tail, edge):
    batch = features.shape[0]

    def kernel(x_ref, w_ref, t_ref, e_ref, mixer_ref, low_ref):
        x = x_ref[...]
        for a, b in CHUNKS:
            mixer = product(x[:, :H], w_ref[:, a:b]) + product(x[:, H:], t_ref[:, a:b])
            mixer_ref[:, a:b] = mixer
            part = x[:, a:b].astype(F32)
            low_ref[:, a:b] = (part * mixer + part).astype(LOW)
        mixer = back(x, e_ref[...])
        mixer_ref[:, H:] = mixer
        part = x[:, H:].astype(F32)
        low_ref[:, H:] = (part * mixer + part).astype(LOW)

    return run(
        "forward_one",
        kernel,
        [by_rows(WIDE), by_rows(WIDE)],
        [shaped(F32, batch, WIDE), shaped(LOW, batch, WIDE)],
        [by_rows(WIDE), whole(H, H), whole(LANES, H), whole(LANES, WIDE)],
        2 * batch * WIDE * WIDE,
        features, matrix, tail, edge,
    )


def forward_two(features, mixer_one, layer_low, matrix, tail, edge):
    batch = features.shape[0]

    def kernel(x_ref, m_ref, l_ref, w_ref, t_ref, e_ref, mixer_ref, low_ref):
        low = l_ref[...]
        for a, b in CHUNKS:
            mixer = product(low[:, :H], w_ref[:, a:b]) + product(low[:, H:], t_ref[:, a:b])
            mixer_ref[:, a:b] = mixer
            part = x_ref[:, a:b].astype(F32)
            layer = part * m_ref[:, a:b] + part
            low_ref[:, a:b] = (part * mixer + layer).astype(LOW)
        mixer = back(low, e_ref[...])
        mixer_ref[:, H:] = mixer
        part = x_ref[:, H:].astype(F32)
        layer = part * m_ref[:, H:] + part
        low_ref[:, H:] = (part * mixer + layer).astype(LOW)

    return run(
        "forward_two",
        kernel,
        [by_rows(WIDE), by_rows(WIDE)],
        [shaped(F32, batch, WIDE), shaped(LOW, batch, WIDE)],
        [by_rows(WIDE)] * 3 + [whole(H, H), whole(LANES, H), whole(LANES, WIDE)],
        2 * batch * WIDE * WIDE,
        features, mixer_one, layer_low, matrix, tail, edge,
    )


def forward_deep(layer_low, matrix, tail):
    batch = layer_low.shape[0]

    def kernel(l_ref, w_ref, t_ref, hidden_ref, slope_ref):
        low = l_ref[...]
        for a, b in CHUNKS:
            value = product(low[:, :H], w_ref[:, a:b]) + product(low[:, H:], t_ref[:, a:b])
            hidden, slope = gelu_both(value)
            hidden_ref[:, a:b] = hidden.astype(LOW)
            slope_ref[:, a:b] = slope

    return run(
        "forward_deep",
        kernel,
        [by_rows(H), by_rows(H)],
        [shaped(LOW, batch, H), shaped(F32, batch, H)],
        [by_rows(WIDE), whole(H, H), whole(LANES, H)],
        2 * batch * WIDE * H,
        layer_low, matrix, tail,
    )


def top(hidden_one, slope_one, examples, matrix, lines, inverse):
    batch = hidden_one.shape[0]

    def kernel(h_ref, s_ref, x_ref, w_ref, n_ref, i_ref, logit_ref, back_ref, grad_ref, sum_ref):
        step = pl.program_id(0)

        @pl.when(step == 0)
        def _():
            grad_ref[...] = jnp.zeros_like(grad_ref)
            sum_ref[...] = jnp.zeros_like(sum_ref)

        hidden = h_ref[...]
        slopes = []
        twos = []
        logits = n_ref[2:3, 0:1]
        for a, b in CHUNKS:
            value = product(hidden, w_ref[:, a:b]) + n_ref[0:1, a:b]
            two, slope = gelu_both(value)
            two = two.astype(LOW).astype(F32)
            logits = logits + jnp.sum(two * n_ref[1:2, a:b], axis=1, keepdims=True)
            twos.append(two)
            slopes.append(slope)
        label = x_ref[:, 0:1]
        day = x_ref[:, 1:2].astype(jnp.int32)
        lane = lax.broadcasted_iota(jnp.int32, (TILE, LANES), 1)
        weight = jnp.sum(jnp.where(lane == day, i_ref[...], 0.0), axis=1, keepdims=True)
        decay = jnp.exp(-jnp.abs(logits))
        entropy = jnp.maximum(logits, 0.0) + jnp.log1p(decay) - label * logits
        chance = jnp.where(logits >= 0.0, 1.0, decay) / (1.0 + decay)
        logit_grad = (chance - label) * weight
        logit_ref[...] = logits
        sum_ref[2:3, 0:LANES] += jnp.broadcast_to(
            jnp.sum(logit_grad, axis=0, keepdims=True), (1, LANES)
        )
        sum_ref[2:3, LANES : 2 * LANES] += jnp.broadcast_to(
            jnp.sum(entropy * weight, axis=0, keepdims=True), (1, LANES)
        )
        lows = []
        for (a, b), two, slope in zip(CHUNKS, twos, slopes):
            low = ((logit_grad * n_ref[1:2, a:b]) * slope).astype(LOW)
            lows.append(low)
            sum_ref[0:1, a:b] += jnp.sum(low.astype(F32), axis=0, keepdims=True)
            sum_ref[1:2, a:b] += jnp.sum(logit_grad * two, axis=0, keepdims=True)
        low = jnp.concatenate(lows, axis=1)
        for a, b in CHUNKS:
            back_ref[:, a:b] = (back(low, w_ref[a:b, :]) * s_ref[:, a:b]).astype(LOW)
        grad_ref[...] += rows_product(hidden, low)

    return run(
        "top",
        kernel,
        [pl.BlockSpec((TILE, 1), lambda i: (i, 0)), by_rows(H), whole(H, H), whole(8, H)],
        [shaped(F32, batch, 1), shaped(LOW, batch, H), shaped(F32, H, H), shaped(F32, 8, H)],
        [
            by_rows(H),
            by_rows(H),
            pl.BlockSpec((TILE, 2), lambda i: (i, 0)),
            whole(H, H),
            whole(8, H),
            whole(1, LANES),
        ],
        6 * batch * H * H,
        hidden_one, slope_one, examples, matrix, lines, inverse,
    )


def back_deep(grad_low, layer_low, features, matrix, tail):
    batch = features.shape[0]

    def kernel(g_ref, l_ref, x_ref, w_ref, t_ref, grad_ref, layer_ref, mixer_ref):
        @pl.when(pl.program_id(0) == 0)
        def _():
            grad_ref[...] = jnp.zeros_like(grad_ref)

        low = g_ref[...]
        for a, b in CHUNKS:
            layer = back(low, w_ref[a:b, :])
            layer_ref[:, a:b] = layer
            mixer_ref[:, a:b] = (layer * x_ref[:, a:b].astype(F32)).astype(LOW)
        layer = keep_extra(back(low, t_ref[...]))
        layer_ref[:, H:] = layer
        mixer_ref[:, H:] = (layer * x_ref[:, H:].astype(F32)).astype(LOW)
        grad_ref[...] += rows_product(l_ref[...], low)

    return run(
        "back_deep",
        kernel,
        [whole(WIDE, H), by_rows(WIDE), by_rows(WIDE)],
        [shaped(F32, WIDE, H), shaped(F32, batch, WIDE), shaped(LOW, batch, WIDE)],
        [by_rows(H), by_rows(WIDE), by_rows(WIDE), whole(H, H), whole(LANES, H)],
        4 * batch * WIDE * H,
        grad_low, layer_low, features, matrix, tail,
    )


def back_two(mixer_low, layer_low, layer_grad, features, mixer_one, mixer_two, matrix, tail, edge):
    batch = features.shape[0]

    def kernel(
        g_ref, l_ref, d_ref, x_ref, one_ref, two_ref, w_ref, t_ref, e_ref,
        grad_ref, side_ref, part_ref, mixer_ref,
    ):
        @pl.when(pl.program_id(0) == 0)
        def _():
            grad_ref[...] = jnp.zeros_like(grad_ref)
            side_ref[...] = jnp.zeros_like(side_ref)

        low = g_ref[...]
        main, rest = low[:, :H], low[:, H:]

        def finish(a, b, layer):
            above = d_ref[:, a:b]
            layer = layer + above
            mixer_ref[:, a:b] = (layer * x_ref[:, a:b].astype(F32)).astype(LOW)
            part_ref[:, a:b] = above * two_ref[:, a:b] + layer * (one_ref[:, a:b] + 1.0)

        for a, b in CHUNKS:
            finish(a, b, back(main, w_ref[a:b, :]) + product(rest, e_ref[:, a:b]))
        finish(H, WIDE, keep_extra(back(main, t_ref[...]) + product(rest, e_ref[:, H:])))
        layer = l_ref[...]
        grad_ref[...] += rows_product(layer, main)
        side_ref[...] += rows_product(rest, layer)

    return run(
        "back_two",
        kernel,
        [whole(WIDE, H), whole(LANES, WIDE), by_rows(WIDE), by_rows(WIDE)],
        [
            shaped(F32, WIDE, H),
            shaped(F32, LANES, WIDE),
            shaped(F32, batch, WIDE),
            shaped(LOW, batch, WIDE),
        ],
        [by_rows(WIDE)] * 6 + [whole(H, H), whole(LANES, H), whole(LANES, WIDE)],
        4 * batch * WIDE * WIDE,
        mixer_low, layer_low, layer_grad, features, mixer_one, mixer_two, matrix, tail, edge,
    )


def grad_one(mixer_low, features):
    batch = features.shape[0]

    def kernel(g_ref, x_ref, grad_ref, side_ref):
        @pl.when(pl.program_id(0) == 0)
        def _():
            grad_ref[...] = jnp.zeros_like(grad_ref)
            side_ref[...] = jnp.zeros_like(side_ref)

        x = x_ref[...]
        grad_ref[...] += rows_product(x, g_ref[:, :H])
        side_ref[...] += rows_product(g_ref[:, H:], x)

    return run(
        "grad_one",
        kernel,
        [whole(WIDE, H), whole(LANES, WIDE)],
        [shaped(F32, WIDE, H), shaped(F32, LANES, WIDE)],
        [by_rows(WIDE), by_rows(WIDE)],
        2 * batch * WIDE * WIDE,
        mixer_low, features,
    )


def back_one(mixer_low, part, matrix, tail, edge):
    batch = part.shape[0]

    def kernel(g_ref, p_ref, w_ref, t_ref, e_ref, out_ref):
        main, rest = g_ref[:, :H], g_ref[:, H:]
        for a, b in CHUNKS:
            out_ref[:, a:b] = p_ref[:, a:b] + (
                back(main, w_ref[a:b, :]) + product(rest, e_ref[:, a:b])
            )
        last = p_ref[:, H:] + (back(main, t_ref[...]) + product(rest, e_ref[:, H:]))
        out_ref[:, H:] = last[:, :EXTRA]

    return run(
        "back_one",
        kernel,
        [by_rows(D)],
        [shaped(F32, batch, D)],
        [by_rows(WIDE), by_rows(WIDE), whole(H, H), whole(LANES, H), whole(LANES, WIDE)],
        2 * batch * WIDE * WIDE,
        mixer_low, part, matrix, tail, edge,
    )[0]


def local(groups, features, labels, days, master, moment_one, moment_two):
    count = lax.axis_size(AXES)
    index = lax.axis_index(AXES)
    slot = index[None].astype(jnp.int32)
    rows = H // count
    starts = starts_of(count)
    sizes = piece_sizes(count)
    wide_piece = sizes[1]
    piece = [master[a : a + l] for a, l in zip(starts, sizes)]
    block_one = to_block(piece[0], index, D, rows, count)
    block_two = to_block(piece[2], index, D, rows, count)
    block_deep = to_block(piece[4], index, H, rows, count)

    day_hot = (days[:, None] == jnp.arange(DAYS, dtype=jnp.int32)[None, :]).astype(F32)
    own_counts = jnp.sum(day_hot, axis=0)
    counts_high = jnp.floor(own_counts / 64.0)
    counts_low = own_counts - 64.0 * counts_high

    def spill_side(block):
        side = block[rows:, H:].T
        return jnp.pad(side, ((0, 0), (0, rows - SPILL_ROWS)))

    misc = [
        piece[5],
        piece[7],
        piece[8],
        block_one[:rows, H:].T,
        block_two[:rows, H:].T,
        spill_side(block_one),
        spill_side(block_two),
        piece[1],
        piece[3],
        piece[9],
        counts_high,
        counts_low,
    ]
    misc = jnp.concatenate([part.reshape(-1) for part in misc])
    misc = jnp.pad(misc, (0, (AUX_ROWS - MISC_ROW) * H - misc.shape[0])).reshape(-1, H)
    first = jnp.concatenate(
        [block_one[:rows, :H], block_one[rows:, :H], block_two[rows:, :H], block_deep[rows:], misc]
    ).astype(LOW)
    stacks_one = gather(first, groups, count)
    stacks_two = gather(block_two[:rows, :H].astype(LOW), groups, count)
    stacks_deep = gather(block_deep[:rows].astype(LOW), groups, count)
    stacks_top = gather(piece[6].reshape(rows, H).astype(LOW), groups, count)

    wide_features = jnp.concatenate(
        [
            features,
            jnp.ones((features.shape[0], 1), LOW),
            jnp.zeros((features.shape[0], WIDE - D - 1), LOW),
        ],
        axis=1,
    )
    examples = jnp.stack([labels.astype(F32), days.astype(F32)], axis=1)

    matrix_one, aux = place(slot, stacks_one, rows, count, spill_at=0)
    matrix_two = place(slot, stacks_two, rows, count, spill_at=SPILL_ROWS, aux=aux)
    matrix_deep = place(slot, stacks_deep, rows, count, spill_at=2 * SPILL_ROWS, aux=aux)
    matrix_top = place(slot, stacks_top, rows, count)

    line = aux[:, MISC_ROW]
    at = UNIT_LINES * rows
    units = line[:, :at].reshape(count, UNIT_LINES, rows).transpose(1, 0, 2).reshape(UNIT_LINES, H)
    biases = line[:, at : at + 2 * wide_piece].reshape(count, 2, wide_piece)
    biases = biases.transpose(1, 0, 2).reshape(2, count * wide_piece)
    at += 2 * wide_piece
    head_bias = line[0, at]
    both_counts = jnp.sum(line[:, at + 1 : at + 1 + 2 * DAYS].astype(F32), axis=0)
    counts = 64.0 * both_counts[:DAYS] + both_counts[DAYS:]
    inverse = jnp.pad(1.0 / counts, (0, LANES - DAYS))[None]
    sides = jnp.pad(units[3:9], ((0, 0), (0, LANES))) + jnp.pad(
        units[9:15], ((0, 0), (rows, LANES - rows))
    )

    def tail_of(at, bias):
        return jnp.concatenate(
            [aux[count - 1, at : at + EXTRA], bias[None, :H], jnp.zeros((LANES - EXTRA - 1, H), LOW)]
        )

    def edge_of(side, bias):
        lane = lax.broadcasted_iota(jnp.int32, side.shape, 1)
        side = jnp.where(lane == D, bias[H:D, None], side)
        return jnp.pad(side, ((0, LANES - EXTRA), (0, 0)))

    tail_one, edge_one = tail_of(0, biases[0]), edge_of(sides[:3], biases[0])
    tail_two, edge_two = tail_of(SPILL_ROWS, biases[1]), edge_of(sides[3:], biases[1])
    tail_deep = tail_of(2 * SPILL_ROWS, units[0])
    lines = jnp.concatenate(
        [units[1:3], jnp.full((1, H), head_bias), jnp.zeros((5, H), LOW)]
    ).astype(F32)

    mixer_one, low_one = forward_one(wide_features, matrix_one, tail_one, edge_one)
    mixer_two, low_two = forward_two(
        wide_features, mixer_one, low_one, matrix_two, tail_two, edge_two
    )
    hidden_one, slope_one = forward_deep(low_two, matrix_deep, tail_deep)
    logits, pre_one_low, top_grad, sums = top(
        hidden_one, slope_one, examples, matrix_top, lines, inverse
    )
    loss = total_of(sums[2, LANES], count)
    deep_grad, layer_grad, mixer_two_low = back_deep(
        pre_one_low, low_two, wide_features, matrix_deep, tail_deep
    )
    two_grad, two_side, part, mixer_one_low = back_two(
        mixer_two_low, low_one, layer_grad, wide_features, mixer_one, mixer_two,
        matrix_two, tail_two, edge_two,
    )
    one_grad, one_side = grad_one(mixer_one_low, wide_features)
    feature_grad = back_one(mixer_one_low, part, matrix_one, tail_one, edge_one)

    def by_device(matrix):
        return matrix[:H].reshape(count, rows, H)

    def overlap(matrix):
        body = matrix[:H].reshape(count, rows, H)[1:, :SPILL_ROWS]
        end = jnp.pad(matrix[H:D], ((0, SPILL_ROWS - EXTRA), (0, 0)))[None]
        return jnp.concatenate([body, end])

    own_top = scatter(top_grad.reshape(count, rows, H), slot, groups, count)
    own_deep = scatter(by_device(deep_grad), slot, groups, count)
    own_two = scatter(by_device(two_grad), slot, groups, count)
    sides = jnp.concatenate([one_side[:3], two_side[:3]])
    unit_lines = jnp.concatenate(
        [deep_grad[D : D + 1], sums[:2], sides[:, :H], sides[:, rows : rows + H]]
    )
    unit_lines = unit_lines.at[9:, H - rows + EXTRA :].set(0.0)
    unit_lines = unit_lines.reshape(UNIT_LINES, count, rows).transpose(1, 0, 2).reshape(count, -1)
    wide_lines = jnp.stack(
        [
            jnp.concatenate([one_grad[D], one_side[:3, D]]),
            jnp.concatenate([two_grad[D], two_side[:3, D]]),
        ]
    )
    wide_lines = jnp.pad(wide_lines, ((0, 0), (0, count * wide_piece - D)))
    wide_lines = wide_lines.reshape(2, count, wide_piece).transpose(1, 0, 2).reshape(count, -1)
    bias_line = jnp.pad(sums[2:3, :1], ((0, count - 1), (0, 0)))
    misc = jnp.concatenate([unit_lines, wide_lines, bias_line], axis=1)
    misc = jnp.pad(misc, ((0, 0), (0, (AUX_ROWS - MISC_ROW) * H - misc.shape[1])))
    last = jnp.concatenate(
        [
            by_device(one_grad),
            overlap(one_grad),
            overlap(two_grad),
            overlap(deep_grad),
            misc.reshape(count, AUX_ROWS - MISC_ROW, H),
        ],
        axis=1,
    )
    own_last = scatter(last, slot, groups, count)
    own_one = own_last[:rows]
    spills = own_last[rows : rows + MISC_ROW]
    misc = own_last[rows + MISC_ROW :].reshape(-1)
    at = UNIT_LINES * rows
    units = misc[:at].reshape(UNIT_LINES, rows)

    def whole_block(main, number):
        low = number * SPILL_ROWS
        body = jnp.concatenate([main, spills[low : low + SPILL_ROWS]])
        if number == 2:
            return body
        low = 3 * number
        side = jnp.concatenate([units[3 + low : 6 + low], units[9 + low : 12 + low, :SPILL_ROWS]], 1)
        return jnp.concatenate([body, side.T], axis=1)

    flat_grad = jnp.concatenate(
        [
            from_block(whole_block(own_one, 0), index, sizes[0], rows, count),
            misc[at : at + wide_piece],
            from_block(whole_block(own_two, 1), index, sizes[2], rows, count),
            misc[at + wide_piece : at + 2 * wide_piece],
            from_block(whole_block(own_deep, 2), index, sizes[4], rows, count),
            units[0],
            own_top.reshape(-1),
            units[1],
            units[2],
            misc[at + 2 * wide_piece : at + 2 * wide_piece + 1],
        ]
    )
    new_moment_one = 0.9 * moment_one + 0.1 * flat_grad
    new_moment_two = 0.999 * moment_two + 0.001 * flat_grad * flat_grad
    corrected_one = new_moment_one / (1.0 - 0.9**STEP)
    corrected_two = new_moment_two / (1.0 - 0.999**STEP)
    new_master = master - 0.03 * (corrected_one / (jnp.sqrt(corrected_two) + 1e-08) + 0.01 * master)
    new_bias = jnp.concatenate(
        [new_master[starts[i] : starts[i] + sizes[i]] for i in (1, 3, 5, 7, 9)]
    )
    return (
        logits.reshape(-1),
        loss,
        feature_grad,
        flat_grad,
        new_moment_one,
        new_moment_two,
        new_master,
        new_bias,
    )


def solution(mesh):
    line = P(AXES)
    table = P(AXES, None)
    groups = bit_groups(mesh)
    return jax.shard_map(
        functools.partial(local, groups),
        mesh=mesh,
        in_specs=(table, line, line, line, line, line),
        out_specs=(line, P(), table, line, line, line, line, line),
        check_vma=False,
    )
```

```python
import functools
import math

import jax
import jax.numpy as jnp
from jax import lax
from jax.experimental import pallas as pl
from jax.experimental.pallas import tpu as pltpu
from jax.sharding import PartitionSpec as P

D = 1027
H = 1024
DAYS = 24
STEP = 10
AXES = ("dp", "cores")
EXTRA = D - H
LANES = 128
WIDE = H + LANES
AUX_ROWS = 16
SPILL_ROWS = 4
MISC_ROW = 12
UNIT_LINES = 15
TILE = 512
TALL = H + 16
MIB = 1024 * 1024
F32 = jnp.float32
LOW = jnp.bfloat16
SMEM = pl.BlockSpec(memory_space=pltpu.SMEM)
VMEM = pl.BlockSpec(memory_space=pltpu.VMEM)
PARAMS = pltpu.CompilerParams(vmem_limit_bytes=56 * MIB)


def shapes():
    return [(D, D), (D,), (D, D), (D,), (D, H), (H,), (H, H), (H,), (H,), (1,)]


def piece_sizes(count):
    return [(math.prod(shape) + count - 1) // count for shape in shapes()[:-1]] + [1]


def starts_of(count):
    starts = []
    position = 0
    for piece in piece_sizes(count):
        starts.append(position)
        position += piece
    return starts


def to_block(piece, index, width, rows, count):
    excess = piece.shape[0] - rows * width
    size = (rows + SPILL_ROWS) * width
    lead = (count - 1) * excess
    padded = jnp.pad(piece, (lead, max(0, size - piece.shape[0])))
    line = lax.dynamic_slice(padded, (lead - index * excess,), (size,))
    return line.reshape(rows + SPILL_ROWS, width)


def from_block(block, index, piece, rows, count):
    width = block.shape[1]
    excess = piece - rows * width
    last = (count - 1) * excess
    line = jnp.pad(block.reshape(-1), (0, max(0, last + piece - block.size)))
    return lax.dynamic_slice(line, (index * excess,), (piece,))


def bit_groups(mesh):
    devices = mesh.devices.reshape(-1)
    groups = {"z": [], "plane": [], "core": []}
    bit = 1
    while bit < devices.size:
        here = getattr(devices[0], "coords", None)
        there = getattr(devices[bit], "coords", None)
        if here is None or there is None:
            name = "core" if bit == 1 else "plane" if bit <= 4 else "z"
        elif tuple(here) == tuple(there):
            name = "core"
        elif here[2] != there[2]:
            name = "z"
        else:
            name = "plane"
        groups[name].append(bit)
        bit *= 2
    return groups


def masks_of(bits):
    masks = [0]
    for bit in bits:
        masks = masks + [mask | bit for mask in masks]
    return masks


def swap(value, mask, count):
    return lax.ppermute(value, AXES, [(k, k ^ mask) for k in range(count)])


def gather(block, groups, count):
    z_masks = masks_of(groups["z"])
    core_masks = masks_of(groups["core"])
    line = jnp.stack([block] + [swap(block, mask, count) for mask in z_masks[1:]])
    plane = [(line, z_masks)]
    if len(groups["plane"]) == 2 and len(z_masks) > 1:
        one, two = groups["plane"]
        half = len(z_masks) // 2
        by_one = swap(line, one, count)
        by_two = swap(line, two, count)
        plane.append((by_one, [one ^ z for z in z_masks]))
        plane.append((by_two, [two ^ z for z in z_masks]))
        both = one ^ two
        plane.append((swap(by_one[:half], two, count), [both ^ z for z in z_masks[:half]]))
        plane.append((swap(by_two[half:], one, count), [both ^ z for z in z_masks[half:]]))
    else:
        for mask in masks_of(groups["plane"])[1:]:
            plane.append((swap(line, mask, count), [mask ^ z for z in z_masks]))
    result = list(plane)
    for core in core_masks[1:]:
        result += [(swap(value, core, count), [core ^ m for m in row]) for value, row in plane]
    return result


def place(index, stacks, rows, count, parts, aux=None):
    sources = [value for value, _ in stacks]
    masks = [row for _, row in stacks]
    carries = aux is None
    top = min(16, rows)

    def kernel(index_ref, *refs):
        refs = list(refs)
        aux_ref = refs.pop() if carries else refs.pop(0)
        outs = refs[len(sources) :]
        for ref, row in zip(refs, masks):
            for j, mask in enumerate(row):
                at = jnp.bitwise_xor(index_ref[0], mask)
                for i, out_ref in enumerate(outs):
                    out_ref[at] = ref[j, i * rows : (i + 1) * rows]
                if carries:
                    aux_ref[at] = ref[j, len(outs) * rows :]
        for spill_at, out_ref in zip(parts, outs):
            if spill_at is None:
                continue
            for k in range(1, count):
                spill = aux_ref[k - 1].astype(F32)[spill_at : spill_at + SPILL_ROWS]
                old = out_ref[k, :top].astype(F32)
                new = old[:SPILL_ROWS] + spill
                if top > SPILL_ROWS:
                    new = jnp.concatenate([new, old[SPILL_ROWS:]], axis=0)
                out_ref[k, :top] = new.astype(LOW)

    out_shape = [jax.ShapeDtypeStruct((count, rows, H), LOW)] * len(parts)
    if carries:
        out_shape.append(jax.ShapeDtypeStruct((count, AUX_ROWS, H), LOW))
    extra = [] if carries else [aux]
    result = pl.pallas_call(
        kernel,
        out_shape=out_shape,
        in_specs=[SMEM] + [VMEM] * (len(extra) + len(sources)),
        out_specs=[VMEM] * len(out_shape),
        compiler_params=PARAMS,
        name="place",
    )(index, *extra, *sources)
    return [value.reshape(H, H) for value in result[: len(parts)]] + list(result[len(parts) :])


def split(index, value, masks, kinds):
    def kernel(index_ref, value_ref, *out_refs):
        for ref, row, kind in zip(out_refs, masks, kinds):
            for j, mask in enumerate(row):
                ref[j] = value_ref[jnp.bitwise_xor(index_ref[0], mask)].astype(kind)

    shape = value.shape[1:]
    return pl.pallas_call(
        kernel,
        out_shape=[
            jax.ShapeDtypeStruct((len(row),) + shape, kind) for row, kind in zip(masks, kinds)
        ],
        in_specs=[SMEM, VMEM],
        out_specs=[VMEM] * len(masks),
        compiler_params=PARAMS,
        name="split",
    )(index, value)


def halves(groups):
    z_masks, plane_masks, core_masks = (masks_of(groups[g]) for g in ("z", "plane", "core"))
    inner = [p ^ z for p in plane_masks for z in z_masks]
    return [[core ^ m for m in inner] for core in core_masks]


def kinds_of(groups):
    return [F32] + [LOW] * (len(halves(groups)) - 1)


def core_stage(stacks, groups, count):
    z_masks, plane_masks, core_masks = (masks_of(groups[g]) for g in ("z", "plane", "core"))
    kept = stacks[0]
    for core, stack in zip(core_masks[1:], stacks[1:]):
        kept = kept + swap(stack, core, count).astype(F32)
    kept = kept.reshape((len(plane_masks), len(z_masks)) + kept.shape[1:])
    return [kept[0]] + [kept[j].astype(LOW) for j in range(1, len(plane_masks))]


def plane_stage(parts, groups, count):
    total = parts[0]
    for mask, part in zip(masks_of(groups["plane"])[1:], parts[1:]):
        total = total + swap(part, mask, count).astype(F32)
    return [total[0]] + [total[j].astype(LOW) for j in range(1, total.shape[0])]


def z_stage(parts, groups, count):
    own = parts[0]
    for mask, part in zip(masks_of(groups["z"])[1:], parts[1:]):
        own = own + swap(part, mask, count).astype(F32)
    return own


def product(left, right):
    return lax.dot_general(left, right, (((1,), (0,)), ((), ())), preferred_element_type=F32)


def outer(left, right):
    return lax.dot_general(left, right, (((1,), (1,)), ((), ())), preferred_element_type=F32)


def gelu_both(value):
    scale = math.sqrt(2.0 / math.pi)
    square = value * value
    curve = jnp.tanh(value * (scale + scale * 0.044715 * square))
    half = 0.5 * (1.0 + curve)
    slope = half + (0.5 * value) * (1.0 - curve * curve) * (scale + 3.0 * scale * 0.044715 * square)
    return value * half, slope


def columns(height, tile=TILE):
    return pl.BlockSpec((height, tile), lambda i: (0, i))


def whole(*shape):
    return pl.BlockSpec(shape, lambda i: (0,) * len(shape))


def shaped(kind, *shape):
    return jax.ShapeDtypeStruct(shape, kind)


def pieces_of(width):
    return [(a, a + 256) for a in range(0, width, 256)]


def run(name, kernel, batch, in_specs, out_specs, out_shape, scratch, flops, *args, tile=TILE):
    moved = sum(a.size * a.dtype.itemsize for a in args)
    moved += sum(math.prod(o.shape) * o.dtype.itemsize for o in out_shape)
    return pl.pallas_call(
        kernel,
        grid=(batch // tile,),
        in_specs=in_specs,
        out_specs=out_specs,
        out_shape=out_shape,
        scratch_shapes=scratch,
        compiler_params=PARAMS,
        cost_estimate=pl.CostEstimate(flops=flops, bytes_accessed=moved, transcendentals=0),
        name=name,
    )(*args)


def first_step():
    return pl.when(pl.program_id(0) == 0)


def last_step():
    return pl.when(pl.program_id(0) == pl.num_programs(0) - 1)


def turn(out_ref, matrix_ref, tail_ref=None, edge_ref=None):
    for a, b in pieces_of(H):
        out_ref[a:b, :H] = matrix_ref[:, a:b].T
    if tail_ref is not None:
        out_ref[:H, H:] = tail_ref[...].T
    if edge_ref is not None:
        out_ref[H:, :] = edge_ref[...]


def straight(out_ref, matrix_ref, tail_ref, edge_ref=None):
    out_ref[:H, :H] = matrix_ref[...]
    row = lax.broadcasted_iota(jnp.int32, (TALL - H, H), 0)
    tail = tail_ref[: TALL - H, :].astype(F32)
    out_ref[H:, :H] = jnp.where(row < EXTRA, tail, 0.0).astype(LOW)
    if edge_ref is not None:
        lane = lax.broadcasted_iota(jnp.int32, (TALL - H, WIDE), 1)
        edge = jnp.where(lane < D, edge_ref[...].astype(F32), 0.0)
        edge = jnp.concatenate([edge, jnp.zeros((LANES - (TALL - H), WIDE), F32)])
        out_ref[:, H:] = edge.T[:TALL].astype(LOW)


class Spread:
    def __init__(self, groups, rows, count):
        self.masks = halves(groups)
        self.kinds = kinds_of(groups)
        self.rows, self.count = rows, count
        self.direct = rows % 16 == 0

    def shapes(self, below=False):
        if not self.direct:
            return [shaped(F32, TALL, H)]
        height = self.rows + (AUX_ROWS if below else 0)
        outs = [shaped(kind, len(row), height, H) for row, kind in zip(self.masks, self.kinds)]
        return outs if below else outs + [shaped(F32, self.count, 8, H)]

    def specs(self, below=False):
        return [whole(*s.shape) for s in self.shapes(below)]

    def write(self, acc_ref, index_ref, out_refs, over_refs=None):
        if not self.direct:
            out_refs[0][...] = acc_ref[...]
            return
        rows = self.rows
        for ref, row, kind in zip(out_refs, self.masks, self.kinds):
            for j, mask in enumerate(row):
                at = jnp.bitwise_xor(index_ref[0], mask)
                start = pl.multiple_of(at * rows, rows)
                ref[j, :rows] = acc_ref[pl.ds(start, rows), :].astype(kind)
                if over_refs is not None:
                    mine = acc_ref[pl.ds(pl.multiple_of(start + rows, 8), 8), :]
                    parts = [mine[:SPILL_ROWS]] + [v[at][:SPILL_ROWS] for v in over_refs]
                    parts.append(jnp.zeros((AUX_ROWS - MISC_ROW, H), F32))
                    ref[j, rows:] = jnp.concatenate(parts).astype(kind)
        if over_refs is None:
            for k in range(self.count):
                out_refs[-1][k] = acc_ref[(k + 1) * rows : (k + 1) * rows + 8, :]

    def finish(self, outs, index, overs=None):
        if self.direct:
            return list(outs)
        grad, rows, count = outs[0], self.rows, self.count
        blocks = grad[:H].reshape(count, rows, H)
        over = jnp.stack([grad[(k + 1) * rows : (k + 1) * rows + 8] for k in range(count)])
        if overs is not None:
            sides = [v[:, :SPILL_ROWS] for v in (over, overs[0], overs[1])]
            sides.append(jnp.zeros((count, AUX_ROWS - MISC_ROW, H), F32))
            blocks = jnp.concatenate([blocks] + sides, axis=1)
        stacks = list(split(index, blocks, self.masks, self.kinds))
        return stacks if overs is not None else stacks + [over]


ANY = pl.BlockSpec(memory_space=pl.ANY)
REST = TALL - H


def forward_one(features, matrix, tail, edge):
    batch = features.shape[1]

    def kernel(f_ref, w_ref, t_ref, e_ref, x_ref, mixer_ref, low_ref, turned):
        @first_step()
        def _():
            turn(turned, w_ref, t_ref, e_ref)

        x_ref[:H] = f_ref[:H]
        last = f_ref[H:].astype(F32)
        last = jnp.concatenate([last, jnp.ones((1, TILE), F32), jnp.zeros((TALL - D - 1, TILE), F32)])
        x_ref[H:] = last.astype(LOW)
        for a, b in pieces_of(TILE):
            mixer = product(turned[:, :TALL], x_ref[:, a:b])
            mixer_ref[:, a:b] = mixer
            part = x_ref[:, a:b].astype(F32)
            low_ref[:, a:b] = (part * mixer + part).astype(LOW)

    return run(
        "forward_one",
        kernel,
        batch,
        [columns(D), whole(H, H), whole(LANES, H), whole(REST, WIDE)],
        [columns(TALL)] * 3,
        [shaped(LOW, TALL, batch), shaped(F32, TALL, batch), shaped(LOW, TALL, batch)],
        [pltpu.VMEM((TALL, WIDE), LOW)],
        2 * batch * TALL * TALL,
        features, matrix, tail, edge,
    )


def forward_two(features, mixer_one, layer_low, matrix, tail, edge):
    batch = features.shape[1]

    def kernel(x_ref, m_ref, l_ref, w_ref, t_ref, e_ref, mixer_ref, low_ref, turned):
        @first_step()
        def _():
            turn(turned, w_ref, t_ref, e_ref)

        for a, b in pieces_of(TILE):
            mixer = product(turned[:, :TALL], l_ref[:, a:b])
            mixer_ref[:, a:b] = mixer
            part = x_ref[:, a:b].astype(F32)
            layer = part * m_ref[:, a:b] + part
            low_ref[:, a:b] = (part * mixer + layer).astype(LOW)

    return run(
        "forward_two",
        kernel,
        batch,
        [columns(TALL)] * 3 + [whole(H, H), whole(LANES, H), whole(REST, WIDE)],
        [columns(TALL), columns(TALL)],
        [shaped(F32, TALL, batch), shaped(LOW, TALL, batch)],
        [pltpu.VMEM((TALL, WIDE), LOW)],
        2 * batch * TALL * TALL,
        features, mixer_one, layer_low, matrix, tail, edge,
    )


def forward_deep(layer_low, matrix, tail):
    batch = layer_low.shape[1]

    def kernel(l_ref, w_ref, t_ref, hidden_ref, slope_ref, turned):
        @first_step()
        def _():
            turn(turned, w_ref, t_ref)

        for a, b in pieces_of(TILE):
            hidden, slope = gelu_both(product(turned[:, :TALL], l_ref[:, a:b]))
            hidden_ref[:H, a:b] = hidden.astype(LOW)
            slope_ref[:, a:b] = slope
        row = lax.broadcasted_iota(jnp.int32, (REST, TILE), 0)
        hidden_ref[H:] = jnp.where(row == 0, 1.0, 0.0).astype(LOW)

    return run(
        "forward_deep",
        kernel,
        batch,
        [columns(TALL), whole(H, H), whole(LANES, H)],
        [columns(TALL), columns(H)],
        [shaped(LOW, TALL, batch), shaped(F32, H, batch)],
        [pltpu.VMEM((H, WIDE), LOW)],
        2 * batch * TALL * H,
        layer_low, matrix, tail,
    )


def top(spread, index, hidden_one, slope_one, examples, matrix, lines, inverse):
    batch = hidden_one.shape[1]
    days = inverse.shape[0]

    def kernel(k_ref, h_ref, s_ref, x_ref, w_ref, n_ref, i_ref, *refs):
        logit_ref, back_ref, line_ref, sum_ref = refs[:4]
        out_refs = refs[4:-5]
        turned, acc_ref, low_ref, two_ref, part_ref = refs[-5:]

        @first_step()
        def _():
            turn(turned, w_ref)
            acc_ref[...] = jnp.zeros_like(acc_ref)
            sum_ref[...] = jnp.zeros_like(sum_ref)
            part_ref[...] = jnp.zeros_like(part_ref)

        head = n_ref[:, 1:2]
        for a, b in pieces_of(TILE):
            two, slope = gelu_both(product(turned[...], h_ref[:H, a:b]) + n_ref[:, 0:1])
            two = two.astype(LOW).astype(F32)
            logits = n_ref[0:1, 2:3] + jnp.sum(two * head, axis=0, keepdims=True)
            label = x_ref[0:1, a:b]
            day = x_ref[1:2, a:b].astype(jnp.int32)
            row = lax.broadcasted_iota(jnp.int32, (days, b - a), 0)
            weight = jnp.sum(jnp.where(row == day, i_ref[:, 0:1], 0.0), axis=0, keepdims=True)
            decay = jnp.exp(-jnp.abs(logits))
            entropy = jnp.maximum(logits, 0.0) + jnp.log1p(decay) - label * logits
            chance = jnp.where(logits >= 0.0, 1.0, decay) / (1.0 + decay)
            logit_grad = (chance - label) * weight
            logit_ref[:, a:b] = logits
            sum_ref[0:1, a:b] += logit_grad
            sum_ref[1:2, a:b] += entropy * weight
            low_ref[:, a:b] = ((logit_grad * head) * slope).astype(LOW)
            one = logit_grad * two
            part = one[:, :LANES]
            for at in range(LANES, b - a, LANES):
                part = part + one[:, at : at + LANES]
            part_ref[...] += part
        for a, b in pieces_of(TILE):
            back_ref[:, a:b] = (product(w_ref[...], low_ref[:, a:b]) * s_ref[:, a:b]).astype(LOW)
        for a, b in pieces_of(H):
            acc_ref[:, a:b] += outer(h_ref[...], low_ref[a:b])

        @last_step()
        def _():
            line_ref[0:8] = jnp.broadcast_to(
                jnp.sum(part_ref[...].T, axis=0, keepdims=True), (8, H)
            )
            line_ref[8:16] = acc_ref[H : H + 8]
            spread.write(acc_ref, k_ref, out_refs)

    return run(
        "top",
        kernel,
        batch,
        [
            SMEM,
            columns(TALL),
            columns(H),
            columns(2),
            whole(H, H),
            whole(H, LANES),
            whole(days, LANES),
        ],
        [columns(1), columns(H), whole(16, H), whole(8, TILE)] + spread.specs(),
        [
            shaped(F32, 1, batch),
            shaped(LOW, H, batch),
            shaped(F32, 16, H),
            shaped(F32, 8, TILE),
        ]
        + spread.shapes(),
        [
            pltpu.VMEM((H, H), LOW),
            pltpu.VMEM((TALL, H), F32),
            pltpu.VMEM((H, TILE), LOW),
            pltpu.VMEM((8, LANES), F32),
            pltpu.VMEM((H, LANES), F32),
        ],
        6 * batch * H * H,
        index, hidden_one, slope_one, examples, matrix, lines, inverse,
    )


def back_deep(spread, index, grad_low, layer_low, features, matrix, tail):
    batch = features.shape[1]

    def kernel(k_ref, g_ref, l_ref, x_ref, w_ref, t_ref, *refs):
        layer_ref, mixer_ref, line_ref = refs[:3]
        out_refs = refs[3:-2]
        held, acc_ref = refs[-2:]

        @first_step()
        def _():
            straight(held, w_ref, t_ref)
            acc_ref[...] = jnp.zeros_like(acc_ref)

        for a, b in pieces_of(TILE):
            layer = product(held[...], g_ref[:, a:b])
            layer_ref[:, a:b] = layer
            mixer_ref[:, a:b] = (layer * x_ref[:, a:b].astype(F32)).astype(LOW)
        for a, b in pieces_of(H):
            acc_ref[:, a:b] += outer(l_ref[...], g_ref[a:b])

        @last_step()
        def _():
            line_ref[...] = acc_ref[H:]
            spread.write(acc_ref, k_ref, out_refs)

    return run(
        "back_deep",
        kernel,
        batch,
        [SMEM, columns(H), columns(TALL), columns(TALL), whole(H, H), whole(LANES, H)],
        [columns(TALL), columns(TALL), whole(REST, H)] + spread.specs(),
        [shaped(F32, TALL, batch), shaped(LOW, TALL, batch), shaped(F32, REST, H)]
        + spread.shapes(),
        [pltpu.VMEM((TALL, H), LOW), pltpu.VMEM((TALL, H), F32)],
        4 * batch * TALL * H,
        index, grad_low, layer_low, features, matrix, tail,
    )


def back_two(
    spread, index, mixer_low, layer_low, layer_grad, features, mixer_one, mixer_two, matrix, tail,
    edge, after,
):
    batch = features.shape[1]
    tile = TILE // 2

    def kernel(k_ref, g_ref, l_ref, d_ref, x_ref, one_ref, two_ref, w_ref, t_ref, e_ref, *refs):
        part_ref, mixer_ref, side_ref, line_ref = refs[len(after) : len(after) + 4]
        out_refs = refs[len(after) + 4 : -2]
        held, acc_ref = refs[-2:]

        @first_step()
        def _():
            straight(held, w_ref, t_ref, e_ref)
            acc_ref[...] = jnp.zeros_like(acc_ref)
            side_ref[...] = jnp.zeros_like(side_ref)

        for a, b in pieces_of(tile):
            above = d_ref[:, a:b]
            layer = product(held[:, :TALL], g_ref[:, a:b]) + above
            mixer_ref[:, a:b] = (layer * x_ref[:, a:b].astype(F32)).astype(LOW)
            part_ref[:, a:b] = above * two_ref[:, a:b] + layer * (one_ref[:, a:b] + 1.0)
        for a, b in pieces_of(H):
            acc_ref[:, a:b] += outer(l_ref[...], g_ref[a:b])
        side_ref[...] += outer(g_ref[H:], l_ref[...])

        @last_step()
        def _():
            line_ref[...] = acc_ref[H:]
            spread.write(acc_ref, k_ref, out_refs)

    return run(
        "back_two",
        kernel,
        batch,
        [SMEM]
        + [columns(TALL, tile)] * 6
        + [whole(H, H), whole(LANES, H), whole(REST, WIDE)]
        + [ANY] * len(after),
        [columns(TALL, tile), columns(TALL, tile), whole(REST, TALL), whole(REST, H)]
        + spread.specs(),
        [
            shaped(F32, TALL, batch),
            shaped(LOW, TALL, batch),
            shaped(F32, REST, TALL),
            shaped(F32, REST, H),
        ]
        + spread.shapes(),
        [pltpu.VMEM((TALL, WIDE), LOW), pltpu.VMEM((TALL, H), F32)],
        4 * batch * TALL * TALL,
        index, mixer_low, layer_low, layer_grad, features, mixer_one, mixer_two, matrix, tail,
        edge, *after,
        tile=tile,
    )


def grad_one(spread, index, mixer_low, features, overs, after):
    batch = features.shape[1]

    def kernel(k_ref, g_ref, x_ref, *refs):
        over_refs = refs[: len(overs)]
        refs = refs[len(overs) + len(after) :]
        side_ref, line_ref = refs[:2]
        out_refs = refs[2:-1]
        acc_ref = refs[-1]

        @first_step()
        def _():
            acc_ref[...] = jnp.zeros_like(acc_ref)
            side_ref[...] = jnp.zeros_like(side_ref)

        for a, b in pieces_of(H):
            acc_ref[:, a:b] += outer(x_ref[...], g_ref[a:b])
        side_ref[...] += outer(g_ref[H:], x_ref[...])

        @last_step()
        def _():
            line_ref[...] = acc_ref[H:]
            spread.write(acc_ref, k_ref, out_refs, over_refs)

    return run(
        "grad_one",
        kernel,
        batch,
        [SMEM, columns(TALL), columns(TALL)]
        + [whole(*v.shape) for v in overs]
        + [ANY] * len(after),
        [whole(REST, TALL), whole(REST, H)] + spread.specs(True),
        [shaped(F32, REST, TALL), shaped(F32, REST, H)] + spread.shapes(True),
        [pltpu.VMEM((TALL, H), F32)],
        2 * batch * TALL * TALL,
        index, mixer_low, features, *overs, *after,
    )


def back_one(mixer_low, part, matrix, tail, edge, after):
    batch = part.shape[1]

    def kernel(g_ref, p_ref, w_ref, t_ref, e_ref, *refs):
        out_ref, held = refs[len(after) :]

        @first_step()
        def _():
            straight(held, w_ref, t_ref, e_ref)

        for a, b in pieces_of(TILE):
            value = p_ref[:, a:b] + product(held[:, :TALL], g_ref[:, a:b])
            out_ref[:H, a:b] = value[:H]
            out_ref[H:, a:b] = value[H:D]

    return run(
        "back_one",
        kernel,
        batch,
        [columns(TALL), columns(TALL), whole(H, H), whole(LANES, H), whole(REST, WIDE)]
        + [ANY] * len(after),
        [columns(D)],
        [shaped(F32, D, batch)],
        [pltpu.VMEM((TALL, WIDE), LOW)],
        2 * batch * TALL * TALL,
        mixer_low, part, matrix, tail, edge, *after,
    )[0]


def local(groups, features, labels, days, master, moment_one, moment_two):
    count = lax.axis_size(AXES)
    index = lax.axis_index(AXES)
    slot = index[None].astype(jnp.int32)
    rows = H // count
    starts = starts_of(count)
    sizes = piece_sizes(count)
    wide_piece = sizes[1]
    piece = [master[a : a + l] for a, l in zip(starts, sizes)]
    block_one = to_block(piece[0], index, D, rows, count)
    block_two = to_block(piece[2], index, D, rows, count)
    block_deep = to_block(piece[4], index, H, rows, count)

    day_hot = (days[:, None] == jnp.arange(DAYS, dtype=jnp.int32)[None, :]).astype(F32)
    own_counts = jnp.sum(day_hot, axis=0)
    counts_high = jnp.floor(own_counts / 64.0)
    counts_low = own_counts - 64.0 * counts_high

    def spill_side(block):
        side = block[rows:, H:].T
        return jnp.pad(side, ((0, 0), (0, rows - SPILL_ROWS)))

    misc = [
        piece[5],
        piece[7],
        piece[8],
        block_one[:rows, H:].T,
        block_two[:rows, H:].T,
        spill_side(block_one),
        spill_side(block_two),
        piece[1],
        piece[3],
        piece[9],
        counts_high,
        counts_low,
    ]
    misc = jnp.concatenate([part.reshape(-1) for part in misc])
    misc = jnp.pad(misc, (0, (AUX_ROWS - MISC_ROW) * H - misc.shape[0])).reshape(-1, H)
    first = jnp.concatenate(
        [block_one[:rows, :H], block_one[rows:, :H], block_two[rows:, :H], block_deep[rows:], misc]
    ).astype(LOW)
    stacks_one = gather(first, groups, count)
    rest = jnp.concatenate(
        [block_two[:rows, :H], block_deep[:rows], piece[6].reshape(rows, H)]
    ).astype(LOW)
    stacks_rest = gather(rest, groups, count)

    examples = jnp.stack([labels.astype(F32), days.astype(F32)])

    matrix_one, aux = place(slot, stacks_one, rows, count, [0])
    matrix_two, matrix_deep, matrix_top = place(
        slot, stacks_rest, rows, count, [SPILL_ROWS, 2 * SPILL_ROWS, None], aux
    )

    line = aux[:, MISC_ROW]
    at = UNIT_LINES * rows
    units = line[:, :at].reshape(count, UNIT_LINES, rows).transpose(1, 0, 2).reshape(UNIT_LINES, H)
    biases = line[:, at : at + 2 * wide_piece].reshape(count, 2, wide_piece)
    biases = biases.transpose(1, 0, 2).reshape(2, count * wide_piece)
    at += 2 * wide_piece
    head_bias = line[0, at]
    both_counts = jnp.sum(line[:, at + 1 : at + 1 + 2 * DAYS].astype(F32), axis=0)
    counts = 64.0 * both_counts[:DAYS] + both_counts[DAYS:]
    inverse = jnp.broadcast_to((1.0 / counts)[:, None], (DAYS, LANES))
    sides = jnp.pad(units[3:9], ((0, 0), (0, LANES))) + jnp.pad(
        units[9:15], ((0, 0), (rows, LANES - rows))
    )

    def tail_of(at, bias):
        return jnp.concatenate(
            [aux[count - 1, at : at + EXTRA], bias[None, :H], jnp.zeros((LANES - EXTRA - 1, H), LOW)]
        )

    def edge_of(side, bias):
        lane = lax.broadcasted_iota(jnp.int32, side.shape, 1)
        side = jnp.where(lane == D, bias[H:D, None], side)
        return jnp.pad(side, ((0, TALL - H - EXTRA), (0, 0)))

    tail_one, edge_one = tail_of(0, biases[0]), edge_of(sides[:3], biases[0])
    tail_two, edge_two = tail_of(SPILL_ROWS, biases[1]), edge_of(sides[3:], biases[1])
    tail_deep = tail_of(2 * SPILL_ROWS, units[0])
    lines = jnp.concatenate(
        [units[1:3], jnp.full((1, H), head_bias), jnp.zeros((LANES - 3, H), LOW)]
    )
    lines = lines.astype(F32).T
    spread = Spread(groups, rows, count)

    wide_features, mixer_one, low_one = forward_one(features.T, matrix_one, tail_one, edge_one)
    mixer_two, low_two = forward_two(
        wide_features, mixer_one, low_one, matrix_two, tail_two, edge_two
    )
    hidden_one, slope_one = forward_deep(low_two, matrix_deep, tail_deep)
    logits, pre_one_low, top_lines, sums, *outs = top(
        spread, slot, hidden_one, slope_one, examples, matrix_top, lines, inverse
    )
    *stacks, _ = spread.finish(outs, slot)
    top_plane = core_stage(stacks, groups, count)
    layer_grad, mixer_two_low, deep_lines, *outs = back_deep(
        spread, slot, pre_one_low, low_two, wide_features, matrix_deep, tail_deep
    )
    *stacks, deep_over = spread.finish(outs, slot)
    deep_plane = core_stage(stacks, groups, count)
    part, mixer_one_low, two_side, two_lines, *outs = back_two(
        spread, slot, mixer_two_low, low_one, layer_grad, wide_features, mixer_one, mixer_two,
        matrix_two, tail_two, edge_two, top_plane[1:],
    )
    *stacks, two_over = spread.finish(outs, slot)
    top_z = plane_stage(top_plane, groups, count)
    two_plane = core_stage(stacks, groups, count)
    overs = (two_over, deep_over)
    one_side, one_lines, *outs = grad_one(
        spread, slot, mixer_one_low, wide_features, overs, deep_plane[1:]
    )
    stacks = spread.finish(outs, slot, overs)
    last_plane = core_stage(stacks, groups, count)
    feature_grad = back_one(
        mixer_one_low, part, matrix_one, tail_one, edge_one, two_plane[1:] + stacks[1:2]
    )

    sums = jnp.pad(jnp.sum(sums[:2], axis=1)[None], ((0, 0), (0, WIDE - 2)))
    vectors = jnp.concatenate(
        [
            jnp.pad(
                jnp.concatenate(
                    [one_lines[EXTRA:4], two_lines[EXTRA:4], deep_lines[EXTRA:4], top_lines[8:9], top_lines[:1]]
                ),
                ((0, 0), (0, LANES)),
            ),
            jnp.pad(jnp.concatenate([one_side[:3], two_side[:3]]), ((0, 0), (0, WIDE - TALL))),
            sums,
            jnp.zeros((4, WIDE), F32),
        ]
    )
    vectors = jnp.sum(lax.all_gather(vectors, AXES, axis=0), axis=0)
    loss = vectors[11, 1]
    side_sums = vectors[5:11]

    own_top = z_stage(top_z, groups, count)
    own_deep = z_stage(plane_stage(deep_plane, groups, count), groups, count)
    own_two = z_stage(plane_stage(two_plane, groups, count), groups, count)
    own_last = z_stage(plane_stage(last_plane, groups, count), groups, count)
    own_one = own_last[:rows]
    spills = own_last[rows : rows + MISC_ROW]
    row = lax.broadcasted_iota(jnp.int32, spills.shape, 0)
    beyond = (row % SPILL_ROWS >= EXTRA) & (index == count - 1)
    spills = jnp.where(beyond, 0.0, spills)
    wide_biases = jnp.concatenate(
        [vectors[:2, :H], side_sums[:, D].reshape(2, EXTRA)], axis=1
    )
    wide_biases = jnp.pad(wide_biases, ((0, 0), (0, count * wide_piece - D)))
    wide_biases = lax.dynamic_slice(wide_biases, (0, index * wide_piece), (2, wide_piece))
    units = lax.dynamic_slice(vectors[2:5], (0, index * rows), (3, rows))
    side_sums = jnp.pad(side_sums[:, :D], ((0, 0), (0, WIDE - D)))
    side_sums = lax.dynamic_slice(side_sums, (0, index * rows), (6, rows + SPILL_ROWS)).T

    def whole_block(main, number):
        low = number * SPILL_ROWS
        body = jnp.concatenate([main, spills[low : low + SPILL_ROWS]])
        if number == 2:
            return body
        return jnp.concatenate([body, side_sums[:, 3 * number : 3 * number + 3]], axis=1)

    flat_grad = jnp.concatenate(
        [
            from_block(whole_block(own_one, 0), index, sizes[0], rows, count),
            wide_biases[0],
            from_block(whole_block(own_two, 1), index, sizes[2], rows, count),
            wide_biases[1],
            from_block(whole_block(own_deep, 2), index, sizes[4], rows, count),
            units[0],
            own_top.reshape(-1),
            units[1],
            units[2],
            jnp.where(index == 0, vectors[11, :1], 0.0),
        ]
    )
    new_moment_one = 0.9 * moment_one + 0.1 * flat_grad
    new_moment_two = 0.999 * moment_two + 0.001 * flat_grad * flat_grad
    corrected_one = new_moment_one / (1.0 - 0.9**STEP)
    corrected_two = new_moment_two / (1.0 - 0.999**STEP)
    new_master = master - 0.03 * (corrected_one / (jnp.sqrt(corrected_two) + 1e-08) + 0.01 * master)
    new_bias = jnp.concatenate(
        [new_master[starts[i] : starts[i] + sizes[i]] for i in (1, 3, 5, 7, 9)]
    )
    return (
        logits.reshape(-1),
        loss,
        feature_grad.T,
        flat_grad,
        new_moment_one,
        new_moment_two,
        new_master,
        new_bias,
    )


def solution(mesh):
    line = P(AXES)
    table = P(AXES, None)
    groups = bit_groups(mesh)
    return jax.shard_map(
        functools.partial(local, groups),
        mesh=mesh,
        in_specs=(table, line, line, line, line, line),
        out_specs=(line, P(), table, line, line, line, line, line),
        check_vma=False,
    )
```

```python
import functools
import math

import jax
import jax.numpy as jnp
from jax import lax
from jax.experimental import pallas as pl
from jax.experimental.pallas import tpu as pltpu
from jax.sharding import PartitionSpec as P

D = 1027
H = 1024
DAYS = 24
STEP = 10
AXES = ("dp", "cores")
EXTRA = D - H
LANES = 128
WIDE = H + LANES
AUX_ROWS = 16
SPILL_ROWS = 4
MISC_ROW = 12
UNIT_LINES = 15
TILE = 512
TALL = H + 16
MIB = 1024 * 1024
F32 = jnp.float32
LOW = jnp.bfloat16
SMEM = pl.BlockSpec(memory_space=pltpu.SMEM)
VMEM = pl.BlockSpec(memory_space=pltpu.VMEM)
PARAMS = pltpu.CompilerParams(vmem_limit_bytes=56 * MIB)


def shapes():
    return [(D, D), (D,), (D, D), (D,), (D, H), (H,), (H, H), (H,), (H,), (1,)]


def piece_sizes(count):
    return [(math.prod(shape) + count - 1) // count for shape in shapes()[:-1]] + [1]


def starts_of(count):
    starts = []
    position = 0
    for piece in piece_sizes(count):
        starts.append(position)
        position += piece
    return starts


def to_block(piece, index, width, rows, count):
    excess = piece.shape[0] - rows * width
    size = (rows + SPILL_ROWS) * width
    lead = (count - 1) * excess
    padded = jnp.pad(piece, (lead, max(0, size - piece.shape[0])))
    line = lax.dynamic_slice(padded, (lead - index * excess,), (size,))
    return line.reshape(rows + SPILL_ROWS, width)


def from_block(block, index, piece, rows, count):
    width = block.shape[1]
    excess = piece - rows * width
    last = (count - 1) * excess
    line = jnp.pad(block.reshape(-1), (0, max(0, last + piece - block.size)))
    return lax.dynamic_slice(line, (index * excess,), (piece,))


def bit_groups(mesh):
    devices = mesh.devices.reshape(-1)
    groups = {"z": [], "plane": [], "core": []}
    bit = 1
    while bit < devices.size:
        here = getattr(devices[0], "coords", None)
        there = getattr(devices[bit], "coords", None)
        if here is None or there is None:
            name = "core" if bit == 1 else "plane" if bit <= 4 else "z"
        elif tuple(here) == tuple(there):
            name = "core"
        elif here[2] != there[2]:
            name = "z"
        else:
            name = "plane"
        groups[name].append(bit)
        bit *= 2
    return groups


def masks_of(bits):
    masks = [0]
    for bit in bits:
        masks = masks + [mask | bit for mask in masks]
    return masks


def teams(bits, count):
    masks = masks_of(bits)
    return [[k | mask for mask in masks] for k in range(count) if not k & masks[-1]]


def line_groups(groups, count):
    return teams(groups["z"], count)


def total_of(value, groups, count):
    for bits in (groups["z"], groups["plane"], groups["core"]):
        if bits:
            parts = lax.all_gather(value, AXES, axis=0, axis_index_groups=teams(bits, count))
            value = jnp.sum(parts, axis=0)
    return value


def owner(index, mask, groups, by_z):
    if by_z:
        index = jnp.bitwise_and(index, ~masks_of(groups["z"])[-1])
    return jnp.bitwise_xor(index, mask)


def swap(value, mask, count):
    return lax.ppermute(value, AXES, [(k, k ^ mask) for k in range(count)])


def gather(block, groups, count):
    z_masks = masks_of(groups["z"])
    core_masks = masks_of(groups["core"])
    if len(z_masks) > 1:
        line = lax.all_gather(block, AXES, axis=0, axis_index_groups=line_groups(groups, count))
    else:
        line = block[None]
    plane = [(line, z_masks)]
    if len(groups["plane"]) == 2 and len(z_masks) > 1:
        one, two = groups["plane"]
        half = len(z_masks) // 2
        by_one = swap(line, one, count)
        by_two = swap(line, two, count)
        plane.append((by_one, [one ^ z for z in z_masks]))
        plane.append((by_two, [two ^ z for z in z_masks]))
        both = one ^ two
        plane.append((swap(by_one[:half], two, count), [both ^ z for z in z_masks[:half]]))
        plane.append((swap(by_two[half:], one, count), [both ^ z for z in z_masks[half:]]))
    else:
        for mask in masks_of(groups["plane"])[1:]:
            plane.append((swap(line, mask, count), [mask ^ z for z in z_masks]))
    result = list(plane)
    for core in core_masks[1:]:
        result += [(swap(value, core, count), [core ^ m for m in row]) for value, row in plane]
    return result


def place(index, stacks, groups, rows, count, parts, aux=None):
    sources = [value for value, _ in stacks]
    masks = [row for _, row in stacks]
    carries = aux is None
    top = min(16, rows)

    def kernel(index_ref, *refs):
        refs = list(refs)
        aux_ref = refs.pop() if carries else refs.pop(0)
        outs = refs[len(sources) :]
        for ref, row in zip(refs, masks):
            for j, mask in enumerate(row):
                at = owner(index_ref[0], mask, groups, True)
                for i, out_ref in enumerate(outs):
                    out_ref[at] = ref[j, i * rows : (i + 1) * rows]
                if carries:
                    aux_ref[at] = ref[j, len(outs) * rows :]
        for spill_at, out_ref in zip(parts, outs):
            if spill_at is None:
                continue
            for k in range(1, count):
                spill = aux_ref[k - 1].astype(F32)[spill_at : spill_at + SPILL_ROWS]
                old = out_ref[k, :top].astype(F32)
                new = old[:SPILL_ROWS] + spill
                if top > SPILL_ROWS:
                    new = jnp.concatenate([new, old[SPILL_ROWS:]], axis=0)
                out_ref[k, :top] = new.astype(LOW)

    out_shape = [jax.ShapeDtypeStruct((count, rows, H), LOW)] * len(parts)
    if carries:
        out_shape.append(jax.ShapeDtypeStruct((count, AUX_ROWS, H), LOW))
    extra = [] if carries else [aux]
    result = pl.pallas_call(
        kernel,
        out_shape=out_shape,
        in_specs=[SMEM] + [VMEM] * (len(extra) + len(sources)),
        out_specs=[VMEM] * len(out_shape),
        compiler_params=PARAMS,
        name="place",
    )(index, *extra, *sources)
    return [value.reshape(H, H) for value in result[: len(parts)]] + list(result[len(parts) :])


def split(index, value, masks, kinds, groups, by_z):
    def kernel(index_ref, value_ref, *out_refs):
        for ref, row, kind in zip(out_refs, masks, kinds):
            for j, mask in enumerate(row):
                ref[j] = value_ref[owner(index_ref[0], mask, groups, by_z)].astype(kind)

    shape = value.shape[1:]
    return pl.pallas_call(
        kernel,
        out_shape=[
            jax.ShapeDtypeStruct((len(row),) + shape, kind) for row, kind in zip(masks, kinds)
        ],
        in_specs=[SMEM, VMEM],
        out_specs=[VMEM] * len(masks),
        compiler_params=PARAMS,
        name="split",
    )(index, value)


def halves(groups):
    z_masks, plane_masks, core_masks = (masks_of(groups[g]) for g in ("z", "plane", "core"))
    inner = [p ^ z for p in plane_masks for z in z_masks]
    return [[core ^ m for m in inner] for core in core_masks]


def kinds_of(groups):
    return [F32] + [LOW] * (len(halves(groups)) - 1)


def core_stage(stacks, groups, count):
    z_masks, plane_masks, core_masks = (masks_of(groups[g]) for g in ("z", "plane", "core"))
    kept = stacks[0]
    for core, stack in zip(core_masks[1:], stacks[1:]):
        kept = kept + swap(stack, core, count).astype(F32)
    kept = kept.reshape((len(plane_masks), len(z_masks)) + kept.shape[1:])
    return [kept[0]] + [kept[j].astype(LOW) for j in range(1, len(plane_masks))]


def plane_stage(parts, groups, count):
    total = parts[0]
    for mask, part in zip(masks_of(groups["plane"])[1:], parts[1:]):
        total = total + swap(part, mask, count).astype(F32)
    return total


def z_stage(total, groups, count, by_z):
    z_masks = masks_of(groups["z"])
    if by_z and len(z_masks) > 1:
        return lax.psum_scatter(
            total, AXES, scatter_dimension=0, axis_index_groups=line_groups(groups, count)
        )
    parts = [total[0]] + [total[j].astype(LOW) for j in range(1, len(z_masks))]
    own = parts[0]
    for mask, part in zip(z_masks[1:], parts[1:]):
        own = own + swap(part, mask, count).astype(F32)
    return own


def product(left, right):
    return lax.dot_general(left, right, (((1,), (0,)), ((), ())), preferred_element_type=F32)


def outer(left, right):
    return lax.dot_general(left, right, (((1,), (1,)), ((), ())), preferred_element_type=F32)


def gelu_both(value):
    scale = math.sqrt(2.0 / math.pi)
    square = value * value
    share = 0.5 + 0.5 * jnp.tanh(value * (scale + scale * 0.044715 * square))
    result = value * share
    slope = share + result * (1.0 - share) * (2.0 * scale + 6.0 * scale * 0.044715 * square)
    return result, slope


def columns(height, tile=TILE):
    return pl.BlockSpec((height, tile), lambda i: (0, i))


def whole(*shape):
    return pl.BlockSpec(shape, lambda i: (0,) * len(shape))


def shaped(kind, *shape):
    return jax.ShapeDtypeStruct(shape, kind)


def pieces_of(width):
    return [(a, a + 256) for a in range(0, width, 256)]


def run(name, kernel, batch, in_specs, out_specs, out_shape, scratch, flops, *args, tile=TILE):
    moved = sum(a.size * a.dtype.itemsize for a in args)
    moved += sum(math.prod(o.shape) * o.dtype.itemsize for o in out_shape)
    return pl.pallas_call(
        kernel,
        grid=(batch // tile,),
        in_specs=in_specs,
        out_specs=out_specs,
        out_shape=out_shape,
        scratch_shapes=scratch,
        compiler_params=PARAMS,
        cost_estimate=pl.CostEstimate(flops=flops, bytes_accessed=moved, transcendentals=0),
        name=name,
    )(*args)


def first_step():
    return pl.when(pl.program_id(0) == 0)


def last_step():
    return pl.when(pl.program_id(0) == pl.num_programs(0) - 1)


def turn(out_ref, matrix_ref, tail_ref=None, edge_ref=None):
    for a, b in pieces_of(H):
        out_ref[a:b, :H] = matrix_ref[:, a:b].T
    if tail_ref is not None:
        out_ref[:H, H:] = tail_ref[...].T
    if edge_ref is not None:
        out_ref[H:, :] = edge_ref[...]


def straight(out_ref, matrix_ref, tail_ref, edge_ref=None):
    out_ref[:H, :H] = matrix_ref[...]
    row = lax.broadcasted_iota(jnp.int32, (TALL - H, H), 0)
    tail = tail_ref[: TALL - H, :].astype(F32)
    out_ref[H:, :H] = jnp.where(row < EXTRA, tail, 0.0).astype(LOW)
    if edge_ref is not None:
        lane = lax.broadcasted_iota(jnp.int32, (TALL - H, WIDE), 1)
        edge = jnp.where(lane < D, edge_ref[...].astype(F32), 0.0)
        edge = jnp.concatenate([edge, jnp.zeros((LANES - (TALL - H), WIDE), F32)])
        out_ref[:, H:] = edge.T[:TALL].astype(LOW)


class Spread:
    def __init__(self, groups, rows, count, by_z):
        self.groups, self.by_z = groups, by_z
        self.masks = halves(groups)
        self.kinds = kinds_of(groups)
        self.rows, self.count = rows, count
        self.direct = rows % 16 == 0

    def shapes(self, below=False):
        if not self.direct:
            return [shaped(F32, TALL, H)]
        height = self.rows + (AUX_ROWS if below else 0)
        outs = [shaped(kind, len(row), height, H) for row, kind in zip(self.masks, self.kinds)]
        return outs if below else outs + [shaped(F32, self.count, 8, H)]

    def specs(self, below=False):
        return [whole(*s.shape) for s in self.shapes(below)]

    def write(self, acc_ref, index_ref, out_refs, over_refs=None):
        if not self.direct:
            out_refs[0][...] = acc_ref[...]
            return
        rows = self.rows
        for ref, row, kind in zip(out_refs, self.masks, self.kinds):
            for j, mask in enumerate(row):
                at = owner(index_ref[0], mask, self.groups, self.by_z)
                start = pl.multiple_of(at * rows, rows)
                ref[j, :rows] = acc_ref[pl.ds(start, rows), :].astype(kind)
                if over_refs is not None:
                    mine = acc_ref[pl.ds(pl.multiple_of(start + rows, 8), 8), :]
                    parts = [mine[:SPILL_ROWS]] + [v[at][:SPILL_ROWS] for v in over_refs]
                    parts.append(jnp.zeros((AUX_ROWS - MISC_ROW, H), F32))
                    ref[j, rows:] = jnp.concatenate(parts).astype(kind)
        if over_refs is None:
            for k in range(self.count):
                out_refs[-1][k] = acc_ref[(k + 1) * rows : (k + 1) * rows + 8, :]

    def finish(self, outs, index, overs=None):
        if self.direct:
            return list(outs)
        grad, rows, count = outs[0], self.rows, self.count
        blocks = grad[:H].reshape(count, rows, H)
        over = jnp.stack([grad[(k + 1) * rows : (k + 1) * rows + 8] for k in range(count)])
        if overs is not None:
            sides = [v[:, :SPILL_ROWS] for v in (over, overs[0], overs[1])]
            sides.append(jnp.zeros((count, AUX_ROWS - MISC_ROW, H), F32))
            blocks = jnp.concatenate([blocks] + sides, axis=1)
        stacks = list(split(index, blocks, self.masks, self.kinds, self.groups, self.by_z))
        return stacks if overs is not None else stacks + [over]


ANY = pl.BlockSpec(memory_space=pl.ANY)
REST = TALL - H


def forward_one(features, matrix, tail, edge):
    batch = features.shape[1]

    def kernel(f_ref, w_ref, t_ref, e_ref, x_ref, mixer_ref, low_ref, turned):
        @first_step()
        def _():
            turn(turned, w_ref, t_ref, e_ref)

        x_ref[:H] = f_ref[:H]
        last = f_ref[H:].astype(F32)
        last = jnp.concatenate([last, jnp.ones((1, TILE), F32), jnp.zeros((TALL - D - 1, TILE), F32)])
        x_ref[H:] = last.astype(LOW)
        for a, b in pieces_of(TILE):
            mixer = product(turned[:, :TALL], x_ref[:, a:b])
            mixer_ref[:, a:b] = mixer
            part = x_ref[:, a:b].astype(F32)
            low_ref[:, a:b] = (part * mixer + part).astype(LOW)

    return run(
        "forward_one",
        kernel,
        batch,
        [columns(D), whole(H, H), whole(LANES, H), whole(REST, WIDE)],
        [columns(TALL)] * 3,
        [shaped(LOW, TALL, batch), shaped(F32, TALL, batch), shaped(LOW, TALL, batch)],
        [pltpu.VMEM((TALL, WIDE), LOW)],
        2 * batch * TALL * TALL,
        features, matrix, tail, edge,
    )


def forward_two(features, mixer_one, layer_low, matrix, tail, edge):
    batch = features.shape[1]

    def kernel(x_ref, m_ref, l_ref, w_ref, t_ref, e_ref, mixer_ref, low_ref, turned):
        @first_step()
        def _():
            turn(turned, w_ref, t_ref, e_ref)

        for a, b in pieces_of(TILE):
            mixer = product(turned[:, :TALL], l_ref[:, a:b])
            mixer_ref[:, a:b] = mixer
            part = x_ref[:, a:b].astype(F32)
            layer = part * m_ref[:, a:b] + part
            low_ref[:, a:b] = (part * mixer + layer).astype(LOW)

    return run(
        "forward_two",
        kernel,
        batch,
        [columns(TALL)] * 3 + [whole(H, H), whole(LANES, H), whole(REST, WIDE)],
        [columns(TALL), columns(TALL)],
        [shaped(F32, TALL, batch), shaped(LOW, TALL, batch)],
        [pltpu.VMEM((TALL, WIDE), LOW)],
        2 * batch * TALL * TALL,
        features, mixer_one, layer_low, matrix, tail, edge,
    )


def forward_deep(layer_low, matrix, tail):
    batch = layer_low.shape[1]

    def kernel(l_ref, w_ref, t_ref, hidden_ref, slope_ref, turned):
        @first_step()
        def _():
            turn(turned, w_ref, t_ref)

        for a, b in pieces_of(TILE):
            hidden, slope = gelu_both(product(turned[:, :TALL], l_ref[:, a:b]))
            hidden_ref[:H, a:b] = hidden.astype(LOW)
            slope_ref[:, a:b] = slope
        row = lax.broadcasted_iota(jnp.int32, (REST, TILE), 0)
        hidden_ref[H:] = jnp.where(row == 0, 1.0, 0.0).astype(LOW)

    return run(
        "forward_deep",
        kernel,
        batch,
        [columns(TALL), whole(H, H), whole(LANES, H)],
        [columns(TALL), columns(H)],
        [shaped(LOW, TALL, batch), shaped(F32, H, batch)],
        [pltpu.VMEM((H, WIDE), LOW)],
        2 * batch * TALL * H,
        layer_low, matrix, tail,
    )


def top(spread, index, hidden_one, slope_one, examples, matrix, lines, inverse):
    batch = hidden_one.shape[1]
    days = inverse.shape[0]

    def kernel(k_ref, h_ref, s_ref, x_ref, w_ref, n_ref, i_ref, *refs):
        logit_ref, back_ref, line_ref, sum_ref = refs[:4]
        out_refs = refs[4:-5]
        turned, acc_ref, low_ref, two_ref, part_ref = refs[-5:]

        @first_step()
        def _():
            turn(turned, w_ref)
            acc_ref[...] = jnp.zeros_like(acc_ref)
            sum_ref[...] = jnp.zeros_like(sum_ref)
            part_ref[...] = jnp.zeros_like(part_ref)

        head = n_ref[:, 1:2]
        for a, b in pieces_of(TILE):
            two, slope = gelu_both(product(turned[...], h_ref[:H, a:b]) + n_ref[:, 0:1])
            two = two.astype(LOW).astype(F32)
            logits = n_ref[0:1, 2:3] + jnp.sum(two * head, axis=0, keepdims=True)
            label = x_ref[0:1, a:b]
            day = x_ref[1:2, a:b].astype(jnp.int32)
            row = lax.broadcasted_iota(jnp.int32, (days, b - a), 0)
            weight = jnp.sum(jnp.where(row == day, i_ref[:, 0:1], 0.0), axis=0, keepdims=True)
            decay = jnp.exp(-jnp.abs(logits))
            entropy = jnp.maximum(logits, 0.0) + jnp.log1p(decay) - label * logits
            chance = jnp.where(logits >= 0.0, 1.0, decay) / (1.0 + decay)
            logit_grad = (chance - label) * weight
            logit_ref[:, a:b] = logits
            sum_ref[0:1, a:b] += logit_grad
            sum_ref[1:2, a:b] += entropy * weight
            low_ref[:, a:b] = ((logit_grad * head) * slope).astype(LOW)
            one = logit_grad * two
            part = one[:, :LANES]
            for at in range(LANES, b - a, LANES):
                part = part + one[:, at : at + LANES]
            part_ref[...] += part
        for a, b in pieces_of(TILE):
            back_ref[:, a:b] = (product(w_ref[...], low_ref[:, a:b]) * s_ref[:, a:b]).astype(LOW)
        for a, b in pieces_of(H):
            acc_ref[:, a:b] += outer(h_ref[...], low_ref[a:b])

        @last_step()
        def _():
            line_ref[0:8] = jnp.broadcast_to(
                jnp.sum(part_ref[...].T, axis=0, keepdims=True), (8, H)
            )
            line_ref[8:16] = acc_ref[H : H + 8]
            spread.write(acc_ref, k_ref, out_refs)

    return run(
        "top",
        kernel,
        batch,
        [
            SMEM,
            columns(TALL),
            columns(H),
            columns(2),
            whole(H, H),
            whole(H, LANES),
            whole(days, LANES),
        ],
        [columns(1), columns(H), whole(16, H), whole(8, TILE)] + spread.specs(),
        [
            shaped(F32, 1, batch),
            shaped(LOW, H, batch),
            shaped(F32, 16, H),
            shaped(F32, 8, TILE),
        ]
        + spread.shapes(),
        [
            pltpu.VMEM((H, H), LOW),
            pltpu.VMEM((TALL, H), F32),
            pltpu.VMEM((H, TILE), LOW),
            pltpu.VMEM((8, LANES), F32),
            pltpu.VMEM((H, LANES), F32),
        ],
        6 * batch * H * H,
        index, hidden_one, slope_one, examples, matrix, lines, inverse,
    )


def back_deep(spread, index, grad_low, layer_low, features, matrix, tail):
    batch = features.shape[1]

    def kernel(k_ref, g_ref, l_ref, x_ref, w_ref, t_ref, *refs):
        layer_ref, mixer_ref, line_ref = refs[:3]
        out_refs = refs[3:-2]
        held, acc_ref = refs[-2:]

        @first_step()
        def _():
            straight(held, w_ref, t_ref)
            acc_ref[...] = jnp.zeros_like(acc_ref)

        for a, b in pieces_of(TILE):
            layer = product(held[...], g_ref[:, a:b])
            layer_ref[:, a:b] = layer
            mixer_ref[:, a:b] = (layer * x_ref[:, a:b].astype(F32)).astype(LOW)
        for a, b in pieces_of(H):
            acc_ref[:, a:b] += outer(l_ref[...], g_ref[a:b])

        @last_step()
        def _():
            line_ref[...] = acc_ref[H:]
            spread.write(acc_ref, k_ref, out_refs)

    return run(
        "back_deep",
        kernel,
        batch,
        [SMEM, columns(H), columns(TALL), columns(TALL), whole(H, H), whole(LANES, H)],
        [columns(TALL), columns(TALL), whole(REST, H)] + spread.specs(),
        [shaped(F32, TALL, batch), shaped(LOW, TALL, batch), shaped(F32, REST, H)]
        + spread.shapes(),
        [pltpu.VMEM((TALL, H), LOW), pltpu.VMEM((TALL, H), F32)],
        4 * batch * TALL * H,
        index, grad_low, layer_low, features, matrix, tail,
    )


def back_two(
    spread, index, mixer_low, layer_low, layer_grad, features, mixer_one, mixer_two, matrix, tail,
    edge, after,
):
    batch = features.shape[1]
    tile = TILE // 2

    def kernel(k_ref, g_ref, l_ref, d_ref, x_ref, one_ref, two_ref, w_ref, t_ref, e_ref, *refs):
        part_ref, mixer_ref, side_ref, line_ref = refs[len(after) : len(after) + 4]
        out_refs = refs[len(after) + 4 : -2]
        held, acc_ref = refs[-2:]

        @first_step()
        def _():
            straight(held, w_ref, t_ref, e_ref)
            acc_ref[...] = jnp.zeros_like(acc_ref)
            side_ref[...] = jnp.zeros_like(side_ref)

        for a, b in pieces_of(tile):
            above = d_ref[:, a:b]
            layer = product(held[:, :TALL], g_ref[:, a:b]) + above
            mixer_ref[:, a:b] = (layer * x_ref[:, a:b].astype(F32)).astype(LOW)
            part_ref[:, a:b] = above * two_ref[:, a:b] + layer * (one_ref[:, a:b] + 1.0)
        for a, b in pieces_of(H):
            acc_ref[:, a:b] += outer(l_ref[...], g_ref[a:b])
        side_ref[...] += outer(g_ref[H:], l_ref[...])

        @last_step()
        def _():
            line_ref[...] = acc_ref[H:]
            spread.write(acc_ref, k_ref, out_refs)

    return run(
        "back_two",
        kernel,
        batch,
        [SMEM]
        + [columns(TALL, tile)] * 6
        + [whole(H, H), whole(LANES, H), whole(REST, WIDE)]
        + [ANY] * len(after),
        [columns(TALL, tile), columns(TALL, tile), whole(REST, TALL), whole(REST, H)]
        + spread.specs(),
        [
            shaped(F32, TALL, batch),
            shaped(LOW, TALL, batch),
            shaped(F32, REST, TALL),
            shaped(F32, REST, H),
        ]
        + spread.shapes(),
        [pltpu.VMEM((TALL, WIDE), LOW), pltpu.VMEM((TALL, H), F32)],
        4 * batch * TALL * TALL,
        index, mixer_low, layer_low, layer_grad, features, mixer_one, mixer_two, matrix, tail,
        edge, *after,
        tile=tile,
    )


def grad_one(spread, index, mixer_low, features, overs, after):
    batch = features.shape[1]

    def kernel(k_ref, g_ref, x_ref, *refs):
        over_refs = refs[: len(overs)]
        refs = refs[len(overs) + len(after) :]
        side_ref, line_ref = refs[:2]
        out_refs = refs[2:-1]
        acc_ref = refs[-1]

        @first_step()
        def _():
            acc_ref[...] = jnp.zeros_like(acc_ref)
            side_ref[...] = jnp.zeros_like(side_ref)

        for a, b in pieces_of(H):
            acc_ref[:, a:b] += outer(x_ref[...], g_ref[a:b])
        side_ref[...] += outer(g_ref[H:], x_ref[...])

        @last_step()
        def _():
            line_ref[...] = acc_ref[H:]
            spread.write(acc_ref, k_ref, out_refs, over_refs)

    return run(
        "grad_one",
        kernel,
        batch,
        [SMEM, columns(TALL), columns(TALL)]
        + [whole(*v.shape) for v in overs]
        + [ANY] * len(after),
        [whole(REST, TALL), whole(REST, H)] + spread.specs(True),
        [shaped(F32, REST, TALL), shaped(F32, REST, H)] + spread.shapes(True),
        [pltpu.VMEM((TALL, H), F32)],
        2 * batch * TALL * TALL,
        index, mixer_low, features, *overs, *after,
    )


def back_one(mixer_low, part, matrix, tail, edge, after):
    batch = part.shape[1]

    def kernel(g_ref, p_ref, w_ref, t_ref, e_ref, *refs):
        out_ref, held = refs[len(after) :]

        @first_step()
        def _():
            straight(held, w_ref, t_ref, e_ref)

        for a, b in pieces_of(TILE):
            value = p_ref[:, a:b] + product(held[:, :TALL], g_ref[:, a:b])
            out_ref[:H, a:b] = value[:H]
            out_ref[H:, a:b] = value[H:D]

    return run(
        "back_one",
        kernel,
        batch,
        [columns(TALL), columns(TALL), whole(H, H), whole(LANES, H), whole(REST, WIDE)]
        + [ANY] * len(after),
        [columns(D)],
        [shaped(F32, D, batch)],
        [pltpu.VMEM((TALL, WIDE), LOW)],
        2 * batch * TALL * TALL,
        mixer_low, part, matrix, tail, edge, *after,
    )[0]


def local(groups, features, labels, days, master, moment_one, moment_two):
    count = lax.axis_size(AXES)
    index = lax.axis_index(AXES)
    slot = index[None].astype(jnp.int32)
    rows = H // count
    starts = starts_of(count)
    sizes = piece_sizes(count)
    wide_piece = sizes[1]
    piece = [master[a : a + l] for a, l in zip(starts, sizes)]
    block_one = to_block(piece[0], index, D, rows, count)
    block_two = to_block(piece[2], index, D, rows, count)
    block_deep = to_block(piece[4], index, H, rows, count)

    day_hot = (days[:, None] == jnp.arange(DAYS, dtype=jnp.int32)[None, :]).astype(F32)
    own_counts = jnp.sum(day_hot, axis=0)
    counts_high = jnp.floor(own_counts / 64.0)
    counts_low = own_counts - 64.0 * counts_high

    def spill_side(block):
        side = block[rows:, H:].T
        return jnp.pad(side, ((0, 0), (0, rows - SPILL_ROWS)))

    misc = [
        piece[5],
        piece[7],
        piece[8],
        block_one[:rows, H:].T,
        block_two[:rows, H:].T,
        spill_side(block_one),
        spill_side(block_two),
        piece[1],
        piece[3],
        piece[9],
        counts_high,
        counts_low,
    ]
    misc = jnp.concatenate([part.reshape(-1) for part in misc])
    misc = jnp.pad(misc, (0, (AUX_ROWS - MISC_ROW) * H - misc.shape[0])).reshape(-1, H)
    first = jnp.concatenate(
        [block_one[:rows, :H], block_one[rows:, :H], block_two[rows:, :H], block_deep[rows:], misc]
    ).astype(LOW)
    stacks_one = gather(first, groups, count)
    stacks_two = gather(block_two[:rows, :H].astype(LOW), groups, count)
    rest = jnp.concatenate([block_deep[:rows], piece[6].reshape(rows, H)]).astype(LOW)
    stacks_rest = gather(rest, groups, count)

    examples = jnp.stack([labels.astype(F32), days.astype(F32)])

    matrix_one, aux = place(slot, stacks_one, groups, rows, count, [0])
    (matrix_two,) = place(slot, stacks_two, groups, rows, count, [SPILL_ROWS], aux)
    matrix_deep, matrix_top = place(
        slot, stacks_rest, groups, rows, count, [2 * SPILL_ROWS, None], aux
    )

    line = aux[:, MISC_ROW]
    at = UNIT_LINES * rows
    units = line[:, :at].reshape(count, UNIT_LINES, rows).transpose(1, 0, 2).reshape(UNIT_LINES, H)
    biases = line[:, at : at + 2 * wide_piece].reshape(count, 2, wide_piece)
    biases = biases.transpose(1, 0, 2).reshape(2, count * wide_piece)
    at += 2 * wide_piece
    head_bias = line[0, at]
    both_counts = jnp.sum(line[:, at + 1 : at + 1 + 2 * DAYS].astype(F32), axis=0)
    counts = 64.0 * both_counts[:DAYS] + both_counts[DAYS:]
    inverse = jnp.broadcast_to((1.0 / counts)[:, None], (DAYS, LANES))
    sides = jnp.pad(units[3:9], ((0, 0), (0, LANES))) + jnp.pad(
        units[9:15], ((0, 0), (rows, LANES - rows))
    )

    def tail_of(at, bias):
        return jnp.concatenate(
            [aux[count - 1, at : at + EXTRA], bias[None, :H], jnp.zeros((LANES - EXTRA - 1, H), LOW)]
        )

    def edge_of(side, bias):
        lane = lax.broadcasted_iota(jnp.int32, side.shape, 1)
        side = jnp.where(lane == D, bias[H:D, None], side)
        return jnp.pad(side, ((0, TALL - H - EXTRA), (0, 0)))

    tail_one, edge_one = tail_of(0, biases[0]), edge_of(sides[:3], biases[0])
    tail_two, edge_two = tail_of(SPILL_ROWS, biases[1]), edge_of(sides[3:], biases[1])
    tail_deep = tail_of(2 * SPILL_ROWS, units[0])
    lines = jnp.concatenate(
        [units[1:3], jnp.full((1, H), head_bias), jnp.zeros((LANES - 3, H), LOW)]
    )
    lines = lines.astype(F32).T
    spread = Spread(groups, rows, count, True)
    spread_last = Spread(groups, rows, count, False)

    wide_features, mixer_one, low_one = forward_one(features.T, matrix_one, tail_one, edge_one)
    mixer_two, low_two = forward_two(
        wide_features, mixer_one, low_one, matrix_two, tail_two, edge_two
    )
    hidden_one, slope_one = forward_deep(low_two, matrix_deep, tail_deep)
    logits, pre_one_low, top_lines, sums, *outs = top(
        spread, slot, hidden_one, slope_one, examples, matrix_top, lines, inverse
    )
    *stacks, _ = spread.finish(outs, slot)
    top_plane = core_stage(stacks, groups, count)
    layer_grad, mixer_two_low, deep_lines, *outs = back_deep(
        spread, slot, pre_one_low, low_two, wide_features, matrix_deep, tail_deep
    )
    *stacks, deep_over = spread.finish(outs, slot)
    deep_plane = core_stage(stacks, groups, count)
    part, mixer_one_low, two_side, two_lines, *outs = back_two(
        spread, slot, mixer_two_low, low_one, layer_grad, wide_features, mixer_one, mixer_two,
        matrix_two, tail_two, edge_two, top_plane[1:],
    )
    *stacks, two_over = spread.finish(outs, slot)
    two_plane = core_stage(stacks, groups, count)
    overs = (two_over, deep_over)
    one_side, one_lines, *outs = grad_one(
        spread_last, slot, mixer_one_low, wide_features, overs, deep_plane[1:]
    )
    stacks = spread_last.finish(outs, slot, overs)
    last_plane = core_stage(stacks, groups, count)
    feature_grad = back_one(
        mixer_one_low, part, matrix_one, tail_one, edge_one, stacks[1:2]
    )

    sums = jnp.pad(jnp.sum(sums[:2], axis=1)[None], ((0, 0), (0, WIDE - 2)))
    vectors = jnp.concatenate(
        [
            jnp.pad(
                jnp.concatenate(
                    [one_lines[EXTRA:4], two_lines[EXTRA:4], deep_lines[EXTRA:4], top_lines[8:9], top_lines[:1]]
                ),
                ((0, 0), (0, LANES)),
            ),
            jnp.pad(jnp.concatenate([one_side[:3], two_side[:3]]), ((0, 0), (0, WIDE - TALL))),
            sums,
            jnp.zeros((4, WIDE), F32),
        ]
    )
    vectors = total_of(vectors, groups, count)
    loss = vectors[11, 1]
    side_sums = vectors[5:11]

    own_top = z_stage(plane_stage(top_plane, groups, count), groups, count, True)
    own_deep = z_stage(plane_stage(deep_plane, groups, count), groups, count, True)
    own_two = z_stage(plane_stage(two_plane, groups, count), groups, count, True)
    own_last = z_stage(plane_stage(last_plane, groups, count), groups, count, False)
    own_one = own_last[:rows]
    spills = own_last[rows : rows + MISC_ROW]
    row = lax.broadcasted_iota(jnp.int32, spills.shape, 0)
    beyond = (row % SPILL_ROWS >= EXTRA) & (index == count - 1)
    spills = jnp.where(beyond, 0.0, spills)
    wide_biases = jnp.concatenate(
        [vectors[:2, :H], side_sums[:, D].reshape(2, EXTRA)], axis=1
    )
    wide_biases = jnp.pad(wide_biases, ((0, 0), (0, count * wide_piece - D)))
    wide_biases = lax.dynamic_slice(wide_biases, (0, index * wide_piece), (2, wide_piece))
    units = lax.dynamic_slice(vectors[2:5], (0, index * rows), (3, rows))
    side_sums = jnp.pad(side_sums[:, :D], ((0, 0), (0, WIDE - D)))
    side_sums = lax.dynamic_slice(side_sums, (0, index * rows), (6, rows + SPILL_ROWS)).T

    def whole_block(main, number):
        low = number * SPILL_ROWS
        body = jnp.concatenate([main, spills[low : low + SPILL_ROWS]])
        if number == 2:
            return body
        return jnp.concatenate([body, side_sums[:, 3 * number : 3 * number + 3]], axis=1)

    flat_grad = jnp.concatenate(
        [
            from_block(whole_block(own_one, 0), index, sizes[0], rows, count),
            wide_biases[0],
            from_block(whole_block(own_two, 1), index, sizes[2], rows, count),
            wide_biases[1],
            from_block(whole_block(own_deep, 2), index, sizes[4], rows, count),
            units[0],
            own_top.reshape(-1),
            units[1],
            units[2],
            jnp.where(index == 0, vectors[11, :1], 0.0),
        ]
    )
    new_moment_one = 0.9 * moment_one + 0.1 * flat_grad
    new_moment_two = 0.999 * moment_two + 0.001 * flat_grad * flat_grad
    corrected_one = new_moment_one / (1.0 - 0.9**STEP)
    corrected_two = new_moment_two / (1.0 - 0.999**STEP)
    new_master = master - 0.03 * (corrected_one / (jnp.sqrt(corrected_two) + 1e-08) + 0.01 * master)
    new_bias = jnp.concatenate(
        [new_master[starts[i] : starts[i] + sizes[i]] for i in (1, 3, 5, 7, 9)]
    )
    return (
        logits.reshape(-1),
        loss,
        feature_grad.T,
        flat_grad,
        new_moment_one,
        new_moment_two,
        new_master,
        new_bias,
    )


def solution(mesh):
    line = P(AXES)
    table = P(AXES, None)
    groups = bit_groups(mesh)
    return jax.shard_map(
        functools.partial(local, groups),
        mesh=mesh,
        in_specs=(table, line, line, line, line, line),
        out_specs=(line, P(), table, line, line, line, line, line),
        check_vma=False,
    )
```

```python
import functools
import math

import jax
import jax.numpy as jnp
from jax import lax
from jax.experimental import pallas as pl
from jax.experimental.pallas import tpu as pltpu
from jax.sharding import PartitionSpec as P

D = 1027
H = 1024
DAYS = 24
STEP = 10
AXES = ("dp", "cores")
EXTRA = D - H
LANES = 128
WIDE = H + LANES
AUX_ROWS = 16
SPILL_ROWS = 4
MISC_ROW = 12
UNIT_LINES = 15
TILE = 512
TALL = H + 16
MIB = 1024 * 1024
F32 = jnp.float32
LOW = jnp.bfloat16
SMEM = pl.BlockSpec(memory_space=pltpu.SMEM)
VMEM = pl.BlockSpec(memory_space=pltpu.VMEM)
PARAMS = pltpu.CompilerParams(vmem_limit_bytes=56 * MIB)


def shapes():
    return [(D, D), (D,), (D, D), (D,), (D, H), (H,), (H, H), (H,), (H,), (1,)]


def piece_sizes(count):
    return [(math.prod(shape) + count - 1) // count for shape in shapes()[:-1]] + [1]


def starts_of(count):
    starts = []
    position = 0
    for piece in piece_sizes(count):
        starts.append(position)
        position += piece
    return starts


def to_block(piece, index, width, rows, count):
    excess = piece.shape[0] - rows * width
    size = (rows + SPILL_ROWS) * width
    lead = (count - 1) * excess
    padded = jnp.pad(piece, (lead, max(0, size - piece.shape[0])))
    line = lax.dynamic_slice(padded, (lead - index * excess,), (size,))
    return line.reshape(rows + SPILL_ROWS, width)


def from_block(block, index, piece, rows, count):
    width = block.shape[1]
    excess = piece - rows * width
    last = (count - 1) * excess
    line = jnp.pad(block.reshape(-1), (0, max(0, last + piece - block.size)))
    return lax.dynamic_slice(line, (index * excess,), (piece,))


def bit_groups(mesh):
    devices = mesh.devices.reshape(-1)
    groups = {"z": [], "plane": [], "core": []}
    bit = 1
    while bit < devices.size:
        here = getattr(devices[0], "coords", None)
        there = getattr(devices[bit], "coords", None)
        if here is None or there is None:
            name = "core" if bit == 1 else "plane" if bit <= 4 else "z"
        elif tuple(here) == tuple(there):
            name = "core"
        elif here[2] != there[2]:
            name = "z"
        else:
            name = "plane"
        groups[name].append(bit)
        bit *= 2
    return groups


def masks_of(bits):
    masks = [0]
    for bit in bits:
        masks = masks + [mask | bit for mask in masks]
    return masks


def swap(value, mask, count):
    return lax.ppermute(value, AXES, [(k, k ^ mask) for k in range(count)])


def gather(block, groups, count):
    z_masks = masks_of(groups["z"])
    core_masks = masks_of(groups["core"])
    line = jnp.stack([block] + [swap(block, mask, count) for mask in z_masks[1:]])
    plane = [(line, z_masks)]
    if len(groups["plane"]) == 2 and len(z_masks) > 1:
        one, two = groups["plane"]
        half = len(z_masks) // 2
        by_one = swap(line, one, count)
        by_two = swap(line, two, count)
        plane.append((by_one, [one ^ z for z in z_masks]))
        plane.append((by_two, [two ^ z for z in z_masks]))
        both = one ^ two
        plane.append((swap(by_one[:half], two, count), [both ^ z for z in z_masks[:half]]))
        plane.append((swap(by_two[half:], one, count), [both ^ z for z in z_masks[half:]]))
    else:
        for mask in masks_of(groups["plane"])[1:]:
            plane.append((swap(line, mask, count), [mask ^ z for z in z_masks]))
    result = list(plane)
    for core in core_masks[1:]:
        result += [(swap(value, core, count), [core ^ m for m in row]) for value, row in plane]
    return result


def place(index, stacks, rows, count, parts, aux=None):
    sources = [value for value, _ in stacks]
    masks = [row for _, row in stacks]
    carries = aux is None
    top = min(16, rows)

    def kernel(index_ref, *refs):
        refs = list(refs)
        aux_ref = refs.pop() if carries else refs.pop(0)
        outs = refs[len(sources) :]
        for ref, row in zip(refs, masks):
            for j, mask in enumerate(row):
                at = jnp.bitwise_xor(index_ref[0], mask)
                for i, out_ref in enumerate(outs):
                    out_ref[at] = ref[j, i * rows : (i + 1) * rows]
                if carries:
                    aux_ref[at] = ref[j, len(outs) * rows :]
        for spill_at, out_ref in zip(parts, outs):
            if spill_at is None:
                continue
            for k in range(1, count):
                spill = aux_ref[k - 1].astype(F32)[spill_at : spill_at + SPILL_ROWS]
                old = out_ref[k, :top].astype(F32)
                new = old[:SPILL_ROWS] + spill
                if top > SPILL_ROWS:
                    new = jnp.concatenate([new, old[SPILL_ROWS:]], axis=0)
                out_ref[k, :top] = new.astype(LOW)

    out_shape = [jax.ShapeDtypeStruct((count, rows, H), LOW)] * len(parts)
    if carries:
        out_shape.append(jax.ShapeDtypeStruct((count, AUX_ROWS, H), LOW))
    extra = [] if carries else [aux]
    result = pl.pallas_call(
        kernel,
        out_shape=out_shape,
        in_specs=[SMEM] + [VMEM] * (len(extra) + len(sources)),
        out_specs=[VMEM] * len(out_shape),
        compiler_params=PARAMS,
        name="place",
    )(index, *extra, *sources)
    return [value.reshape(H, H) for value in result[: len(parts)]] + list(result[len(parts) :])


def split(index, value, masks, kinds):
    def kernel(index_ref, value_ref, *out_refs):
        for ref, row, kind in zip(out_refs, masks, kinds):
            for j, mask in enumerate(row):
                ref[j] = value_ref[jnp.bitwise_xor(index_ref[0], mask)].astype(kind)

    shape = value.shape[1:]
    return pl.pallas_call(
        kernel,
        out_shape=[
            jax.ShapeDtypeStruct((len(row),) + shape, kind) for row, kind in zip(masks, kinds)
        ],
        in_specs=[SMEM, VMEM],
        out_specs=[VMEM] * len(masks),
        compiler_params=PARAMS,
        name="split",
    )(index, value)


def halves(groups):
    z_masks, plane_masks, core_masks = (masks_of(groups[g]) for g in ("z", "plane", "core"))
    inner = [p ^ z for p in plane_masks for z in z_masks]
    return [[core ^ m for m in inner] for core in core_masks]


def kinds_of(groups):
    return [F32] + [LOW] * (len(halves(groups)) - 1)


def core_stage(stacks, groups, count):
    z_masks, plane_masks, core_masks = (masks_of(groups[g]) for g in ("z", "plane", "core"))
    kept = stacks[0]
    for core, stack in zip(core_masks[1:], stacks[1:]):
        kept = kept + swap(stack, core, count).astype(F32)
    kept = kept.reshape((len(plane_masks), len(z_masks)) + kept.shape[1:])
    return [kept[0]] + [kept[j].astype(LOW) for j in range(1, len(plane_masks))]


def plane_stage(parts, groups, count):
    total = parts[0]
    for mask, part in zip(masks_of(groups["plane"])[1:], parts[1:]):
        total = total + swap(part, mask, count).astype(F32)
    return [total[0]] + [total[j].astype(LOW) for j in range(1, total.shape[0])]


def z_stage(parts, groups, count):
    own = parts[0]
    for mask, part in zip(masks_of(groups["z"])[1:], parts[1:]):
        own = own + swap(part, mask, count).astype(F32)
    return own


def product(left, right):
    return lax.dot_general(left, right, (((1,), (0,)), ((), ())), preferred_element_type=F32)


def outer(left, right):
    return lax.dot_general(left, right, (((1,), (1,)), ((), ())), preferred_element_type=F32)


def gelu_both(value):
    scale = math.sqrt(2.0 / math.pi)
    square = value * value
    share = 0.5 + 0.5 * jnp.tanh(value * (scale + scale * 0.044715 * square))
    result = value * share
    slope = share + result * (1.0 - share) * (2.0 * scale + 6.0 * scale * 0.044715 * square)
    return result, slope


def columns(height, tile=TILE):
    return pl.BlockSpec((height, tile), lambda i: (0, i))


def whole(*shape):
    return pl.BlockSpec(shape, lambda i: (0,) * len(shape))


def once(*shape):
    return pl.BlockSpec(shape, lambda i: (0,) * len(shape), pipeline_mode=pl.Buffered(1))


def shaped(kind, *shape):
    return jax.ShapeDtypeStruct(shape, kind)


def pieces_of(width):
    return [(a, a + 256) for a in range(0, width, 256)]


def run(name, kernel, batch, in_specs, out_specs, out_shape, scratch, flops, *args, tile=TILE):
    moved = sum(a.size * a.dtype.itemsize for a in args)
    moved += sum(math.prod(o.shape) * o.dtype.itemsize for o in out_shape)
    return pl.pallas_call(
        kernel,
        grid=(batch // tile,),
        in_specs=in_specs,
        out_specs=out_specs,
        out_shape=out_shape,
        scratch_shapes=scratch,
        compiler_params=PARAMS,
        cost_estimate=pl.CostEstimate(flops=flops, bytes_accessed=moved, transcendentals=0),
        name=name,
    )(*args)


def first_step():
    return pl.when(pl.program_id(0) == 0)


def last_step():
    return pl.when(pl.program_id(0) == pl.num_programs(0) - 1)


def turn(out_ref, matrix_ref, tail_ref=None, edge_ref=None):
    for a, b in pieces_of(H):
        out_ref[a:b, :H] = matrix_ref[:, a:b].T
    if tail_ref is not None:
        out_ref[:H, H:] = tail_ref[...].T
    if edge_ref is not None:
        out_ref[H:, :] = edge_ref[...]


def straight(out_ref, matrix_ref, tail_ref, edge_ref=None):
    out_ref[:H, :H] = matrix_ref[...]
    row = lax.broadcasted_iota(jnp.int32, (TALL - H, H), 0)
    tail = tail_ref[: TALL - H, :].astype(F32)
    out_ref[H:, :H] = jnp.where(row < EXTRA, tail, 0.0).astype(LOW)
    if edge_ref is not None:
        lane = lax.broadcasted_iota(jnp.int32, (TALL - H, WIDE), 1)
        edge = jnp.where(lane < D, edge_ref[...].astype(F32), 0.0)
        edge = jnp.concatenate([edge, jnp.zeros((LANES - (TALL - H), WIDE), F32)])
        out_ref[:, H:] = edge.T[:TALL].astype(LOW)


def widen(out_ref, value_ref):
    @first_step()
    def _():
        out_ref[TALL:] = jnp.zeros((WIDE - TALL, out_ref.shape[1]), LOW)

    out_ref[:TALL] = value_ref[...]


class Spread:
    def __init__(self, groups, rows, count, parts=1, below=False):
        self.masks = halves(groups)
        self.kinds = kinds_of(groups)
        self.rows, self.count, self.parts, self.below = rows, count, parts, below
        self.direct = rows % 16 == 0

    def shapes(self):
        if not self.direct:
            return [shaped(F32, TALL, H)] * self.parts
        height = self.rows * self.parts + (AUX_ROWS if self.below else 0)
        outs = [shaped(kind, len(row), height, H) for row, kind in zip(self.masks, self.kinds)]
        overs = 0 if self.below else self.parts
        return outs + [shaped(F32, self.count, 8, H)] * overs

    def specs(self):
        return [whole(*s.shape) for s in self.shapes()]

    def write(self, acc_refs, index_ref, out_refs, over_refs=None):
        if not self.direct:
            for acc_ref, ref in zip(acc_refs, out_refs):
                ref[...] = acc_ref[...]
            return
        rows = self.rows
        for ref, row, kind in zip(out_refs, self.masks, self.kinds):
            for j, mask in enumerate(row):
                at = jnp.bitwise_xor(index_ref[0], mask)
                start = pl.multiple_of(at * rows, rows)
                for i, acc_ref in enumerate(acc_refs):
                    block = acc_ref[pl.ds(start, rows), :]
                    ref[j, i * rows : (i + 1) * rows] = block.astype(kind)
                if self.below:
                    mine = acc_ref[pl.ds(pl.multiple_of(start + rows, 8), 8), :]
                    parts = [mine[:SPILL_ROWS]] + [v[at][:SPILL_ROWS] for v in over_refs]
                    parts.append(jnp.zeros((AUX_ROWS - MISC_ROW, H), F32))
                    ref[j, rows:] = jnp.concatenate(parts).astype(kind)
        if not self.below:
            for acc_ref, ref in zip(acc_refs, out_refs[len(self.masks) :]):
                for k in range(self.count):
                    ref[k] = acc_ref[(k + 1) * rows : (k + 1) * rows + 8, :]

    def finish(self, outs, index, overs=None):
        if self.direct:
            return list(outs)
        rows, count = self.rows, self.count
        blocks = [grad[:H].reshape(count, rows, H) for grad in outs]
        own = [
            jnp.stack([grad[(k + 1) * rows : (k + 1) * rows + 8] for k in range(count)])
            for grad in outs
        ]
        if self.below:
            blocks += [v[:, :SPILL_ROWS] for v in own + list(overs)]
            blocks.append(jnp.zeros((count, AUX_ROWS - MISC_ROW, H), F32))
        stacks = list(split(index, jnp.concatenate(blocks, axis=1), self.masks, self.kinds))
        return stacks if self.below else stacks + own


ANY = pl.BlockSpec(memory_space=pl.ANY)
REST = TALL - H


def forward_cross(features, one, two):
    batch = features.shape[1]

    def kernel(f_ref, *refs):
        x_ref, mixer_one_ref, mixer_two_ref, one_ref, two_ref = refs[6:11]
        turned_one, turned_two, wide_ref = refs[11:]

        @first_step()
        def _():
            turn(turned_one, *refs[:3])
            turn(turned_two, *refs[3:6])

        x_ref[:H] = f_ref[:H]
        last = f_ref[H:].astype(F32)
        last = jnp.concatenate([last, jnp.ones((1, TILE), F32), jnp.zeros((TALL - D - 1, TILE), F32)])
        x_ref[H:] = last.astype(LOW)
        widen(wide_ref, x_ref)
        layers = []
        for a, b in pieces_of(TILE):
            mixer = product(turned_one[...], wide_ref[:, a:b])
            mixer_one_ref[:, a:b] = mixer.astype(LOW)
            part = x_ref[:, a:b].astype(F32)
            layer = part * mixer + part
            layers.append(layer)
            one_ref[:, a:b] = layer.astype(LOW)
        wide_ref[:TALL] = one_ref[...]
        for (a, b), layer in zip(pieces_of(TILE), layers):
            mixer = product(turned_two[...], wide_ref[:, a:b])
            mixer_two_ref[:, a:b] = mixer.astype(LOW)
            two_ref[:, a:b] = (x_ref[:, a:b].astype(F32) * mixer + layer).astype(LOW)

    return run(
        "forward_cross",
        kernel,
        batch,
        [columns(D)] + [once(H, H), once(LANES, H), once(REST, WIDE)] * 2,
        [columns(TALL)] * 5,
        [shaped(LOW, TALL, batch)] * 5,
        [pltpu.VMEM((TALL, WIDE), LOW)] * 2 + [pltpu.VMEM((WIDE, TILE), LOW)],
        4 * batch * TALL * TALL,
        features, *one, *two,
    )


def deep(spread, index, layer_low, examples, matrix_one, tail, matrix, lines, inverse):
    batch = layer_low.shape[1]
    days = inverse.shape[0]

    def kernel(k_ref, l_ref, x_ref, w_one_ref, t_ref, w_ref, n_ref, i_ref, *refs):
        logit_ref, back_ref, line_ref, sum_ref = refs[:4]
        out_refs = refs[4:-8]
        turned_one, turned, acc_ref, hidden_ref, slope_ref, low_ref, part_ref, wide_ref = refs[-8:]

        @first_step()
        def _():
            turn(turned_one, w_one_ref, t_ref)
            turn(turned, w_ref)
            acc_ref[...] = jnp.zeros_like(acc_ref)
            sum_ref[...] = jnp.zeros_like(sum_ref)
            part_ref[...] = jnp.zeros_like(part_ref)
            row = lax.broadcasted_iota(jnp.int32, (REST, TILE), 0)
            hidden_ref[H:] = jnp.where(row == 0, 1.0, 0.0).astype(LOW)

        widen(wide_ref, l_ref)
        for a, b in pieces_of(TILE):
            hidden, slope = gelu_both(product(turned_one[...], wide_ref[:, a:b]))
            hidden_ref[:H, a:b] = hidden.astype(LOW)
            slope_ref[:, a:b] = slope
        head = n_ref[:, 1:2]
        for a, b in pieces_of(TILE):
            two, slope = gelu_both(product(turned[...], hidden_ref[:H, a:b]) + n_ref[:, 0:1])
            two = two.astype(LOW).astype(F32)
            logits = n_ref[0:1, 2:3] + jnp.sum(two * head, axis=0, keepdims=True)
            label = x_ref[0:1, a:b]
            day = x_ref[1:2, a:b].astype(jnp.int32)
            row = lax.broadcasted_iota(jnp.int32, (days, b - a), 0)
            weight = jnp.sum(jnp.where(row == day, i_ref[:, 0:1], 0.0), axis=0, keepdims=True)
            decay = jnp.exp(-jnp.abs(logits))
            entropy = jnp.maximum(logits, 0.0) + jnp.log1p(decay) - label * logits
            chance = jnp.where(logits >= 0.0, 1.0, decay) / (1.0 + decay)
            logit_grad = (chance - label) * weight
            logit_ref[:, a:b] = logits
            sum_ref[0:1, a:b] += logit_grad
            sum_ref[1:2, a:b] += entropy * weight
            low_ref[:, a:b] = ((logit_grad * head) * slope).astype(LOW)
            one = logit_grad * two
            part = one[:, :LANES]
            for at in range(LANES, b - a, LANES):
                part = part + one[:, at : at + LANES]
            part_ref[...] += part
        for a, b in pieces_of(TILE):
            back_ref[:, a:b] = (product(w_ref[...], low_ref[:, a:b]) * slope_ref[:, a:b]).astype(LOW)
        for a, b in pieces_of(H):
            acc_ref[:, a:b] += outer(hidden_ref[...], low_ref[a:b])

        @last_step()
        def _():
            line_ref[0:8] = jnp.broadcast_to(
                jnp.sum(part_ref[...].T, axis=0, keepdims=True), (8, H)
            )
            line_ref[8:16] = acc_ref[H : H + 8]
            spread.write([acc_ref], k_ref, out_refs)

    return run(
        "deep",
        kernel,
        batch,
        [
            SMEM,
            columns(TALL),
            columns(2),
            once(H, H),
            once(LANES, H),
            once(H, H),
            whole(H, LANES),
            whole(days, LANES),
        ],
        [columns(1), columns(H), whole(16, H), whole(8, TILE)] + spread.specs(),
        [
            shaped(F32, 1, batch),
            shaped(LOW, H, batch),
            shaped(F32, 16, H),
            shaped(F32, 8, TILE),
        ]
        + spread.shapes(),
        [
            pltpu.VMEM((H, WIDE), LOW),
            pltpu.VMEM((H, H), LOW),
            pltpu.VMEM((TALL, H), F32),
            pltpu.VMEM((TALL, TILE), LOW),
            pltpu.VMEM((H, TILE), F32),
            pltpu.VMEM((H, TILE), LOW),
            pltpu.VMEM((H, LANES), F32),
            pltpu.VMEM((WIDE, TILE), LOW),
        ],
        8 * batch * H * H,
        index, layer_low, examples, matrix_one, tail, matrix, lines, inverse,
    )


def back_layers(
    spread, index, grad_low, low_two, features, low_one, mixer_one, mixer_two, matrix_deep,
    tail_deep, matrix, tail, edge,
):
    batch = features.shape[1]
    tile = TILE // 2

    def kernel(k_ref, g_ref, two_ref, x_ref, one_ref, m_one_ref, m_two_ref, *refs):
        weights, refs = refs[:5], refs[5:]
        part_ref, mixer_ref, side_ref, deep_line_ref, line_ref = refs[:5]
        out_refs = refs[5:-6]
        held_deep, held, deep_acc, acc_ref, low_ref, above_ref = refs[-6:]

        @first_step()
        def _():
            straight(held_deep, *weights[:2])
            straight(held, *weights[2:])
            deep_acc[...] = jnp.zeros_like(deep_acc)
            acc_ref[...] = jnp.zeros_like(acc_ref)
            side_ref[...] = jnp.zeros_like(side_ref)
            low_ref[TALL:] = jnp.zeros((WIDE - TALL, tile), LOW)

        x = x_ref[...].astype(F32)
        above_ref[...] = product(held_deep[...], g_ref[...])
        above = above_ref[...]
        low_ref[:TALL] = (above * x).astype(LOW)
        layer = product(held[...], low_ref[...]) + jnp.maximum(above, jnp.finfo(F32).min)
        mixer_ref[...] = (layer * x).astype(LOW)
        part = above * m_two_ref[...].astype(F32) + layer * (m_one_ref[...].astype(F32) + 1.0)
        part_ref[...] = part.astype(LOW)
        for a, b in pieces_of(H):
            deep_acc[:, a:b] += outer(two_ref[...], g_ref[a:b])
        for a, b in pieces_of(H):
            acc_ref[:, a:b] += outer(one_ref[...], low_ref[a:b])
        side_ref[...] += outer(low_ref[H:TALL], one_ref[...])

        @last_step()
        def _():
            deep_line_ref[...] = deep_acc[H:]
            line_ref[...] = acc_ref[H:]
            spread.write([deep_acc, acc_ref], k_ref, out_refs)

    return run(
        "back_layers",
        kernel,
        batch,
        [SMEM, columns(H, tile)]
        + [columns(TALL, tile)] * 5
        + [once(H, H), once(LANES, H), once(H, H), once(LANES, H), once(REST, WIDE)],
        [columns(TALL, tile), columns(TALL, tile), whole(REST, TALL), whole(REST, H), whole(REST, H)]
        + spread.specs(),
        [
            shaped(LOW, TALL, batch),
            shaped(LOW, TALL, batch),
            shaped(F32, REST, TALL),
            shaped(F32, REST, H),
            shaped(F32, REST, H),
        ]
        + spread.shapes(),
        [
            pltpu.VMEM((TALL, H), LOW),
            pltpu.VMEM((TALL, WIDE), LOW),
            pltpu.VMEM((TALL, H), F32),
            pltpu.VMEM((TALL, H), F32),
            pltpu.VMEM((WIDE, tile), LOW),
            pltpu.VMEM((TALL, tile), F32),
        ],
        8 * batch * TALL * TALL,
        index, grad_low, low_two, features, low_one, mixer_one, mixer_two, matrix_deep, tail_deep,
        matrix, tail, edge,
        tile=tile,
    )


def grad_one(spread, index, mixer_low, features, overs, after):
    batch = features.shape[1]

    def kernel(k_ref, g_ref, x_ref, *refs):
        over_refs = refs[: len(overs)]
        refs = refs[len(overs) + len(after) :]
        side_ref, line_ref = refs[:2]
        out_refs = refs[2:-1]
        acc_ref = refs[-1]

        @first_step()
        def _():
            acc_ref[...] = jnp.zeros_like(acc_ref)
            side_ref[...] = jnp.zeros_like(side_ref)

        for a, b in pieces_of(H):
            acc_ref[:, a:b] += outer(x_ref[...], g_ref[a:b])
        side_ref[...] += outer(g_ref[H:], x_ref[...])

        @last_step()
        def _():
            line_ref[...] = acc_ref[H:]
            spread.write([acc_ref], k_ref, out_refs, over_refs)

    return run(
        "grad_one",
        kernel,
        batch,
        [SMEM, columns(TALL), columns(TALL)]
        + [whole(*v.shape) for v in overs]
        + [ANY] * len(after),
        [whole(REST, TALL), whole(REST, H)] + spread.specs(),
        [shaped(F32, REST, TALL), shaped(F32, REST, H)] + spread.shapes(),
        [pltpu.VMEM((TALL, H), F32)],
        2 * batch * TALL * TALL,
        index, mixer_low, features, *overs, *after,
    )


def back_one(mixer_low, part, matrix, tail, edge, after):
    batch = part.shape[1]

    def kernel(g_ref, p_ref, w_ref, t_ref, e_ref, *refs):
        out_ref, held, wide_ref = refs[len(after) :]

        @first_step()
        def _():
            straight(held, w_ref, t_ref, e_ref)

        widen(wide_ref, g_ref)
        for a, b in pieces_of(TILE):
            value = p_ref[:, a:b].astype(F32) + product(held[...], wide_ref[:, a:b])
            out_ref[:H, a:b] = value[:H]
            out_ref[H:, a:b] = value[H:D]

    return run(
        "back_one",
        kernel,
        batch,
        [columns(TALL), columns(TALL), whole(H, H), whole(LANES, H), whole(REST, WIDE)]
        + [ANY] * len(after),
        [columns(D)],
        [shaped(F32, D, batch)],
        [pltpu.VMEM((TALL, WIDE), LOW), pltpu.VMEM((WIDE, TILE), LOW)],
        2 * batch * TALL * TALL,
        mixer_low, part, matrix, tail, edge, *after,
    )[0]


def local(groups, features, labels, days, master, moment_one, moment_two):
    count = lax.axis_size(AXES)
    index = lax.axis_index(AXES)
    slot = index[None].astype(jnp.int32)
    rows = H // count
    starts = starts_of(count)
    sizes = piece_sizes(count)
    wide_piece = sizes[1]
    piece = [master[a : a + l] for a, l in zip(starts, sizes)]
    block_one = to_block(piece[0], index, D, rows, count)
    block_two = to_block(piece[2], index, D, rows, count)
    block_deep = to_block(piece[4], index, H, rows, count)

    day_hot = (days[:, None] == jnp.arange(DAYS, dtype=jnp.int32)[None, :]).astype(F32)
    own_counts = jnp.sum(day_hot, axis=0)
    counts_high = jnp.floor(own_counts / 64.0)
    counts_low = own_counts - 64.0 * counts_high

    def spill_side(block):
        side = block[rows:, H:].T
        return jnp.pad(side, ((0, 0), (0, rows - SPILL_ROWS)))

    misc = [
        piece[5],
        piece[7],
        piece[8],
        block_one[:rows, H:].T,
        block_two[:rows, H:].T,
        spill_side(block_one),
        spill_side(block_two),
        piece[1],
        piece[3],
        piece[9],
        counts_high,
        counts_low,
    ]
    misc = jnp.concatenate([part.reshape(-1) for part in misc])
    misc = jnp.pad(misc, (0, (AUX_ROWS - MISC_ROW) * H - misc.shape[0])).reshape(-1, H)
    first = jnp.concatenate(
        [
            block_one[:rows, :H],
            block_two[:rows, :H],
            block_one[rows:, :H],
            block_two[rows:, :H],
            block_deep[rows:],
            misc,
        ]
    ).astype(LOW)
    stacks_cross = gather(first, groups, count)
    rest = jnp.concatenate([block_deep[:rows], piece[6].reshape(rows, H)]).astype(LOW)
    stacks_rest = gather(rest, groups, count)
    examples = jnp.stack([labels.astype(F32), days.astype(F32)])

    matrix_one, matrix_two, aux = place(slot, stacks_cross, rows, count, [0, SPILL_ROWS])
    matrix_deep, matrix_top = place(slot, stacks_rest, rows, count, [2 * SPILL_ROWS, None], aux)

    line = aux[:, MISC_ROW]
    at = UNIT_LINES * rows
    units = line[:, :at].reshape(count, UNIT_LINES, rows).transpose(1, 0, 2).reshape(UNIT_LINES, H)
    biases = line[:, at : at + 2 * wide_piece].reshape(count, 2, wide_piece)
    biases = biases.transpose(1, 0, 2).reshape(2, count * wide_piece)
    at += 2 * wide_piece
    head_bias = line[0, at]
    both_counts = jnp.sum(line[:, at + 1 : at + 1 + 2 * DAYS].astype(F32), axis=0)
    counts = 64.0 * both_counts[:DAYS] + both_counts[DAYS:]
    inverse = jnp.broadcast_to((1.0 / counts)[:, None], (DAYS, LANES))
    sides = jnp.pad(units[3:9], ((0, 0), (0, LANES))) + jnp.pad(
        units[9:15], ((0, 0), (rows, LANES - rows))
    )

    def tail_of(at, bias):
        return jnp.concatenate(
            [aux[count - 1, at : at + EXTRA], bias[None, :H], jnp.zeros((LANES - EXTRA - 1, H), LOW)]
        )

    def edge_of(side, bias):
        lane = lax.broadcasted_iota(jnp.int32, side.shape, 1)
        side = jnp.where(lane == D, bias[H:D, None], side)
        return jnp.pad(side, ((0, TALL - H - EXTRA), (0, 0)))

    tail_one, edge_one = tail_of(0, biases[0]), edge_of(sides[:3], biases[0])
    tail_two, edge_two = tail_of(SPILL_ROWS, biases[1]), edge_of(sides[3:], biases[1])
    tail_deep = tail_of(2 * SPILL_ROWS, units[0])
    lines = jnp.concatenate(
        [units[1:3], jnp.full((1, H), head_bias), jnp.zeros((LANES - 3, H), LOW)]
    )
    lines = lines.astype(F32).T
    spread = Spread(groups, rows, count)
    spread_two = Spread(groups, rows, count, 2)
    spread_last = Spread(groups, rows, count, below=True)

    wide_features, mixer_one, mixer_two, low_one, low_two = forward_cross(
        features.T, (matrix_one, tail_one, edge_one), (matrix_two, tail_two, edge_two)
    )
    logits, pre_one_low, top_lines, sums, *outs = deep(
        spread, slot, low_two, examples, matrix_deep, tail_deep, matrix_top, lines, inverse
    )
    *stacks, _ = spread.finish(outs, slot)
    top_plane = core_stage(stacks, groups, count)
    part, mixer_one_low, two_side, deep_lines, two_lines, *outs = back_layers(
        spread_two, slot, pre_one_low, low_two, wide_features, low_one, mixer_one, mixer_two,
        matrix_deep, tail_deep, matrix_two, tail_two, edge_two,
    )
    *stacks, deep_over, two_over = spread_two.finish(outs, slot)
    both_plane = core_stage(stacks, groups, count)
    overs = (two_over, deep_over)
    one_side, one_lines, *outs = grad_one(
        spread_last, slot, mixer_one_low, wide_features, overs, top_plane[1:]
    )
    stacks = spread_last.finish(outs, slot, overs)
    last_plane = core_stage(stacks, groups, count)
    feature_grad = back_one(
        mixer_one_low, part, matrix_one, tail_one, edge_one, both_plane[1:] + stacks[1:2]
    )

    sums = jnp.pad(jnp.sum(sums[:2], axis=1)[None], ((0, 0), (0, WIDE - 2)))
    vectors = jnp.concatenate(
        [
            jnp.pad(
                jnp.concatenate(
                    [one_lines[EXTRA:4], two_lines[EXTRA:4], deep_lines[EXTRA:4], top_lines[8:9], top_lines[:1]]
                ),
                ((0, 0), (0, LANES)),
            ),
            jnp.pad(jnp.concatenate([one_side[:3], two_side[:3]]), ((0, 0), (0, WIDE - TALL))),
            sums,
            jnp.zeros((4, WIDE), F32),
        ]
    )
    vectors = jnp.sum(lax.all_gather(vectors, AXES, axis=0), axis=0)
    loss = vectors[11, 1]
    side_sums = vectors[5:11]

    own_top = z_stage(plane_stage(top_plane, groups, count), groups, count)
    own_both = z_stage(plane_stage(both_plane, groups, count), groups, count)
    own_deep, own_two = own_both[:rows], own_both[rows:]
    own_last = z_stage(plane_stage(last_plane, groups, count), groups, count)
    own_one = own_last[:rows]
    spills = own_last[rows : rows + MISC_ROW]
    row = lax.broadcasted_iota(jnp.int32, spills.shape, 0)
    beyond = (row % SPILL_ROWS >= EXTRA) & (index == count - 1)
    spills = jnp.where(beyond, 0.0, spills)
    wide_biases = jnp.concatenate(
        [vectors[:2, :H], side_sums[:, D].reshape(2, EXTRA)], axis=1
    )
    wide_biases = jnp.pad(wide_biases, ((0, 0), (0, count * wide_piece - D)))
    wide_biases = lax.dynamic_slice(wide_biases, (0, index * wide_piece), (2, wide_piece))
    units = lax.dynamic_slice(vectors[2:5], (0, index * rows), (3, rows))
    side_sums = jnp.pad(side_sums[:, :D], ((0, 0), (0, WIDE - D)))
    side_sums = lax.dynamic_slice(side_sums, (0, index * rows), (6, rows + SPILL_ROWS)).T

    def whole_block(main, number):
        low = number * SPILL_ROWS
        body = jnp.concatenate([main, spills[low : low + SPILL_ROWS]])
        if number == 2:
            return body
        return jnp.concatenate([body, side_sums[:, 3 * number : 3 * number + 3]], axis=1)

    flat_grad = jnp.concatenate(
        [
            from_block(whole_block(own_one, 0), index, sizes[0], rows, count),
            wide_biases[0],
            from_block(whole_block(own_two, 1), index, sizes[2], rows, count),
            wide_biases[1],
            from_block(whole_block(own_deep, 2), index, sizes[4], rows, count),
            units[0],
            own_top.reshape(-1),
            units[1],
            units[2],
            jnp.where(index == 0, vectors[11, :1], 0.0),
        ]
    )
    new_moment_one = 0.9 * moment_one + 0.1 * flat_grad
    new_moment_two = 0.999 * moment_two + 0.001 * flat_grad * flat_grad
    corrected_one = new_moment_one / (1.0 - 0.9**STEP)
    corrected_two = new_moment_two / (1.0 - 0.999**STEP)
    new_master = master - 0.03 * (corrected_one / (jnp.sqrt(corrected_two) + 1e-08) + 0.01 * master)
    new_bias = jnp.concatenate(
        [new_master[starts[i] : starts[i] + sizes[i]] for i in (1, 3, 5, 7, 9)]
    )
    return (
        logits.reshape(-1),
        loss,
        feature_grad.T,
        flat_grad,
        new_moment_one,
        new_moment_two,
        new_master,
        new_bias,
    )


def solution(mesh):
    line = P(AXES)
    table = P(AXES, None)
    groups = bit_groups(mesh)
    return jax.shard_map(
        functools.partial(local, groups),
        mesh=mesh,
        in_specs=(table, line, line, line, line, line),
        out_specs=(line, P(), table, line, line, line, line, line),
        check_vma=False,
    )
```

```python
import functools
import math

import jax
import jax.numpy as jnp
from jax import lax
from jax.experimental import pallas as pl
from jax.experimental.pallas import tpu as pltpu
from jax.sharding import PartitionSpec as P

D = 1027
H = 1024
DAYS = 24
STEP = 10
AXES = ("dp", "cores")
EXTRA = D - H
LANES = 128
WIDE = H + LANES
AUX_ROWS = 16
SPILL_ROWS = 4
MISC_ROW = 12
UNIT_LINES = 15
TILE = 512
TALL = H + 16
MIB = 1024 * 1024
F32 = jnp.float32
LOW = jnp.bfloat16
SMEM = pl.BlockSpec(memory_space=pltpu.SMEM)
VMEM = pl.BlockSpec(memory_space=pltpu.VMEM)
PARAMS = pltpu.CompilerParams(vmem_limit_bytes=56 * MIB)


def shapes():
    return [(D, D), (D,), (D, D), (D,), (D, H), (H,), (H, H), (H,), (H,), (1,)]


def piece_sizes(count):
    return [(math.prod(shape) + count - 1) // count for shape in shapes()[:-1]] + [1]


def starts_of(count):
    starts = []
    position = 0
    for piece in piece_sizes(count):
        starts.append(position)
        position += piece
    return starts


def to_block(piece, index, width, rows, count):
    excess = piece.shape[0] - rows * width
    size = (rows + SPILL_ROWS) * width
    lead = (count - 1) * excess
    padded = jnp.pad(piece, (lead, max(0, size - piece.shape[0])))
    line = lax.dynamic_slice(padded, (lead - index * excess,), (size,))
    return line.reshape(rows + SPILL_ROWS, width)


def from_block(block, index, piece, rows, count):
    width = block.shape[1]
    excess = piece - rows * width
    last = (count - 1) * excess
    line = jnp.pad(block.reshape(-1), (0, max(0, last + piece - block.size)))
    return lax.dynamic_slice(line, (index * excess,), (piece,))


def bit_groups(mesh):
    devices = mesh.devices.reshape(-1)
    groups = {"z": [], "plane": [], "core": []}
    bit = 1
    while bit < devices.size:
        here = getattr(devices[0], "coords", None)
        there = getattr(devices[bit], "coords", None)
        if here is None or there is None:
            name = "core" if bit == 1 else "plane" if bit <= 4 else "z"
        elif tuple(here) == tuple(there):
            name = "core"
        elif here[2] != there[2]:
            name = "z"
        else:
            name = "plane"
        groups[name].append(bit)
        bit *= 2
    return groups


def masks_of(bits):
    masks = [0]
    for bit in bits:
        masks = masks + [mask | bit for mask in masks]
    return masks


def teams(bits, count):
    masks = masks_of(bits)
    return [[k | mask for mask in masks] for k in range(count) if not k & masks[-1]]


def owner(index, mask, groups, by_z):
    if by_z:
        index = jnp.bitwise_and(index, ~masks_of(groups["z"])[-1])
    return jnp.bitwise_xor(index, mask)


def swap(value, mask, count):
    return lax.ppermute(value, AXES, [(k, k ^ mask) for k in range(count)])


def gather(block, groups, count, direct=False):
    z_masks = masks_of(groups["z"])
    core_masks = masks_of(groups["core"])
    line = jnp.stack([block] + [swap(block, mask, count) for mask in z_masks[1:]])
    plane = [(line, z_masks)]
    if len(groups["plane"]) == 2 and len(z_masks) > 1 and not direct:
        one, two = groups["plane"]
        half = len(z_masks) // 2
        by_one = swap(line, one, count)
        by_two = swap(line, two, count)
        plane.append((by_one, [one ^ z for z in z_masks]))
        plane.append((by_two, [two ^ z for z in z_masks]))
        both = one ^ two
        plane.append((swap(by_one[:half], two, count), [both ^ z for z in z_masks[:half]]))
        plane.append((swap(by_two[half:], one, count), [both ^ z for z in z_masks[half:]]))
    else:
        for mask in masks_of(groups["plane"])[1:]:
            plane.append((swap(line, mask, count), [mask ^ z for z in z_masks]))
    result = list(plane)
    for core in core_masks[1:]:
        result += [(swap(value, core, count), [core ^ m for m in row]) for value, row in plane]
    return result


def place(index, stacks, rows, count, parts, aux=None):
    sources = [value for value, _ in stacks]
    masks = [row for _, row in stacks]
    carries = aux is None
    top = min(16, rows)

    def kernel(index_ref, *refs):
        refs = list(refs)
        aux_ref = refs.pop() if carries else refs.pop(0)
        outs = refs[len(sources) :]
        for ref, row in zip(refs, masks):
            for j, mask in enumerate(row):
                at = jnp.bitwise_xor(index_ref[0], mask)
                for i, out_ref in enumerate(outs):
                    out_ref[at] = ref[j, i * rows : (i + 1) * rows]
                if carries:
                    aux_ref[at] = ref[j, len(outs) * rows :]
        for spill_at, out_ref in zip(parts, outs):
            if spill_at is None:
                continue
            for k in range(1, count):
                spill = aux_ref[k - 1].astype(F32)[spill_at : spill_at + SPILL_ROWS]
                old = out_ref[k, :top].astype(F32)
                new = old[:SPILL_ROWS] + spill
                if top > SPILL_ROWS:
                    new = jnp.concatenate([new, old[SPILL_ROWS:]], axis=0)
                out_ref[k, :top] = new.astype(LOW)

    out_shape = [jax.ShapeDtypeStruct((count, rows, H), LOW)] * len(parts)
    if carries:
        out_shape.append(jax.ShapeDtypeStruct((count, AUX_ROWS, H), LOW))
    extra = [] if carries else [aux]
    result = pl.pallas_call(
        kernel,
        out_shape=out_shape,
        in_specs=[SMEM] + [VMEM] * (len(extra) + len(sources)),
        out_specs=[VMEM] * len(out_shape),
        compiler_params=PARAMS,
        name="place",
    )(index, *extra, *sources)
    return [value.reshape(H, H) for value in result[: len(parts)]] + list(result[len(parts) :])


def split(index, value, masks, kinds, groups, by_z):
    def kernel(index_ref, value_ref, *out_refs):
        for ref, row, kind in zip(out_refs, masks, kinds):
            for j, mask in enumerate(row):
                ref[j] = value_ref[owner(index_ref[0], mask, groups, by_z)].astype(kind)

    shape = value.shape[1:]
    return pl.pallas_call(
        kernel,
        out_shape=[
            jax.ShapeDtypeStruct((len(row),) + shape, kind) for row, kind in zip(masks, kinds)
        ],
        in_specs=[SMEM, VMEM],
        out_specs=[VMEM] * len(masks),
        compiler_params=PARAMS,
        name="split",
    )(index, value)


def halves(groups):
    z_masks, plane_masks, core_masks = (masks_of(groups[g]) for g in ("z", "plane", "core"))
    inner = [p ^ z for p in plane_masks for z in z_masks]
    return [[core ^ m for m in inner] for core in core_masks]


def kinds_of(groups):
    return [F32] + [LOW] * (len(halves(groups)) - 1)


def core_stage(stacks, groups, count):
    z_masks, plane_masks, core_masks = (masks_of(groups[g]) for g in ("z", "plane", "core"))
    kept = stacks[0]
    for core, stack in zip(core_masks[1:], stacks[1:]):
        kept = kept + swap(stack, core, count).astype(F32)
    kept = kept.reshape((len(plane_masks), len(z_masks)) + kept.shape[1:])
    return [kept[0]] + [kept[j].astype(LOW) for j in range(1, len(plane_masks))]


def plane_stage(parts, groups, count):
    total = parts[0]
    for mask, part in zip(masks_of(groups["plane"])[1:], parts[1:]):
        total = total + swap(part, mask, count).astype(F32)
    return total


def z_parts(total):
    return [total[0]] + [total[j].astype(LOW) for j in range(1, total.shape[0])]


def z_stage(parts, groups, count):
    own = parts[0]
    for mask, part in zip(masks_of(groups["z"])[1:], parts[1:]):
        own = own + swap(part, mask, count).astype(F32)
    return own


def z_scatter(total, groups, count):
    if not groups["z"]:
        return total[0]
    return lax.psum_scatter(
        total, AXES, scatter_dimension=0, axis_index_groups=teams(groups["z"], count)
    )


def product(left, right):
    return lax.dot_general(left, right, (((1,), (0,)), ((), ())), preferred_element_type=F32)


def outer(left, right):
    return lax.dot_general(left, right, (((1,), (1,)), ((), ())), preferred_element_type=F32)


def gelu_both(value):
    scale = math.sqrt(2.0 / math.pi)
    square = value * value
    share = 0.5 + 0.5 * jnp.tanh(value * (scale + scale * 0.044715 * square))
    result = value * share
    slope = share + result * (1.0 - share) * (2.0 * scale + 6.0 * scale * 0.044715 * square)
    return result, slope


def columns(height, tile=TILE):
    return pl.BlockSpec((height, tile), lambda i: (0, i))


def whole(*shape):
    return pl.BlockSpec(shape, lambda i: (0,) * len(shape))


def once(*shape):
    return pl.BlockSpec(shape, lambda i: (0,) * len(shape), pipeline_mode=pl.Buffered(1))


def shaped(kind, *shape):
    return jax.ShapeDtypeStruct(shape, kind)


def pieces_of(width):
    return [(a, a + 256) for a in range(0, width, 256)]


def run(name, kernel, batch, in_specs, out_specs, out_shape, scratch, flops, *args, tile=TILE):
    moved = sum(a.size * a.dtype.itemsize for a in args)
    moved += sum(math.prod(o.shape) * o.dtype.itemsize for o in out_shape)
    return pl.pallas_call(
        kernel,
        grid=(batch // tile,),
        in_specs=in_specs,
        out_specs=out_specs,
        out_shape=out_shape,
        scratch_shapes=scratch,
        compiler_params=PARAMS,
        cost_estimate=pl.CostEstimate(flops=flops, bytes_accessed=moved, transcendentals=0),
        name=name,
    )(*args)


def first_step():
    return pl.when(pl.program_id(0) == 0)


def last_step():
    return pl.when(pl.program_id(0) == pl.num_programs(0) - 1)


def turn(out_ref, matrix_ref, tail_ref=None, edge_ref=None):
    for a, b in pieces_of(H):
        out_ref[a:b, :H] = matrix_ref[:, a:b].T
    if tail_ref is not None:
        out_ref[:H, H:] = tail_ref[...].T
    if edge_ref is not None:
        out_ref[H:, :] = edge_ref[...]


def straight(out_ref, matrix_ref, tail_ref, edge_ref=None):
    out_ref[:H, :H] = matrix_ref[...]
    row = lax.broadcasted_iota(jnp.int32, (TALL - H, H), 0)
    tail = tail_ref[: TALL - H, :].astype(F32)
    out_ref[H:, :H] = jnp.where(row < EXTRA, tail, 0.0).astype(LOW)
    if edge_ref is not None:
        lane = lax.broadcasted_iota(jnp.int32, (TALL - H, WIDE), 1)
        edge = jnp.where(lane < D, edge_ref[...].astype(F32), 0.0)
        edge = jnp.concatenate([edge, jnp.zeros((LANES - (TALL - H), WIDE), F32)])
        out_ref[:, H:] = edge.T[:TALL].astype(LOW)


def widen(out_ref, value_ref):
    @first_step()
    def _():
        out_ref[TALL:] = jnp.zeros((WIDE - TALL, out_ref.shape[1]), LOW)

    out_ref[:TALL] = value_ref[...]


class Spread:
    def __init__(self, groups, rows, count, parts=1, below=False, by_z=False):
        self.groups, self.by_z = groups, by_z
        self.masks = halves(groups)
        self.kinds = kinds_of(groups)
        self.rows, self.count, self.parts, self.below = rows, count, parts, below
        self.direct = rows % 16 == 0

    def shapes(self):
        if not self.direct:
            return [shaped(F32, TALL, H)] * self.parts
        height = self.rows * self.parts + (AUX_ROWS if self.below else 0)
        outs = [shaped(kind, len(row), height, H) for row, kind in zip(self.masks, self.kinds)]
        overs = 0 if self.below else self.parts
        return outs + [shaped(F32, self.count, 8, H)] * overs

    def specs(self):
        return [whole(*s.shape) for s in self.shapes()]

    def write(self, acc_refs, index_ref, out_refs, over_refs=None):
        if not self.direct:
            for acc_ref, ref in zip(acc_refs, out_refs):
                ref[...] = acc_ref[...]
            return
        rows = self.rows
        for ref, row, kind in zip(out_refs, self.masks, self.kinds):
            for j, mask in enumerate(row):
                at = owner(index_ref[0], mask, self.groups, self.by_z)
                start = pl.multiple_of(at * rows, rows)
                for i, acc_ref in enumerate(acc_refs):
                    block = acc_ref[pl.ds(start, rows), :]
                    ref[j, i * rows : (i + 1) * rows] = block.astype(kind)
                if self.below:
                    mine = acc_ref[pl.ds(pl.multiple_of(start + rows, 8), 8), :]
                    parts = [mine[:SPILL_ROWS]] + [v[at][:SPILL_ROWS] for v in over_refs]
                    parts.append(jnp.zeros((AUX_ROWS - MISC_ROW, H), F32))
                    ref[j, rows:] = jnp.concatenate(parts).astype(kind)
        if not self.below:
            for acc_ref, ref in zip(acc_refs, out_refs[len(self.masks) :]):
                for k in range(self.count):
                    ref[k] = acc_ref[(k + 1) * rows : (k + 1) * rows + 8, :]

    def finish(self, outs, index, overs=None):
        if self.direct:
            return list(outs)
        rows, count = self.rows, self.count
        blocks = [grad[:H].reshape(count, rows, H) for grad in outs]
        own = [
            jnp.stack([grad[(k + 1) * rows : (k + 1) * rows + 8] for k in range(count)])
            for grad in outs
        ]
        if self.below:
            blocks += [v[:, :SPILL_ROWS] for v in own + list(overs)]
            blocks.append(jnp.zeros((count, AUX_ROWS - MISC_ROW, H), F32))
        stacks = split(
            index, jnp.concatenate(blocks, axis=1), self.masks, self.kinds, self.groups, self.by_z
        )
        stacks = list(stacks)
        return stacks if self.below else stacks + own


ANY = pl.BlockSpec(memory_space=pl.ANY)
REST = TALL - H


def forward_cross(features, one, two):
    batch = features.shape[1]

    def kernel(f_ref, *refs):
        x_ref, mixer_one_ref, mixer_two_ref, one_ref, two_ref = refs[6:11]
        turned_one, turned_two, wide_ref = refs[11:]

        @first_step()
        def _():
            turn(turned_one, *refs[:3])
            turn(turned_two, *refs[3:6])

        x_ref[:H] = f_ref[:H]
        last = f_ref[H:].astype(F32)
        last = jnp.concatenate([last, jnp.ones((1, TILE), F32), jnp.zeros((TALL - D - 1, TILE), F32)])
        x_ref[H:] = last.astype(LOW)
        widen(wide_ref, x_ref)
        layers = []
        for a, b in [(0, TILE)]:
            mixer = product(turned_one[...], wide_ref[:, a:b])
            mixer_one_ref[:, a:b] = mixer.astype(LOW)
            part = x_ref[:, a:b].astype(F32)
            layer = part * mixer + part
            layers.append(layer)
            one_ref[:, a:b] = layer.astype(LOW)
        wide_ref[:TALL] = one_ref[...]
        for (a, b), layer in zip([(0, TILE)], layers):
            mixer = product(turned_two[...], wide_ref[:, a:b])
            mixer_two_ref[:, a:b] = mixer.astype(LOW)
            two_ref[:, a:b] = (x_ref[:, a:b].astype(F32) * mixer + layer).astype(LOW)

    return run(
        "forward_cross",
        kernel,
        batch,
        [columns(D)] + [once(H, H), once(LANES, H), once(REST, WIDE)] * 2,
        [columns(TALL)] * 5,
        [shaped(LOW, TALL, batch)] * 5,
        [pltpu.VMEM((TALL, WIDE), LOW)] * 2 + [pltpu.VMEM((WIDE, TILE), LOW)],
        4 * batch * TALL * TALL,
        features, *one, *two,
    )


def deep(spread, index, layer_low, examples, matrix_one, tail, matrix, lines, inverse):
    batch = layer_low.shape[1]
    days = inverse.shape[0]

    def kernel(k_ref, l_ref, x_ref, w_one_ref, t_ref, w_ref, n_ref, i_ref, *refs):
        logit_ref, back_ref, line_ref, sum_ref = refs[:4]
        out_refs = refs[4:-8]
        turned_one, turned, acc_ref, hidden_ref, slope_ref, low_ref, part_ref, wide_ref = refs[-8:]

        @first_step()
        def _():
            turn(turned_one, w_one_ref, t_ref)
            turn(turned, w_ref)
            acc_ref[...] = jnp.zeros_like(acc_ref)
            sum_ref[...] = jnp.zeros_like(sum_ref)
            part_ref[...] = jnp.zeros_like(part_ref)
            row = lax.broadcasted_iota(jnp.int32, (REST, TILE), 0)
            hidden_ref[H:] = jnp.where(row == 0, 1.0, 0.0).astype(LOW)

        widen(wide_ref, l_ref)
        for a, b in pieces_of(TILE):
            hidden, slope = gelu_both(product(turned_one[...], wide_ref[:, a:b]))
            hidden_ref[:H, a:b] = hidden.astype(LOW)
            slope_ref[:, a:b] = slope
        head = n_ref[:, 1:2]
        for a, b in pieces_of(TILE):
            two, slope = gelu_both(product(turned[...], hidden_ref[:H, a:b]) + n_ref[:, 0:1])
            two = two.astype(LOW).astype(F32)
            logits = n_ref[0:1, 2:3] + jnp.sum(two * head, axis=0, keepdims=True)
            label = x_ref[0:1, a:b]
            day = x_ref[1:2, a:b].astype(jnp.int32)
            row = lax.broadcasted_iota(jnp.int32, (days, b - a), 0)
            weight = jnp.sum(jnp.where(row == day, i_ref[:, 0:1], 0.0), axis=0, keepdims=True)
            decay = jnp.exp(-jnp.abs(logits))
            entropy = jnp.maximum(logits, 0.0) + jnp.log1p(decay) - label * logits
            chance = jnp.where(logits >= 0.0, 1.0, decay) / (1.0 + decay)
            logit_grad = (chance - label) * weight
            logit_ref[:, a:b] = logits
            sum_ref[0:1, a:b] += logit_grad
            sum_ref[1:2, a:b] += entropy * weight
            low_ref[:, a:b] = ((logit_grad * head) * slope).astype(LOW)
            one = logit_grad * two
            part = one[:, :LANES]
            for at in range(LANES, b - a, LANES):
                part = part + one[:, at : at + LANES]
            part_ref[...] += part
        for a, b in pieces_of(TILE):
            back_ref[:, a:b] = (product(w_ref[...], low_ref[:, a:b]) * slope_ref[:, a:b]).astype(LOW)
        for a, b in pieces_of(H):
            acc_ref[:, a:b] += outer(hidden_ref[...], low_ref[a:b])

        @last_step()
        def _():
            line_ref[0:8] = jnp.broadcast_to(
                jnp.sum(part_ref[...].T, axis=0, keepdims=True), (8, H)
            )
            line_ref[8:16] = acc_ref[H : H + 8]
            spread.write([acc_ref], k_ref, out_refs)

    return run(
        "deep",
        kernel,
        batch,
        [
            SMEM,
            columns(TALL),
            columns(2),
            once(H, H),
            once(LANES, H),
            once(H, H),
            whole(H, LANES),
            whole(days, LANES),
        ],
        [columns(1), columns(H), whole(16, H), whole(8, TILE)] + spread.specs(),
        [
            shaped(F32, 1, batch),
            shaped(LOW, H, batch),
            shaped(F32, 16, H),
            shaped(F32, 8, TILE),
        ]
        + spread.shapes(),
        [
            pltpu.VMEM((H, WIDE), LOW),
            pltpu.VMEM((H, H), LOW),
            pltpu.VMEM((TALL, H), F32),
            pltpu.VMEM((TALL, TILE), LOW),
            pltpu.VMEM((H, TILE), F32),
            pltpu.VMEM((H, TILE), LOW),
            pltpu.VMEM((H, LANES), F32),
            pltpu.VMEM((WIDE, TILE), LOW),
        ],
        8 * batch * H * H,
        index, layer_low, examples, matrix_one, tail, matrix, lines, inverse,
    )


def back_deep(spread, index, grad_low, layer_low, features, matrix, tail, after):
    batch = features.shape[1]

    def kernel(k_ref, g_ref, l_ref, x_ref, w_ref, t_ref, *refs):
        refs = refs[len(after) :]
        layer_ref, mixer_ref, line_ref = refs[:3]
        out_refs = refs[3:-2]
        held, acc_ref = refs[-2:]

        @first_step()
        def _():
            straight(held, w_ref, t_ref)
            acc_ref[...] = jnp.zeros_like(acc_ref)

        for a, b in pieces_of(TILE):
            layer = product(held[...], g_ref[:, a:b])
            layer_ref[:, a:b] = layer
            mixer_ref[:, a:b] = (layer * x_ref[:, a:b].astype(F32)).astype(LOW)
        for a, b in pieces_of(H):
            acc_ref[:, a:b] += outer(l_ref[...], g_ref[a:b])

        @last_step()
        def _():
            line_ref[...] = acc_ref[H:]
            spread.write([acc_ref], k_ref, out_refs)

    return run(
        "back_deep",
        kernel,
        batch,
        [SMEM, columns(H), columns(TALL), columns(TALL), once(H, H), once(LANES, H)]
        + [ANY] * len(after),
        [columns(TALL), columns(TALL), whole(REST, H)] + spread.specs(),
        [shaped(F32, TALL, batch), shaped(LOW, TALL, batch), shaped(F32, REST, H)]
        + spread.shapes(),
        [pltpu.VMEM((TALL, H), LOW), pltpu.VMEM((TALL, H), F32)],
        4 * batch * TALL * H,
        index, grad_low, layer_low, features, matrix, tail, *after,
    )


def back_two(
    spread, index, mixer_low, layer_low, layer_grad, features, mixer_one, mixer_two, matrix, tail,
    edge, after,
):
    batch = features.shape[1]

    def kernel(k_ref, g_ref, l_ref, d_ref, x_ref, one_ref, two_ref, w_ref, t_ref, e_ref, *refs):
        refs = refs[len(after) :]
        part_ref, mixer_ref, side_ref, line_ref = refs[:4]
        out_refs = refs[4:-3]
        held, acc_ref, wide_ref = refs[-3:]

        @first_step()
        def _():
            straight(held, w_ref, t_ref, e_ref)
            acc_ref[...] = jnp.zeros_like(acc_ref)
            side_ref[...] = jnp.zeros_like(side_ref)

        widen(wide_ref, g_ref)
        for a, b in pieces_of(TILE):
            above = d_ref[:, a:b]
            layer = product(held[...], wide_ref[:, a:b]) + above
            mixer_ref[:, a:b] = (layer * x_ref[:, a:b].astype(F32)).astype(LOW)
            part = above * two_ref[:, a:b].astype(F32)
            part = part + layer * (one_ref[:, a:b].astype(F32) + 1.0)
            part_ref[:, a:b] = part.astype(LOW)
        for a, b in pieces_of(H):
            acc_ref[:, a:b] += outer(l_ref[...], g_ref[a:b])
        side_ref[...] += outer(g_ref[H:], l_ref[...])

        @last_step()
        def _():
            line_ref[...] = acc_ref[H:]
            spread.write([acc_ref], k_ref, out_refs)

    return run(
        "back_two",
        kernel,
        batch,
        [SMEM]
        + [columns(TALL)] * 6
        + [once(H, H), once(LANES, H), once(REST, WIDE)]
        + [ANY] * len(after),
        [columns(TALL), columns(TALL), whole(REST, TALL), whole(REST, H)] + spread.specs(),
        [
            shaped(LOW, TALL, batch),
            shaped(LOW, TALL, batch),
            shaped(F32, REST, TALL),
            shaped(F32, REST, H),
        ]
        + spread.shapes(),
        [
            pltpu.VMEM((TALL, WIDE), LOW),
            pltpu.VMEM((TALL, H), F32),
            pltpu.VMEM((WIDE, TILE), LOW),
        ],
        4 * batch * TALL * TALL,
        index, mixer_low, layer_low, layer_grad, features, mixer_one, mixer_two, matrix, tail,
        edge, *after,
    )


def grad_one(spread, index, mixer_low, features, overs, after):
    batch = features.shape[1]

    def kernel(k_ref, g_ref, x_ref, *refs):
        over_refs = refs[: len(overs)]
        refs = refs[len(overs) + len(after) :]
        side_ref, line_ref = refs[:2]
        out_refs = refs[2:-1]
        acc_ref = refs[-1]

        @first_step()
        def _():
            acc_ref[...] = jnp.zeros_like(acc_ref)
            side_ref[...] = jnp.zeros_like(side_ref)

        for a, b in pieces_of(H):
            acc_ref[:, a:b] += outer(x_ref[...], g_ref[a:b])
        side_ref[...] += outer(g_ref[H:], x_ref[...])

        @last_step()
        def _():
            line_ref[...] = acc_ref[H:]
            spread.write([acc_ref], k_ref, out_refs, over_refs)

    return run(
        "grad_one",
        kernel,
        batch,
        [SMEM, columns(TALL), columns(TALL)]
        + [whole(*v.shape) for v in overs]
        + [ANY] * len(after),
        [whole(REST, TALL), whole(REST, H)] + spread.specs(),
        [shaped(F32, REST, TALL), shaped(F32, REST, H)] + spread.shapes(),
        [pltpu.VMEM((TALL, H), F32)],
        2 * batch * TALL * TALL,
        index, mixer_low, features, *overs, *after,
    )


def back_one(mixer_low, part, matrix, tail, edge, after):
    batch = part.shape[1]

    def kernel(g_ref, p_ref, w_ref, t_ref, e_ref, *refs):
        out_ref, held, wide_ref = refs[len(after) :]

        @first_step()
        def _():
            straight(held, w_ref, t_ref, e_ref)

        widen(wide_ref, g_ref)
        for a, b in [(0, TILE)]:
            value = p_ref[:, a:b].astype(F32) + product(held[...], wide_ref[:, a:b])
            out_ref[:H, a:b] = value[:H]
            out_ref[H:, a:b] = value[H:D]

    return run(
        "back_one",
        kernel,
        batch,
        [columns(TALL), columns(TALL), whole(H, H), whole(LANES, H), whole(REST, WIDE)]
        + [ANY] * len(after),
        [columns(D)],
        [shaped(F32, D, batch)],
        [pltpu.VMEM((TALL, WIDE), LOW), pltpu.VMEM((WIDE, TILE), LOW)],
        2 * batch * TALL * TALL,
        mixer_low, part, matrix, tail, edge, *after,
    )[0]


def local(groups, features, labels, days, master, moment_one, moment_two):
    count = lax.axis_size(AXES)
    index = lax.axis_index(AXES)
    slot = index[None].astype(jnp.int32)
    rows = H // count
    starts = starts_of(count)
    sizes = piece_sizes(count)
    wide_piece = sizes[1]
    piece = [master[a : a + l] for a, l in zip(starts, sizes)]
    block_one = to_block(piece[0], index, D, rows, count)
    block_two = to_block(piece[2], index, D, rows, count)
    block_deep = to_block(piece[4], index, H, rows, count)

    day_hot = (days[:, None] == jnp.arange(DAYS, dtype=jnp.int32)[None, :]).astype(F32)
    own_counts = jnp.sum(day_hot, axis=0)
    counts_high = jnp.floor(own_counts / 64.0)
    counts_low = own_counts - 64.0 * counts_high

    def spill_side(block):
        side = block[rows:, H:].T
        return jnp.pad(side, ((0, 0), (0, rows - SPILL_ROWS)))

    misc = [
        piece[5],
        piece[7],
        piece[8],
        block_one[:rows, H:].T,
        block_two[:rows, H:].T,
        spill_side(block_one),
        spill_side(block_two),
        piece[1],
        piece[3],
        piece[9],
        counts_high,
        counts_low,
    ]
    misc = jnp.concatenate([part.reshape(-1) for part in misc])
    misc = jnp.pad(misc, (0, (AUX_ROWS - MISC_ROW) * H - misc.shape[0])).reshape(-1, H)
    first = jnp.concatenate(
        [
            block_one[:rows, :H],
            block_two[:rows, :H],
            block_one[rows:, :H],
            block_two[rows:, :H],
            block_deep[rows:],
            misc,
        ]
    ).astype(LOW)
    stacks_cross = gather(first, groups, count)
    rest = jnp.concatenate([block_deep[:rows], piece[6].reshape(rows, H)]).astype(LOW)
    stacks_rest = gather(rest, groups, count, direct=True)
    examples = jnp.stack([labels.astype(F32), days.astype(F32)])

    matrix_one, matrix_two, aux = place(slot, stacks_cross, rows, count, [0, SPILL_ROWS])
    matrix_deep, matrix_top = place(slot, stacks_rest, rows, count, [2 * SPILL_ROWS, None], aux)

    line = aux[:, MISC_ROW]
    at = UNIT_LINES * rows
    units = line[:, :at].reshape(count, UNIT_LINES, rows).transpose(1, 0, 2).reshape(UNIT_LINES, H)
    biases = line[:, at : at + 2 * wide_piece].reshape(count, 2, wide_piece)
    biases = biases.transpose(1, 0, 2).reshape(2, count * wide_piece)
    at += 2 * wide_piece
    head_bias = line[0, at]
    both_counts = jnp.sum(line[:, at + 1 : at + 1 + 2 * DAYS].astype(F32), axis=0)
    counts = 64.0 * both_counts[:DAYS] + both_counts[DAYS:]
    inverse = jnp.broadcast_to((1.0 / counts)[:, None], (DAYS, LANES))
    sides = jnp.pad(units[3:9], ((0, 0), (0, LANES))) + jnp.pad(
        units[9:15], ((0, 0), (rows, LANES - rows))
    )

    def tail_of(at, bias):
        return jnp.concatenate(
            [aux[count - 1, at : at + EXTRA], bias[None, :H], jnp.zeros((LANES - EXTRA - 1, H), LOW)]
        )

    def edge_of(side, bias):
        lane = lax.broadcasted_iota(jnp.int32, side.shape, 1)
        side = jnp.where(lane == D, bias[H:D, None], side)
        return jnp.pad(side, ((0, TALL - H - EXTRA), (0, 0)))

    tail_one, edge_one = tail_of(0, biases[0]), edge_of(sides[:3], biases[0])
    tail_two, edge_two = tail_of(SPILL_ROWS, biases[1]), edge_of(sides[3:], biases[1])
    tail_deep = tail_of(2 * SPILL_ROWS, units[0])
    lines = jnp.concatenate(
        [units[1:3], jnp.full((1, H), head_bias), jnp.zeros((LANES - 3, H), LOW)]
    )
    lines = lines.astype(F32).T
    spread_top = Spread(groups, rows, count, by_z=True)
    spread = Spread(groups, rows, count)
    spread_last = Spread(groups, rows, count, below=True)

    wide_features, mixer_one, mixer_two, low_one, low_two = forward_cross(
        features.T, (matrix_one, tail_one, edge_one), (matrix_two, tail_two, edge_two)
    )
    logits, pre_one_low, top_lines, sums, *outs = deep(
        spread_top, slot, low_two, examples, matrix_deep, tail_deep, matrix_top, lines, inverse
    )
    *stacks, _ = spread_top.finish(outs, slot)
    top_plane = core_stage(stacks, groups, count)
    layer_grad, mixer_two_low, deep_lines, *outs = back_deep(
        spread, slot, pre_one_low, low_two, wide_features, matrix_deep, tail_deep, stacks[1:2]
    )
    *stacks, deep_over = spread.finish(outs, slot)
    deep_plane = core_stage(stacks, groups, count)
    part, mixer_one_low, two_side, two_lines, *outs = back_two(
        spread, slot, mixer_two_low, low_one, layer_grad, wide_features, mixer_one, mixer_two,
        matrix_two, tail_two, edge_two, top_plane[1:] + stacks[1:2],
    )
    *stacks, two_over = spread.finish(outs, slot)
    top_total = plane_stage(top_plane, groups, count)
    two_plane = core_stage(stacks, groups, count)
    overs = (two_over, deep_over)
    one_side, one_lines, *outs = grad_one(
        spread_last, slot, mixer_one_low, wide_features, overs, deep_plane[1:] + [top_total]
    )
    stacks = spread_last.finish(outs, slot, overs)
    last_plane = core_stage(stacks, groups, count)
    deep_z = z_parts(plane_stage(deep_plane, groups, count))
    feature_grad = back_one(
        mixer_one_low, part, matrix_one, tail_one, edge_one, two_plane[1:] + deep_z[1:]
    )

    sums = jnp.pad(jnp.sum(sums[:2], axis=1)[None], ((0, 0), (0, WIDE - 2)))
    vectors = jnp.concatenate(
        [
            jnp.pad(
                jnp.concatenate(
                    [one_lines[EXTRA:4], two_lines[EXTRA:4], deep_lines[EXTRA:4], top_lines[8:9], top_lines[:1]]
                ),
                ((0, 0), (0, LANES)),
            ),
            jnp.pad(jnp.concatenate([one_side[:3], two_side[:3]]), ((0, 0), (0, WIDE - TALL))),
            sums,
            jnp.zeros((4, WIDE), F32),
        ]
    )
    vectors = jnp.sum(lax.all_gather(vectors, AXES, axis=0), axis=0)
    loss = vectors[11, 1]
    side_sums = vectors[5:11]

    own_top = z_scatter(top_total, groups, count)
    own_deep = z_stage(deep_z, groups, count)
    own_two = z_stage(z_parts(plane_stage(two_plane, groups, count)), groups, count)
    own_last = z_stage(z_parts(plane_stage(last_plane, groups, count)), groups, count)
    own_one = own_last[:rows]
    spills = own_last[rows : rows + MISC_ROW]
    row = lax.broadcasted_iota(jnp.int32, spills.shape, 0)
    beyond = (row % SPILL_ROWS >= EXTRA) & (index == count - 1)
    spills = jnp.where(beyond, 0.0, spills)
    wide_biases = jnp.concatenate(
        [vectors[:2, :H], side_sums[:, D].reshape(2, EXTRA)], axis=1
    )
    wide_biases = jnp.pad(wide_biases, ((0, 0), (0, count * wide_piece - D)))
    wide_biases = lax.dynamic_slice(wide_biases, (0, index * wide_piece), (2, wide_piece))
    units = lax.dynamic_slice(vectors[2:5], (0, index * rows), (3, rows))
    side_sums = jnp.pad(side_sums[:, :D], ((0, 0), (0, WIDE - D)))
    side_sums = lax.dynamic_slice(side_sums, (0, index * rows), (6, rows + SPILL_ROWS)).T

    def whole_block(main, number):
        low = number * SPILL_ROWS
        body = jnp.concatenate([main, spills[low : low + SPILL_ROWS]])
        if number == 2:
            return body
        return jnp.concatenate([body, side_sums[:, 3 * number : 3 * number + 3]], axis=1)

    flat_grad = jnp.concatenate(
        [
            from_block(whole_block(own_one, 0), index, sizes[0], rows, count),
            wide_biases[0],
            from_block(whole_block(own_two, 1), index, sizes[2], rows, count),
            wide_biases[1],
            from_block(whole_block(own_deep, 2), index, sizes[4], rows, count),
            units[0],
            own_top.reshape(-1),
            units[1],
            units[2],
            jnp.where(index == 0, vectors[11, :1], 0.0),
        ]
    )
    new_moment_one = 0.9 * moment_one + 0.1 * flat_grad
    new_moment_two = 0.999 * moment_two + 0.001 * flat_grad * flat_grad
    corrected_one = new_moment_one / (1.0 - 0.9**STEP)
    corrected_two = new_moment_two / (1.0 - 0.999**STEP)
    new_master = master - 0.03 * (corrected_one / (jnp.sqrt(corrected_two) + 1e-08) + 0.01 * master)
    new_bias = jnp.concatenate(
        [new_master[starts[i] : starts[i] + sizes[i]] for i in (1, 3, 5, 7, 9)]
    )
    return (
        logits.reshape(-1),
        loss,
        feature_grad.T,
        flat_grad,
        new_moment_one,
        new_moment_two,
        new_master,
        new_bias,
    )


def solution(mesh):
    line = P(AXES)
    table = P(AXES, None)
    groups = bit_groups(mesh)
    return jax.shard_map(
        functools.partial(local, groups),
        mesh=mesh,
        in_specs=(table, line, line, line, line, line),
        out_specs=(line, P(), table, line, line, line, line, line),
        check_vma=False,
    )
```

```python
import functools
import math

import jax
import jax.numpy as jnp
from jax import lax
from jax.experimental import pallas as pl
from jax.experimental.pallas import tpu as pltpu
from jax.sharding import PartitionSpec as P

D = 1027
H = 1024
DAYS = 24
STEP = 10
AXES = ("dp", "cores")
EXTRA = D - H
LANES = 128
WIDE = H + LANES
AUX_ROWS = 16
SPILL_ROWS = 4
MISC_ROW = 12
UNIT_LINES = 15
TILE = 512
TALL = H + 16
MIB = 1024 * 1024
F32 = jnp.float32
LOW = jnp.bfloat16
SMEM = pl.BlockSpec(memory_space=pltpu.SMEM)
VMEM = pl.BlockSpec(memory_space=pltpu.VMEM)
PARAMS = pltpu.CompilerParams(vmem_limit_bytes=56 * MIB)


def shapes():
    return [(D, D), (D,), (D, D), (D,), (D, H), (H,), (H, H), (H,), (H,), (1,)]


def piece_sizes(count):
    return [(math.prod(shape) + count - 1) // count for shape in shapes()[:-1]] + [1]


def starts_of(count):
    starts = []
    position = 0
    for piece in piece_sizes(count):
        starts.append(position)
        position += piece
    return starts


def to_block(piece, index, width, rows, count):
    excess = piece.shape[0] - rows * width
    size = (rows + SPILL_ROWS) * width
    lead = (count - 1) * excess
    padded = jnp.pad(piece, (lead, max(0, size - piece.shape[0])))
    line = lax.dynamic_slice(padded, (lead - index * excess,), (size,))
    return line.reshape(rows + SPILL_ROWS, width)


def from_block(block, index, piece, rows, count):
    width = block.shape[1]
    excess = piece - rows * width
    last = (count - 1) * excess
    line = jnp.pad(block.reshape(-1), (0, max(0, last + piece - block.size)))
    return lax.dynamic_slice(line, (index * excess,), (piece,))


def bit_groups(mesh):
    devices = mesh.devices.reshape(-1)
    groups = {"z": [], "plane": [], "core": []}
    bit = 1
    while bit < devices.size:
        here = getattr(devices[0], "coords", None)
        there = getattr(devices[bit], "coords", None)
        if here is None or there is None:
            name = "core" if bit == 1 else "plane" if bit <= 4 else "z"
        elif tuple(here) == tuple(there):
            name = "core"
        elif here[2] != there[2]:
            name = "z"
        else:
            name = "plane"
        groups[name].append(bit)
        bit *= 2
    return groups


def masks_of(bits):
    masks = [0]
    for bit in bits:
        masks = masks + [mask | bit for mask in masks]
    return masks


def teams(bits, count):
    masks = masks_of(bits)
    return [[k | mask for mask in masks] for k in range(count) if not k & masks[-1]]


def owner(index, mask, groups, by_z):
    if by_z:
        index = jnp.bitwise_and(index, ~masks_of(groups["z"])[-1])
    return jnp.bitwise_xor(index, mask)


def swap(value, mask, count):
    return lax.ppermute(value, AXES, [(k, k ^ mask) for k in range(count)])


def join(parts, after):
    def kernel(*refs):
        for j in range(len(parts)):
            refs[-1][j] = refs[j][...]

    return pl.pallas_call(
        kernel,
        out_shape=jax.ShapeDtypeStruct((len(parts),) + parts[0].shape, parts[0].dtype),
        in_specs=[VMEM] * len(parts) + [pl.BlockSpec(memory_space=pl.ANY)] * len(after),
        out_specs=VMEM,
        compiler_params=PARAMS,
        name="join",
    )(*parts, *after)


def gather(block, groups, count, direct=False, after=()):
    z_masks = masks_of(groups["z"])
    core_masks = masks_of(groups["core"])
    line = join([block] + [swap(block, mask, count) for mask in z_masks[1:]], after)
    plane = [(line, z_masks)]
    if len(groups["plane"]) == 2 and len(z_masks) > 1 and not direct:
        one, two = groups["plane"]
        half = len(z_masks) // 2
        by_one = swap(line, one, count)
        by_two = swap(line, two, count)
        plane.append((by_one, [one ^ z for z in z_masks]))
        plane.append((by_two, [two ^ z for z in z_masks]))
        both = one ^ two
        plane.append((swap(by_one[:half], two, count), [both ^ z for z in z_masks[:half]]))
        plane.append((swap(by_two[half:], one, count), [both ^ z for z in z_masks[half:]]))
    else:
        for mask in masks_of(groups["plane"])[1:]:
            plane.append((swap(line, mask, count), [mask ^ z for z in z_masks]))
    result = list(plane)
    for core in core_masks[1:]:
        result += [(swap(value, core, count), [core ^ m for m in row]) for value, row in plane]
    return result


def place(index, stacks, rows, count, parts, aux=None):
    sources = [value for value, _ in stacks]
    masks = [row for _, row in stacks]
    carries = aux is None
    top = min(16, rows)

    def kernel(index_ref, *refs):
        refs = list(refs)
        aux_ref = refs.pop() if carries else refs.pop(0)
        outs = refs[len(sources) :]
        for ref, row in zip(refs, masks):
            for j, mask in enumerate(row):
                at = jnp.bitwise_xor(index_ref[0], mask)
                for i, out_ref in enumerate(outs):
                    out_ref[at] = ref[j, i * rows : (i + 1) * rows]
                if carries:
                    aux_ref[at] = ref[j, len(outs) * rows :]
        for spill_at, out_ref in zip(parts, outs):
            if spill_at is None:
                continue
            for k in range(1, count):
                spill = aux_ref[k - 1].astype(F32)[spill_at : spill_at + SPILL_ROWS]
                old = out_ref[k, :top].astype(F32)
                new = old[:SPILL_ROWS] + spill
                if top > SPILL_ROWS:
                    new = jnp.concatenate([new, old[SPILL_ROWS:]], axis=0)
                out_ref[k, :top] = new.astype(LOW)

    out_shape = [jax.ShapeDtypeStruct((count, rows, H), LOW)] * len(parts)
    if carries:
        out_shape.append(jax.ShapeDtypeStruct((count, AUX_ROWS, H), LOW))
    extra = [] if carries else [aux]
    result = pl.pallas_call(
        kernel,
        out_shape=out_shape,
        in_specs=[SMEM] + [VMEM] * (len(extra) + len(sources)),
        out_specs=[VMEM] * len(out_shape),
        compiler_params=PARAMS,
        name="place",
    )(index, *extra, *sources)
    return [value.reshape(H, H) for value in result[: len(parts)]] + list(result[len(parts) :])


def split(index, value, masks, kinds, groups, by_z):
    def kernel(index_ref, value_ref, *out_refs):
        for ref, row, kind in zip(out_refs, masks, kinds):
            for j, mask in enumerate(row):
                ref[j] = value_ref[owner(index_ref[0], mask, groups, by_z)].astype(kind)

    shape = value.shape[1:]
    return pl.pallas_call(
        kernel,
        out_shape=[
            jax.ShapeDtypeStruct((len(row),) + shape, kind) for row, kind in zip(masks, kinds)
        ],
        in_specs=[SMEM, VMEM],
        out_specs=[VMEM] * len(masks),
        compiler_params=PARAMS,
        name="split",
    )(index, value)


def halves(groups):
    z_masks, plane_masks, core_masks = (masks_of(groups[g]) for g in ("z", "plane", "core"))
    inner = [p ^ z for p in plane_masks for z in z_masks]
    return [[core ^ m for m in inner] for core in core_masks]


def kinds_of(groups):
    return [F32] + [LOW] * (len(halves(groups)) - 1)


def core_stage(stacks, groups, count):
    z_masks, plane_masks, core_masks = (masks_of(groups[g]) for g in ("z", "plane", "core"))
    kept = stacks[0]
    for core, stack in zip(core_masks[1:], stacks[1:]):
        kept = kept + swap(stack, core, count).astype(F32)
    kept = kept.reshape((len(plane_masks), len(z_masks)) + kept.shape[1:])
    return [kept[0]] + [kept[j].astype(LOW) for j in range(1, len(plane_masks))]


def plane_stage(parts, groups, count):
    total = parts[0]
    for mask, part in zip(masks_of(groups["plane"])[1:], parts[1:]):
        total = total + swap(part, mask, count).astype(F32)
    return total


def plane_stage_after(parts, groups, count, after):
    gotten = [
        swap(part, mask, count) for mask, part in zip(masks_of(groups["plane"])[1:], parts[1:])
    ]
    n, rows, width = parts[0].shape

    def kernel(*refs):
        outs = refs[-n:]
        for j in range(n):
            total = refs[0][j]
            for ref in refs[1 : 1 + len(gotten)]:
                total = total + ref[j].astype(F32)
            outs[j][...] = total.astype(outs[j].dtype)

    return pl.pallas_call(
        kernel,
        out_shape=[jax.ShapeDtypeStruct((rows, width), F32 if j == 0 else LOW) for j in range(n)],
        in_specs=[VMEM] * (1 + len(gotten)) + [pl.BlockSpec(memory_space=pl.ANY)] * len(after),
        out_specs=[VMEM] * n,
        compiler_params=PARAMS,
        name="plane_sum",
    )(parts[0], *gotten, *after)


def z_parts(total):
    return [total[0]] + [total[j].astype(LOW) for j in range(1, total.shape[0])]


def z_stage(parts, groups, count):
    own = parts[0]
    for mask, part in zip(masks_of(groups["z"])[1:], parts[1:]):
        own = own + swap(part, mask, count).astype(F32)
    return own


def z_scatter(total, groups, count):
    if not groups["z"]:
        return total[0]
    return lax.psum_scatter(
        total, AXES, scatter_dimension=0, axis_index_groups=teams(groups["z"], count)
    )


def product(left, right):
    return lax.dot_general(left, right, (((1,), (0,)), ((), ())), preferred_element_type=F32)


def outer(left, right):
    return lax.dot_general(left, right, (((1,), (1,)), ((), ())), preferred_element_type=F32)


def gelu_both(value):
    scale = math.sqrt(2.0 / math.pi)
    square = value * value
    share = 0.5 + 0.5 * jnp.tanh(value * (scale + scale * 0.044715 * square))
    result = value * share
    slope = share + result * (1.0 - share) * (2.0 * scale + 6.0 * scale * 0.044715 * square)
    return result, slope


def columns(height, tile=TILE):
    return pl.BlockSpec((height, tile), lambda i: (0, i))


def whole(*shape):
    return pl.BlockSpec(shape, lambda i: (0,) * len(shape))


def once(*shape):
    return pl.BlockSpec(shape, lambda i: (0,) * len(shape), pipeline_mode=pl.Buffered(1))


def shaped(kind, *shape):
    return jax.ShapeDtypeStruct(shape, kind)


def pieces_of(width):
    return [(a, a + 256) for a in range(0, width, 256)]


def run(name, kernel, batch, in_specs, out_specs, out_shape, scratch, flops, *args, tile=TILE):
    moved = sum(a.size * a.dtype.itemsize for a in args)
    moved += sum(math.prod(o.shape) * o.dtype.itemsize for o in out_shape)
    return pl.pallas_call(
        kernel,
        grid=(batch // tile,),
        in_specs=in_specs,
        out_specs=out_specs,
        out_shape=out_shape,
        scratch_shapes=scratch,
        compiler_params=PARAMS,
        cost_estimate=pl.CostEstimate(flops=flops, bytes_accessed=moved, transcendentals=0),
        name=name,
    )(*args)


def first_step():
    return pl.when(pl.program_id(0) == 0)


def last_step():
    return pl.when(pl.program_id(0) == pl.num_programs(0) - 1)


def turn(out_ref, matrix_ref, tail_ref=None, edge_ref=None):
    for a, b in pieces_of(H):
        out_ref[a:b, :H] = matrix_ref[:, a:b].T
    if tail_ref is not None:
        out_ref[:H, H:] = tail_ref[...].T
    if edge_ref is not None:
        out_ref[H:, :] = edge_ref[...]


def straight(out_ref, matrix_ref, tail_ref, edge_ref=None):
    out_ref[:H, :H] = matrix_ref[...]
    row = lax.broadcasted_iota(jnp.int32, (TALL - H, H), 0)
    tail = tail_ref[: TALL - H, :].astype(F32)
    out_ref[H:, :H] = jnp.where(row < EXTRA, tail, 0.0).astype(LOW)
    if edge_ref is not None:
        lane = lax.broadcasted_iota(jnp.int32, (TALL - H, WIDE), 1)
        edge = jnp.where(lane < D, edge_ref[...].astype(F32), 0.0)
        edge = jnp.concatenate([edge, jnp.zeros((LANES - (TALL - H), WIDE), F32)])
        out_ref[:, H:] = edge.T[:TALL].astype(LOW)


def widen(out_ref, value_ref):
    @first_step()
    def _():
        out_ref[TALL:] = jnp.zeros((WIDE - TALL, out_ref.shape[1]), LOW)

    out_ref[:TALL] = value_ref[...]


class Spread:
    def __init__(self, groups, rows, count, parts=1, below=False, by_z=False):
        self.groups, self.by_z = groups, by_z
        self.masks = halves(groups)
        self.kinds = kinds_of(groups)
        self.rows, self.count, self.parts, self.below = rows, count, parts, below
        self.direct = rows % 16 == 0

    def shapes(self):
        if not self.direct:
            return [shaped(F32, TALL, H)] * self.parts
        height = self.rows * self.parts + (AUX_ROWS if self.below else 0)
        outs = [shaped(kind, len(row), height, H) for row, kind in zip(self.masks, self.kinds)]
        overs = 0 if self.below else self.parts
        return outs + [shaped(F32, self.count, 8, H)] * overs

    def specs(self):
        return [whole(*s.shape) for s in self.shapes()]

    def write(self, acc_refs, index_ref, out_refs, over_refs=None):
        if not self.direct:
            for acc_ref, ref in zip(acc_refs, out_refs):
                ref[...] = acc_ref[...]
            return
        rows = self.rows
        for ref, row, kind in zip(out_refs, self.masks, self.kinds):
            for j, mask in enumerate(row):
                at = owner(index_ref[0], mask, self.groups, self.by_z)
                start = pl.multiple_of(at * rows, rows)
                for i, acc_ref in enumerate(acc_refs):
                    block = acc_ref[pl.ds(start, rows), :]
                    ref[j, i * rows : (i + 1) * rows] = block.astype(kind)
                if self.below:
                    mine = acc_ref[pl.ds(pl.multiple_of(start + rows, 8), 8), :]
                    parts = [mine[:SPILL_ROWS]] + [v[at][:SPILL_ROWS] for v in over_refs]
                    parts.append(jnp.zeros((AUX_ROWS - MISC_ROW, H), F32))
                    ref[j, rows:] = jnp.concatenate(parts).astype(kind)
        if not self.below:
            for acc_ref, ref in zip(acc_refs, out_refs[len(self.masks) :]):
                for k in range(self.count):
                    ref[k] = acc_ref[(k + 1) * rows : (k + 1) * rows + 8, :]

    def finish(self, outs, index, overs=None):
        if self.direct:
            return list(outs)
        rows, count = self.rows, self.count
        blocks = [grad[:H].reshape(count, rows, H) for grad in outs]
        own = [
            jnp.stack([grad[(k + 1) * rows : (k + 1) * rows + 8] for k in range(count)])
            for grad in outs
        ]
        if self.below:
            blocks += [v[:, :SPILL_ROWS] for v in own + list(overs)]
            blocks.append(jnp.zeros((count, AUX_ROWS - MISC_ROW, H), F32))
        stacks = split(
            index, jnp.concatenate(blocks, axis=1), self.masks, self.kinds, self.groups, self.by_z
        )
        stacks = list(stacks)
        return stacks if self.below else stacks + own


ANY = pl.BlockSpec(memory_space=pl.ANY)
REST = TALL - H


def forward_cross(features, one, two):
    batch = features.shape[1]

    def kernel(f_ref, *refs):
        x_ref, mixer_one_ref, mixer_two_ref, one_ref, two_ref = refs[6:11]
        turned_one, turned_two, wide_ref = refs[11:]

        @first_step()
        def _():
            turn(turned_one, *refs[:3])
            turn(turned_two, *refs[3:6])

        x_ref[:H] = f_ref[:H]
        last = f_ref[H:].astype(F32)
        last = jnp.concatenate([last, jnp.ones((1, TILE), F32), jnp.zeros((TALL - D - 1, TILE), F32)])
        x_ref[H:] = last.astype(LOW)
        widen(wide_ref, x_ref)
        layers = []
        for a, b in [(0, TILE)]:
            mixer = product(turned_one[...], wide_ref[:, a:b])
            mixer_one_ref[:, a:b] = mixer.astype(LOW)
            part = x_ref[:, a:b].astype(F32)
            layer = part * mixer + part
            layers.append(layer)
            one_ref[:, a:b] = layer.astype(LOW)
        wide_ref[:TALL] = one_ref[...]
        for (a, b), layer in zip([(0, TILE)], layers):
            mixer = product(turned_two[...], wide_ref[:, a:b])
            mixer_two_ref[:, a:b] = mixer.astype(LOW)
            two_ref[:, a:b] = (x_ref[:, a:b].astype(F32) * mixer + layer).astype(LOW)

    return run(
        "forward_cross",
        kernel,
        batch,
        [columns(D)] + [once(H, H), once(LANES, H), once(REST, WIDE)] * 2,
        [columns(TALL)] * 5,
        [shaped(LOW, TALL, batch)] * 5,
        [pltpu.VMEM((TALL, WIDE), LOW)] * 2 + [pltpu.VMEM((WIDE, TILE), LOW)],
        4 * batch * TALL * TALL,
        features, *one, *two,
    )


def deep(spread, index, layer_low, examples, matrix_one, tail, matrix, lines, inverse):
    batch = layer_low.shape[1]
    days = inverse.shape[0]

    def kernel(k_ref, l_ref, x_ref, w_one_ref, t_ref, w_ref, n_ref, i_ref, *refs):
        logit_ref, back_ref, line_ref, sum_ref = refs[:4]
        out_refs = refs[4:-8]
        turned_one, turned, acc_ref, hidden_ref, slope_ref, low_ref, part_ref, wide_ref = refs[-8:]

        @first_step()
        def _():
            turn(turned_one, w_one_ref, t_ref)
            turn(turned, w_ref)
            acc_ref[...] = jnp.zeros_like(acc_ref)
            sum_ref[...] = jnp.zeros_like(sum_ref)
            part_ref[...] = jnp.zeros_like(part_ref)
            row = lax.broadcasted_iota(jnp.int32, (REST, TILE), 0)
            hidden_ref[H:] = jnp.where(row == 0, 1.0, 0.0).astype(LOW)

        widen(wide_ref, l_ref)
        for a, b in pieces_of(TILE):
            hidden, slope = gelu_both(product(turned_one[...], wide_ref[:, a:b]))
            hidden_ref[:H, a:b] = hidden.astype(LOW)
            slope_ref[:, a:b] = slope
        head = n_ref[:, 1:2]
        for a, b in pieces_of(TILE):
            two, slope = gelu_both(product(turned[...], hidden_ref[:H, a:b]) + n_ref[:, 0:1])
            two = two.astype(LOW).astype(F32)
            logits = n_ref[0:1, 2:3] + jnp.sum(two * head, axis=0, keepdims=True)
            label = x_ref[0:1, a:b]
            day = x_ref[1:2, a:b].astype(jnp.int32)
            row = lax.broadcasted_iota(jnp.int32, (days, b - a), 0)
            weight = jnp.sum(jnp.where(row == day, i_ref[:, 0:1], 0.0), axis=0, keepdims=True)
            decay = jnp.exp(-jnp.abs(logits))
            entropy = jnp.maximum(logits, 0.0) + jnp.log1p(decay) - label * logits
            chance = jnp.where(logits >= 0.0, 1.0, decay) / (1.0 + decay)
            logit_grad = (chance - label) * weight
            logit_ref[:, a:b] = logits
            sum_ref[0:1, a:b] += logit_grad
            sum_ref[1:2, a:b] += entropy * weight
            low_ref[:, a:b] = ((logit_grad * head) * slope).astype(LOW)
            one = logit_grad * two
            part = one[:, :LANES]
            for at in range(LANES, b - a, LANES):
                part = part + one[:, at : at + LANES]
            part_ref[...] += part
        for a, b in pieces_of(TILE):
            back_ref[:, a:b] = (product(w_ref[...], low_ref[:, a:b]) * slope_ref[:, a:b]).astype(LOW)
        for a, b in pieces_of(H):
            acc_ref[:, a:b] += outer(hidden_ref[...], low_ref[a:b])

        @last_step()
        def _():
            line_ref[0:8] = jnp.broadcast_to(
                jnp.sum(part_ref[...].T, axis=0, keepdims=True), (8, H)
            )
            line_ref[8:16] = acc_ref[H : H + 8]
            spread.write([acc_ref], k_ref, out_refs)

    return run(
        "deep",
        kernel,
        batch,
        [
            SMEM,
            columns(TALL),
            columns(2),
            once(H, H),
            once(LANES, H),
            once(H, H),
            whole(H, LANES),
            whole(days, LANES),
        ],
        [columns(1), columns(H), whole(16, H), whole(8, TILE)] + spread.specs(),
        [
            shaped(F32, 1, batch),
            shaped(LOW, H, batch),
            shaped(F32, 16, H),
            shaped(F32, 8, TILE),
        ]
        + spread.shapes(),
        [
            pltpu.VMEM((H, WIDE), LOW),
            pltpu.VMEM((H, H), LOW),
            pltpu.VMEM((TALL, H), F32),
            pltpu.VMEM((TALL, TILE), LOW),
            pltpu.VMEM((H, TILE), F32),
            pltpu.VMEM((H, TILE), LOW),
            pltpu.VMEM((H, LANES), F32),
            pltpu.VMEM((WIDE, TILE), LOW),
        ],
        8 * batch * H * H,
        index, layer_low, examples, matrix_one, tail, matrix, lines, inverse,
    )


def back_deep(spread, index, grad_low, layer_low, features, matrix, tail, after):
    batch = features.shape[1]

    def kernel(k_ref, g_ref, l_ref, x_ref, w_ref, t_ref, *refs):
        refs = refs[len(after) :]
        layer_ref, mixer_ref, line_ref = refs[:3]
        out_refs = refs[3:-2]
        held, acc_ref = refs[-2:]

        @first_step()
        def _():
            straight(held, w_ref, t_ref)
            acc_ref[...] = jnp.zeros_like(acc_ref)

        for a, b in pieces_of(TILE):
            layer = product(held[...], g_ref[:, a:b])
            layer_ref[:, a:b] = layer
            mixer_ref[:, a:b] = (layer * x_ref[:, a:b].astype(F32)).astype(LOW)
        for a, b in pieces_of(H):
            acc_ref[:, a:b] += outer(l_ref[...], g_ref[a:b])

        @last_step()
        def _():
            line_ref[...] = acc_ref[H:]
            spread.write([acc_ref], k_ref, out_refs)

    return run(
        "back_deep",
        kernel,
        batch,
        [SMEM, columns(H), columns(TALL), columns(TALL), once(H, H), once(LANES, H)]
        + [ANY] * len(after),
        [columns(TALL), columns(TALL), whole(REST, H)] + spread.specs(),
        [shaped(F32, TALL, batch), shaped(LOW, TALL, batch), shaped(F32, REST, H)]
        + spread.shapes(),
        [pltpu.VMEM((TALL, H), LOW), pltpu.VMEM((TALL, H), F32)],
        4 * batch * TALL * H,
        index, grad_low, layer_low, features, matrix, tail, *after,
    )


def back_two(
    spread, index, mixer_low, layer_low, layer_grad, features, mixer_one, mixer_two, matrix, tail,
    edge, after,
):
    batch = features.shape[1]

    def kernel(k_ref, g_ref, l_ref, d_ref, x_ref, one_ref, two_ref, w_ref, t_ref, e_ref, *refs):
        refs = refs[len(after) :]
        part_ref, mixer_ref, side_ref, line_ref, next_side_ref, next_line_ref = refs[:6]
        out_refs = refs[6:-4]
        held, acc_ref, wide_ref, sum_ref = refs[-4:]

        @first_step()
        def _():
            straight(held, w_ref, t_ref, e_ref)
            acc_ref[...] = jnp.zeros_like(acc_ref)
            side_ref[...] = jnp.zeros_like(side_ref)
            next_side_ref[...] = jnp.zeros_like(next_side_ref)
            sum_ref[...] = jnp.zeros_like(sum_ref)

        widen(wide_ref, g_ref)
        for a, b in pieces_of(TILE):
            above = d_ref[:, a:b]
            layer = product(held[...], wide_ref[:, a:b]) + above
            mixer = (layer * x_ref[:, a:b].astype(F32)).astype(LOW)
            mixer_ref[:, a:b] = mixer
            mixer = mixer[:H].astype(F32)
            total = mixer[:, :LANES]
            for at in range(LANES, b - a, LANES):
                total = total + mixer[:, at : at + LANES]
            sum_ref[...] += total
            part = above * two_ref[:, a:b].astype(F32)
            part = part + layer * (one_ref[:, a:b].astype(F32) + 1.0)
            part_ref[:, a:b] = part.astype(LOW)
        for a, b in pieces_of(H):
            acc_ref[:, a:b] += outer(l_ref[...], g_ref[a:b])
        side_ref[...] += outer(g_ref[H:], l_ref[...])
        next_side_ref[...] += outer(mixer_ref[H:], x_ref[...])

        @last_step()
        def _():
            line_ref[...] = acc_ref[H:]
            next_line_ref[...] = jnp.broadcast_to(
                jnp.sum(sum_ref[...].T, axis=0, keepdims=True), (8, H)
            )
            spread.write([acc_ref], k_ref, out_refs)

    return run(
        "back_two",
        kernel,
        batch,
        [SMEM]
        + [columns(TALL)] * 6
        + [once(H, H), once(LANES, H), once(REST, WIDE)]
        + [ANY] * len(after),
        [columns(TALL), columns(TALL)]
        + [whole(REST, TALL), whole(REST, H), whole(REST, TALL), whole(8, H)]
        + spread.specs(),
        [
            shaped(LOW, TALL, batch),
            shaped(LOW, TALL, batch),
            shaped(F32, REST, TALL),
            shaped(F32, REST, H),
            shaped(F32, REST, TALL),
            shaped(F32, 8, H),
        ]
        + spread.shapes(),
        [
            pltpu.VMEM((TALL, WIDE), LOW),
            pltpu.VMEM((TALL, H), F32),
            pltpu.VMEM((WIDE, TILE), LOW),
            pltpu.VMEM((H, LANES), F32),
        ],
        4 * batch * TALL * TALL,
        index, mixer_low, layer_low, layer_grad, features, mixer_one, mixer_two, matrix, tail,
        edge, *after,
    )


def grad_one(spread, index, mixer_low, features, overs, after):
    batch = features.shape[1]

    def kernel(k_ref, g_ref, x_ref, *refs):
        over_refs = refs[: len(overs)]
        out_refs = refs[len(overs) + len(after) : -1]
        acc_ref = refs[-1]

        @first_step()
        def _():
            acc_ref[...] = jnp.zeros_like(acc_ref)

        for a, b in pieces_of(H):
            acc_ref[:, a:b] += outer(x_ref[...], g_ref[a:b])

        @last_step()
        def _():
            spread.write([acc_ref], k_ref, out_refs, over_refs)

    return run(
        "grad_one",
        kernel,
        batch,
        [SMEM, columns(TALL), columns(TALL)]
        + [once(*v.shape) for v in overs]
        + [ANY] * len(after),
        spread.specs(),
        spread.shapes(),
        [pltpu.VMEM((TALL, H), F32)],
        2 * batch * TALL * TALL,
        index, mixer_low, features, *overs, *after,
    )


def back_one(mixer_low, part, matrix, tail, edge, after):
    batch = part.shape[1]

    def kernel(g_ref, p_ref, w_ref, t_ref, e_ref, *refs):
        out_ref, held, wide_ref = refs[len(after) :]

        @first_step()
        def _():
            straight(held, w_ref, t_ref, e_ref)

        widen(wide_ref, g_ref)
        for a, b in [(0, TILE)]:
            value = p_ref[:, a:b].astype(F32) + product(held[...], wide_ref[:, a:b])
            out_ref[:H, a:b] = value[:H]
            out_ref[H:, a:b] = value[H:D]

    return run(
        "back_one",
        kernel,
        batch,
        [columns(TALL), columns(TALL), whole(H, H), whole(LANES, H), whole(REST, WIDE)]
        + [ANY] * len(after),
        [columns(D)],
        [shaped(F32, D, batch)],
        [pltpu.VMEM((TALL, WIDE), LOW), pltpu.VMEM((WIDE, TILE), LOW)],
        2 * batch * TALL * TALL,
        mixer_low, part, matrix, tail, edge, *after,
    )[0]


def local(groups, features, labels, days, master, moment_one, moment_two):
    count = lax.axis_size(AXES)
    index = lax.axis_index(AXES)
    slot = index[None].astype(jnp.int32)
    rows = H // count
    starts = starts_of(count)
    sizes = piece_sizes(count)
    wide_piece = sizes[1]
    piece = [master[a : a + l] for a, l in zip(starts, sizes)]
    block_one = to_block(piece[0], index, D, rows, count)
    block_two = to_block(piece[2], index, D, rows, count)
    block_deep = to_block(piece[4], index, H, rows, count)

    day_hot = (days[:, None] == jnp.arange(DAYS, dtype=jnp.int32)[None, :]).astype(F32)
    own_counts = jnp.sum(day_hot, axis=0)
    counts_high = jnp.floor(own_counts / 64.0)
    counts_low = own_counts - 64.0 * counts_high

    def spill_side(block):
        side = block[rows:, H:].T
        return jnp.pad(side, ((0, 0), (0, rows - SPILL_ROWS)))

    misc = [
        piece[5],
        piece[7],
        piece[8],
        block_one[:rows, H:].T,
        block_two[:rows, H:].T,
        spill_side(block_one),
        spill_side(block_two),
        piece[1],
        piece[3],
        piece[9],
        counts_high,
        counts_low,
    ]
    misc = jnp.concatenate([part.reshape(-1) for part in misc])
    misc = jnp.pad(misc, (0, (AUX_ROWS - MISC_ROW) * H - misc.shape[0])).reshape(-1, H)
    first = jnp.concatenate(
        [
            block_one[:rows, :H],
            block_two[:rows, :H],
            block_one[rows:, :H],
            block_two[rows:, :H],
            block_deep[rows:],
            misc,
        ]
    ).astype(LOW)
    stacks_cross = gather(first, groups, count)
    rest = jnp.concatenate([block_deep[:rows], piece[6].reshape(rows, H)]).astype(LOW)
    crossed = [value for value, _ in stacks_cross[3:5]]
    stacks_rest = gather(rest, groups, count, direct=True, after=crossed)
    examples = jnp.stack([labels.astype(F32), days.astype(F32)])

    matrix_one, matrix_two, aux = place(slot, stacks_cross, rows, count, [0, SPILL_ROWS])
    matrix_deep, matrix_top = place(slot, stacks_rest, rows, count, [2 * SPILL_ROWS, None], aux)

    line = aux[:, MISC_ROW]
    at = UNIT_LINES * rows
    units = line[:, :at].reshape(count, UNIT_LINES, rows).transpose(1, 0, 2).reshape(UNIT_LINES, H)
    biases = line[:, at : at + 2 * wide_piece].reshape(count, 2, wide_piece)
    biases = biases.transpose(1, 0, 2).reshape(2, count * wide_piece)
    at += 2 * wide_piece
    head_bias = line[0, at]
    both_counts = jnp.sum(line[:, at + 1 : at + 1 + 2 * DAYS].astype(F32), axis=0)
    counts = 64.0 * both_counts[:DAYS] + both_counts[DAYS:]
    inverse = jnp.broadcast_to((1.0 / counts)[:, None], (DAYS, LANES))
    sides = jnp.pad(units[3:9], ((0, 0), (0, LANES))) + jnp.pad(
        units[9:15], ((0, 0), (rows, LANES - rows))
    )

    def tail_of(at, bias):
        return jnp.concatenate(
            [aux[count - 1, at : at + EXTRA], bias[None, :H], jnp.zeros((LANES - EXTRA - 1, H), LOW)]
        )

    def edge_of(side, bias):
        lane = lax.broadcasted_iota(jnp.int32, side.shape, 1)
        side = jnp.where(lane == D, bias[H:D, None], side)
        return jnp.pad(side, ((0, TALL - H - EXTRA), (0, 0)))

    tail_one, edge_one = tail_of(0, biases[0]), edge_of(sides[:3], biases[0])
    tail_two, edge_two = tail_of(SPILL_ROWS, biases[1]), edge_of(sides[3:], biases[1])
    tail_deep = tail_of(2 * SPILL_ROWS, units[0])
    lines = jnp.concatenate(
        [units[1:3], jnp.full((1, H), head_bias), jnp.zeros((LANES - 3, H), LOW)]
    )
    lines = lines.astype(F32).T
    spread = Spread(groups, rows, count, by_z=True)
    spread_two = Spread(groups, rows, count)
    spread_last = Spread(groups, rows, count, below=True)

    wide_features, mixer_one, mixer_two, low_one, low_two = forward_cross(
        features.T, (matrix_one, tail_one, edge_one), (matrix_two, tail_two, edge_two)
    )
    logits, pre_one_low, top_lines, sums, *outs = deep(
        spread, slot, low_two, examples, matrix_deep, tail_deep, matrix_top, lines, inverse
    )
    *stacks, _ = spread.finish(outs, slot)
    top_plane = core_stage(stacks, groups, count)
    layer_grad, mixer_two_low, deep_lines, *outs = back_deep(
        spread, slot, pre_one_low, low_two, wide_features, matrix_deep, tail_deep, stacks[1:2]
    )
    *stacks, deep_over = spread.finish(outs, slot)
    deep_plane = core_stage(stacks, groups, count)
    part, mixer_one_low, two_side, two_lines, one_side, one_line, *outs = back_two(
        spread_two, slot, mixer_two_low, low_one, layer_grad, wide_features, mixer_one, mixer_two,
        matrix_two, tail_two, edge_two, top_plane[1:] + stacks[1:2],
    )
    *stacks, two_over = spread_two.finish(outs, slot)
    top_total = plane_stage(top_plane, groups, count)
    two_plane = core_stage(stacks, groups, count)
    overs = (two_over, deep_over)
    outs = grad_one(
        spread_last, slot, mixer_one_low, wide_features, overs, deep_plane[1:] + [top_total]
    )
    stacks = spread_last.finish(outs, slot, overs)
    last_plane = core_stage(stacks, groups, count)
    deep_total = plane_stage(deep_plane, groups, count)
    feature_grad = back_one(
        mixer_one_low, part, matrix_one, tail_one, edge_one,
        last_plane[1:] + two_plane[1:] + [deep_total],
    )

    sums = jnp.pad(jnp.sum(sums[:2], axis=1)[None], ((0, 0), (0, WIDE - 2)))
    vectors = jnp.concatenate(
        [
            jnp.pad(
                jnp.concatenate(
                    [one_line[:1], two_lines[EXTRA:4], deep_lines[EXTRA:4], top_lines[8:9], top_lines[:1]]
                ),
                ((0, 0), (0, LANES)),
            ),
            jnp.pad(jnp.concatenate([one_side[:3], two_side[:3]]), ((0, 0), (0, WIDE - TALL))),
            sums,
            jnp.zeros((4, WIDE), F32),
        ]
    )
    vectors = jnp.sum(lax.all_gather(vectors, AXES, axis=0), axis=0)
    loss = vectors[11, 1]
    side_sums = vectors[5:11]

    own_top = z_scatter(top_total, groups, count)
    own_deep = z_scatter(deep_total, groups, count)
    own_two = z_stage(z_parts(plane_stage(two_plane, groups, count)), groups, count)
    last_z = plane_stage_after(last_plane, groups, count, [feature_grad])
    own_last = z_stage(last_z, groups, count)
    own_one = own_last[:rows]
    spills = own_last[rows : rows + MISC_ROW]
    row = lax.broadcasted_iota(jnp.int32, spills.shape, 0)
    beyond = (row % SPILL_ROWS >= EXTRA) & (index == count - 1)
    spills = jnp.where(beyond, 0.0, spills)
    wide_biases = jnp.concatenate(
        [vectors[:2, :H], side_sums[:, D].reshape(2, EXTRA)], axis=1
    )
    wide_biases = jnp.pad(wide_biases, ((0, 0), (0, count * wide_piece - D)))
    wide_biases = lax.dynamic_slice(wide_biases, (0, index * wide_piece), (2, wide_piece))
    units = lax.dynamic_slice(vectors[2:5], (0, index * rows), (3, rows))
    side_sums = jnp.pad(side_sums[:, :D], ((0, 0), (0, WIDE - D)))
    side_sums = lax.dynamic_slice(side_sums, (0, index * rows), (6, rows + SPILL_ROWS)).T

    def whole_block(main, number):
        low = number * SPILL_ROWS
        body = jnp.concatenate([main, spills[low : low + SPILL_ROWS]])
        if number == 2:
            return body
        return jnp.concatenate([body, side_sums[:, 3 * number : 3 * number + 3]], axis=1)

    flat_grad = jnp.concatenate(
        [
            from_block(whole_block(own_one, 0), index, sizes[0], rows, count),
            wide_biases[0],
            from_block(whole_block(own_two, 1), index, sizes[2], rows, count),
            wide_biases[1],
            from_block(whole_block(own_deep, 2), index, sizes[4], rows, count),
            units[0],
            own_top.reshape(-1),
            units[1],
            units[2],
            jnp.where(index == 0, vectors[11, :1], 0.0),
        ]
    )
    new_moment_one = 0.9 * moment_one + 0.1 * flat_grad
    new_moment_two = 0.999 * moment_two + 0.001 * flat_grad * flat_grad
    corrected_one = new_moment_one / (1.0 - 0.9**STEP)
    corrected_two = new_moment_two / (1.0 - 0.999**STEP)
    new_master = master - 0.03 * (corrected_one / (jnp.sqrt(corrected_two) + 1e-08) + 0.01 * master)
    new_bias = jnp.concatenate(
        [new_master[starts[i] : starts[i] + sizes[i]] for i in (1, 3, 5, 7, 9)]
    )
    return (
        logits.reshape(-1),
        loss,
        feature_grad.T,
        flat_grad,
        new_moment_one,
        new_moment_two,
        new_master,
        new_bias,
    )


def solution(mesh):
    line = P(AXES)
    table = P(AXES, None)
    groups = bit_groups(mesh)
    return jax.shard_map(
        functools.partial(local, groups),
        mesh=mesh,
        in_specs=(table, line, line, line, line, line),
        out_specs=(line, P(), table, line, line, line, line, line),
        check_vma=False,
    )
```

```python
import functools
import math

import jax
import jax.numpy as jnp
from jax import lax
from jax.experimental import pallas as pl
from jax.experimental.pallas import tpu as pltpu
from jax.sharding import PartitionSpec as P

D = 1027
H = 1024
DAYS = 24
STEP = 10
AXES = ("dp", "cores")
EXTRA = D - H
LANES = 128
WIDE = H + LANES
AUX_ROWS = 16
SPILL_ROWS = 4
MISC_ROW = 12
UNIT_LINES = 15
TILE = 512
TALL = H + 16
MIB = 1024 * 1024
F32 = jnp.float32
LOW = jnp.bfloat16
SMEM = pl.BlockSpec(memory_space=pltpu.SMEM)
VMEM = pl.BlockSpec(memory_space=pltpu.VMEM)
PARAMS = pltpu.CompilerParams(vmem_limit_bytes=56 * MIB)


def shapes():
    return [(D, D), (D,), (D, D), (D,), (D, H), (H,), (H, H), (H,), (H,), (1,)]


def piece_sizes(count):
    return [(math.prod(shape) + count - 1) // count for shape in shapes()[:-1]] + [1]


def starts_of(count):
    starts = []
    position = 0
    for piece in piece_sizes(count):
        starts.append(position)
        position += piece
    return starts


def to_block(piece, index, width, rows, count):
    excess = piece.shape[0] - rows * width
    size = (rows + SPILL_ROWS) * width
    lead = (count - 1) * excess
    padded = jnp.pad(piece, (lead, max(0, size - piece.shape[0])))
    line = lax.dynamic_slice(padded, (lead - index * excess,), (size,))
    return line.reshape(rows + SPILL_ROWS, width)


def from_block(block, index, piece, rows, count):
    width = block.shape[1]
    excess = piece - rows * width
    last = (count - 1) * excess
    line = jnp.pad(block.reshape(-1), (0, max(0, last + piece - block.size)))
    return lax.dynamic_slice(line, (index * excess,), (piece,))


def bit_groups(mesh):
    devices = mesh.devices.reshape(-1)
    groups = {"z": [], "plane": [], "core": []}
    bit = 1
    while bit < devices.size:
        here = getattr(devices[0], "coords", None)
        there = getattr(devices[bit], "coords", None)
        if here is None or there is None:
            name = "core" if bit == 1 else "plane" if bit <= 4 else "z"
        elif tuple(here) == tuple(there):
            name = "core"
        elif here[2] != there[2]:
            name = "z"
        else:
            name = "plane"
        groups[name].append(bit)
        bit *= 2
    return groups


def masks_of(bits):
    masks = [0]
    for bit in bits:
        masks = masks + [mask | bit for mask in masks]
    return masks


def teams(bits, count):
    masks = masks_of(bits)
    return [[k | mask for mask in masks] for k in range(count) if not k & masks[-1]]


def owner(index, mask, groups, by_z):
    if by_z:
        index = jnp.bitwise_and(index, ~masks_of(groups["z"])[-1])
    return jnp.bitwise_xor(index, mask)


def swap(value, mask, count):
    return lax.ppermute(value, AXES, [(k, k ^ mask) for k in range(count)])


def join(parts, after):
    def kernel(*refs):
        for j in range(len(parts)):
            refs[-1][j] = refs[j][...]

    return pl.pallas_call(
        kernel,
        out_shape=jax.ShapeDtypeStruct((len(parts),) + parts[0].shape, parts[0].dtype),
        in_specs=[VMEM] * len(parts) + [pl.BlockSpec(memory_space=pl.ANY)] * len(after),
        out_specs=VMEM,
        compiler_params=PARAMS,
        name="join",
    )(*parts, *after)


def gather(block, groups, count, direct=False, after=()):
    z_masks = masks_of(groups["z"])
    core_masks = masks_of(groups["core"])
    line = [block] + [swap(block, mask, count) for mask in z_masks[1:]]
    line = join(line, after) if after else jnp.stack(line)
    plane = [(line, z_masks)]
    if len(groups["plane"]) == 2 and len(z_masks) > 1 and not direct:
        one, two = groups["plane"]
        half = len(z_masks) // 2
        by_one = swap(line, one, count)
        by_two = swap(line, two, count)
        plane.append((by_one, [one ^ z for z in z_masks]))
        plane.append((by_two, [two ^ z for z in z_masks]))
        both = one ^ two
        plane.append((swap(by_one[:half], two, count), [both ^ z for z in z_masks[:half]]))
        plane.append((swap(by_two[half:], one, count), [both ^ z for z in z_masks[half:]]))
    else:
        for mask in masks_of(groups["plane"])[1:]:
            plane.append((swap(line, mask, count), [mask ^ z for z in z_masks]))
    result = list(plane)
    for core in core_masks[1:]:
        result += [(swap(value, core, count), [core ^ m for m in row]) for value, row in plane]
    return result


def place(index, stacks, rows, count, parts, aux=None):
    sources = [value for value, _ in stacks]
    masks = [row for _, row in stacks]
    carries = aux is None
    top = min(16, rows)

    def kernel(index_ref, *refs):
        refs = list(refs)
        aux_ref = refs.pop() if carries else refs.pop(0)
        outs = refs[len(sources) :]
        for ref, row in zip(refs, masks):
            for j, mask in enumerate(row):
                at = jnp.bitwise_xor(index_ref[0], mask)
                for i, out_ref in enumerate(outs):
                    out_ref[at] = ref[j, i * rows : (i + 1) * rows]
                if carries:
                    aux_ref[at] = ref[j, len(outs) * rows :]
        for spill_at, out_ref in zip(parts, outs):
            if spill_at is None:
                continue
            for k in range(1, count):
                spill = aux_ref[k - 1].astype(F32)[spill_at : spill_at + SPILL_ROWS]
                old = out_ref[k, :top].astype(F32)
                new = old[:SPILL_ROWS] + spill
                if top > SPILL_ROWS:
                    new = jnp.concatenate([new, old[SPILL_ROWS:]], axis=0)
                out_ref[k, :top] = new.astype(LOW)

    out_shape = [jax.ShapeDtypeStruct((count, rows, H), LOW)] * len(parts)
    if carries:
        out_shape.append(jax.ShapeDtypeStruct((count, AUX_ROWS, H), LOW))
    extra = [] if carries else [aux]
    result = pl.pallas_call(
        kernel,
        out_shape=out_shape,
        in_specs=[SMEM] + [VMEM] * (len(extra) + len(sources)),
        out_specs=[VMEM] * len(out_shape),
        compiler_params=PARAMS,
        name="place",
    )(index, *extra, *sources)
    return [value.reshape(H, H) for value in result[: len(parts)]] + list(result[len(parts) :])


def split(index, value, masks, kinds, groups, by_z):
    def kernel(index_ref, value_ref, *out_refs):
        for ref, row, kind in zip(out_refs, masks, kinds):
            for j, mask in enumerate(row):
                ref[j] = value_ref[owner(index_ref[0], mask, groups, by_z)].astype(kind)

    shape = value.shape[1:]
    return pl.pallas_call(
        kernel,
        out_shape=[
            jax.ShapeDtypeStruct((len(row),) + shape, kind) for row, kind in zip(masks, kinds)
        ],
        in_specs=[SMEM, VMEM],
        out_specs=[VMEM] * len(masks),
        compiler_params=PARAMS,
        name="split",
    )(index, value)


def halves(groups):
    z_masks, plane_masks, core_masks = (masks_of(groups[g]) for g in ("z", "plane", "core"))
    inner = [p ^ z for p in plane_masks for z in z_masks]
    return [[core ^ m for m in inner] for core in core_masks]


def kinds_of(groups):
    return [F32] + [LOW] * (len(halves(groups)) - 1)


def adder(name, body, ins, outs, after):
    def kernel(*refs):
        body(refs[: len(ins)], refs[len(ins) + len(after) :])

    result = pl.pallas_call(
        kernel,
        out_shape=outs,
        in_specs=[VMEM] * len(ins) + [pl.BlockSpec(memory_space=pl.ANY)] * len(after),
        out_specs=[VMEM] * len(outs),
        compiler_params=PARAMS,
        name=name,
    )(*ins, *after)
    return list(result)


def core_stage(stacks, groups, count, after=()):
    z_count, plane_count = len(masks_of(groups["z"])), len(masks_of(groups["plane"]))
    cores = masks_of(groups["core"])[1:]
    gotten = [swap(stack, core, count) for core, stack in zip(cores, stacks[1:])]
    shape = (z_count,) + stacks[0].shape[1:]

    def body(ins, outs):
        for p, out_ref in enumerate(outs):
            for z in range(z_count):
                total = ins[0][p * z_count + z]
                for ref in ins[1:]:
                    total = total + ref[p * z_count + z].astype(F32)
                out_ref[z] = total.astype(out_ref.dtype)

    outs = [jax.ShapeDtypeStruct(shape, F32 if p == 0 else LOW) for p in range(plane_count)]
    return adder("core_sum", body, [stacks[0]] + gotten, outs, after)


def plane_swaps(parts, groups, count):
    masks = masks_of(groups["plane"])[1:]
    return [parts[0]] + [swap(part, mask, count) for mask, part in zip(masks, parts[1:])]


def plane_stage(parts, groups, count, after=()):
    def body(ins, outs):
        for z in range(ins[0].shape[0]):
            total = ins[0][z]
            for ref in ins[1:]:
                total = total + ref[z].astype(F32)
            outs[0][z] = total

    outs = [jax.ShapeDtypeStruct(parts[0].shape, F32)]
    return adder("plane_sum", body, plane_swaps(parts, groups, count), outs, after)[0]


def plane_stage_joint(one, two, groups, count, after=()):
    ins = plane_swaps(one, groups, count) + plane_swaps(two, groups, count)
    many = len(one)
    first = one[0].shape[1]
    rows = first + two[0].shape[1]

    def body(refs, outs):
        for z, out_ref in enumerate(outs):
            for start, end, part in ((0, first, refs[:many]), (first, rows, refs[many:])):
                total = part[0][z]
                for ref in part[1:]:
                    total = total + ref[z].astype(F32)
                out_ref[start:end] = total.astype(out_ref.dtype)

    outs = [
        jax.ShapeDtypeStruct((rows, H), F32 if z == 0 else LOW) for z in range(one[0].shape[0])
    ]
    return adder("plane_sum", body, ins, outs, after)


def z_stage(parts, groups, count):
    own = parts[0]
    for mask, part in zip(masks_of(groups["z"])[1:], parts[1:]):
        own = own + swap(part, mask, count).astype(F32)
    return own


def z_scatter(total, groups, count):
    if not groups["z"]:
        return total[0]
    return lax.psum_scatter(
        total, AXES, scatter_dimension=0, axis_index_groups=teams(groups["z"], count)
    )


def product(left, right):
    return lax.dot_general(left, right, (((1,), (0,)), ((), ())), preferred_element_type=F32)


def outer(left, right):
    return lax.dot_general(left, right, (((1,), (1,)), ((), ())), preferred_element_type=F32)


def gelu_both(value):
    scale = math.sqrt(2.0 / math.pi)
    square = value * value
    share = 0.5 + 0.5 * jnp.tanh(value * (scale + scale * 0.044715 * square))
    result = value * share
    slope = share + result * (1.0 - share) * (2.0 * scale + 6.0 * scale * 0.044715 * square)
    return result, slope


def columns(height, tile=TILE):
    return pl.BlockSpec((height, tile), lambda i: (0, i))


def whole(*shape):
    return pl.BlockSpec(shape, lambda i: (0,) * len(shape))


def once(*shape):
    return pl.BlockSpec(shape, lambda i: (0,) * len(shape), pipeline_mode=pl.Buffered(1))


def shaped(kind, *shape):
    return jax.ShapeDtypeStruct(shape, kind)


def pieces_of(width):
    return [(a, a + 256) for a in range(0, width, 256)]


def run(name, kernel, batch, in_specs, out_specs, out_shape, scratch, flops, *args, tile=TILE):
    moved = sum(a.size * a.dtype.itemsize for a in args)
    moved += sum(math.prod(o.shape) * o.dtype.itemsize for o in out_shape)
    return pl.pallas_call(
        kernel,
        grid=(batch // tile,),
        in_specs=in_specs,
        out_specs=out_specs,
        out_shape=out_shape,
        scratch_shapes=scratch,
        compiler_params=PARAMS,
        cost_estimate=pl.CostEstimate(flops=flops, bytes_accessed=moved, transcendentals=0),
        name=name,
    )(*args)


def first_step():
    return pl.when(pl.program_id(0) == 0)


def last_step():
    return pl.when(pl.program_id(0) == pl.num_programs(0) - 1)


def turn(out_ref, matrix_ref, tail_ref=None, edge_ref=None):
    for a, b in pieces_of(H):
        out_ref[a:b, :H] = matrix_ref[:, a:b].T
    if tail_ref is not None:
        out_ref[:H, H:] = tail_ref[...].T
    if edge_ref is not None:
        out_ref[H:, :] = edge_ref[...]


def straight(out_ref, matrix_ref, tail_ref, edge_ref=None):
    out_ref[:H, :H] = matrix_ref[...]
    row = lax.broadcasted_iota(jnp.int32, (TALL - H, H), 0)
    tail = tail_ref[: TALL - H, :].astype(F32)
    out_ref[H:, :H] = jnp.where(row < EXTRA, tail, 0.0).astype(LOW)
    if edge_ref is not None:
        lane = lax.broadcasted_iota(jnp.int32, (TALL - H, WIDE), 1)
        edge = jnp.where(lane < D, edge_ref[...].astype(F32), 0.0)
        edge = jnp.concatenate([edge, jnp.zeros((LANES - (TALL - H), WIDE), F32)])
        out_ref[:, H:] = edge.T[:TALL].astype(LOW)


def widen(out_ref, value_ref):
    @first_step()
    def _():
        out_ref[TALL:] = jnp.zeros((WIDE - TALL, out_ref.shape[1]), LOW)

    out_ref[:TALL] = value_ref[...]


class Spread:
    def __init__(self, groups, rows, count, parts=1, below=False, by_z=False):
        self.groups, self.by_z = groups, by_z
        self.masks = halves(groups)
        self.kinds = kinds_of(groups)
        self.rows, self.count, self.parts, self.below = rows, count, parts, below
        self.direct = rows % 16 == 0

    def shapes(self):
        if not self.direct:
            return [shaped(F32, TALL, H)] * self.parts
        height = self.rows * self.parts + (AUX_ROWS if self.below else 0)
        outs = [shaped(kind, len(row), height, H) for row, kind in zip(self.masks, self.kinds)]
        overs = 0 if self.below else self.parts
        return outs + [shaped(F32, self.count, 8, H)] * overs

    def specs(self):
        return [whole(*s.shape) for s in self.shapes()]

    def write(self, acc_refs, index_ref, out_refs, over_refs=None):
        if not self.direct:
            for acc_ref, ref in zip(acc_refs, out_refs):
                ref[...] = acc_ref[...]
            return
        rows = self.rows
        for ref, row, kind in zip(out_refs, self.masks, self.kinds):
            for j, mask in enumerate(row):
                at = owner(index_ref[0], mask, self.groups, self.by_z)
                start = pl.multiple_of(at * rows, rows)
                for i, acc_ref in enumerate(acc_refs):
                    block = acc_ref[pl.ds(start, rows), :]
                    ref[j, i * rows : (i + 1) * rows] = block.astype(kind)
                if self.below:
                    mine = acc_ref[pl.ds(pl.multiple_of(start + rows, 8), 8), :]
                    parts = [mine[:SPILL_ROWS]] + [v[at][:SPILL_ROWS] for v in over_refs]
                    parts.append(jnp.zeros((AUX_ROWS - MISC_ROW, H), F32))
                    ref[j, rows:] = jnp.concatenate(parts).astype(kind)
        if not self.below:
            for acc_ref, ref in zip(acc_refs, out_refs[len(self.masks) :]):
                for k in range(self.count):
                    ref[k] = acc_ref[(k + 1) * rows : (k + 1) * rows + 8, :]

    def finish(self, outs, index, overs=None):
        if self.direct:
            return list(outs)
        rows, count = self.rows, self.count
        blocks = [grad[:H].reshape(count, rows, H) for grad in outs]
        own = [
            jnp.stack([grad[(k + 1) * rows : (k + 1) * rows + 8] for k in range(count)])
            for grad in outs
        ]
        if self.below:
            blocks += [v[:, :SPILL_ROWS] for v in own + list(overs)]
            blocks.append(jnp.zeros((count, AUX_ROWS - MISC_ROW, H), F32))
        stacks = split(
            index, jnp.concatenate(blocks, axis=1), self.masks, self.kinds, self.groups, self.by_z
        )
        stacks = list(stacks)
        return stacks if self.below else stacks + own


ANY = pl.BlockSpec(memory_space=pl.ANY)
REST = TALL - H


def forward_cross(features, one, two):
    batch = features.shape[1]

    def kernel(f_ref, *refs):
        x_ref, mixer_one_ref, mixer_two_ref, one_ref, two_ref = refs[6:11]
        turned_one, turned_two, wide_ref = refs[11:]

        @first_step()
        def _():
            turn(turned_one, *refs[:3])
            turn(turned_two, *refs[3:6])

        x_ref[:H] = f_ref[:H]
        last = f_ref[H:].astype(F32)
        last = jnp.concatenate([last, jnp.ones((1, TILE), F32), jnp.zeros((TALL - D - 1, TILE), F32)])
        x_ref[H:] = last.astype(LOW)
        widen(wide_ref, x_ref)
        layers = []
        for a, b in [(0, TILE)]:
            mixer = product(turned_one[...], wide_ref[:, a:b])
            mixer_one_ref[:, a:b] = mixer.astype(LOW)
            part = x_ref[:, a:b].astype(F32)
            layer = part * mixer + part
            layers.append(layer)
            one_ref[:, a:b] = layer.astype(LOW)
        wide_ref[:TALL] = one_ref[...]
        for (a, b), layer in zip([(0, TILE)], layers):
            mixer = product(turned_two[...], wide_ref[:, a:b])
            mixer_two_ref[:, a:b] = mixer.astype(LOW)
            two_ref[:, a:b] = (x_ref[:, a:b].astype(F32) * mixer + layer).astype(LOW)

    return run(
        "forward_cross",
        kernel,
        batch,
        [columns(D)] + [once(H, H), once(LANES, H), once(REST, WIDE)] * 2,
        [columns(TALL)] * 5,
        [shaped(LOW, TALL, batch)] * 5,
        [pltpu.VMEM((TALL, WIDE), LOW)] * 2 + [pltpu.VMEM((WIDE, TILE), LOW)],
        4 * batch * TALL * TALL,
        features, *one, *two,
    )


def deep(spread, index, layer_low, examples, matrix_one, tail, matrix, lines, inverse):
    batch = layer_low.shape[1]
    days = inverse.shape[0]

    def kernel(k_ref, l_ref, x_ref, w_one_ref, t_ref, w_ref, n_ref, i_ref, *refs):
        logit_ref, back_ref, line_ref, sum_ref = refs[:4]
        out_refs = refs[4:-8]
        turned_one, turned, acc_ref, hidden_ref, slope_ref, low_ref, part_ref, wide_ref = refs[-8:]

        @first_step()
        def _():
            turn(turned_one, w_one_ref, t_ref)
            turn(turned, w_ref)
            acc_ref[...] = jnp.zeros_like(acc_ref)
            sum_ref[...] = jnp.zeros_like(sum_ref)
            part_ref[...] = jnp.zeros_like(part_ref)
            row = lax.broadcasted_iota(jnp.int32, (REST, TILE), 0)
            hidden_ref[H:] = jnp.where(row == 0, 1.0, 0.0).astype(LOW)

        widen(wide_ref, l_ref)
        for a, b in pieces_of(TILE):
            hidden, slope = gelu_both(product(turned_one[...], wide_ref[:, a:b]))
            hidden_ref[:H, a:b] = hidden.astype(LOW)
            slope_ref[:, a:b] = slope
        head = n_ref[:, 1:2]
        for a, b in pieces_of(TILE):
            two, slope = gelu_both(product(turned[...], hidden_ref[:H, a:b]) + n_ref[:, 0:1])
            two = two.astype(LOW).astype(F32)
            logits = n_ref[0:1, 2:3] + jnp.sum(two * head, axis=0, keepdims=True)
            label = x_ref[0:1, a:b]
            day = x_ref[1:2, a:b].astype(jnp.int32)
            row = lax.broadcasted_iota(jnp.int32, (days, b - a), 0)
            weight = jnp.sum(jnp.where(row == day, i_ref[:, 0:1], 0.0), axis=0, keepdims=True)
            decay = jnp.exp(-jnp.abs(logits))
            entropy = jnp.maximum(logits, 0.0) + jnp.log1p(decay) - label * logits
            chance = jnp.where(logits >= 0.0, 1.0, decay) / (1.0 + decay)
            logit_grad = (chance - label) * weight
            logit_ref[:, a:b] = logits
            sum_ref[0:1, a:b] += logit_grad
            sum_ref[1:2, a:b] += entropy * weight
            low_ref[:, a:b] = ((logit_grad * head) * slope).astype(LOW)
            one = logit_grad * two
            part = one[:, :LANES]
            for at in range(LANES, b - a, LANES):
                part = part + one[:, at : at + LANES]
            part_ref[...] += part
        for a, b in pieces_of(TILE):
            back_ref[:, a:b] = (product(w_ref[...], low_ref[:, a:b]) * slope_ref[:, a:b]).astype(LOW)
        for a, b in pieces_of(H):
            acc_ref[:, a:b] += outer(hidden_ref[...], low_ref[a:b])

        @last_step()
        def _():
            line_ref[0:8] = jnp.broadcast_to(
                jnp.sum(part_ref[...].T, axis=0, keepdims=True), (8, H)
            )
            line_ref[8:16] = acc_ref[H : H + 8]
            spread.write([acc_ref], k_ref, out_refs)

    return run(
        "deep",
        kernel,
        batch,
        [
            SMEM,
            columns(TALL),
            columns(2),
            once(H, H),
            once(LANES, H),
            once(H, H),
            whole(H, LANES),
            whole(days, LANES),
        ],
        [columns(1), columns(H), whole(16, H), whole(8, TILE)] + spread.specs(),
        [
            shaped(F32, 1, batch),
            shaped(LOW, H, batch),
            shaped(F32, 16, H),
            shaped(F32, 8, TILE),
        ]
        + spread.shapes(),
        [
            pltpu.VMEM((H, WIDE), LOW),
            pltpu.VMEM((H, H), LOW),
            pltpu.VMEM((TALL, H), F32),
            pltpu.VMEM((TALL, TILE), LOW),
            pltpu.VMEM((H, TILE), F32),
            pltpu.VMEM((H, TILE), LOW),
            pltpu.VMEM((H, LANES), F32),
            pltpu.VMEM((WIDE, TILE), LOW),
        ],
        8 * batch * H * H,
        index, layer_low, examples, matrix_one, tail, matrix, lines, inverse,
    )


def back_deep(spread, index, grad_low, layer_low, features, matrix, tail, after):
    batch = features.shape[1]

    def kernel(k_ref, g_ref, l_ref, x_ref, w_ref, t_ref, *refs):
        refs = refs[len(after) :]
        layer_ref, mixer_ref, line_ref = refs[:3]
        out_refs = refs[3:-2]
        held, acc_ref = refs[-2:]

        @first_step()
        def _():
            straight(held, w_ref, t_ref)
            acc_ref[...] = jnp.zeros_like(acc_ref)

        for a, b in pieces_of(TILE):
            layer = product(held[...], g_ref[:, a:b])
            layer_ref[:, a:b] = layer
            mixer_ref[:, a:b] = (layer * x_ref[:, a:b].astype(F32)).astype(LOW)
        for a, b in pieces_of(H):
            acc_ref[:, a:b] += outer(l_ref[...], g_ref[a:b])

        @last_step()
        def _():
            line_ref[...] = acc_ref[H:]
            spread.write([acc_ref], k_ref, out_refs)

    return run(
        "back_deep",
        kernel,
        batch,
        [SMEM, columns(H), columns(TALL), columns(TALL), once(H, H), once(LANES, H)]
        + [ANY] * len(after),
        [columns(TALL), columns(TALL), whole(REST, H)] + spread.specs(),
        [shaped(F32, TALL, batch), shaped(LOW, TALL, batch), shaped(F32, REST, H)]
        + spread.shapes(),
        [pltpu.VMEM((TALL, H), LOW), pltpu.VMEM((TALL, H), F32)],
        4 * batch * TALL * H,
        index, grad_low, layer_low, features, matrix, tail, *after,
    )


def back_two(
    spread, index, mixer_low, layer_low, layer_grad, features, mixer_one, mixer_two, matrix, tail,
    edge, after,
):
    batch = features.shape[1]

    def kernel(k_ref, g_ref, l_ref, d_ref, x_ref, one_ref, two_ref, w_ref, t_ref, e_ref, *refs):
        refs = refs[len(after) :]
        part_ref, mixer_ref, side_ref, line_ref, next_side_ref, next_line_ref = refs[:6]
        out_refs = refs[6:-4]
        held, acc_ref, wide_ref, sum_ref = refs[-4:]

        @first_step()
        def _():
            straight(held, w_ref, t_ref, e_ref)
            acc_ref[...] = jnp.zeros_like(acc_ref)
            side_ref[...] = jnp.zeros_like(side_ref)
            next_side_ref[...] = jnp.zeros_like(next_side_ref)
            sum_ref[...] = jnp.zeros_like(sum_ref)

        widen(wide_ref, g_ref)
        for a, b in pieces_of(TILE):
            above = d_ref[:, a:b]
            layer = product(held[...], wide_ref[:, a:b]) + above
            mixer = (layer * x_ref[:, a:b].astype(F32)).astype(LOW)
            mixer_ref[:, a:b] = mixer
            mixer = mixer[:H].astype(F32)
            total = mixer[:, :LANES]
            for at in range(LANES, b - a, LANES):
                total = total + mixer[:, at : at + LANES]
            sum_ref[...] += total
            part = above * two_ref[:, a:b].astype(F32)
            part = part + layer * (one_ref[:, a:b].astype(F32) + 1.0)
            part_ref[:, a:b] = part.astype(LOW)
        for a, b in pieces_of(H):
            acc_ref[:, a:b] += outer(l_ref[...], g_ref[a:b])
        side_ref[...] += outer(g_ref[H:], l_ref[...])
        next_side_ref[...] += outer(mixer_ref[H:], x_ref[...])

        @last_step()
        def _():
            line_ref[...] = acc_ref[H:]
            next_line_ref[...] = jnp.broadcast_to(
                jnp.sum(sum_ref[...].T, axis=0, keepdims=True), (8, H)
            )
            spread.write([acc_ref], k_ref, out_refs)

    return run(
        "back_two",
        kernel,
        batch,
        [SMEM]
        + [columns(TALL)] * 6
        + [once(H, H), once(LANES, H), once(REST, WIDE)]
        + [ANY] * len(after),
        [columns(TALL), columns(TALL)]
        + [whole(REST, TALL), whole(REST, H), whole(REST, TALL), whole(8, H)]
        + spread.specs(),
        [
            shaped(LOW, TALL, batch),
            shaped(LOW, TALL, batch),
            shaped(F32, REST, TALL),
            shaped(F32, REST, H),
            shaped(F32, REST, TALL),
            shaped(F32, 8, H),
        ]
        + spread.shapes(),
        [
            pltpu.VMEM((TALL, WIDE), LOW),
            pltpu.VMEM((TALL, H), F32),
            pltpu.VMEM((WIDE, TILE), LOW),
            pltpu.VMEM((H, LANES), F32),
        ],
        4 * batch * TALL * TALL,
        index, mixer_low, layer_low, layer_grad, features, mixer_one, mixer_two, matrix, tail,
        edge, *after,
    )


def grad_one(spread, index, mixer_low, features, overs, after):
    batch = features.shape[1]

    def kernel(k_ref, g_ref, x_ref, *refs):
        over_refs = refs[: len(overs)]
        out_refs = refs[len(overs) + len(after) : -1]
        acc_ref = refs[-1]

        @first_step()
        def _():
            acc_ref[...] = jnp.zeros_like(acc_ref)

        for a, b in pieces_of(H):
            acc_ref[:, a:b] += outer(x_ref[...], g_ref[a:b])

        @last_step()
        def _():
            spread.write([acc_ref], k_ref, out_refs, over_refs)

    return run(
        "grad_one",
        kernel,
        batch,
        [SMEM, columns(TALL), columns(TALL)]
        + [once(*v.shape) for v in overs]
        + [ANY] * len(after),
        spread.specs(),
        spread.shapes(),
        [pltpu.VMEM((TALL, H), F32)],
        2 * batch * TALL * TALL,
        index, mixer_low, features, *overs, *after,
    )


def back_one(mixer_low, part, matrix, tail, edge, after):
    batch = part.shape[1]

    def kernel(g_ref, p_ref, w_ref, t_ref, e_ref, *refs):
        out_ref, held, wide_ref = refs[len(after) :]

        @first_step()
        def _():
            straight(held, w_ref, t_ref, e_ref)

        widen(wide_ref, g_ref)
        for a, b in [(0, TILE)]:
            value = p_ref[:, a:b].astype(F32) + product(held[...], wide_ref[:, a:b])
            out_ref[:H, a:b] = value[:H]
            out_ref[H:, a:b] = value[H:D]

    return run(
        "back_one",
        kernel,
        batch,
        [columns(TALL), columns(TALL), whole(H, H), whole(LANES, H), whole(REST, WIDE)]
        + [ANY] * len(after),
        [columns(D)],
        [shaped(F32, D, batch)],
        [pltpu.VMEM((TALL, WIDE), LOW), pltpu.VMEM((WIDE, TILE), LOW)],
        2 * batch * TALL * TALL,
        mixer_low, part, matrix, tail, edge, *after,
    )[0]


def local(groups, features, labels, days, master, moment_one, moment_two):
    count = lax.axis_size(AXES)
    index = lax.axis_index(AXES)
    slot = index[None].astype(jnp.int32)
    rows = H // count
    starts = starts_of(count)
    sizes = piece_sizes(count)
    wide_piece = sizes[1]
    piece = [master[a : a + l] for a, l in zip(starts, sizes)]
    block_one = to_block(piece[0], index, D, rows, count)
    block_two = to_block(piece[2], index, D, rows, count)
    block_deep = to_block(piece[4], index, H, rows, count)

    day_hot = (days[:, None] == jnp.arange(DAYS, dtype=jnp.int32)[None, :]).astype(F32)
    own_counts = jnp.sum(day_hot, axis=0)
    counts_high = jnp.floor(own_counts / 64.0)
    counts_low = own_counts - 64.0 * counts_high

    def spill_side(block):
        side = block[rows:, H:].T
        return jnp.pad(side, ((0, 0), (0, rows - SPILL_ROWS)))

    misc = [
        piece[5],
        piece[7],
        piece[8],
        block_one[:rows, H:].T,
        block_two[:rows, H:].T,
        spill_side(block_one),
        spill_side(block_two),
        piece[1],
        piece[3],
        piece[9],
        counts_high,
        counts_low,
    ]
    misc = jnp.concatenate([part.reshape(-1) for part in misc])
    misc = jnp.pad(misc, (0, (AUX_ROWS - MISC_ROW) * H - misc.shape[0])).reshape(-1, H)
    first = jnp.concatenate(
        [
            block_one[:rows, :H],
            block_two[:rows, :H],
            block_one[rows:, :H],
            block_two[rows:, :H],
            block_deep[rows:],
            misc,
        ]
    ).astype(LOW)
    stacks_cross = gather(first, groups, count)
    rest = jnp.concatenate([block_deep[:rows], piece[6].reshape(rows, H)]).astype(LOW)
    crossed = [value for value, _ in stacks_cross[3:5]]
    stacks_rest = gather(rest, groups, count, direct=True, after=crossed)
    examples = jnp.stack([labels.astype(F32), days.astype(F32)])

    matrix_one, matrix_two, aux = place(slot, stacks_cross, rows, count, [0, SPILL_ROWS])
    matrix_deep, matrix_top = place(slot, stacks_rest, rows, count, [2 * SPILL_ROWS, None], aux)

    line = aux[:, MISC_ROW]
    at = UNIT_LINES * rows
    units = line[:, :at].reshape(count, UNIT_LINES, rows).transpose(1, 0, 2).reshape(UNIT_LINES, H)
    biases = line[:, at : at + 2 * wide_piece].reshape(count, 2, wide_piece)
    biases = biases.transpose(1, 0, 2).reshape(2, count * wide_piece)
    at += 2 * wide_piece
    head_bias = line[0, at]
    both_counts = jnp.sum(line[:, at + 1 : at + 1 + 2 * DAYS].astype(F32), axis=0)
    counts = 64.0 * both_counts[:DAYS] + both_counts[DAYS:]
    inverse = jnp.broadcast_to((1.0 / counts)[:, None], (DAYS, LANES))
    sides = jnp.pad(units[3:9], ((0, 0), (0, LANES))) + jnp.pad(
        units[9:15], ((0, 0), (rows, LANES - rows))
    )

    def tail_of(at, bias):
        return jnp.concatenate(
            [aux[count - 1, at : at + EXTRA], bias[None, :H], jnp.zeros((LANES - EXTRA - 1, H), LOW)]
        )

    def edge_of(side, bias):
        lane = lax.broadcasted_iota(jnp.int32, side.shape, 1)
        side = jnp.where(lane == D, bias[H:D, None], side)
        return jnp.pad(side, ((0, TALL - H - EXTRA), (0, 0)))

    tail_one, edge_one = tail_of(0, biases[0]), edge_of(sides[:3], biases[0])
    tail_two, edge_two = tail_of(SPILL_ROWS, biases[1]), edge_of(sides[3:], biases[1])
    tail_deep = tail_of(2 * SPILL_ROWS, units[0])
    lines = jnp.concatenate(
        [units[1:3], jnp.full((1, H), head_bias), jnp.zeros((LANES - 3, H), LOW)]
    )
    lines = lines.astype(F32).T
    spread = Spread(groups, rows, count, by_z=True)
    spread_two = Spread(groups, rows, count)
    spread_last = Spread(groups, rows, count, below=True)

    wide_features, mixer_one, mixer_two, low_one, low_two = forward_cross(
        features.T, (matrix_one, tail_one, edge_one), (matrix_two, tail_two, edge_two)
    )
    logits, pre_one_low, top_lines, sums, *outs = deep(
        spread, slot, low_two, examples, matrix_deep, tail_deep, matrix_top, lines, inverse
    )
    *top_stacks, _ = spread.finish(outs, slot)
    layer_grad, mixer_two_low, deep_lines, *outs = back_deep(
        spread, slot, pre_one_low, low_two, wide_features, matrix_deep, tail_deep, []
    )
    *deep_stacks, deep_over = spread.finish(outs, slot)
    top_plane = core_stage(top_stacks, groups, count, [mixer_two_low])
    part, mixer_one_low, two_side, two_lines, one_side, one_line, *outs = back_two(
        spread_two, slot, mixer_two_low, low_one, layer_grad, wide_features, mixer_one, mixer_two,
        matrix_two, tail_two, edge_two, top_plane[1:],
    )
    *two_stacks, two_over = spread_two.finish(outs, slot)
    top_total = plane_stage(top_plane, groups, count, [mixer_one_low])
    deep_plane = core_stage(deep_stacks, groups, count, [mixer_one_low])
    overs = (two_over, deep_over)
    outs = grad_one(
        spread_last, slot, mixer_one_low, wide_features, overs, deep_plane[1:] + [top_total]
    )
    last_stacks = spread_last.finish(outs, slot, overs)
    two_plane = core_stage(two_stacks, groups, count, last_stacks[:1])
    deep_total = plane_stage(deep_plane, groups, count, last_stacks[:1])
    last_plane = core_stage(last_stacks, groups, count)
    feature_grad = back_one(
        mixer_one_low, part, matrix_one, tail_one, edge_one,
        last_plane[1:] + two_plane[1:] + [deep_total],
    )

    sums = jnp.pad(jnp.sum(sums[:2], axis=1)[None], ((0, 0), (0, WIDE - 2)))
    vectors = jnp.concatenate(
        [
            jnp.pad(
                jnp.concatenate(
                    [one_line[:1], two_lines[EXTRA:4], deep_lines[EXTRA:4], top_lines[8:9], top_lines[:1]]
                ),
                ((0, 0), (0, LANES)),
            ),
            jnp.pad(jnp.concatenate([one_side[:3], two_side[:3]]), ((0, 0), (0, WIDE - TALL))),
            sums,
            jnp.zeros((4, WIDE), F32),
        ]
    )
    vectors = jnp.sum(lax.all_gather(vectors, AXES, axis=0), axis=0)
    loss = vectors[11, 1]
    side_sums = vectors[5:11]

    own_top = z_scatter(top_total, groups, count)
    own_deep = z_scatter(deep_total, groups, count)
    joint = plane_stage_joint(two_plane, last_plane, groups, count, [feature_grad])
    joint = z_stage(joint, groups, count)
    own_two, own_last = joint[:rows], joint[rows:]
    own_one = own_last[:rows]
    spills = own_last[rows : rows + MISC_ROW]
    row = lax.broadcasted_iota(jnp.int32, spills.shape, 0)
    beyond = (row % SPILL_ROWS >= EXTRA) & (index == count - 1)
    spills = jnp.where(beyond, 0.0, spills)
    wide_biases = jnp.concatenate(
        [vectors[:2, :H], side_sums[:, D].reshape(2, EXTRA)], axis=1
    )
    wide_biases = jnp.pad(wide_biases, ((0, 0), (0, count * wide_piece - D)))
    wide_biases = lax.dynamic_slice(wide_biases, (0, index * wide_piece), (2, wide_piece))
    units = lax.dynamic_slice(vectors[2:5], (0, index * rows), (3, rows))
    side_sums = jnp.pad(side_sums[:, :D], ((0, 0), (0, WIDE - D)))
    side_sums = lax.dynamic_slice(side_sums, (0, index * rows), (6, rows + SPILL_ROWS)).T

    def whole_block(main, number):
        low = number * SPILL_ROWS
        body = jnp.concatenate([main, spills[low : low + SPILL_ROWS]])
        if number == 2:
            return body
        return jnp.concatenate([body, side_sums[:, 3 * number : 3 * number + 3]], axis=1)

    flat_grad = jnp.concatenate(
        [
            from_block(whole_block(own_one, 0), index, sizes[0], rows, count),
            wide_biases[0],
            from_block(whole_block(own_two, 1), index, sizes[2], rows, count),
            wide_biases[1],
            from_block(whole_block(own_deep, 2), index, sizes[4], rows, count),
            units[0],
            own_top.reshape(-1),
            units[1],
            units[2],
            jnp.where(index == 0, vectors[11, :1], 0.0),
        ]
    )
    new_moment_one = 0.9 * moment_one + 0.1 * flat_grad
    new_moment_two = 0.999 * moment_two + 0.001 * flat_grad * flat_grad
    corrected_one = new_moment_one / (1.0 - 0.9**STEP)
    corrected_two = new_moment_two / (1.0 - 0.999**STEP)
    new_master = master - 0.03 * (corrected_one / (jnp.sqrt(corrected_two) + 1e-08) + 0.01 * master)
    new_bias = jnp.concatenate(
        [new_master[starts[i] : starts[i] + sizes[i]] for i in (1, 3, 5, 7, 9)]
    )
    return (
        logits.reshape(-1),
        loss,
        feature_grad.T,
        flat_grad,
        new_moment_one,
        new_moment_two,
        new_master,
        new_bias,
    )


def solution(mesh):
    line = P(AXES)
    table = P(AXES, None)
    groups = bit_groups(mesh)
    return jax.shard_map(
        functools.partial(local, groups),
        mesh=mesh,
        in_specs=(table, line, line, line, line, line),
        out_specs=(line, P(), table, line, line, line, line, line),
        check_vma=False,
    )
```

```python
import functools
import math

import jax
import jax.numpy as jnp
from jax import lax
from jax.experimental import pallas as pl
from jax.experimental.pallas import tpu as pltpu
from jax.sharding import PartitionSpec as P

D = 1027
H = 1024
DAYS = 24
STEP = 10
AXES = ("dp", "cores")
EXTRA = D - H
LANES = 128
WIDE = H + LANES
AUX_ROWS = 16
SPILL_ROWS = 4
MISC_ROW = 12
UNIT_LINES = 15
TILE = 512
TALL = H + 16
MIB = 1024 * 1024
F32 = jnp.float32
LOW = jnp.bfloat16
SMEM = pl.BlockSpec(memory_space=pltpu.SMEM)
VMEM = pl.BlockSpec(memory_space=pltpu.VMEM)
PARAMS = pltpu.CompilerParams(vmem_limit_bytes=56 * MIB)


def shapes():
    return [(D, D), (D,), (D, D), (D,), (D, H), (H,), (H, H), (H,), (H,), (1,)]


def piece_sizes(count):
    return [(math.prod(shape) + count - 1) // count for shape in shapes()[:-1]] + [1]


def starts_of(count):
    starts = []
    position = 0
    for piece in piece_sizes(count):
        starts.append(position)
        position += piece
    return starts


def to_block(piece, index, width, rows, count):
    excess = piece.shape[0] - rows * width
    size = (rows + SPILL_ROWS) * width
    lead = (count - 1) * excess
    padded = jnp.pad(piece, (lead, max(0, size - piece.shape[0])))
    line = lax.dynamic_slice(padded, (lead - index * excess,), (size,))
    return line.reshape(rows + SPILL_ROWS, width)


def from_block(block, index, piece, rows, count):
    width = block.shape[1]
    excess = piece - rows * width
    last = (count - 1) * excess
    line = jnp.pad(block.reshape(-1), (0, max(0, last + piece - block.size)))
    return lax.dynamic_slice(line, (index * excess,), (piece,))


def bit_groups(mesh):
    devices = mesh.devices.reshape(-1)
    groups = {"z": [], "plane": [], "core": []}
    bit = 1
    while bit < devices.size:
        here = getattr(devices[0], "coords", None)
        there = getattr(devices[bit], "coords", None)
        if here is None or there is None:
            name = "core" if bit == 1 else "plane" if bit <= 4 else "z"
        elif tuple(here) == tuple(there):
            name = "core"
        elif here[2] != there[2]:
            name = "z"
        else:
            name = "plane"
        groups[name].append(bit)
        bit *= 2
    return groups


def masks_of(bits):
    masks = [0]
    for bit in bits:
        masks = masks + [mask | bit for mask in masks]
    return masks


def teams(bits, count):
    masks = masks_of(bits)
    return [[k | mask for mask in masks] for k in range(count) if not k & masks[-1]]


def owner(index, mask, groups, by_z):
    if by_z:
        index = jnp.bitwise_and(index, ~masks_of(groups["z"])[-1])
    return jnp.bitwise_xor(index, mask)


def swap(value, mask, count):
    return lax.ppermute(value, AXES, [(k, k ^ mask) for k in range(count)])


def join(parts, after):
    def kernel(*refs):
        for j in range(len(parts)):
            refs[-1][j] = refs[j][...]

    return pl.pallas_call(
        kernel,
        out_shape=jax.ShapeDtypeStruct((len(parts),) + parts[0].shape, parts[0].dtype),
        in_specs=[VMEM] * len(parts) + [pl.BlockSpec(memory_space=pl.ANY)] * len(after),
        out_specs=VMEM,
        compiler_params=PARAMS,
        name="join",
    )(*parts, *after)


def gather(block, groups, count, direct=False, after=()):
    z_masks = masks_of(groups["z"])
    core_masks = masks_of(groups["core"])
    line = [block] + [swap(block, mask, count) for mask in z_masks[1:]]
    if len(groups["plane"]) == 2 and len(z_masks) > 2 and not direct:
        one, two = groups["plane"]
        both = one ^ two
        cut = len(z_masks) // 2
        own = jnp.stack([block] + [swap(block, mask, count) for mask in (one, two, both)])
        rest, masks = jnp.stack(line[1:]), z_masks[1:]
        by_one = swap(rest, one, count)
        by_two = swap(rest, two, count)
        plane = [
            (own, [0, one, two, both]),
            (rest, masks),
            (by_one, [one ^ z for z in masks]),
            (by_two, [two ^ z for z in masks]),
            (swap(by_one[:cut], two, count), [both ^ z for z in masks[:cut]]),
            (swap(by_two[cut:], one, count), [both ^ z for z in masks[cut:]]),
        ]
    else:
        line = join(line, after) if after else jnp.stack(line)
        plane = [(line, z_masks)]
        for mask in masks_of(groups["plane"])[1:]:
            plane.append((swap(line, mask, count), [mask ^ z for z in z_masks]))
    result = list(plane)
    for core in core_masks[1:]:
        result += [(swap(value, core, count), [core ^ m for m in row]) for value, row in plane]
    return result


def place(index, stacks, rows, count, parts, aux=None):
    sources = [value for value, _ in stacks]
    masks = [row for _, row in stacks]
    carries = aux is None
    top = min(16, rows)

    def kernel(index_ref, *refs):
        refs = list(refs)
        aux_ref = refs.pop() if carries else refs.pop(0)
        outs = refs[len(sources) :]
        for ref, row in zip(refs, masks):
            for j, mask in enumerate(row):
                at = jnp.bitwise_xor(index_ref[0], mask)
                for i, out_ref in enumerate(outs):
                    out_ref[at] = ref[j, i * rows : (i + 1) * rows]
                if carries:
                    aux_ref[at] = ref[j, len(outs) * rows :]
        for spill_at, out_ref in zip(parts, outs):
            if spill_at is None:
                continue
            for k in range(1, count):
                spill = aux_ref[k - 1].astype(F32)[spill_at : spill_at + SPILL_ROWS]
                old = out_ref[k, :top].astype(F32)
                new = old[:SPILL_ROWS] + spill
                if top > SPILL_ROWS:
                    new = jnp.concatenate([new, old[SPILL_ROWS:]], axis=0)
                out_ref[k, :top] = new.astype(LOW)

    out_shape = [jax.ShapeDtypeStruct((count, rows, H), LOW)] * len(parts)
    if carries:
        out_shape.append(jax.ShapeDtypeStruct((count, AUX_ROWS, H), LOW))
    extra = [] if carries else [aux]
    result = pl.pallas_call(
        kernel,
        out_shape=out_shape,
        in_specs=[SMEM] + [VMEM] * (len(extra) + len(sources)),
        out_specs=[VMEM] * len(out_shape),
        compiler_params=PARAMS,
        name="place",
    )(index, *extra, *sources)
    return [value.reshape(H, H) for value in result[: len(parts)]] + list(result[len(parts) :])


def split(index, value, masks, kinds, groups, by_z):
    def kernel(index_ref, value_ref, *out_refs):
        for ref, row, kind in zip(out_refs, masks, kinds):
            for j, mask in enumerate(row):
                ref[j] = value_ref[owner(index_ref[0], mask, groups, by_z)].astype(kind)

    shape = value.shape[1:]
    return pl.pallas_call(
        kernel,
        out_shape=[
            jax.ShapeDtypeStruct((len(row),) + shape, kind) for row, kind in zip(masks, kinds)
        ],
        in_specs=[SMEM, VMEM],
        out_specs=[VMEM] * len(masks),
        compiler_params=PARAMS,
        name="split",
    )(index, value)


def halves(groups):
    z_masks, plane_masks, core_masks = (masks_of(groups[g]) for g in ("z", "plane", "core"))
    inner = [p ^ z for p in plane_masks for z in z_masks]
    return [[core ^ m for m in inner] for core in core_masks]


def kinds_of(groups):
    return [F32] + [LOW] * (len(halves(groups)) - 1)


def adder(name, body, ins, outs, after):
    def kernel(*refs):
        body(refs[: len(ins)], refs[len(ins) + len(after) :])

    result = pl.pallas_call(
        kernel,
        out_shape=outs,
        in_specs=[VMEM] * len(ins) + [pl.BlockSpec(memory_space=pl.ANY)] * len(after),
        out_specs=[VMEM] * len(outs),
        compiler_params=PARAMS,
        name=name,
    )(*ins, *after)
    return list(result)


def core_stage(stacks, groups, count, after=()):
    z_count, plane_count = len(masks_of(groups["z"])), len(masks_of(groups["plane"]))
    cores = masks_of(groups["core"])[1:]
    gotten = [swap(stack, core, count) for core, stack in zip(cores, stacks[1:])]
    shape = (z_count,) + stacks[0].shape[1:]

    def body(ins, outs):
        for p, out_ref in enumerate(outs):
            for z in range(z_count):
                total = ins[0][p * z_count + z]
                for ref in ins[1:]:
                    total = total + ref[p * z_count + z].astype(F32)
                out_ref[z] = total.astype(out_ref.dtype)

    outs = [jax.ShapeDtypeStruct(shape, F32 if p == 0 else LOW) for p in range(plane_count)]
    return adder("core_sum", body, [stacks[0]] + gotten, outs, after)


def plane_swaps(parts, groups, count):
    masks = masks_of(groups["plane"])[1:]
    return [parts[0]] + [swap(part, mask, count) for mask, part in zip(masks, parts[1:])]


def plane_stage(parts, groups, count, after=()):
    def body(ins, outs):
        for z in range(ins[0].shape[0]):
            total = ins[0][z]
            for ref in ins[1:]:
                total = total + ref[z].astype(F32)
            outs[0][z] = total

    outs = [jax.ShapeDtypeStruct(parts[0].shape, F32)]
    return adder("plane_sum", body, plane_swaps(parts, groups, count), outs, after)[0]


def plane_stage_z(parts, groups, count, after=()):
    def body(ins, outs):
        for z, out_ref in enumerate(outs):
            total = ins[0][z]
            for ref in ins[1:]:
                total = total + ref[z].astype(F32)
            out_ref[...] = total.astype(out_ref.dtype)

    many, rows, width = parts[0].shape
    outs = [jax.ShapeDtypeStruct((rows, width), F32 if z == 0 else LOW) for z in range(many)]
    return adder("plane_sum", body, plane_swaps(parts, groups, count), outs, after)


def z_stage(parts, groups, count):
    own = parts[0]
    for mask, part in zip(masks_of(groups["z"])[1:], parts[1:]):
        own = own + swap(part, mask, count).astype(F32)
    return own


def z_scatter(total, groups, count):
    if not groups["z"]:
        return total[0]
    return lax.psum_scatter(
        total, AXES, scatter_dimension=0, axis_index_groups=teams(groups["z"], count)
    )


def product(left, right):
    return lax.dot_general(left, right, (((1,), (0,)), ((), ())), preferred_element_type=F32)


def outer(left, right):
    return lax.dot_general(left, right, (((1,), (1,)), ((), ())), preferred_element_type=F32)


def gelu_both(value):
    scale = math.sqrt(2.0 / math.pi)
    square = value * value
    share = 0.5 + 0.5 * jnp.tanh(value * (scale + scale * 0.044715 * square))
    result = value * share
    slope = share + result * (1.0 - share) * (2.0 * scale + 6.0 * scale * 0.044715 * square)
    return result, slope


def columns(height, tile=TILE):
    return pl.BlockSpec((height, tile), lambda i: (0, i))


def whole(*shape):
    return pl.BlockSpec(shape, lambda i: (0,) * len(shape))


def once(*shape):
    return pl.BlockSpec(shape, lambda i: (0,) * len(shape), pipeline_mode=pl.Buffered(1))


def shaped(kind, *shape):
    return jax.ShapeDtypeStruct(shape, kind)


def pieces_of(width):
    return [(a, a + 256) for a in range(0, width, 256)]


def run(name, kernel, batch, in_specs, out_specs, out_shape, scratch, flops, *args, tile=TILE):
    moved = sum(a.size * a.dtype.itemsize for a in args)
    moved += sum(math.prod(o.shape) * o.dtype.itemsize for o in out_shape)
    return pl.pallas_call(
        kernel,
        grid=(batch // tile,),
        in_specs=in_specs,
        out_specs=out_specs,
        out_shape=out_shape,
        scratch_shapes=scratch,
        compiler_params=PARAMS,
        cost_estimate=pl.CostEstimate(flops=flops, bytes_accessed=moved, transcendentals=0),
        name=name,
    )(*args)


def first_step():
    return pl.when(pl.program_id(0) == 0)


def last_step():
    return pl.when(pl.program_id(0) == pl.num_programs(0) - 1)


def turn(out_ref, matrix_ref, tail_ref=None, edge_ref=None):
    for a, b in pieces_of(H):
        out_ref[a:b, :H] = matrix_ref[:, a:b].T
    if tail_ref is not None:
        out_ref[:H, H:] = tail_ref[...].T
    if edge_ref is not None:
        out_ref[H:, :] = edge_ref[...]


def straight(out_ref, matrix_ref, tail_ref, edge_ref=None):
    out_ref[:H, :H] = matrix_ref[...]
    row = lax.broadcasted_iota(jnp.int32, (TALL - H, H), 0)
    tail = tail_ref[: TALL - H, :].astype(F32)
    out_ref[H:, :H] = jnp.where(row < EXTRA, tail, 0.0).astype(LOW)
    if edge_ref is not None:
        lane = lax.broadcasted_iota(jnp.int32, (TALL - H, WIDE), 1)
        edge = jnp.where(lane < D, edge_ref[...].astype(F32), 0.0)
        edge = jnp.concatenate([edge, jnp.zeros((LANES - (TALL - H), WIDE), F32)])
        out_ref[:, H:] = edge.T[:TALL].astype(LOW)


def widen(out_ref, value_ref):
    @first_step()
    def _():
        out_ref[TALL:] = jnp.zeros((WIDE - TALL, out_ref.shape[1]), LOW)

    out_ref[:TALL] = value_ref[...]


class Spread:
    def __init__(self, groups, rows, count, parts=1, below=False, by_z=False):
        self.groups, self.by_z = groups, by_z
        self.masks = halves(groups)
        self.kinds = kinds_of(groups)
        self.rows, self.count, self.parts, self.below = rows, count, parts, below
        self.direct = rows % 16 == 0

    def shapes(self):
        if not self.direct:
            return [shaped(F32, TALL, H)] * self.parts
        height = self.rows * self.parts + (AUX_ROWS if self.below else 0)
        outs = [shaped(kind, len(row), height, H) for row, kind in zip(self.masks, self.kinds)]
        overs = 0 if self.below else self.parts
        return outs + [shaped(F32, self.count, 8, H)] * overs

    def specs(self):
        return [whole(*s.shape) for s in self.shapes()]

    def write(self, acc_refs, index_ref, out_refs, over_refs=None):
        if not self.direct:
            for acc_ref, ref in zip(acc_refs, out_refs):
                ref[...] = acc_ref[...]
            return
        rows = self.rows
        for ref, row, kind in zip(out_refs, self.masks, self.kinds):
            for j, mask in enumerate(row):
                at = owner(index_ref[0], mask, self.groups, self.by_z)
                start = pl.multiple_of(at * rows, rows)
                for i, acc_ref in enumerate(acc_refs):
                    block = acc_ref[pl.ds(start, rows), :]
                    ref[j, i * rows : (i + 1) * rows] = block.astype(kind)
                if self.below:
                    mine = acc_ref[pl.ds(pl.multiple_of(start + rows, 8), 8), :]
                    parts = [mine[:SPILL_ROWS]] + [v[at][:SPILL_ROWS] for v in over_refs]
                    parts.append(jnp.zeros((AUX_ROWS - MISC_ROW, H), F32))
                    ref[j, rows:] = jnp.concatenate(parts).astype(kind)
        if not self.below:
            for acc_ref, ref in zip(acc_refs, out_refs[len(self.masks) :]):
                for k in range(self.count):
                    ref[k] = acc_ref[(k + 1) * rows : (k + 1) * rows + 8, :]

    def finish(self, outs, index, overs=None):
        if self.direct:
            return list(outs)
        rows, count = self.rows, self.count
        blocks = [grad[:H].reshape(count, rows, H) for grad in outs]
        own = [
            jnp.stack([grad[(k + 1) * rows : (k + 1) * rows + 8] for k in range(count)])
            for grad in outs
        ]
        if self.below:
            blocks += [v[:, :SPILL_ROWS] for v in own + list(overs)]
            blocks.append(jnp.zeros((count, AUX_ROWS - MISC_ROW, H), F32))
        stacks = split(
            index, jnp.concatenate(blocks, axis=1), self.masks, self.kinds, self.groups, self.by_z
        )
        stacks = list(stacks)
        return stacks if self.below else stacks + own


ANY = pl.BlockSpec(memory_space=pl.ANY)
REST = TALL - H


def forward_cross(features, one, two):
    batch = features.shape[1]

    def kernel(f_ref, *refs):
        x_ref, mixer_one_ref, mixer_two_ref, one_ref, two_ref = refs[6:11]
        turned_one, turned_two, wide_ref = refs[11:]

        @first_step()
        def _():
            turn(turned_one, *refs[:3])
            turn(turned_two, *refs[3:6])

        x_ref[:H] = f_ref[:H]
        last = f_ref[H:].astype(F32)
        last = jnp.concatenate([last, jnp.ones((1, TILE), F32), jnp.zeros((TALL - D - 1, TILE), F32)])
        x_ref[H:] = last.astype(LOW)
        widen(wide_ref, x_ref)
        layers = []
        for a, b in [(0, TILE)]:
            mixer = product(turned_one[...], wide_ref[:, a:b])
            mixer_one_ref[:, a:b] = mixer.astype(LOW)
            part = x_ref[:, a:b].astype(F32)
            layer = part * mixer + part
            layers.append(layer)
            one_ref[:, a:b] = layer.astype(LOW)
        wide_ref[:TALL] = one_ref[...]
        for (a, b), layer in zip([(0, TILE)], layers):
            mixer = product(turned_two[...], wide_ref[:, a:b])
            mixer_two_ref[:, a:b] = mixer.astype(LOW)
            two_ref[:, a:b] = (x_ref[:, a:b].astype(F32) * mixer + layer).astype(LOW)

    return run(
        "forward_cross",
        kernel,
        batch,
        [columns(D)] + [once(H, H), once(LANES, H), once(REST, WIDE)] * 2,
        [columns(TALL)] * 5,
        [shaped(LOW, TALL, batch)] * 5,
        [pltpu.VMEM((TALL, WIDE), LOW)] * 2 + [pltpu.VMEM((WIDE, TILE), LOW)],
        4 * batch * TALL * TALL,
        features, *one, *two,
    )


def deep(spread, index, layer_low, examples, matrix_one, tail, matrix, lines, inverse):
    batch = layer_low.shape[1]
    days = inverse.shape[0]

    def kernel(k_ref, l_ref, x_ref, w_one_ref, t_ref, w_ref, n_ref, i_ref, *refs):
        logit_ref, back_ref, line_ref, sum_ref = refs[:4]
        out_refs = refs[4:-8]
        turned_one, turned, acc_ref, hidden_ref, slope_ref, low_ref, part_ref, wide_ref = refs[-8:]

        @first_step()
        def _():
            turn(turned_one, w_one_ref, t_ref)
            turn(turned, w_ref)
            acc_ref[...] = jnp.zeros_like(acc_ref)
            sum_ref[...] = jnp.zeros_like(sum_ref)
            part_ref[...] = jnp.zeros_like(part_ref)
            row = lax.broadcasted_iota(jnp.int32, (REST, TILE), 0)
            hidden_ref[H:] = jnp.where(row == 0, 1.0, 0.0).astype(LOW)

        widen(wide_ref, l_ref)
        for a, b in pieces_of(TILE):
            hidden, slope = gelu_both(product(turned_one[...], wide_ref[:, a:b]))
            hidden_ref[:H, a:b] = hidden.astype(LOW)
            slope_ref[:, a:b] = slope
        head = n_ref[:, 1:2]
        for a, b in pieces_of(TILE):
            two, slope = gelu_both(product(turned[...], hidden_ref[:H, a:b]) + n_ref[:, 0:1])
            two = two.astype(LOW).astype(F32)
            logits = n_ref[0:1, 2:3] + jnp.sum(two * head, axis=0, keepdims=True)
            label = x_ref[0:1, a:b]
            day = x_ref[1:2, a:b].astype(jnp.int32)
            row = lax.broadcasted_iota(jnp.int32, (days, b - a), 0)
            weight = jnp.sum(jnp.where(row == day, i_ref[:, 0:1], 0.0), axis=0, keepdims=True)
            decay = jnp.exp(-jnp.abs(logits))
            entropy = jnp.maximum(logits, 0.0) + jnp.log1p(decay) - label * logits
            chance = jnp.where(logits >= 0.0, 1.0, decay) / (1.0 + decay)
            logit_grad = (chance - label) * weight
            logit_ref[:, a:b] = logits
            sum_ref[0:1, a:b] += logit_grad
            sum_ref[1:2, a:b] += entropy * weight
            low_ref[:, a:b] = ((logit_grad * head) * slope).astype(LOW)
            one = logit_grad * two
            part = one[:, :LANES]
            for at in range(LANES, b - a, LANES):
                part = part + one[:, at : at + LANES]
            part_ref[...] += part
        for a, b in pieces_of(TILE):
            back_ref[:, a:b] = (product(w_ref[...], low_ref[:, a:b]) * slope_ref[:, a:b]).astype(LOW)
        for a, b in pieces_of(H):
            acc_ref[:, a:b] += outer(hidden_ref[...], low_ref[a:b])

        @last_step()
        def _():
            line_ref[0:8] = jnp.broadcast_to(
                jnp.sum(part_ref[...].T, axis=0, keepdims=True), (8, H)
            )
            line_ref[8:16] = acc_ref[H : H + 8]
            spread.write([acc_ref], k_ref, out_refs)

    return run(
        "deep",
        kernel,
        batch,
        [
            SMEM,
            columns(TALL),
            columns(2),
            once(H, H),
            once(LANES, H),
            once(H, H),
            whole(H, LANES),
            whole(days, LANES),
        ],
        [columns(1), columns(H), whole(16, H), whole(8, TILE)] + spread.specs(),
        [
            shaped(F32, 1, batch),
            shaped(LOW, H, batch),
            shaped(F32, 16, H),
            shaped(F32, 8, TILE),
        ]
        + spread.shapes(),
        [
            pltpu.VMEM((H, WIDE), LOW),
            pltpu.VMEM((H, H), LOW),
            pltpu.VMEM((TALL, H), F32),
            pltpu.VMEM((TALL, TILE), LOW),
            pltpu.VMEM((H, TILE), F32),
            pltpu.VMEM((H, TILE), LOW),
            pltpu.VMEM((H, LANES), F32),
            pltpu.VMEM((WIDE, TILE), LOW),
        ],
        8 * batch * H * H,
        index, layer_low, examples, matrix_one, tail, matrix, lines, inverse,
    )


def back_deep(spread, index, grad_low, layer_low, features, matrix, tail, after):
    batch = features.shape[1]

    def kernel(k_ref, g_ref, l_ref, x_ref, w_ref, t_ref, *refs):
        refs = refs[len(after) :]
        layer_ref, mixer_ref, line_ref = refs[:3]
        out_refs = refs[3:-2]
        held, acc_ref = refs[-2:]

        @first_step()
        def _():
            straight(held, w_ref, t_ref)
            acc_ref[...] = jnp.zeros_like(acc_ref)

        for a, b in pieces_of(TILE):
            layer = product(held[...], g_ref[:, a:b])
            layer_ref[:, a:b] = layer
            mixer_ref[:, a:b] = (layer * x_ref[:, a:b].astype(F32)).astype(LOW)
        for a, b in pieces_of(H):
            acc_ref[:, a:b] += outer(l_ref[...], g_ref[a:b])

        @last_step()
        def _():
            line_ref[...] = acc_ref[H:]
            spread.write([acc_ref], k_ref, out_refs)

    return run(
        "back_deep",
        kernel,
        batch,
        [SMEM, columns(H), columns(TALL), columns(TALL), once(H, H), once(LANES, H)]
        + [ANY] * len(after),
        [columns(TALL), columns(TALL), whole(REST, H)] + spread.specs(),
        [shaped(F32, TALL, batch), shaped(LOW, TALL, batch), shaped(F32, REST, H)]
        + spread.shapes(),
        [pltpu.VMEM((TALL, H), LOW), pltpu.VMEM((TALL, H), F32)],
        4 * batch * TALL * H,
        index, grad_low, layer_low, features, matrix, tail, *after,
    )


def back_two(
    spread, index, mixer_low, layer_low, layer_grad, features, mixer_one, mixer_two, matrix, tail,
    edge, lines, after,
):
    batch = features.shape[1]

    def kernel(k_ref, g_ref, l_ref, d_ref, x_ref, one_ref, two_ref, w_ref, t_ref, e_ref, *refs):
        top_ref, deep_ref, sums_ref = refs[:3]
        refs = refs[3 + len(after) :]
        part_ref, mixer_ref, vector_ref = refs[:3]
        out_refs = refs[3:-6]
        held, acc_ref, wide_ref, sum_ref, side_ref, next_side_ref = refs[-6:]

        @first_step()
        def _():
            straight(held, w_ref, t_ref, e_ref)
            acc_ref[...] = jnp.zeros_like(acc_ref)
            side_ref[...] = jnp.zeros_like(side_ref)
            next_side_ref[...] = jnp.zeros_like(next_side_ref)
            sum_ref[...] = jnp.zeros_like(sum_ref)

        widen(wide_ref, g_ref)
        for a, b in pieces_of(TILE):
            above = d_ref[:, a:b]
            layer = product(held[...], wide_ref[:, a:b]) + above
            mixer = (layer * x_ref[:, a:b].astype(F32)).astype(LOW)
            mixer_ref[:, a:b] = mixer
            mixer = mixer[:H].astype(F32)
            total = mixer[:, :LANES]
            for at in range(LANES, b - a, LANES):
                total = total + mixer[:, at : at + LANES]
            sum_ref[...] += total
            part = above * two_ref[:, a:b].astype(F32)
            part = part + layer * (one_ref[:, a:b].astype(F32) + 1.0)
            part_ref[:, a:b] = part.astype(LOW)
        for a, b in pieces_of(H):
            acc_ref[:, a:b] += outer(l_ref[...], g_ref[a:b])
        side_ref[...] += outer(g_ref[H:], l_ref[...])
        next_side_ref[...] += outer(mixer_ref[H:], x_ref[...])

        @last_step()
        def _():
            vector_ref[...] = jnp.zeros_like(vector_ref)
            vector_ref[0:1, :H] = jnp.sum(sum_ref[...].T, axis=0, keepdims=True)
            vector_ref[1:2, :H] = acc_ref[D : D + 1]
            vector_ref[2:3, :H] = deep_ref[EXTRA : EXTRA + 1]
            vector_ref[3:4, :H] = top_ref[8:9]
            vector_ref[4:5, :H] = top_ref[0:1]
            vector_ref[5:8, :TALL] = next_side_ref[:EXTRA]
            vector_ref[8:11, :TALL] = side_ref[:EXTRA]
            lane = lax.broadcasted_iota(jnp.int32, (1, LANES), 1)
            bias = jnp.sum(sums_ref[0:1], axis=1, keepdims=True)
            loss = jnp.sum(sums_ref[1:2], axis=1, keepdims=True)
            vector_ref[11:12, :LANES] = jnp.where(lane == 0, bias, jnp.where(lane == 1, loss, 0.0))
            spread.write([acc_ref], k_ref, out_refs)

    return run(
        "back_two",
        kernel,
        batch,
        [SMEM]
        + [columns(TALL)] * 6
        + [once(H, H), once(LANES, H), once(REST, WIDE)]
        + [whole(*v.shape) for v in lines]
        + [ANY] * len(after),
        [columns(TALL), columns(TALL)]
        + [whole(16, WIDE)]
        + spread.specs(),
        [
            shaped(LOW, TALL, batch),
            shaped(LOW, TALL, batch),
            shaped(F32, 16, WIDE),
        ]
        + spread.shapes(),
        [
            pltpu.VMEM((TALL, WIDE), LOW),
            pltpu.VMEM((TALL, H), F32),
            pltpu.VMEM((WIDE, TILE), LOW),
            pltpu.VMEM((H, LANES), F32),
            pltpu.VMEM((REST, TALL), F32),
            pltpu.VMEM((REST, TALL), F32),
        ],
        4 * batch * TALL * TALL,
        index, mixer_low, layer_low, layer_grad, features, mixer_one, mixer_two, matrix, tail,
        edge, *lines, *after,
    )


def grad_one(spread, index, mixer_low, features, overs, after):
    batch = features.shape[1]

    def kernel(k_ref, g_ref, x_ref, *refs):
        over_refs = refs[: len(overs)]
        out_refs = refs[len(overs) + len(after) : -1]
        acc_ref = refs[-1]

        @first_step()
        def _():
            acc_ref[...] = jnp.zeros_like(acc_ref)

        for a, b in pieces_of(H):
            acc_ref[:, a:b] += outer(x_ref[...], g_ref[a:b])

        @last_step()
        def _():
            spread.write([acc_ref], k_ref, out_refs, over_refs)

    return run(
        "grad_one",
        kernel,
        batch,
        [SMEM, columns(TALL), columns(TALL)]
        + [once(*v.shape) for v in overs]
        + [ANY] * len(after),
        spread.specs(),
        spread.shapes(),
        [pltpu.VMEM((TALL, H), F32)],
        2 * batch * TALL * TALL,
        index, mixer_low, features, *overs, *after,
    )


def back_one(mixer_low, part, matrix, tail, edge, after):
    batch = part.shape[1]

    def kernel(g_ref, p_ref, w_ref, t_ref, e_ref, *refs):
        out_ref, held, wide_ref = refs[len(after) :]

        @first_step()
        def _():
            straight(held, w_ref, t_ref, e_ref)

        widen(wide_ref, g_ref)
        for a, b in [(0, TILE)]:
            value = p_ref[:, a:b].astype(F32) + product(held[...], wide_ref[:, a:b])
            out_ref[:H, a:b] = value[:H]
            out_ref[H:, a:b] = value[H:D]

    return run(
        "back_one",
        kernel,
        batch,
        [columns(TALL), columns(TALL), whole(H, H), whole(LANES, H), whole(REST, WIDE)]
        + [ANY] * len(after),
        [columns(D)],
        [shaped(F32, D, batch)],
        [pltpu.VMEM((TALL, WIDE), LOW), pltpu.VMEM((WIDE, TILE), LOW)],
        2 * batch * TALL * TALL,
        mixer_low, part, matrix, tail, edge, *after,
    )[0]


def local(groups, features, labels, days, master, moment_one, moment_two):
    count = lax.axis_size(AXES)
    index = lax.axis_index(AXES)
    slot = index[None].astype(jnp.int32)
    rows = H // count
    starts = starts_of(count)
    sizes = piece_sizes(count)
    wide_piece = sizes[1]
    piece = [master[a : a + l] for a, l in zip(starts, sizes)]
    block_one = to_block(piece[0], index, D, rows, count)
    block_two = to_block(piece[2], index, D, rows, count)
    block_deep = to_block(piece[4], index, H, rows, count)

    day_hot = (days[:, None] == jnp.arange(DAYS, dtype=jnp.int32)[None, :]).astype(F32)
    own_counts = jnp.sum(day_hot, axis=0)
    counts_high = jnp.floor(own_counts / 64.0)
    counts_low = own_counts - 64.0 * counts_high

    def spill_side(block):
        side = block[rows:, H:].T
        return jnp.pad(side, ((0, 0), (0, rows - SPILL_ROWS)))

    misc = [
        piece[5],
        piece[7],
        piece[8],
        block_one[:rows, H:].T,
        block_two[:rows, H:].T,
        spill_side(block_one),
        spill_side(block_two),
        piece[1],
        piece[3],
        piece[9],
        counts_high,
        counts_low,
    ]
    misc = jnp.concatenate([part.reshape(-1) for part in misc])
    misc = jnp.pad(misc, (0, (AUX_ROWS - MISC_ROW) * H - misc.shape[0])).reshape(-1, H)
    first = jnp.concatenate(
        [
            block_one[:rows, :H],
            block_two[:rows, :H],
            block_one[rows:, :H],
            block_two[rows:, :H],
            block_deep[rows:],
            misc,
        ]
    ).astype(LOW)
    stacks_cross = gather(first, groups, count)
    rest = jnp.concatenate([block_deep[:rows], piece[6].reshape(rows, H)]).astype(LOW)
    crossed = [value for value, _ in stacks_cross[4:6]]
    stacks_rest = gather(rest, groups, count, direct=True, after=crossed)
    examples = jnp.stack([labels.astype(F32), days.astype(F32)])

    matrix_one, matrix_two, aux = place(slot, stacks_cross, rows, count, [0, SPILL_ROWS])
    matrix_deep, matrix_top = place(slot, stacks_rest, rows, count, [2 * SPILL_ROWS, None], aux)

    line = aux[:, MISC_ROW]
    at = UNIT_LINES * rows
    units = line[:, :at].reshape(count, UNIT_LINES, rows).transpose(1, 0, 2).reshape(UNIT_LINES, H)
    biases = line[:, at : at + 2 * wide_piece].reshape(count, 2, wide_piece)
    biases = biases.transpose(1, 0, 2).reshape(2, count * wide_piece)
    at += 2 * wide_piece
    head_bias = line[0, at]
    both_counts = jnp.sum(line[:, at + 1 : at + 1 + 2 * DAYS].astype(F32), axis=0)
    counts = 64.0 * both_counts[:DAYS] + both_counts[DAYS:]
    inverse = jnp.broadcast_to((1.0 / counts)[:, None], (DAYS, LANES))
    sides = jnp.pad(units[3:9], ((0, 0), (0, LANES))) + jnp.pad(
        units[9:15], ((0, 0), (rows, LANES - rows))
    )

    def tail_of(at, bias):
        return jnp.concatenate(
            [aux[count - 1, at : at + EXTRA], bias[None, :H], jnp.zeros((LANES - EXTRA - 1, H), LOW)]
        )

    def edge_of(side, bias):
        lane = lax.broadcasted_iota(jnp.int32, side.shape, 1)
        side = jnp.where(lane == D, bias[H:D, None], side)
        return jnp.pad(side, ((0, TALL - H - EXTRA), (0, 0)))

    tail_one, edge_one = tail_of(0, biases[0]), edge_of(sides[:3], biases[0])
    tail_two, edge_two = tail_of(SPILL_ROWS, biases[1]), edge_of(sides[3:], biases[1])
    tail_deep = tail_of(2 * SPILL_ROWS, units[0])
    lines = jnp.concatenate(
        [units[1:3], jnp.full((1, H), head_bias), jnp.zeros((LANES - 3, H), LOW)]
    )
    lines = lines.astype(F32).T
    spread = Spread(groups, rows, count, by_z=True)
    spread_last = Spread(groups, rows, count, below=True)

    wide_features, mixer_one, mixer_two, low_one, low_two = forward_cross(
        features.T, (matrix_one, tail_one, edge_one), (matrix_two, tail_two, edge_two)
    )
    logits, pre_one_low, top_lines, sums, *outs = deep(
        spread, slot, low_two, examples, matrix_deep, tail_deep, matrix_top, lines, inverse
    )
    *top_stacks, _ = spread.finish(outs, slot)
    layer_grad, mixer_two_low, deep_lines, *outs = back_deep(
        spread, slot, pre_one_low, low_two, wide_features, matrix_deep, tail_deep, []
    )
    *deep_stacks, deep_over = spread.finish(outs, slot)
    top_plane = core_stage(top_stacks, groups, count, [mixer_two_low])
    part, mixer_one_low, vectors, *outs = back_two(
        spread, slot, mixer_two_low, low_one, layer_grad, wide_features, mixer_one, mixer_two,
        matrix_two, tail_two, edge_two, (top_lines, deep_lines, sums), top_plane[1:],
    )
    *two_stacks, two_over = spread.finish(outs, slot)
    top_total = plane_stage(top_plane, groups, count, [mixer_one_low])
    deep_plane = core_stage(deep_stacks, groups, count, [mixer_one_low])
    two_plane = core_stage(two_stacks, groups, count)
    overs = (two_over, deep_over)
    outs = grad_one(
        spread_last, slot, mixer_one_low, wide_features, overs,
        two_plane[1:] + deep_plane[1:] + [top_total],
    )
    last_stacks = spread_last.finish(outs, slot, overs)
    deep_total = plane_stage(deep_plane, groups, count, last_stacks[:1])
    two_total = plane_stage(two_plane, groups, count, last_stacks[:1])
    last_plane = core_stage(last_stacks, groups, count)
    feature_grad = back_one(
        mixer_one_low, part, matrix_one, tail_one, edge_one,
        last_plane[1:] + [deep_total, two_total],
    )

    vectors = jnp.sum(lax.all_gather(vectors, AXES, axis=0), axis=0)
    loss = vectors[11, 1]
    side_sums = vectors[5:11]

    own_top = z_scatter(top_total, groups, count)
    own_deep = z_scatter(deep_total, groups, count)
    own_two = z_scatter(two_total, groups, count)
    own_last = z_stage(plane_stage_z(last_plane, groups, count, [feature_grad]), groups, count)
    own_one = own_last[:rows]
    spills = own_last[rows : rows + MISC_ROW]
    row = lax.broadcasted_iota(jnp.int32, spills.shape, 0)
    beyond = (row % SPILL_ROWS >= EXTRA) & (index == count - 1)
    spills = jnp.where(beyond, 0.0, spills)
    wide_biases = jnp.concatenate(
        [vectors[:2, :H], side_sums[:, D].reshape(2, EXTRA)], axis=1
    )
    wide_biases = jnp.pad(wide_biases, ((0, 0), (0, count * wide_piece - D)))
    wide_biases = lax.dynamic_slice(wide_biases, (0, index * wide_piece), (2, wide_piece))
    units = lax.dynamic_slice(vectors[2:5], (0, index * rows), (3, rows))
    side_sums = jnp.pad(side_sums[:, :D], ((0, 0), (0, WIDE - D)))
    side_sums = lax.dynamic_slice(side_sums, (0, index * rows), (6, rows + SPILL_ROWS)).T

    def whole_block(main, number):
        low = number * SPILL_ROWS
        body = jnp.concatenate([main, spills[low : low + SPILL_ROWS]])
        if number == 2:
            return body
        return jnp.concatenate([body, side_sums[:, 3 * number : 3 * number + 3]], axis=1)

    flat_grad = jnp.concatenate(
        [
            from_block(whole_block(own_one, 0), index, sizes[0], rows, count),
            wide_biases[0],
            from_block(whole_block(own_two, 1), index, sizes[2], rows, count),
            wide_biases[1],
            from_block(whole_block(own_deep, 2), index, sizes[4], rows, count),
            units[0],
            own_top.reshape(-1),
            units[1],
            units[2],
            jnp.where(index == 0, vectors[11, :1], 0.0),
        ]
    )
    new_moment_one = 0.9 * moment_one + 0.1 * flat_grad
    new_moment_two = 0.999 * moment_two + 0.001 * flat_grad * flat_grad
    corrected_one = new_moment_one / (1.0 - 0.9**STEP)
    corrected_two = new_moment_two / (1.0 - 0.999**STEP)
    new_master = master - 0.03 * (corrected_one / (jnp.sqrt(corrected_two) + 1e-08) + 0.01 * master)
    new_bias = jnp.concatenate(
        [new_master[starts[i] : starts[i] + sizes[i]] for i in (1, 3, 5, 7, 9)]
    )
    return (
        logits.reshape(-1),
        loss,
        feature_grad.T,
        flat_grad,
        new_moment_one,
        new_moment_two,
        new_master,
        new_bias,
    )


def solution(mesh):
    line = P(AXES)
    table = P(AXES, None)
    groups = bit_groups(mesh)
    return jax.shard_map(
        functools.partial(local, groups),
        mesh=mesh,
        in_specs=(table, line, line, line, line, line),
        out_specs=(line, P(), table, line, line, line, line, line),
        check_vma=False,
    )
```

```python
import functools
import math

import jax
import jax.numpy as jnp
from jax import lax
from jax.experimental import pallas as pl
from jax.experimental.pallas import tpu as pltpu
from jax.sharding import PartitionSpec as P

D = 1027
H = 1024
DAYS = 24
STEP = 10
AXES = ("dp", "cores")
EXTRA = D - H
LANES = 128
WIDE = H + LANES
AUX_ROWS = 16
SPILL_ROWS = 4
MISC_ROW = 12
UNIT_LINES = 15
TILE = 512
TALL = H + 16
MIB = 1024 * 1024
F32 = jnp.float32
LOW = jnp.bfloat16
SMEM = pl.BlockSpec(memory_space=pltpu.SMEM)
VMEM = pl.BlockSpec(memory_space=pltpu.VMEM)
PARAMS = pltpu.CompilerParams(vmem_limit_bytes=56 * MIB)


def shapes():
    return [(D, D), (D,), (D, D), (D,), (D, H), (H,), (H, H), (H,), (H,), (1,)]


def piece_sizes(count):
    return [(math.prod(shape) + count - 1) // count for shape in shapes()[:-1]] + [1]


def starts_of(count):
    starts = []
    position = 0
    for piece in piece_sizes(count):
        starts.append(position)
        position += piece
    return starts


def to_block(piece, index, width, rows, count):
    excess = piece.shape[0] - rows * width
    size = (rows + SPILL_ROWS) * width
    lead = (count - 1) * excess
    padded = jnp.pad(piece, (lead, max(0, size - piece.shape[0])))
    line = lax.dynamic_slice(padded, (lead - index * excess,), (size,))
    return line.reshape(rows + SPILL_ROWS, width)


def from_block(block, index, piece, rows, count):
    width = block.shape[1]
    excess = piece - rows * width
    last = (count - 1) * excess
    line = jnp.pad(block.reshape(-1), (0, max(0, last + piece - block.size)))
    return lax.dynamic_slice(line, (index * excess,), (piece,))


def bit_groups(mesh):
    devices = mesh.devices.reshape(-1)
    groups = {"z": [], "plane": [], "core": []}
    bit = 1
    while bit < devices.size:
        here = getattr(devices[0], "coords", None)
        there = getattr(devices[bit], "coords", None)
        if here is None or there is None:
            name = "core" if bit == 1 else "plane" if bit <= 4 else "z"
        elif tuple(here) == tuple(there):
            name = "core"
        elif here[2] != there[2]:
            name = "z"
        else:
            name = "plane"
        groups[name].append(bit)
        bit *= 2
    return groups


def masks_of(bits):
    masks = [0]
    for bit in bits:
        masks = masks + [mask | bit for mask in masks]
    return masks


def teams(bits, count):
    masks = masks_of(bits)
    return [[k | mask for mask in masks] for k in range(count) if not k & masks[-1]]


def owner(index, mask, groups, by_z):
    if by_z:
        index = jnp.bitwise_and(index, ~masks_of(groups["z"])[-1])
    return jnp.bitwise_xor(index, mask)


def swap(value, mask, count):
    return lax.ppermute(value, AXES, [(k, k ^ mask) for k in range(count)])


def join(parts, after):
    def kernel(*refs):
        for j in range(len(parts)):
            refs[-1][j] = refs[j][...]

    return pl.pallas_call(
        kernel,
        out_shape=jax.ShapeDtypeStruct((len(parts),) + parts[0].shape, parts[0].dtype),
        in_specs=[VMEM] * len(parts) + [pl.BlockSpec(memory_space=pl.ANY)] * len(after),
        out_specs=VMEM,
        compiler_params=PARAMS,
        name="join",
    )(*parts, *after)


def gather(block, groups, count, direct=False, after=()):
    z_masks = masks_of(groups["z"])
    core_masks = masks_of(groups["core"])
    line = [block] + [swap(block, mask, count) for mask in z_masks[1:]]
    line = join(line, after) if after else jnp.stack(line)
    plane = [(line, z_masks)]
    if len(groups["plane"]) == 2 and len(z_masks) > 1 and not direct:
        one, two = groups["plane"]
        half = len(z_masks) // 2
        by_one = swap(line, one, count)
        by_two = swap(line, two, count)
        plane.append((by_one, [one ^ z for z in z_masks]))
        plane.append((by_two, [two ^ z for z in z_masks]))
        both = one ^ two
        plane.append((swap(by_one[:half], two, count), [both ^ z for z in z_masks[:half]]))
        plane.append((swap(by_two[half:], one, count), [both ^ z for z in z_masks[half:]]))
    else:
        for mask in masks_of(groups["plane"])[1:]:
            plane.append((swap(line, mask, count), [mask ^ z for z in z_masks]))
    result = list(plane)
    for core in core_masks[1:]:
        result += [(swap(value, core, count), [core ^ m for m in row]) for value, row in plane]
    return result


def place(index, stacks, rows, count, parts, aux=None):
    sources = [value for value, _ in stacks]
    masks = [row for _, row in stacks]
    carries = aux is None
    top = min(16, rows)

    def kernel(index_ref, *refs):
        refs = list(refs)
        aux_ref = refs.pop() if carries else refs.pop(0)
        outs = refs[len(sources) :]
        for ref, row in zip(refs, masks):
            for j, mask in enumerate(row):
                at = jnp.bitwise_xor(index_ref[0], mask)
                for i, out_ref in enumerate(outs):
                    out_ref[at] = ref[j, i * rows : (i + 1) * rows]
                if carries:
                    aux_ref[at] = ref[j, len(outs) * rows :]
        for spill_at, out_ref in zip(parts, outs):
            if spill_at is None:
                continue
            for k in range(1, count):
                spill = aux_ref[k - 1].astype(F32)[spill_at : spill_at + SPILL_ROWS]
                old = out_ref[k, :top].astype(F32)
                new = old[:SPILL_ROWS] + spill
                if top > SPILL_ROWS:
                    new = jnp.concatenate([new, old[SPILL_ROWS:]], axis=0)
                out_ref[k, :top] = new.astype(LOW)

    out_shape = [jax.ShapeDtypeStruct((count, rows, H), LOW)] * len(parts)
    if carries:
        out_shape.append(jax.ShapeDtypeStruct((count, AUX_ROWS, H), LOW))
    extra = [] if carries else [aux]
    result = pl.pallas_call(
        kernel,
        out_shape=out_shape,
        in_specs=[SMEM] + [VMEM] * (len(extra) + len(sources)),
        out_specs=[VMEM] * len(out_shape),
        compiler_params=PARAMS,
        name="place",
    )(index, *extra, *sources)
    return [value.reshape(H, H) for value in result[: len(parts)]] + list(result[len(parts) :])


def split(index, value, masks, kinds, groups, by_z):
    def kernel(index_ref, value_ref, *out_refs):
        for ref, row, kind in zip(out_refs, masks, kinds):
            for j, mask in enumerate(row):
                ref[j] = value_ref[owner(index_ref[0], mask, groups, by_z)].astype(kind)

    shape = value.shape[1:]
    return pl.pallas_call(
        kernel,
        out_shape=[
            jax.ShapeDtypeStruct((len(row),) + shape, kind) for row, kind in zip(masks, kinds)
        ],
        in_specs=[SMEM, VMEM],
        out_specs=[VMEM] * len(masks),
        compiler_params=PARAMS,
        name="split",
    )(index, value)


def halves(groups):
    z_masks, plane_masks, core_masks = (masks_of(groups[g]) for g in ("z", "plane", "core"))
    inner = [p ^ z for p in plane_masks for z in z_masks]
    return [[core ^ m for m in inner] for core in core_masks]


def kinds_of(groups):
    return [F32] + [LOW] * (len(halves(groups)) - 1)


def adder(name, body, ins, outs, after):
    def kernel(*refs):
        body(refs[: len(ins)], refs[len(ins) + len(after) :])

    result = pl.pallas_call(
        kernel,
        out_shape=outs,
        in_specs=[VMEM] * len(ins) + [pl.BlockSpec(memory_space=pl.ANY)] * len(after),
        out_specs=[VMEM] * len(outs),
        compiler_params=PARAMS,
        name=name,
    )(*ins, *after)
    return list(result)


def core_stage(stacks, groups, count, after=()):
    z_count, plane_count = len(masks_of(groups["z"])), len(masks_of(groups["plane"]))
    cores = masks_of(groups["core"])[1:]
    gotten = [swap(stack, core, count) for core, stack in zip(cores, stacks[1:])]
    shape = (z_count,) + stacks[0].shape[1:]

    def body(ins, outs):
        for p, out_ref in enumerate(outs):
            for z in range(z_count):
                total = ins[0][p * z_count + z]
                for ref in ins[1:]:
                    total = total + ref[p * z_count + z].astype(F32)
                out_ref[z] = total.astype(out_ref.dtype)

    outs = [jax.ShapeDtypeStruct(shape, F32 if p == 0 else LOW) for p in range(plane_count)]
    return adder("core_sum", body, [stacks[0]] + gotten, outs, after)


def plane_swaps(parts, groups, count):
    masks = masks_of(groups["plane"])[1:]
    return [parts[0]] + [swap(part, mask, count) for mask, part in zip(masks, parts[1:])]


def plane_stage(parts, groups, count, after=()):
    def body(ins, outs):
        for z in range(ins[0].shape[0]):
            total = ins[0][z]
            for ref in ins[1:]:
                total = total + ref[z].astype(F32)
            outs[0][z] = total

    outs = [jax.ShapeDtypeStruct(parts[0].shape, F32)]
    return adder("plane_sum", body, plane_swaps(parts, groups, count), outs, after)[0]


def plane_stage_z(parts, groups, count, after=()):
    def body(ins, outs):
        for z, out_ref in enumerate(outs):
            total = ins[0][z]
            for ref in ins[1:]:
                total = total + ref[z].astype(F32)
            out_ref[...] = total.astype(out_ref.dtype)

    many, rows, width = parts[0].shape
    outs = [jax.ShapeDtypeStruct((rows, width), F32 if z == 0 else LOW) for z in range(many)]
    return adder("plane_sum", body, plane_swaps(parts, groups, count), outs, after)


def z_stage(parts, groups, count):
    own = parts[0]
    for mask, part in zip(masks_of(groups["z"])[1:], parts[1:]):
        own = own + swap(part, mask, count).astype(F32)
    return own


def z_scatter(total, groups, count):
    if not groups["z"]:
        return total[0]
    return lax.psum_scatter(
        total, AXES, scatter_dimension=0, axis_index_groups=teams(groups["z"], count)
    )


def product(left, right):
    return lax.dot_general(left, right, (((1,), (0,)), ((), ())), preferred_element_type=F32)


def outer(left, right):
    return lax.dot_general(left, right, (((1,), (1,)), ((), ())), preferred_element_type=F32)


def gelu_both(value):
    scale = math.sqrt(2.0 / math.pi)
    square = value * value
    share = 0.5 + 0.5 * jnp.tanh(value * (scale + scale * 0.044715 * square))
    result = value * share
    slope = share + result * (1.0 - share) * (2.0 * scale + 6.0 * scale * 0.044715 * square)
    return result, slope


def columns(height, tile=TILE):
    return pl.BlockSpec((height, tile), lambda i: (0, i))


def whole(*shape):
    return pl.BlockSpec(shape, lambda i: (0,) * len(shape))


def once(*shape):
    return pl.BlockSpec(shape, lambda i: (0,) * len(shape), pipeline_mode=pl.Buffered(1))


def shaped(kind, *shape):
    return jax.ShapeDtypeStruct(shape, kind)


def pieces_of(width):
    return [(a, a + 256) for a in range(0, width, 256)]


def run(name, kernel, batch, in_specs, out_specs, out_shape, scratch, flops, *args, tile=TILE):
    moved = sum(a.size * a.dtype.itemsize for a in args)
    moved += sum(math.prod(o.shape) * o.dtype.itemsize for o in out_shape)
    return pl.pallas_call(
        kernel,
        grid=(batch // tile,),
        in_specs=in_specs,
        out_specs=out_specs,
        out_shape=out_shape,
        scratch_shapes=scratch,
        compiler_params=PARAMS,
        cost_estimate=pl.CostEstimate(flops=flops, bytes_accessed=moved, transcendentals=0),
        name=name,
    )(*args)


def first_step():
    return pl.when(pl.program_id(0) == 0)


def last_step():
    return pl.when(pl.program_id(0) == pl.num_programs(0) - 1)


def turn(out_ref, matrix_ref, tail_ref=None, edge_ref=None):
    for a, b in pieces_of(H):
        out_ref[a:b, :H] = matrix_ref[:, a:b].T
    if tail_ref is not None:
        out_ref[:H, H:] = tail_ref[...].T
    if edge_ref is not None:
        out_ref[H:, :] = edge_ref[...]


def straight(out_ref, matrix_ref, tail_ref, edge_ref=None):
    out_ref[:H, :H] = matrix_ref[...]
    row = lax.broadcasted_iota(jnp.int32, (TALL - H, H), 0)
    tail = tail_ref[: TALL - H, :].astype(F32)
    out_ref[H:, :H] = jnp.where(row < EXTRA, tail, 0.0).astype(LOW)
    if edge_ref is not None:
        lane = lax.broadcasted_iota(jnp.int32, (TALL - H, WIDE), 1)
        edge = jnp.where(lane < D, edge_ref[...].astype(F32), 0.0)
        edge = jnp.concatenate([edge, jnp.zeros((LANES - (TALL - H), WIDE), F32)])
        out_ref[:, H:] = edge.T[:TALL].astype(LOW)


def widen(out_ref, value_ref):
    @first_step()
    def _():
        out_ref[TALL:] = jnp.zeros((WIDE - TALL, out_ref.shape[1]), LOW)

    out_ref[:TALL] = value_ref[...]


class Spread:
    def __init__(self, groups, rows, count, parts=1, below=False, by_z=False):
        self.groups, self.by_z = groups, by_z
        self.masks = halves(groups)
        self.kinds = kinds_of(groups)
        self.rows, self.count, self.parts, self.below = rows, count, parts, below
        self.direct = rows % 16 == 0

    def shapes(self):
        if not self.direct:
            return [shaped(F32, TALL, H)] * self.parts
        height = self.rows * self.parts + (AUX_ROWS if self.below else 0)
        outs = [shaped(kind, len(row), height, H) for row, kind in zip(self.masks, self.kinds)]
        overs = 0 if self.below else self.parts
        return outs + [shaped(F32, self.count, 8, H)] * overs

    def specs(self):
        return [whole(*s.shape) for s in self.shapes()]

    def write(self, acc_refs, index_ref, out_refs, over_refs=None):
        if not self.direct:
            for acc_ref, ref in zip(acc_refs, out_refs):
                ref[...] = acc_ref[...]
            return
        rows = self.rows
        for ref, row, kind in zip(out_refs, self.masks, self.kinds):
            for j, mask in enumerate(row):
                at = owner(index_ref[0], mask, self.groups, self.by_z)
                start = pl.multiple_of(at * rows, rows)
                for i, acc_ref in enumerate(acc_refs):
                    block = acc_ref[pl.ds(start, rows), :]
                    ref[j, i * rows : (i + 1) * rows] = block.astype(kind)
                if self.below:
                    mine = acc_ref[pl.ds(pl.multiple_of(start + rows, 8), 8), :]
                    parts = [mine[:SPILL_ROWS]] + [v[at][:SPILL_ROWS] for v in over_refs]
                    parts.append(jnp.zeros((AUX_ROWS - MISC_ROW, H), F32))
                    ref[j, rows:] = jnp.concatenate(parts).astype(kind)
        if not self.below:
            for acc_ref, ref in zip(acc_refs, out_refs[len(self.masks) :]):
                for k in range(self.count):
                    ref[k] = acc_ref[(k + 1) * rows : (k + 1) * rows + 8, :]

    def finish(self, outs, index, overs=None):
        if self.direct:
            return list(outs)
        rows, count = self.rows, self.count
        blocks = [grad[:H].reshape(count, rows, H) for grad in outs]
        own = [
            jnp.stack([grad[(k + 1) * rows : (k + 1) * rows + 8] for k in range(count)])
            for grad in outs
        ]
        if self.below:
            blocks += [v[:, :SPILL_ROWS] for v in own + list(overs)]
            blocks.append(jnp.zeros((count, AUX_ROWS - MISC_ROW, H), F32))
        stacks = split(
            index, jnp.concatenate(blocks, axis=1), self.masks, self.kinds, self.groups, self.by_z
        )
        stacks = list(stacks)
        return stacks if self.below else stacks + own


ANY = pl.BlockSpec(memory_space=pl.ANY)
REST = TALL - H


def forward_cross(features, one, two):
    batch = features.shape[1]

    def kernel(f_ref, *refs):
        x_ref, mixer_one_ref, mixer_two_ref, one_ref, two_ref = refs[6:11]
        turned_one, turned_two, wide_ref = refs[11:]

        @first_step()
        def _():
            turn(turned_one, *refs[:3])
            turn(turned_two, *refs[3:6])

        x_ref[:H] = f_ref[:H]
        last = f_ref[H:].astype(F32)
        last = jnp.concatenate([last, jnp.ones((1, TILE), F32), jnp.zeros((TALL - D - 1, TILE), F32)])
        x_ref[H:] = last.astype(LOW)
        widen(wide_ref, x_ref)
        layers = []
        for a, b in [(0, TILE)]:
            mixer = product(turned_one[...], wide_ref[:, a:b])
            mixer_one_ref[:, a:b] = mixer.astype(LOW)
            part = x_ref[:, a:b].astype(F32)
            layer = part * mixer + part
            layers.append(layer)
            one_ref[:, a:b] = layer.astype(LOW)
        wide_ref[:TALL] = one_ref[...]
        for (a, b), layer in zip([(0, TILE)], layers):
            mixer = product(turned_two[...], wide_ref[:, a:b])
            mixer_two_ref[:, a:b] = mixer.astype(LOW)
            two_ref[:, a:b] = (x_ref[:, a:b].astype(F32) * mixer + layer).astype(LOW)

    return run(
        "forward_cross",
        kernel,
        batch,
        [columns(D)] + [once(H, H), once(LANES, H), once(REST, WIDE)] * 2,
        [columns(TALL)] * 5,
        [shaped(LOW, TALL, batch)] * 5,
        [pltpu.VMEM((TALL, WIDE), LOW)] * 2 + [pltpu.VMEM((WIDE, TILE), LOW)],
        4 * batch * TALL * TALL,
        features, *one, *two,
    )


def deep(spread, index, layer_low, examples, matrix_one, tail, matrix, lines, inverse):
    batch = layer_low.shape[1]
    days = inverse.shape[0]

    def kernel(k_ref, l_ref, x_ref, w_one_ref, t_ref, w_ref, n_ref, i_ref, *refs):
        logit_ref, back_ref, line_ref, sum_ref = refs[:4]
        out_refs = refs[4:-8]
        turned_one, turned, acc_ref, hidden_ref, slope_ref, low_ref, part_ref, wide_ref = refs[-8:]

        @first_step()
        def _():
            turn(turned_one, w_one_ref, t_ref)
            turn(turned, w_ref)
            acc_ref[...] = jnp.zeros_like(acc_ref)
            sum_ref[...] = jnp.zeros_like(sum_ref)
            part_ref[...] = jnp.zeros_like(part_ref)
            row = lax.broadcasted_iota(jnp.int32, (REST, TILE), 0)
            hidden_ref[H:] = jnp.where(row == 0, 1.0, 0.0).astype(LOW)

        widen(wide_ref, l_ref)
        for a, b in pieces_of(TILE):
            hidden, slope = gelu_both(product(turned_one[...], wide_ref[:, a:b]))
            hidden_ref[:H, a:b] = hidden.astype(LOW)
            slope_ref[:, a:b] = slope
        head = n_ref[:, 1:2]
        for a, b in pieces_of(TILE):
            two, slope = gelu_both(product(turned[...], hidden_ref[:H, a:b]) + n_ref[:, 0:1])
            two = two.astype(LOW).astype(F32)
            logits = n_ref[0:1, 2:3] + jnp.sum(two * head, axis=0, keepdims=True)
            label = x_ref[0:1, a:b]
            day = x_ref[1:2, a:b].astype(jnp.int32)
            row = lax.broadcasted_iota(jnp.int32, (days, b - a), 0)
            weight = jnp.sum(jnp.where(row == day, i_ref[:, 0:1], 0.0), axis=0, keepdims=True)
            decay = jnp.exp(-jnp.abs(logits))
            entropy = jnp.maximum(logits, 0.0) + jnp.log1p(decay) - label * logits
            chance = jnp.where(logits >= 0.0, 1.0, decay) / (1.0 + decay)
            logit_grad = (chance - label) * weight
            logit_ref[:, a:b] = logits
            sum_ref[0:1, a:b] += logit_grad
            sum_ref[1:2, a:b] += entropy * weight
            low_ref[:, a:b] = ((logit_grad * head) * slope).astype(LOW)
            one = logit_grad * two
            part = one[:, :LANES]
            for at in range(LANES, b - a, LANES):
                part = part + one[:, at : at + LANES]
            part_ref[...] += part
        for a, b in pieces_of(TILE):
            back_ref[:, a:b] = (product(w_ref[...], low_ref[:, a:b]) * slope_ref[:, a:b]).astype(LOW)
        for a, b in pieces_of(H):
            acc_ref[:, a:b] += outer(hidden_ref[...], low_ref[a:b])

        @last_step()
        def _():
            line_ref[0:8] = jnp.broadcast_to(
                jnp.sum(part_ref[...].T, axis=0, keepdims=True), (8, H)
            )
            line_ref[8:16] = acc_ref[H : H + 8]
            spread.write([acc_ref], k_ref, out_refs)

    return run(
        "deep",
        kernel,
        batch,
        [
            SMEM,
            columns(TALL),
            columns(2),
            once(H, H),
            once(LANES, H),
            once(H, H),
            whole(H, LANES),
            whole(days, LANES),
        ],
        [columns(1), columns(H), whole(16, H), whole(8, TILE)] + spread.specs(),
        [
            shaped(F32, 1, batch),
            shaped(LOW, H, batch),
            shaped(F32, 16, H),
            shaped(F32, 8, TILE),
        ]
        + spread.shapes(),
        [
            pltpu.VMEM((H, WIDE), LOW),
            pltpu.VMEM((H, H), LOW),
            pltpu.VMEM((TALL, H), F32),
            pltpu.VMEM((TALL, TILE), LOW),
            pltpu.VMEM((H, TILE), F32),
            pltpu.VMEM((H, TILE), LOW),
            pltpu.VMEM((H, LANES), F32),
            pltpu.VMEM((WIDE, TILE), LOW),
        ],
        8 * batch * H * H,
        index, layer_low, examples, matrix_one, tail, matrix, lines, inverse,
    )


def back_deep(spread, index, grad_low, layer_low, features, matrix, tail, after):
    batch = features.shape[1]

    def kernel(k_ref, g_ref, l_ref, x_ref, w_ref, t_ref, *refs):
        refs = refs[len(after) :]
        layer_ref, mixer_ref, line_ref = refs[:3]
        out_refs = refs[3:-2]
        held, acc_ref = refs[-2:]

        @first_step()
        def _():
            straight(held, w_ref, t_ref)
            acc_ref[...] = jnp.zeros_like(acc_ref)

        for a, b in pieces_of(TILE):
            layer = product(held[...], g_ref[:, a:b])
            layer_ref[:, a:b] = layer
            mixer_ref[:, a:b] = (layer * x_ref[:, a:b].astype(F32)).astype(LOW)
        for a, b in pieces_of(H):
            acc_ref[:, a:b] += outer(l_ref[...], g_ref[a:b])

        @last_step()
        def _():
            line_ref[...] = acc_ref[H:]
            spread.write([acc_ref], k_ref, out_refs)

    return run(
        "back_deep",
        kernel,
        batch,
        [SMEM, columns(H), columns(TALL), columns(TALL), once(H, H), once(LANES, H)]
        + [ANY] * len(after),
        [columns(TALL), columns(TALL), whole(REST, H)] + spread.specs(),
        [shaped(F32, TALL, batch), shaped(LOW, TALL, batch), shaped(F32, REST, H)]
        + spread.shapes(),
        [pltpu.VMEM((TALL, H), LOW), pltpu.VMEM((TALL, H), F32)],
        4 * batch * TALL * H,
        index, grad_low, layer_low, features, matrix, tail, *after,
    )


def back_two(
    spread, index, mixer_low, layer_low, layer_grad, features, mixer_one, mixer_two, matrix, tail,
    edge, lines, after,
):
    batch = features.shape[1]

    def kernel(k_ref, g_ref, l_ref, d_ref, x_ref, one_ref, two_ref, w_ref, t_ref, e_ref, *refs):
        top_ref, deep_ref, sums_ref = refs[:3]
        refs = refs[3 + len(after) :]
        part_ref, mixer_ref, vector_ref = refs[:3]
        out_refs = refs[3:-6]
        held, acc_ref, wide_ref, sum_ref, side_ref, next_side_ref = refs[-6:]

        @first_step()
        def _():
            straight(held, w_ref, t_ref, e_ref)
            acc_ref[...] = jnp.zeros_like(acc_ref)
            side_ref[...] = jnp.zeros_like(side_ref)
            next_side_ref[...] = jnp.zeros_like(next_side_ref)
            sum_ref[...] = jnp.zeros_like(sum_ref)

        widen(wide_ref, g_ref)
        for a, b in pieces_of(TILE):
            above = d_ref[:, a:b]
            layer = product(held[...], wide_ref[:, a:b]) + above
            mixer = (layer * x_ref[:, a:b].astype(F32)).astype(LOW)
            mixer_ref[:, a:b] = mixer
            mixer = mixer[:H].astype(F32)
            total = mixer[:, :LANES]
            for at in range(LANES, b - a, LANES):
                total = total + mixer[:, at : at + LANES]
            sum_ref[...] += total
            part = above * two_ref[:, a:b].astype(F32)
            part = part + layer * (one_ref[:, a:b].astype(F32) + 1.0)
            part_ref[:, a:b] = part.astype(LOW)
        for a, b in pieces_of(H):
            acc_ref[:, a:b] += outer(l_ref[...], g_ref[a:b])
        side_ref[...] += outer(g_ref[H:], l_ref[...])
        next_side_ref[...] += outer(mixer_ref[H:], x_ref[...])

        @last_step()
        def _():
            vector_ref[...] = jnp.zeros_like(vector_ref)
            vector_ref[0:1, :H] = jnp.sum(sum_ref[...].T, axis=0, keepdims=True)
            vector_ref[1:2, :H] = acc_ref[D : D + 1]
            vector_ref[2:3, :H] = deep_ref[EXTRA : EXTRA + 1]
            vector_ref[3:4, :H] = top_ref[8:9]
            vector_ref[4:5, :H] = top_ref[0:1]
            vector_ref[5:8, :TALL] = next_side_ref[:EXTRA]
            vector_ref[8:11, :TALL] = side_ref[:EXTRA]
            lane = lax.broadcasted_iota(jnp.int32, (1, LANES), 1)
            bias = jnp.sum(sums_ref[0:1], axis=1, keepdims=True)
            loss = jnp.sum(sums_ref[1:2], axis=1, keepdims=True)
            vector_ref[11:12, :LANES] = jnp.where(lane == 0, bias, jnp.where(lane == 1, loss, 0.0))
            spread.write([acc_ref], k_ref, out_refs)

    return run(
        "back_two",
        kernel,
        batch,
        [SMEM]
        + [columns(TALL)] * 6
        + [once(H, H), once(LANES, H), once(REST, WIDE)]
        + [whole(*v.shape) for v in lines]
        + [ANY] * len(after),
        [columns(TALL), columns(TALL)]
        + [whole(16, WIDE)]
        + spread.specs(),
        [
            shaped(LOW, TALL, batch),
            shaped(LOW, TALL, batch),
            shaped(F32, 16, WIDE),
        ]
        + spread.shapes(),
        [
            pltpu.VMEM((TALL, WIDE), LOW),
            pltpu.VMEM((TALL, H), F32),
            pltpu.VMEM((WIDE, TILE), LOW),
            pltpu.VMEM((H, LANES), F32),
            pltpu.VMEM((REST, TALL), F32),
            pltpu.VMEM((REST, TALL), F32),
        ],
        4 * batch * TALL * TALL,
        index, mixer_low, layer_low, layer_grad, features, mixer_one, mixer_two, matrix, tail,
        edge, *lines, *after,
    )


def grad_one(spread, index, mixer_low, features, overs, after):
    batch = features.shape[1]

    def kernel(k_ref, g_ref, x_ref, *refs):
        over_refs = refs[: len(overs)]
        out_refs = refs[len(overs) + len(after) : -1]
        acc_ref = refs[-1]

        @first_step()
        def _():
            acc_ref[...] = jnp.zeros_like(acc_ref)

        for a, b in pieces_of(H):
            acc_ref[:, a:b] += outer(x_ref[...], g_ref[a:b])

        @last_step()
        def _():
            spread.write([acc_ref], k_ref, out_refs, over_refs)

    return run(
        "grad_one",
        kernel,
        batch,
        [SMEM, columns(TALL), columns(TALL)]
        + [once(*v.shape) for v in overs]
        + [ANY] * len(after),
        spread.specs(),
        spread.shapes(),
        [pltpu.VMEM((TALL, H), F32)],
        2 * batch * TALL * TALL,
        index, mixer_low, features, *overs, *after,
    )


def back_one(mixer_low, part, matrix, tail, edge, after):
    batch = part.shape[1]

    def kernel(g_ref, p_ref, w_ref, t_ref, e_ref, *refs):
        out_ref, held, wide_ref = refs[len(after) :]

        @first_step()
        def _():
            straight(held, w_ref, t_ref, e_ref)

        widen(wide_ref, g_ref)
        for a, b in [(0, TILE)]:
            value = p_ref[:, a:b].astype(F32) + product(held[...], wide_ref[:, a:b])
            out_ref[:H, a:b] = value[:H]
            out_ref[H:, a:b] = value[H:D]

    return run(
        "back_one",
        kernel,
        batch,
        [columns(TALL), columns(TALL), whole(H, H), whole(LANES, H), whole(REST, WIDE)]
        + [ANY] * len(after),
        [columns(D)],
        [shaped(F32, D, batch)],
        [pltpu.VMEM((TALL, WIDE), LOW), pltpu.VMEM((WIDE, TILE), LOW)],
        2 * batch * TALL * TALL,
        mixer_low, part, matrix, tail, edge, *after,
    )[0]


def local(groups, features, labels, days, master, moment_one, moment_two):
    count = lax.axis_size(AXES)
    index = lax.axis_index(AXES)
    slot = index[None].astype(jnp.int32)
    rows = H // count
    starts = starts_of(count)
    sizes = piece_sizes(count)
    wide_piece = sizes[1]
    piece = [master[a : a + l] for a, l in zip(starts, sizes)]
    block_one = to_block(piece[0], index, D, rows, count)
    block_two = to_block(piece[2], index, D, rows, count)
    block_deep = to_block(piece[4], index, H, rows, count)

    day_hot = (days[:, None] == jnp.arange(DAYS, dtype=jnp.int32)[None, :]).astype(F32)
    own_counts = jnp.sum(day_hot, axis=0)
    counts_high = jnp.floor(own_counts / 64.0)
    counts_low = own_counts - 64.0 * counts_high

    def spill_side(block):
        side = block[rows:, H:].T
        return jnp.pad(side, ((0, 0), (0, rows - SPILL_ROWS)))

    misc = [
        piece[5],
        piece[7],
        piece[8],
        block_one[:rows, H:].T,
        block_two[:rows, H:].T,
        spill_side(block_one),
        spill_side(block_two),
        piece[1],
        piece[3],
        piece[9],
        counts_high,
        counts_low,
    ]
    misc = jnp.concatenate([part.reshape(-1) for part in misc])
    misc = jnp.pad(misc, (0, (AUX_ROWS - MISC_ROW) * H - misc.shape[0])).reshape(-1, H)
    first = jnp.concatenate(
        [
            block_one[:rows, :H],
            block_two[:rows, :H],
            block_one[rows:, :H],
            block_two[rows:, :H],
            block_deep[rows:],
            misc,
        ]
    ).astype(LOW)
    stacks_cross = gather(first, groups, count)
    rest = jnp.concatenate([block_deep[:rows], piece[6].reshape(rows, H)]).astype(LOW)
    crossed = [value for value, _ in stacks_cross[3:5]]
    stacks_rest = gather(rest, groups, count, direct=True, after=crossed)
    examples = jnp.stack([labels.astype(F32), days.astype(F32)])

    matrix_one, matrix_two, aux = place(slot, stacks_cross, rows, count, [0, SPILL_ROWS])
    matrix_deep, matrix_top = place(slot, stacks_rest, rows, count, [2 * SPILL_ROWS, None], aux)

    line = aux[:, MISC_ROW]
    at = UNIT_LINES * rows
    units = line[:, :at].reshape(count, UNIT_LINES, rows).transpose(1, 0, 2).reshape(UNIT_LINES, H)
    biases = line[:, at : at + 2 * wide_piece].reshape(count, 2, wide_piece)
    biases = biases.transpose(1, 0, 2).reshape(2, count * wide_piece)
    at += 2 * wide_piece
    head_bias = line[0, at]
    both_counts = jnp.sum(line[:, at + 1 : at + 1 + 2 * DAYS].astype(F32), axis=0)
    counts = 64.0 * both_counts[:DAYS] + both_counts[DAYS:]
    inverse = jnp.broadcast_to((1.0 / counts)[:, None], (DAYS, LANES))
    sides = jnp.pad(units[3:9], ((0, 0), (0, LANES))) + jnp.pad(
        units[9:15], ((0, 0), (rows, LANES - rows))
    )

    def tail_of(at, bias):
        return jnp.concatenate(
            [aux[count - 1, at : at + EXTRA], bias[None, :H], jnp.zeros((LANES - EXTRA - 1, H), LOW)]
        )

    def edge_of(side, bias):
        lane = lax.broadcasted_iota(jnp.int32, side.shape, 1)
        side = jnp.where(lane == D, bias[H:D, None], side)
        return jnp.pad(side, ((0, TALL - H - EXTRA), (0, 0)))

    tail_one, edge_one = tail_of(0, biases[0]), edge_of(sides[:3], biases[0])
    tail_two, edge_two = tail_of(SPILL_ROWS, biases[1]), edge_of(sides[3:], biases[1])
    tail_deep = tail_of(2 * SPILL_ROWS, units[0])
    lines = jnp.concatenate(
        [units[1:3], jnp.full((1, H), head_bias), jnp.zeros((LANES - 3, H), LOW)]
    )
    lines = lines.astype(F32).T
    spread = Spread(groups, rows, count, by_z=True)
    spread_last = Spread(groups, rows, count, below=True)

    wide_features, mixer_one, mixer_two, low_one, low_two = forward_cross(
        features.T, (matrix_one, tail_one, edge_one), (matrix_two, tail_two, edge_two)
    )
    logits, pre_one_low, top_lines, sums, *outs = deep(
        spread, slot, low_two, examples, matrix_deep, tail_deep, matrix_top, lines, inverse
    )
    *top_stacks, _ = spread.finish(outs, slot)
    layer_grad, mixer_two_low, deep_lines, *outs = back_deep(
        spread, slot, pre_one_low, low_two, wide_features, matrix_deep, tail_deep, []
    )
    *deep_stacks, deep_over = spread.finish(outs, slot)
    top_plane = core_stage(top_stacks, groups, count, [mixer_two_low])
    part, mixer_one_low, vectors, *outs = back_two(
        spread, slot, mixer_two_low, low_one, layer_grad, wide_features, mixer_one, mixer_two,
        matrix_two, tail_two, edge_two, (top_lines, deep_lines, sums), top_plane[1:],
    )
    *two_stacks, two_over = spread.finish(outs, slot)
    top_total = plane_stage(top_plane, groups, count, [mixer_one_low])
    deep_plane = core_stage(deep_stacks, groups, count, [mixer_one_low])
    overs = (two_over, deep_over)
    outs = grad_one(
        spread_last, slot, mixer_one_low, wide_features, overs,
        deep_plane[1:] + [top_total],
    )
    last_stacks = spread_last.finish(outs, slot, overs)
    deep_total = plane_stage(deep_plane, groups, count, last_stacks[:1])
    two_plane = core_stage(two_stacks, groups, count, last_stacks[:1])
    last_plane = core_stage(last_stacks, groups, count)
    feature_grad = back_one(
        mixer_one_low, part, matrix_one, tail_one, edge_one,
        last_plane[1:] + two_plane[1:] + [deep_total],
    )

    vectors = jnp.sum(lax.all_gather(vectors, AXES, axis=0), axis=0)
    loss = vectors[11, 1]
    side_sums = vectors[5:11]

    own_top = z_scatter(top_total, groups, count)
    own_deep = z_scatter(deep_total, groups, count)
    two_total = plane_stage(two_plane, groups, count, [feature_grad])
    own_two = z_scatter(two_total, groups, count)
    own_last = z_stage(plane_stage_z(last_plane, groups, count, [feature_grad]), groups, count)
    own_one = own_last[:rows]
    spills = own_last[rows : rows + MISC_ROW]
    row = lax.broadcasted_iota(jnp.int32, spills.shape, 0)
    beyond = (row % SPILL_ROWS >= EXTRA) & (index == count - 1)
    spills = jnp.where(beyond, 0.0, spills)
    wide_biases = jnp.concatenate(
        [vectors[:2, :H], side_sums[:, D].reshape(2, EXTRA)], axis=1
    )
    wide_biases = jnp.pad(wide_biases, ((0, 0), (0, count * wide_piece - D)))
    wide_biases = lax.dynamic_slice(wide_biases, (0, index * wide_piece), (2, wide_piece))
    units = lax.dynamic_slice(vectors[2:5], (0, index * rows), (3, rows))
    side_sums = jnp.pad(side_sums[:, :D], ((0, 0), (0, WIDE - D)))
    side_sums = lax.dynamic_slice(side_sums, (0, index * rows), (6, rows + SPILL_ROWS)).T

    def whole_block(main, number):
        low = number * SPILL_ROWS
        body = jnp.concatenate([main, spills[low : low + SPILL_ROWS]])
        if number == 2:
            return body
        return jnp.concatenate([body, side_sums[:, 3 * number : 3 * number + 3]], axis=1)

    flat_grad = jnp.concatenate(
        [
            from_block(whole_block(own_one, 0), index, sizes[0], rows, count),
            wide_biases[0],
            from_block(whole_block(own_two, 1), index, sizes[2], rows, count),
            wide_biases[1],
            from_block(whole_block(own_deep, 2), index, sizes[4], rows, count),
            units[0],
            own_top.reshape(-1),
            units[1],
            units[2],
            jnp.where(index == 0, vectors[11, :1], 0.0),
        ]
    )
    new_moment_one = 0.9 * moment_one + 0.1 * flat_grad
    new_moment_two = 0.999 * moment_two + 0.001 * flat_grad * flat_grad
    corrected_one = new_moment_one / (1.0 - 0.9**STEP)
    corrected_two = new_moment_two / (1.0 - 0.999**STEP)
    new_master = master - 0.03 * (corrected_one / (jnp.sqrt(corrected_two) + 1e-08) + 0.01 * master)
    new_bias = jnp.concatenate(
        [new_master[starts[i] : starts[i] + sizes[i]] for i in (1, 3, 5, 7, 9)]
    )
    return (
        logits.reshape(-1),
        loss,
        feature_grad.T,
        flat_grad,
        new_moment_one,
        new_moment_two,
        new_master,
        new_bias,
    )


def solution(mesh):
    line = P(AXES)
    table = P(AXES, None)
    groups = bit_groups(mesh)
    return jax.shard_map(
        functools.partial(local, groups),
        mesh=mesh,
        in_specs=(table, line, line, line, line, line),
        out_specs=(line, P(), table, line, line, line, line, line),
        check_vma=False,
    )
```

```python
import functools
import math

import jax
import jax.numpy as jnp
from jax import lax
from jax.experimental import pallas as pl
from jax.experimental.pallas import tpu as pltpu
from jax.sharding import PartitionSpec as P

D = 1027
H = 1024
DAYS = 24
STEP = 10
AXES = ("dp", "cores")
EXTRA = D - H
LANES = 128
WIDE = H + LANES
AUX_ROWS = 16
SPILL_ROWS = 4
MISC_ROW = 12
UNIT_LINES = 15
TILE = 512
TALL = H + 16
MIB = 1024 * 1024
F32 = jnp.float32
LOW = jnp.bfloat16
SMEM = pl.BlockSpec(memory_space=pltpu.SMEM)
VMEM = pl.BlockSpec(memory_space=pltpu.VMEM)
PARAMS = pltpu.CompilerParams(vmem_limit_bytes=56 * MIB)


def shapes():
    return [(D, D), (D,), (D, D), (D,), (D, H), (H,), (H, H), (H,), (H,), (1,)]


def piece_sizes(count):
    return [(math.prod(shape) + count - 1) // count for shape in shapes()[:-1]] + [1]


def starts_of(count):
    starts = []
    position = 0
    for piece in piece_sizes(count):
        starts.append(position)
        position += piece
    return starts


def to_block(piece, index, width, rows, count):
    excess = piece.shape[0] - rows * width
    size = (rows + SPILL_ROWS) * width
    lead = (count - 1) * excess
    padded = jnp.pad(piece, (lead, max(0, size - piece.shape[0])))
    line = lax.dynamic_slice(padded, (lead - index * excess,), (size,))
    return line.reshape(rows + SPILL_ROWS, width)


def from_block(block, index, piece, rows, count):
    width = block.shape[1]
    excess = piece - rows * width
    last = (count - 1) * excess
    line = jnp.pad(block.reshape(-1), (0, max(0, last + piece - block.size)))
    return lax.dynamic_slice(line, (index * excess,), (piece,))


def bit_groups(mesh):
    devices = mesh.devices.reshape(-1)
    groups = {"z": [], "plane": [], "core": []}
    bit = 1
    while bit < devices.size:
        here = getattr(devices[0], "coords", None)
        there = getattr(devices[bit], "coords", None)
        if here is None or there is None:
            name = "core" if bit == 1 else "plane" if bit <= 4 else "z"
        elif tuple(here) == tuple(there):
            name = "core"
        elif here[2] != there[2]:
            name = "z"
        else:
            name = "plane"
        groups[name].append(bit)
        bit *= 2
    return groups


def masks_of(bits):
    masks = [0]
    for bit in bits:
        masks = masks + [mask | bit for mask in masks]
    return masks


def teams(bits, count):
    masks = masks_of(bits)
    return [[k | mask for mask in masks] for k in range(count) if not k & masks[-1]]


def owner(index, mask, groups, fixed):
    for name in fixed:
        index = jnp.bitwise_and(index, ~masks_of(groups[name])[-1])
    return jnp.bitwise_xor(index, mask)


def swap(value, mask, count):
    return lax.ppermute(value, AXES, [(k, k ^ mask) for k in range(count)])


def join(parts, after):
    def kernel(*refs):
        for j in range(len(parts)):
            refs[-1][j] = refs[j][...]

    return pl.pallas_call(
        kernel,
        out_shape=jax.ShapeDtypeStruct((len(parts),) + parts[0].shape, parts[0].dtype),
        in_specs=[VMEM] * len(parts) + [pl.BlockSpec(memory_space=pl.ANY)] * len(after),
        out_specs=VMEM,
        compiler_params=PARAMS,
        name="join",
    )(*parts, *after)


def gather(block, groups, count, direct=False, after=()):
    z_masks = masks_of(groups["z"])
    core_masks = masks_of(groups["core"])
    line = [block] + [swap(block, mask, count) for mask in z_masks[1:]]
    line = join(line, after) if after else jnp.stack(line)
    plane = [(line, z_masks)]
    if len(groups["plane"]) == 2 and len(z_masks) > 1 and not direct:
        one, two = groups["plane"]
        half = len(z_masks) // 2
        by_one = swap(line, one, count)
        by_two = swap(line, two, count)
        plane.append((by_one, [one ^ z for z in z_masks]))
        plane.append((by_two, [two ^ z for z in z_masks]))
        both = one ^ two
        plane.append((swap(by_one[:half], two, count), [both ^ z for z in z_masks[:half]]))
        plane.append((swap(by_two[half:], one, count), [both ^ z for z in z_masks[half:]]))
    else:
        for mask in masks_of(groups["plane"])[1:]:
            plane.append((swap(line, mask, count), [mask ^ z for z in z_masks]))
    result = list(plane)
    for core in core_masks[1:]:
        result += [(swap(value, core, count), [core ^ m for m in row]) for value, row in plane]
    return result


def place(index, stacks, rows, count, parts, aux=None):
    sources = [value for value, _ in stacks]
    masks = [row for _, row in stacks]
    carries = aux is None
    top = min(16, rows)

    def kernel(index_ref, *refs):
        refs = list(refs)
        aux_ref = refs.pop() if carries else refs.pop(0)
        outs = refs[len(sources) :]
        for ref, row in zip(refs, masks):
            for j, mask in enumerate(row):
                at = jnp.bitwise_xor(index_ref[0], mask)
                for i, out_ref in enumerate(outs):
                    out_ref[at] = ref[j, i * rows : (i + 1) * rows]
                if carries:
                    aux_ref[at] = ref[j, len(outs) * rows :]
        for spill_at, out_ref in zip(parts, outs):
            if spill_at is None:
                continue
            for k in range(1, count):
                spill = aux_ref[k - 1].astype(F32)[spill_at : spill_at + SPILL_ROWS]
                old = out_ref[k, :top].astype(F32)
                new = old[:SPILL_ROWS] + spill
                if top > SPILL_ROWS:
                    new = jnp.concatenate([new, old[SPILL_ROWS:]], axis=0)
                out_ref[k, :top] = new.astype(LOW)

    out_shape = [jax.ShapeDtypeStruct((count, rows, H), LOW)] * len(parts)
    if carries:
        out_shape.append(jax.ShapeDtypeStruct((count, AUX_ROWS, H), LOW))
    extra = [] if carries else [aux]
    result = pl.pallas_call(
        kernel,
        out_shape=out_shape,
        in_specs=[SMEM] + [VMEM] * (len(extra) + len(sources)),
        out_specs=[VMEM] * len(out_shape),
        compiler_params=PARAMS,
        name="place",
    )(index, *extra, *sources)
    return [value.reshape(H, H) for value in result[: len(parts)]] + list(result[len(parts) :])


def split(index, value, masks, kinds, groups, fixed):
    def kernel(index_ref, value_ref, *out_refs):
        for ref, row, kind in zip(out_refs, masks, kinds):
            for j, mask in enumerate(row):
                ref[j] = value_ref[owner(index_ref[0], mask, groups, fixed)].astype(kind)

    shape = value.shape[1:]
    return pl.pallas_call(
        kernel,
        out_shape=[
            jax.ShapeDtypeStruct((len(row),) + shape, kind) for row, kind in zip(masks, kinds)
        ],
        in_specs=[SMEM, VMEM],
        out_specs=[VMEM] * len(masks),
        compiler_params=PARAMS,
        name="split",
    )(index, value)


def halves(groups):
    z_masks, plane_masks, core_masks = (masks_of(groups[g]) for g in ("z", "plane", "core"))
    inner = [p ^ z for p in plane_masks for z in z_masks]
    return [[core ^ m for m in inner] for core in core_masks]


def kinds_of(groups):
    return [F32] + [LOW] * (len(halves(groups)) - 1)


def adder(name, body, ins, outs, after):
    def kernel(*refs):
        body(refs[: len(ins)], refs[len(ins) + len(after) :])

    result = pl.pallas_call(
        kernel,
        out_shape=outs,
        in_specs=[VMEM] * len(ins) + [pl.BlockSpec(memory_space=pl.ANY)] * len(after),
        out_specs=[VMEM] * len(outs),
        compiler_params=PARAMS,
        name=name,
    )(*ins, *after)
    return list(result)


def core_stage(stacks, groups, count, after=()):
    z_count, plane_count = len(masks_of(groups["z"])), len(masks_of(groups["plane"]))
    cores = masks_of(groups["core"])[1:]
    gotten = [swap(stack, core, count) for core, stack in zip(cores, stacks[1:])]
    shape = (z_count,) + stacks[0].shape[1:]

    def body(ins, outs):
        for p, out_ref in enumerate(outs):
            for z in range(z_count):
                total = ins[0][p * z_count + z]
                for ref in ins[1:]:
                    total = total + ref[p * z_count + z].astype(F32)
                out_ref[z] = total.astype(out_ref.dtype)

    outs = [jax.ShapeDtypeStruct(shape, F32 if p == 0 else LOW) for p in range(plane_count)]
    return adder("core_sum", body, [stacks[0]] + gotten, outs, after)


def core_stage_whole(stacks, groups, count, after=()):
    z_count, plane_count = len(masks_of(groups["z"])), len(masks_of(groups["plane"]))
    cores = masks_of(groups["core"])[1:]
    gotten = [swap(stack, core, count) for core, stack in zip(cores, stacks[1:])]

    def body(ins, outs):
        for p in range(plane_count):
            for z in range(z_count):
                total = ins[0][p * z_count + z]
                for ref in ins[1:]:
                    total = total + ref[p * z_count + z].astype(F32)
                outs[0][p, z] = total.astype(LOW)

    outs = [jax.ShapeDtypeStruct((plane_count, z_count) + stacks[0].shape[1:], LOW)]
    return adder("core_sum", body, [stacks[0]] + gotten, outs, after)[0]


def team_scatter(total, bits, count):
    if not bits:
        return total[0]
    return lax.psum_scatter(
        total, AXES, scatter_dimension=0, axis_index_groups=teams(bits, count)
    )


def plane_swaps(parts, groups, count):
    masks = masks_of(groups["plane"])[1:]
    return [parts[0]] + [swap(part, mask, count) for mask, part in zip(masks, parts[1:])]


def plane_stage_z(parts, groups, count, after=()):
    def body(ins, outs):
        for z, out_ref in enumerate(outs):
            total = ins[0][z]
            for ref in ins[1:]:
                total = total + ref[z].astype(F32)
            out_ref[...] = total.astype(out_ref.dtype)

    many, rows, width = parts[0].shape
    outs = [jax.ShapeDtypeStruct((rows, width), F32 if z == 0 else LOW) for z in range(many)]
    return adder("plane_sum", body, plane_swaps(parts, groups, count), outs, after)


def z_stage(parts, groups, count):
    own = parts[0]
    for mask, part in zip(masks_of(groups["z"])[1:], parts[1:]):
        own = own + swap(part, mask, count).astype(F32)
    return own


def product(left, right):
    return lax.dot_general(left, right, (((1,), (0,)), ((), ())), preferred_element_type=F32)


def outer(left, right):
    return lax.dot_general(left, right, (((1,), (1,)), ((), ())), preferred_element_type=F32)


def gelu_both(value):
    scale = math.sqrt(2.0 / math.pi)
    square = value * value
    share = 0.5 + 0.5 * jnp.tanh(value * (scale + scale * 0.044715 * square))
    result = value * share
    slope = share + result * (1.0 - share) * (2.0 * scale + 6.0 * scale * 0.044715 * square)
    return result, slope


def columns(height, tile=TILE):
    return pl.BlockSpec((height, tile), lambda i: (0, i))


def whole(*shape):
    return pl.BlockSpec(shape, lambda i: (0,) * len(shape))


def once(*shape):
    return pl.BlockSpec(shape, lambda i: (0,) * len(shape), pipeline_mode=pl.Buffered(1))


def shaped(kind, *shape):
    return jax.ShapeDtypeStruct(shape, kind)


def pieces_of(width):
    return [(a, a + 256) for a in range(0, width, 256)]


def run(name, kernel, batch, in_specs, out_specs, out_shape, scratch, flops, *args, tile=TILE):
    moved = sum(a.size * a.dtype.itemsize for a in args)
    moved += sum(math.prod(o.shape) * o.dtype.itemsize for o in out_shape)
    return pl.pallas_call(
        kernel,
        grid=(batch // tile,),
        in_specs=in_specs,
        out_specs=out_specs,
        out_shape=out_shape,
        scratch_shapes=scratch,
        compiler_params=PARAMS,
        cost_estimate=pl.CostEstimate(flops=flops, bytes_accessed=moved, transcendentals=0),
        name=name,
    )(*args)


def first_step():
    return pl.when(pl.program_id(0) == 0)


def last_step():
    return pl.when(pl.program_id(0) == pl.num_programs(0) - 1)


def turn(out_ref, matrix_ref, tail_ref=None, edge_ref=None):
    for a, b in pieces_of(H):
        out_ref[a:b, :H] = matrix_ref[:, a:b].T
    if tail_ref is not None:
        out_ref[:H, H:] = tail_ref[...].T
    if edge_ref is not None:
        out_ref[H:, :] = edge_ref[...]


def straight(out_ref, matrix_ref, tail_ref, edge_ref=None):
    out_ref[:H, :H] = matrix_ref[...]
    row = lax.broadcasted_iota(jnp.int32, (TALL - H, H), 0)
    tail = tail_ref[: TALL - H, :].astype(F32)
    out_ref[H:, :H] = jnp.where(row < EXTRA, tail, 0.0).astype(LOW)
    if edge_ref is not None:
        lane = lax.broadcasted_iota(jnp.int32, (TALL - H, WIDE), 1)
        edge = jnp.where(lane < D, edge_ref[...].astype(F32), 0.0)
        edge = jnp.concatenate([edge, jnp.zeros((LANES - (TALL - H), WIDE), F32)])
        out_ref[:, H:] = edge.T[:TALL].astype(LOW)


def widen(out_ref, value_ref):
    @first_step()
    def _():
        out_ref[TALL:] = jnp.zeros((WIDE - TALL, out_ref.shape[1]), LOW)

    out_ref[:TALL] = value_ref[...]


class Spread:
    def __init__(self, groups, rows, count, parts=1, below=False, fixed=()):
        self.groups, self.fixed = groups, fixed
        self.masks = halves(groups)
        self.kinds = kinds_of(groups)
        self.rows, self.count, self.parts, self.below = rows, count, parts, below
        self.direct = rows % 16 == 0

    def shapes(self):
        if not self.direct:
            return [shaped(F32, TALL, H)] * self.parts
        height = self.rows * self.parts + (AUX_ROWS if self.below else 0)
        outs = [shaped(kind, len(row), height, H) for row, kind in zip(self.masks, self.kinds)]
        overs = 0 if self.below else self.parts
        return outs + [shaped(F32, self.count, 8, H)] * overs

    def specs(self):
        return [whole(*s.shape) for s in self.shapes()]

    def write(self, acc_refs, index_ref, out_refs, over_refs=None):
        if not self.direct:
            for acc_ref, ref in zip(acc_refs, out_refs):
                ref[...] = acc_ref[...]
            return
        rows = self.rows
        for ref, row, kind in zip(out_refs, self.masks, self.kinds):
            for j, mask in enumerate(row):
                at = owner(index_ref[0], mask, self.groups, self.fixed)
                start = pl.multiple_of(at * rows, rows)
                for i, acc_ref in enumerate(acc_refs):
                    block = acc_ref[pl.ds(start, rows), :]
                    ref[j, i * rows : (i + 1) * rows] = block.astype(kind)
                if self.below:
                    mine = acc_ref[pl.ds(pl.multiple_of(start + rows, 8), 8), :]
                    parts = [mine[:SPILL_ROWS]] + [v[at][:SPILL_ROWS] for v in over_refs]
                    parts.append(jnp.zeros((AUX_ROWS - MISC_ROW, H), F32))
                    ref[j, rows:] = jnp.concatenate(parts).astype(kind)
        if not self.below:
            for acc_ref, ref in zip(acc_refs, out_refs[len(self.masks) :]):
                for k in range(self.count):
                    ref[k] = acc_ref[(k + 1) * rows : (k + 1) * rows + 8, :]

    def finish(self, outs, index, overs=None):
        if self.direct:
            return list(outs)
        rows, count = self.rows, self.count
        blocks = [grad[:H].reshape(count, rows, H) for grad in outs]
        own = [
            jnp.stack([grad[(k + 1) * rows : (k + 1) * rows + 8] for k in range(count)])
            for grad in outs
        ]
        if self.below:
            blocks += [v[:, :SPILL_ROWS] for v in own + list(overs)]
            blocks.append(jnp.zeros((count, AUX_ROWS - MISC_ROW, H), F32))
        stacks = split(
            index, jnp.concatenate(blocks, axis=1), self.masks, self.kinds, self.groups, self.fixed
        )
        stacks = list(stacks)
        return stacks if self.below else stacks + own


ANY = pl.BlockSpec(memory_space=pl.ANY)
REST = TALL - H


def forward_cross(features, one, two):
    batch = features.shape[1]

    def kernel(f_ref, *refs):
        x_ref, mixer_one_ref, mixer_two_ref, one_ref, two_ref = refs[6:11]
        turned_one, turned_two, wide_ref = refs[11:]

        @first_step()
        def _():
            turn(turned_one, *refs[:3])
            turn(turned_two, *refs[3:6])

        x_ref[:H] = f_ref[:H]
        last = f_ref[H:].astype(F32)
        last = jnp.concatenate([last, jnp.ones((1, TILE), F32), jnp.zeros((TALL - D - 1, TILE), F32)])
        x_ref[H:] = last.astype(LOW)
        widen(wide_ref, x_ref)
        layers = []
        for a, b in [(0, TILE)]:
            mixer = product(turned_one[...], wide_ref[:, a:b])
            mixer_one_ref[:, a:b] = mixer.astype(LOW)
            part = x_ref[:, a:b].astype(F32)
            layer = part * mixer + part
            layers.append(layer)
            one_ref[:, a:b] = layer.astype(LOW)
        wide_ref[:TALL] = one_ref[...]
        for (a, b), layer in zip([(0, TILE)], layers):
            mixer = product(turned_two[...], wide_ref[:, a:b])
            mixer_two_ref[:, a:b] = mixer.astype(LOW)
            two_ref[:, a:b] = (x_ref[:, a:b].astype(F32) * mixer + layer).astype(LOW)

    return run(
        "forward_cross",
        kernel,
        batch,
        [columns(D)] + [once(H, H), once(LANES, H), once(REST, WIDE)] * 2,
        [columns(TALL)] * 5,
        [shaped(LOW, TALL, batch)] * 5,
        [pltpu.VMEM((TALL, WIDE), LOW)] * 2 + [pltpu.VMEM((WIDE, TILE), LOW)],
        4 * batch * TALL * TALL,
        features, *one, *two,
    )


def deep(spread, index, layer_low, examples, matrix_one, tail, matrix, lines, inverse):
    batch = layer_low.shape[1]
    days = inverse.shape[0]

    def kernel(k_ref, l_ref, x_ref, w_one_ref, t_ref, w_ref, n_ref, i_ref, *refs):
        logit_ref, back_ref, line_ref, sum_ref = refs[:4]
        out_refs = refs[4:-8]
        turned_one, turned, acc_ref, hidden_ref, slope_ref, low_ref, part_ref, wide_ref = refs[-8:]

        @first_step()
        def _():
            turn(turned_one, w_one_ref, t_ref)
            turn(turned, w_ref)
            acc_ref[...] = jnp.zeros_like(acc_ref)
            sum_ref[...] = jnp.zeros_like(sum_ref)
            part_ref[...] = jnp.zeros_like(part_ref)
            row = lax.broadcasted_iota(jnp.int32, (REST, TILE), 0)
            hidden_ref[H:] = jnp.where(row == 0, 1.0, 0.0).astype(LOW)

        widen(wide_ref, l_ref)
        for a, b in pieces_of(TILE):
            hidden, slope = gelu_both(product(turned_one[...], wide_ref[:, a:b]))
            hidden_ref[:H, a:b] = hidden.astype(LOW)
            slope_ref[:, a:b] = slope
        head = n_ref[:, 1:2]
        for a, b in pieces_of(TILE):
            two, slope = gelu_both(product(turned[...], hidden_ref[:H, a:b]) + n_ref[:, 0:1])
            two = two.astype(LOW).astype(F32)
            logits = n_ref[0:1, 2:3] + jnp.sum(two * head, axis=0, keepdims=True)
            label = x_ref[0:1, a:b]
            day = x_ref[1:2, a:b].astype(jnp.int32)
            row = lax.broadcasted_iota(jnp.int32, (days, b - a), 0)
            weight = jnp.sum(jnp.where(row == day, i_ref[:, 0:1], 0.0), axis=0, keepdims=True)
            decay = jnp.exp(-jnp.abs(logits))
            entropy = jnp.maximum(logits, 0.0) + jnp.log1p(decay) - label * logits
            chance = jnp.where(logits >= 0.0, 1.0, decay) / (1.0 + decay)
            logit_grad = (chance - label) * weight
            logit_ref[:, a:b] = logits
            sum_ref[0:1, a:b] += logit_grad
            sum_ref[1:2, a:b] += entropy * weight
            low_ref[:, a:b] = ((logit_grad * head) * slope).astype(LOW)
            one = logit_grad * two
            part = one[:, :LANES]
            for at in range(LANES, b - a, LANES):
                part = part + one[:, at : at + LANES]
            part_ref[...] += part
        for a, b in pieces_of(TILE):
            back_ref[:, a:b] = (product(w_ref[...], low_ref[:, a:b]) * slope_ref[:, a:b]).astype(LOW)
        for a, b in pieces_of(H):
            acc_ref[:, a:b] += outer(hidden_ref[...], low_ref[a:b])

        @last_step()
        def _():
            line_ref[0:8] = jnp.broadcast_to(
                jnp.sum(part_ref[...].T, axis=0, keepdims=True), (8, H)
            )
            line_ref[8:16] = acc_ref[H : H + 8]
            spread.write([acc_ref], k_ref, out_refs)

    return run(
        "deep",
        kernel,
        batch,
        [
            SMEM,
            columns(TALL),
            columns(2),
            once(H, H),
            once(LANES, H),
            once(H, H),
            whole(H, LANES),
            whole(days, LANES),
        ],
        [columns(1), columns(H), whole(16, H), whole(8, TILE)] + spread.specs(),
        [
            shaped(F32, 1, batch),
            shaped(LOW, H, batch),
            shaped(F32, 16, H),
            shaped(F32, 8, TILE),
        ]
        + spread.shapes(),
        [
            pltpu.VMEM((H, WIDE), LOW),
            pltpu.VMEM((H, H), LOW),
            pltpu.VMEM((TALL, H), F32),
            pltpu.VMEM((TALL, TILE), LOW),
            pltpu.VMEM((H, TILE), F32),
            pltpu.VMEM((H, TILE), LOW),
            pltpu.VMEM((H, LANES), F32),
            pltpu.VMEM((WIDE, TILE), LOW),
        ],
        8 * batch * H * H,
        index, layer_low, examples, matrix_one, tail, matrix, lines, inverse,
    )


def back_deep(spread, index, grad_low, layer_low, features, matrix, tail, after):
    batch = features.shape[1]

    def kernel(k_ref, g_ref, l_ref, x_ref, w_ref, t_ref, *refs):
        refs = refs[len(after) :]
        layer_ref, mixer_ref, line_ref = refs[:3]
        out_refs = refs[3:-2]
        held, acc_ref = refs[-2:]

        @first_step()
        def _():
            straight(held, w_ref, t_ref)
            acc_ref[...] = jnp.zeros_like(acc_ref)

        for a, b in pieces_of(TILE):
            layer = product(held[...], g_ref[:, a:b])
            layer_ref[:, a:b] = layer
            mixer_ref[:, a:b] = (layer * x_ref[:, a:b].astype(F32)).astype(LOW)
        for a, b in pieces_of(H):
            acc_ref[:, a:b] += outer(l_ref[...], g_ref[a:b])

        @last_step()
        def _():
            line_ref[...] = acc_ref[H:]
            spread.write([acc_ref], k_ref, out_refs)

    return run(
        "back_deep",
        kernel,
        batch,
        [SMEM, columns(H), columns(TALL), columns(TALL), once(H, H), once(LANES, H)]
        + [ANY] * len(after),
        [columns(TALL), columns(TALL), whole(REST, H)] + spread.specs(),
        [shaped(F32, TALL, batch), shaped(LOW, TALL, batch), shaped(F32, REST, H)]
        + spread.shapes(),
        [pltpu.VMEM((TALL, H), LOW), pltpu.VMEM((TALL, H), F32)],
        4 * batch * TALL * H,
        index, grad_low, layer_low, features, matrix, tail, *after,
    )


def back_two(
    spread, index, mixer_low, layer_low, layer_grad, features, mixer_one, mixer_two, matrix, tail,
    edge, lines, after,
):
    batch = features.shape[1]

    def kernel(k_ref, g_ref, l_ref, d_ref, x_ref, one_ref, two_ref, w_ref, t_ref, e_ref, *refs):
        top_ref, deep_ref, sums_ref = refs[:3]
        refs = refs[3 + len(after) :]
        part_ref, mixer_ref, vector_ref = refs[:3]
        out_refs = refs[3:-6]
        held, acc_ref, wide_ref, sum_ref, side_ref, next_side_ref = refs[-6:]

        @first_step()
        def _():
            straight(held, w_ref, t_ref, e_ref)
            acc_ref[...] = jnp.zeros_like(acc_ref)
            side_ref[...] = jnp.zeros_like(side_ref)
            next_side_ref[...] = jnp.zeros_like(next_side_ref)
            sum_ref[...] = jnp.zeros_like(sum_ref)

        widen(wide_ref, g_ref)
        for a, b in pieces_of(TILE):
            above = d_ref[:, a:b]
            layer = product(held[...], wide_ref[:, a:b]) + above
            mixer = (layer * x_ref[:, a:b].astype(F32)).astype(LOW)
            mixer_ref[:, a:b] = mixer
            mixer = mixer[:H].astype(F32)
            total = mixer[:, :LANES]
            for at in range(LANES, b - a, LANES):
                total = total + mixer[:, at : at + LANES]
            sum_ref[...] += total
            part = above * two_ref[:, a:b].astype(F32)
            part = part + layer * (one_ref[:, a:b].astype(F32) + 1.0)
            part_ref[:, a:b] = part.astype(LOW)
        for a, b in pieces_of(H):
            acc_ref[:, a:b] += outer(l_ref[...], g_ref[a:b])
        side_ref[...] += outer(g_ref[H:], l_ref[...])
        next_side_ref[...] += outer(mixer_ref[H:], x_ref[...])

        @last_step()
        def _():
            vector_ref[...] = jnp.zeros_like(vector_ref)
            vector_ref[0:1, :H] = jnp.sum(sum_ref[...].T, axis=0, keepdims=True)
            vector_ref[1:2, :H] = acc_ref[D : D + 1]
            vector_ref[2:3, :H] = deep_ref[EXTRA : EXTRA + 1]
            vector_ref[3:4, :H] = top_ref[8:9]
            vector_ref[4:5, :H] = top_ref[0:1]
            vector_ref[5:8, :TALL] = next_side_ref[:EXTRA]
            vector_ref[8:11, :TALL] = side_ref[:EXTRA]
            lane = lax.broadcasted_iota(jnp.int32, (1, LANES), 1)
            bias = jnp.sum(sums_ref[0:1], axis=1, keepdims=True)
            loss = jnp.sum(sums_ref[1:2], axis=1, keepdims=True)
            vector_ref[11:12, :LANES] = jnp.where(lane == 0, bias, jnp.where(lane == 1, loss, 0.0))
            spread.write([acc_ref], k_ref, out_refs)

    return run(
        "back_two",
        kernel,
        batch,
        [SMEM]
        + [columns(TALL)] * 6
        + [once(H, H), once(LANES, H), once(REST, WIDE)]
        + [whole(*v.shape) for v in lines]
        + [ANY] * len(after),
        [columns(TALL), columns(TALL)]
        + [whole(16, WIDE)]
        + spread.specs(),
        [
            shaped(LOW, TALL, batch),
            shaped(LOW, TALL, batch),
            shaped(F32, 16, WIDE),
        ]
        + spread.shapes(),
        [
            pltpu.VMEM((TALL, WIDE), LOW),
            pltpu.VMEM((TALL, H), F32),
            pltpu.VMEM((WIDE, TILE), LOW),
            pltpu.VMEM((H, LANES), F32),
            pltpu.VMEM((REST, TALL), F32),
            pltpu.VMEM((REST, TALL), F32),
        ],
        4 * batch * TALL * TALL,
        index, mixer_low, layer_low, layer_grad, features, mixer_one, mixer_two, matrix, tail,
        edge, *lines, *after,
    )


def grad_one(spread, index, mixer_low, features, overs, after):
    batch = features.shape[1]

    def kernel(k_ref, g_ref, x_ref, *refs):
        over_refs = refs[: len(overs)]
        out_refs = refs[len(overs) + len(after) : -1]
        acc_ref = refs[-1]

        @first_step()
        def _():
            acc_ref[...] = jnp.zeros_like(acc_ref)

        for a, b in pieces_of(H):
            acc_ref[:, a:b] += outer(x_ref[...], g_ref[a:b])

        @last_step()
        def _():
            spread.write([acc_ref], k_ref, out_refs, over_refs)

    return run(
        "grad_one",
        kernel,
        batch,
        [SMEM, columns(TALL), columns(TALL)]
        + [once(*v.shape) for v in overs]
        + [ANY] * len(after),
        spread.specs(),
        spread.shapes(),
        [pltpu.VMEM((TALL, H), F32)],
        2 * batch * TALL * TALL,
        index, mixer_low, features, *overs, *after,
    )


def back_one(mixer_low, part, matrix, tail, edge, after):
    batch = part.shape[1]

    def kernel(g_ref, p_ref, w_ref, t_ref, e_ref, *refs):
        out_ref, held, wide_ref = refs[len(after) :]

        @first_step()
        def _():
            straight(held, w_ref, t_ref, e_ref)

        widen(wide_ref, g_ref)
        for a, b in [(0, TILE)]:
            value = p_ref[:, a:b].astype(F32) + product(held[...], wide_ref[:, a:b])
            out_ref[:H, a:b] = value[:H]
            out_ref[H:, a:b] = value[H:D]

    return run(
        "back_one",
        kernel,
        batch,
        [columns(TALL), columns(TALL), whole(H, H), whole(LANES, H), whole(REST, WIDE)]
        + [ANY] * len(after),
        [columns(D)],
        [shaped(F32, D, batch)],
        [pltpu.VMEM((TALL, WIDE), LOW), pltpu.VMEM((WIDE, TILE), LOW)],
        2 * batch * TALL * TALL,
        mixer_low, part, matrix, tail, edge, *after,
    )[0]


def local(groups, features, labels, days, master, moment_one, moment_two):
    count = lax.axis_size(AXES)
    index = lax.axis_index(AXES)
    slot = index[None].astype(jnp.int32)
    rows = H // count
    starts = starts_of(count)
    sizes = piece_sizes(count)
    wide_piece = sizes[1]
    piece = [master[a : a + l] for a, l in zip(starts, sizes)]
    block_one = to_block(piece[0], index, D, rows, count)
    block_two = to_block(piece[2], index, D, rows, count)
    block_deep = to_block(piece[4], index, H, rows, count)

    day_hot = (days[:, None] == jnp.arange(DAYS, dtype=jnp.int32)[None, :]).astype(F32)
    own_counts = jnp.sum(day_hot, axis=0)
    counts_high = jnp.floor(own_counts / 64.0)
    counts_low = own_counts - 64.0 * counts_high

    def spill_side(block):
        side = block[rows:, H:].T
        return jnp.pad(side, ((0, 0), (0, rows - SPILL_ROWS)))

    misc = [
        piece[5],
        piece[7],
        piece[8],
        block_one[:rows, H:].T,
        block_two[:rows, H:].T,
        spill_side(block_one),
        spill_side(block_two),
        piece[1],
        piece[3],
        piece[9],
        counts_high,
        counts_low,
    ]
    misc = jnp.concatenate([part.reshape(-1) for part in misc])
    misc = jnp.pad(misc, (0, (AUX_ROWS - MISC_ROW) * H - misc.shape[0])).reshape(-1, H)
    first = jnp.concatenate(
        [
            block_one[:rows, :H],
            block_two[:rows, :H],
            block_one[rows:, :H],
            block_two[rows:, :H],
            block_deep[rows:],
            misc,
        ]
    ).astype(LOW)
    stacks_cross = gather(first, groups, count)
    rest = jnp.concatenate([block_deep[:rows], piece[6].reshape(rows, H)]).astype(LOW)
    crossed = [value for value, _ in stacks_cross[3:5]]
    stacks_rest = gather(rest, groups, count, direct=True, after=crossed)
    examples = jnp.stack([labels.astype(F32), days.astype(F32)])

    matrix_one, matrix_two, aux = place(slot, stacks_cross, rows, count, [0, SPILL_ROWS])
    matrix_deep, matrix_top = place(slot, stacks_rest, rows, count, [2 * SPILL_ROWS, None], aux)

    line = aux[:, MISC_ROW]
    at = UNIT_LINES * rows
    units = line[:, :at].reshape(count, UNIT_LINES, rows).transpose(1, 0, 2).reshape(UNIT_LINES, H)
    biases = line[:, at : at + 2 * wide_piece].reshape(count, 2, wide_piece)
    biases = biases.transpose(1, 0, 2).reshape(2, count * wide_piece)
    at += 2 * wide_piece
    head_bias = line[0, at]
    both_counts = jnp.sum(line[:, at + 1 : at + 1 + 2 * DAYS].astype(F32), axis=0)
    counts = 64.0 * both_counts[:DAYS] + both_counts[DAYS:]
    inverse = jnp.broadcast_to((1.0 / counts)[:, None], (DAYS, LANES))
    sides = jnp.pad(units[3:9], ((0, 0), (0, LANES))) + jnp.pad(
        units[9:15], ((0, 0), (rows, LANES - rows))
    )

    def tail_of(at, bias):
        return jnp.concatenate(
            [aux[count - 1, at : at + EXTRA], bias[None, :H], jnp.zeros((LANES - EXTRA - 1, H), LOW)]
        )

    def edge_of(side, bias):
        lane = lax.broadcasted_iota(jnp.int32, side.shape, 1)
        side = jnp.where(lane == D, bias[H:D, None], side)
        return jnp.pad(side, ((0, TALL - H - EXTRA), (0, 0)))

    tail_one, edge_one = tail_of(0, biases[0]), edge_of(sides[:3], biases[0])
    tail_two, edge_two = tail_of(SPILL_ROWS, biases[1]), edge_of(sides[3:], biases[1])
    tail_deep = tail_of(2 * SPILL_ROWS, units[0])
    lines = jnp.concatenate(
        [units[1:3], jnp.full((1, H), head_bias), jnp.zeros((LANES - 3, H), LOW)]
    )
    lines = lines.astype(F32).T
    spread_fixed = Spread(groups, rows, count, fixed=("plane", "z"))
    spread = Spread(groups, rows, count)
    spread_last = Spread(groups, rows, count, below=True)

    wide_features, mixer_one, mixer_two, low_one, low_two = forward_cross(
        features.T, (matrix_one, tail_one, edge_one), (matrix_two, tail_two, edge_two)
    )
    logits, pre_one_low, top_lines, sums, *outs = deep(
        spread_fixed, slot, low_two, examples, matrix_deep, tail_deep, matrix_top, lines, inverse
    )
    *top_stacks, _ = spread_fixed.finish(outs, slot)
    layer_grad, mixer_two_low, deep_lines, *outs = back_deep(
        spread, slot, pre_one_low, low_two, wide_features, matrix_deep, tail_deep, []
    )
    *deep_stacks, deep_over = spread.finish(outs, slot)
    top_sum = core_stage_whole(top_stacks, groups, count, [mixer_two_low])
    part, mixer_one_low, vectors, *outs = back_two(
        spread_fixed, slot, mixer_two_low, low_one, layer_grad, wide_features, mixer_one, mixer_two,
        matrix_two, tail_two, edge_two, (top_lines, deep_lines, sums), [top_sum],
    )
    *two_stacks, two_over = spread_fixed.finish(outs, slot)
    top_total = team_scatter(top_sum, groups["plane"], count)
    deep_plane = core_stage(deep_stacks, groups, count, [mixer_one_low])
    overs = (two_over, deep_over)
    outs = grad_one(
        spread_last, slot, mixer_one_low, wide_features, overs,
        deep_plane[1:],
    )
    last_stacks = spread_last.finish(outs, slot, overs)
    deep_z = plane_stage_z(deep_plane, groups, count, last_stacks[:1])
    last_plane = core_stage(last_stacks, groups, count)
    two_sum = core_stage_whole(two_stacks, groups, count, last_plane[:1])
    feature_grad = back_one(
        mixer_one_low, part, matrix_one, tail_one, edge_one,
        last_plane[1:] + deep_z[1:] + [two_sum],
    )

    vectors = jnp.sum(lax.all_gather(vectors, AXES, axis=0), axis=0)
    loss = vectors[11, 1]
    side_sums = vectors[5:11]

    own_top = team_scatter(top_total, groups["z"], count).astype(F32)
    own_deep = z_stage(deep_z, groups, count)
    two_total = team_scatter(two_sum, groups["plane"], count)
    own_two = team_scatter(two_total, groups["z"], count).astype(F32)
    own_last = z_stage(plane_stage_z(last_plane, groups, count, [feature_grad]), groups, count)
    own_one = own_last[:rows]
    spills = own_last[rows : rows + MISC_ROW]
    row = lax.broadcasted_iota(jnp.int32, spills.shape, 0)
    beyond = (row % SPILL_ROWS >= EXTRA) & (index == count - 1)
    spills = jnp.where(beyond, 0.0, spills)
    wide_biases = jnp.concatenate(
        [vectors[:2, :H], side_sums[:, D].reshape(2, EXTRA)], axis=1
    )
    wide_biases = jnp.pad(wide_biases, ((0, 0), (0, count * wide_piece - D)))
    wide_biases = lax.dynamic_slice(wide_biases, (0, index * wide_piece), (2, wide_piece))
    units = lax.dynamic_slice(vectors[2:5], (0, index * rows), (3, rows))
    side_sums = jnp.pad(side_sums[:, :D], ((0, 0), (0, WIDE - D)))
    side_sums = lax.dynamic_slice(side_sums, (0, index * rows), (6, rows + SPILL_ROWS)).T

    def whole_block(main, number):
        low = number * SPILL_ROWS
        body = jnp.concatenate([main, spills[low : low + SPILL_ROWS]])
        if number == 2:
            return body
        return jnp.concatenate([body, side_sums[:, 3 * number : 3 * number + 3]], axis=1)

    flat_grad = jnp.concatenate(
        [
            from_block(whole_block(own_one, 0), index, sizes[0], rows, count),
            wide_biases[0],
            from_block(whole_block(own_two, 1), index, sizes[2], rows, count),
            wide_biases[1],
            from_block(whole_block(own_deep, 2), index, sizes[4], rows, count),
            units[0],
            own_top.reshape(-1),
            units[1],
            units[2],
            jnp.where(index == 0, vectors[11, :1], 0.0),
        ]
    )
    new_moment_one = 0.9 * moment_one + 0.1 * flat_grad
    new_moment_two = 0.999 * moment_two + 0.001 * flat_grad * flat_grad
    corrected_one = new_moment_one / (1.0 - 0.9**STEP)
    corrected_two = new_moment_two / (1.0 - 0.999**STEP)
    new_master = master - 0.03 * (corrected_one / (jnp.sqrt(corrected_two) + 1e-08) + 0.01 * master)
    new_bias = jnp.concatenate(
        [new_master[starts[i] : starts[i] + sizes[i]] for i in (1, 3, 5, 7, 9)]
    )
    return (
        logits.reshape(-1),
        loss,
        feature_grad.T,
        flat_grad,
        new_moment_one,
        new_moment_two,
        new_master,
        new_bias,
    )


def solution(mesh):
    line = P(AXES)
    table = P(AXES, None)
    groups = bit_groups(mesh)
    return jax.shard_map(
        functools.partial(local, groups),
        mesh=mesh,
        in_specs=(table, line, line, line, line, line),
        out_specs=(line, P(), table, line, line, line, line, line),
        check_vma=False,
    )
```

```python
import functools
import math

import jax
import jax.numpy as jnp
from jax import lax
from jax.experimental import pallas as pl
from jax.experimental.pallas import tpu as pltpu
from jax.sharding import PartitionSpec as P

D = 1027
H = 1024
DAYS = 24
STEP = 10
AXES = ("dp", "cores")
EXTRA = D - H
LANES = 128
WIDE = H + LANES
AUX_ROWS = 16
SPILL_ROWS = 4
MISC_ROW = 12
UNIT_LINES = 15
TILE = 512
TALL = H + 16
MIB = 1024 * 1024
F32 = jnp.float32
LOW = jnp.bfloat16
SMEM = pl.BlockSpec(memory_space=pltpu.SMEM)
VMEM = pl.BlockSpec(memory_space=pltpu.VMEM)
PARAMS = pltpu.CompilerParams(vmem_limit_bytes=56 * MIB)


def shapes():
    return [(D, D), (D,), (D, D), (D,), (D, H), (H,), (H, H), (H,), (H,), (1,)]


def piece_sizes(count):
    return [(math.prod(shape) + count - 1) // count for shape in shapes()[:-1]] + [1]


def starts_of(count):
    starts = []
    position = 0
    for piece in piece_sizes(count):
        starts.append(position)
        position += piece
    return starts


def to_block(piece, index, width, rows, count):
    excess = piece.shape[0] - rows * width
    size = (rows + SPILL_ROWS) * width
    lead = (count - 1) * excess
    padded = jnp.pad(piece, (lead, max(0, size - piece.shape[0])))
    line = lax.dynamic_slice(padded, (lead - index * excess,), (size,))
    return line.reshape(rows + SPILL_ROWS, width)


def from_block(block, index, piece, rows, count):
    width = block.shape[1]
    excess = piece - rows * width
    last = (count - 1) * excess
    line = jnp.pad(block.reshape(-1), (0, max(0, last + piece - block.size)))
    return lax.dynamic_slice(line, (index * excess,), (piece,))


def bit_groups(mesh):
    devices = mesh.devices.reshape(-1)
    groups = {"z": [], "plane": [], "core": []}
    bit = 1
    while bit < devices.size:
        here = getattr(devices[0], "coords", None)
        there = getattr(devices[bit], "coords", None)
        if here is None or there is None:
            name = "core" if bit == 1 else "plane" if bit <= 4 else "z"
        elif tuple(here) == tuple(there):
            name = "core"
        elif here[2] != there[2]:
            name = "z"
        else:
            name = "plane"
        groups[name].append(bit)
        bit *= 2
    return groups


def masks_of(bits):
    masks = [0]
    for bit in bits:
        masks = masks + [mask | bit for mask in masks]
    return masks


def teams(bits, count):
    masks = masks_of(bits)
    return [[k | mask for mask in masks] for k in range(count) if not k & masks[-1]]


def owner(index, mask, groups, fixed):
    for name in fixed:
        index = jnp.bitwise_and(index, ~masks_of(groups[name])[-1])
    return jnp.bitwise_xor(index, mask)


def swap(value, mask, count):
    return lax.ppermute(value, AXES, [(k, k ^ mask) for k in range(count)])


def join(parts, after):
    def kernel(*refs):
        for j in range(len(parts)):
            refs[-1][j] = refs[j][...]

    return pl.pallas_call(
        kernel,
        out_shape=jax.ShapeDtypeStruct((len(parts),) + parts[0].shape, parts[0].dtype),
        in_specs=[VMEM] * len(parts) + [pl.BlockSpec(memory_space=pl.ANY)] * len(after),
        out_specs=VMEM,
        compiler_params=PARAMS,
        name="join",
    )(*parts, *after)


def gather(block, groups, count, direct=False, after=()):
    z_masks = masks_of(groups["z"])
    core_masks = masks_of(groups["core"])
    line = [block] + [swap(block, mask, count) for mask in z_masks[1:]]
    line = join(line, after) if after else jnp.stack(line)
    plane = [(line, z_masks)]
    if len(groups["plane"]) == 2 and len(z_masks) > 1 and not direct:
        one, two = groups["plane"]
        half = len(z_masks) // 2
        by_one = swap(line, one, count)
        by_two = swap(line, two, count)
        plane.append((by_one, [one ^ z for z in z_masks]))
        plane.append((by_two, [two ^ z for z in z_masks]))
        both = one ^ two
        plane.append((swap(by_one[:half], two, count), [both ^ z for z in z_masks[:half]]))
        plane.append((swap(by_two[half:], one, count), [both ^ z for z in z_masks[half:]]))
    else:
        for mask in masks_of(groups["plane"])[1:]:
            plane.append((swap(line, mask, count), [mask ^ z for z in z_masks]))
    result = list(plane)
    for core in core_masks[1:]:
        result += [(swap(value, core, count), [core ^ m for m in row]) for value, row in plane]
    return result


def place(index, stacks, rows, count, parts, aux=None):
    sources = [value for value, _ in stacks]
    masks = [row for _, row in stacks]
    carries = aux is None
    top = min(16, rows)

    def kernel(index_ref, *refs):
        refs = list(refs)
        aux_ref = refs.pop() if carries else refs.pop(0)
        outs = refs[len(sources) :]
        for ref, row in zip(refs, masks):
            for j, mask in enumerate(row):
                at = jnp.bitwise_xor(index_ref[0], mask)
                for i, out_ref in enumerate(outs):
                    out_ref[at] = ref[j, i * rows : (i + 1) * rows]
                if carries:
                    aux_ref[at] = ref[j, len(outs) * rows :]
        for spill_at, out_ref in zip(parts, outs):
            if spill_at is None:
                continue
            for k in range(1, count):
                spill = aux_ref[k - 1].astype(F32)[spill_at : spill_at + SPILL_ROWS]
                old = out_ref[k, :top].astype(F32)
                new = old[:SPILL_ROWS] + spill
                if top > SPILL_ROWS:
                    new = jnp.concatenate([new, old[SPILL_ROWS:]], axis=0)
                out_ref[k, :top] = new.astype(LOW)

    out_shape = [jax.ShapeDtypeStruct((count, rows, H), LOW)] * len(parts)
    if carries:
        out_shape.append(jax.ShapeDtypeStruct((count, AUX_ROWS, H), LOW))
    extra = [] if carries else [aux]
    result = pl.pallas_call(
        kernel,
        out_shape=out_shape,
        in_specs=[SMEM] + [VMEM] * (len(extra) + len(sources)),
        out_specs=[VMEM] * len(out_shape),
        compiler_params=PARAMS,
        name="place",
    )(index, *extra, *sources)
    return [value.reshape(H, H) for value in result[: len(parts)]] + list(result[len(parts) :])


def split(index, value, masks, kinds, groups, fixed):
    def kernel(index_ref, value_ref, *out_refs):
        for ref, row, kind in zip(out_refs, masks, kinds):
            for j, mask in enumerate(row):
                ref[j] = value_ref[owner(index_ref[0], mask, groups, fixed)].astype(kind)

    shape = value.shape[1:]
    return pl.pallas_call(
        kernel,
        out_shape=[
            jax.ShapeDtypeStruct((len(row),) + shape, kind) for row, kind in zip(masks, kinds)
        ],
        in_specs=[SMEM, VMEM],
        out_specs=[VMEM] * len(masks),
        compiler_params=PARAMS,
        name="split",
    )(index, value)


def halves(groups):
    z_masks, plane_masks, core_masks = (masks_of(groups[g]) for g in ("z", "plane", "core"))
    inner = [p ^ z for p in plane_masks for z in z_masks]
    return [[core ^ m for m in inner] for core in core_masks]


def kinds_of(groups):
    return [F32] + [LOW] * (len(halves(groups)) - 1)


def adder(name, body, ins, outs, after):
    def kernel(*refs):
        body(refs[: len(ins)], refs[len(ins) + len(after) :])

    result = pl.pallas_call(
        kernel,
        out_shape=outs,
        in_specs=[VMEM] * len(ins) + [pl.BlockSpec(memory_space=pl.ANY)] * len(after),
        out_specs=[VMEM] * len(outs),
        compiler_params=PARAMS,
        name=name,
    )(*ins, *after)
    return list(result)


def core_stage(stacks, groups, count, after=()):
    z_count, plane_count = len(masks_of(groups["z"])), len(masks_of(groups["plane"]))
    cores = masks_of(groups["core"])[1:]
    gotten = [swap(stack, core, count) for core, stack in zip(cores, stacks[1:])]
    shape = (z_count,) + stacks[0].shape[1:]

    def body(ins, outs):
        for p, out_ref in enumerate(outs):
            for z in range(z_count):
                total = ins[0][p * z_count + z]
                for ref in ins[1:]:
                    total = total + ref[p * z_count + z].astype(F32)
                out_ref[z] = total.astype(out_ref.dtype)

    outs = [jax.ShapeDtypeStruct(shape, F32 if p == 0 else LOW) for p in range(plane_count)]
    return adder("core_sum", body, [stacks[0]] + gotten, outs, after)


def core_stage_whole(stacks, groups, count, after=()):
    z_count, plane_count = len(masks_of(groups["z"])), len(masks_of(groups["plane"]))
    cores = masks_of(groups["core"])[1:]
    gotten = [swap(stack, core, count) for core, stack in zip(cores, stacks[1:])]

    def body(ins, outs):
        for p in range(plane_count):
            for z in range(z_count):
                total = ins[0][p * z_count + z]
                for ref in ins[1:]:
                    total = total + ref[p * z_count + z].astype(F32)
                outs[0][p, z] = total.astype(LOW)

    outs = [jax.ShapeDtypeStruct((plane_count, z_count) + stacks[0].shape[1:], LOW)]
    return adder("core_sum", body, [stacks[0]] + gotten, outs, after)[0]


def team_scatter(total, bits, count):
    if not bits:
        return total[0]
    return lax.psum_scatter(
        total, AXES, scatter_dimension=0, axis_index_groups=teams(bits, count)
    )


def plane_swaps(parts, groups, count):
    masks = masks_of(groups["plane"])[1:]
    return [parts[0]] + [swap(part, mask, count) for mask, part in zip(masks, parts[1:])]


def plane_stage_z(parts, groups, count, after=()):
    def body(ins, outs):
        for z, out_ref in enumerate(outs):
            total = ins[0][z]
            for ref in ins[1:]:
                total = total + ref[z].astype(F32)
            out_ref[...] = total.astype(out_ref.dtype)

    many, rows, width = parts[0].shape
    outs = [jax.ShapeDtypeStruct((rows, width), F32 if z == 0 else LOW) for z in range(many)]
    return adder("plane_sum", body, plane_swaps(parts, groups, count), outs, after)


def plane_stage_joint(one, two, groups, count, after=()):
    ins = plane_swaps(one, groups, count) + plane_swaps(two, groups, count)
    many = len(one)
    first = one[0].shape[1]
    rows = first + two[0].shape[1]

    def body(refs, outs):
        for z, out_ref in enumerate(outs):
            for start, end, part in ((0, first, refs[:many]), (first, rows, refs[many:])):
                total = part[0][z]
                for ref in part[1:]:
                    total = total + ref[z].astype(F32)
                out_ref[start:end] = total.astype(out_ref.dtype)

    outs = [
        jax.ShapeDtypeStruct((rows, H), F32 if z == 0 else LOW) for z in range(one[0].shape[0])
    ]
    return adder("plane_sum", body, ins, outs, after)


def z_stage(parts, groups, count):
    own = parts[0]
    for mask, part in zip(masks_of(groups["z"])[1:], parts[1:]):
        own = own + swap(part, mask, count).astype(F32)
    return own


def product(left, right):
    return lax.dot_general(left, right, (((1,), (0,)), ((), ())), preferred_element_type=F32)


def outer(left, right):
    return lax.dot_general(left, right, (((1,), (1,)), ((), ())), preferred_element_type=F32)


def gelu_both(value):
    scale = math.sqrt(2.0 / math.pi)
    square = value * value
    share = 0.5 + 0.5 * jnp.tanh(value * (scale + scale * 0.044715 * square))
    result = value * share
    slope = share + result * (1.0 - share) * (2.0 * scale + 6.0 * scale * 0.044715 * square)
    return result, slope


def columns(height, tile=TILE):
    return pl.BlockSpec((height, tile), lambda i: (0, i))


def whole(*shape):
    return pl.BlockSpec(shape, lambda i: (0,) * len(shape))


def once(*shape):
    return pl.BlockSpec(shape, lambda i: (0,) * len(shape), pipeline_mode=pl.Buffered(1))


def shaped(kind, *shape):
    return jax.ShapeDtypeStruct(shape, kind)


def pieces_of(width):
    return [(a, a + 256) for a in range(0, width, 256)]


def run(name, kernel, batch, in_specs, out_specs, out_shape, scratch, flops, *args, tile=TILE):
    moved = sum(a.size * a.dtype.itemsize for a in args)
    moved += sum(math.prod(o.shape) * o.dtype.itemsize for o in out_shape)
    return pl.pallas_call(
        kernel,
        grid=(batch // tile,),
        in_specs=in_specs,
        out_specs=out_specs,
        out_shape=out_shape,
        scratch_shapes=scratch,
        compiler_params=PARAMS,
        cost_estimate=pl.CostEstimate(flops=flops, bytes_accessed=moved, transcendentals=0),
        name=name,
    )(*args)


def first_step():
    return pl.when(pl.program_id(0) == 0)


def last_step():
    return pl.when(pl.program_id(0) == pl.num_programs(0) - 1)


def turn(out_ref, matrix_ref, tail_ref=None, edge_ref=None):
    for a, b in pieces_of(H):
        out_ref[a:b, :H] = matrix_ref[:, a:b].T
    if tail_ref is not None:
        out_ref[:H, H:] = tail_ref[...].T
    if edge_ref is not None:
        out_ref[H:, :] = edge_ref[...]


def straight(out_ref, matrix_ref, tail_ref, edge_ref=None):
    out_ref[:H, :H] = matrix_ref[...]
    row = lax.broadcasted_iota(jnp.int32, (TALL - H, H), 0)
    tail = tail_ref[: TALL - H, :].astype(F32)
    out_ref[H:, :H] = jnp.where(row < EXTRA, tail, 0.0).astype(LOW)
    if edge_ref is not None:
        lane = lax.broadcasted_iota(jnp.int32, (TALL - H, WIDE), 1)
        edge = jnp.where(lane < D, edge_ref[...].astype(F32), 0.0)
        edge = jnp.concatenate([edge, jnp.zeros((LANES - (TALL - H), WIDE), F32)])
        out_ref[:, H:] = edge.T[:TALL].astype(LOW)


def widen(out_ref, value_ref):
    @first_step()
    def _():
        out_ref[TALL:] = jnp.zeros((WIDE - TALL, out_ref.shape[1]), LOW)

    out_ref[:TALL] = value_ref[...]


class Spread:
    def __init__(self, groups, rows, count, parts=1, below=False, fixed=()):
        self.groups, self.fixed = groups, fixed
        self.masks = halves(groups)
        self.kinds = kinds_of(groups)
        self.rows, self.count, self.parts, self.below = rows, count, parts, below
        self.direct = rows % 16 == 0

    def shapes(self):
        if not self.direct:
            return [shaped(F32, TALL, H)] * self.parts
        height = self.rows * self.parts + (AUX_ROWS if self.below else 0)
        outs = [shaped(kind, len(row), height, H) for row, kind in zip(self.masks, self.kinds)]
        overs = 0 if self.below else self.parts
        return outs + [shaped(F32, self.count, 8, H)] * overs

    def specs(self):
        return [whole(*s.shape) for s in self.shapes()]

    def write(self, acc_refs, index_ref, out_refs, over_refs=None):
        if not self.direct:
            for acc_ref, ref in zip(acc_refs, out_refs):
                ref[...] = acc_ref[...]
            return
        rows = self.rows
        for ref, row, kind in zip(out_refs, self.masks, self.kinds):
            for j, mask in enumerate(row):
                at = owner(index_ref[0], mask, self.groups, self.fixed)
                start = pl.multiple_of(at * rows, rows)
                for i, acc_ref in enumerate(acc_refs):
                    block = acc_ref[pl.ds(start, rows), :]
                    ref[j, i * rows : (i + 1) * rows] = block.astype(kind)
                if self.below:
                    mine = acc_ref[pl.ds(pl.multiple_of(start + rows, 8), 8), :]
                    parts = [mine[:SPILL_ROWS]] + [v[at][:SPILL_ROWS] for v in over_refs]
                    parts.append(jnp.zeros((AUX_ROWS - MISC_ROW, H), F32))
                    ref[j, rows:] = jnp.concatenate(parts).astype(kind)
        if not self.below:
            for acc_ref, ref in zip(acc_refs, out_refs[len(self.masks) :]):
                for k in range(self.count):
                    ref[k] = acc_ref[(k + 1) * rows : (k + 1) * rows + 8, :]

    def finish(self, outs, index, overs=None):
        if self.direct:
            return list(outs)
        rows, count = self.rows, self.count
        blocks = [grad[:H].reshape(count, rows, H) for grad in outs]
        own = [
            jnp.stack([grad[(k + 1) * rows : (k + 1) * rows + 8] for k in range(count)])
            for grad in outs
        ]
        if self.below:
            blocks += [v[:, :SPILL_ROWS] for v in own + list(overs)]
            blocks.append(jnp.zeros((count, AUX_ROWS - MISC_ROW, H), F32))
        stacks = split(
            index, jnp.concatenate(blocks, axis=1), self.masks, self.kinds, self.groups, self.fixed
        )
        stacks = list(stacks)
        return stacks if self.below else stacks + own


ANY = pl.BlockSpec(memory_space=pl.ANY)
REST = TALL - H


def forward_cross(features, one, two):
    batch = features.shape[1]

    def kernel(f_ref, *refs):
        x_ref, mixer_one_ref, mixer_two_ref, one_ref, two_ref = refs[6:11]
        turned_one, turned_two, wide_ref = refs[11:]

        @first_step()
        def _():
            turn(turned_one, *refs[:3])
            turn(turned_two, *refs[3:6])

        x_ref[:H] = f_ref[:H]
        last = f_ref[H:].astype(F32)
        last = jnp.concatenate([last, jnp.ones((1, TILE), F32), jnp.zeros((TALL - D - 1, TILE), F32)])
        x_ref[H:] = last.astype(LOW)
        widen(wide_ref, x_ref)
        layers = []
        for a, b in [(0, TILE)]:
            mixer = product(turned_one[...], wide_ref[:, a:b])
            mixer_one_ref[:, a:b] = mixer.astype(LOW)
            part = x_ref[:, a:b].astype(F32)
            layer = part * mixer + part
            layers.append(layer)
            one_ref[:, a:b] = layer.astype(LOW)
        wide_ref[:TALL] = one_ref[...]
        for (a, b), layer in zip([(0, TILE)], layers):
            mixer = product(turned_two[...], wide_ref[:, a:b])
            mixer_two_ref[:, a:b] = mixer.astype(LOW)
            two_ref[:, a:b] = (x_ref[:, a:b].astype(F32) * mixer + layer).astype(LOW)

    return run(
        "forward_cross",
        kernel,
        batch,
        [columns(D)] + [once(H, H), once(LANES, H), once(REST, WIDE)] * 2,
        [columns(TALL)] * 5,
        [shaped(LOW, TALL, batch)] * 5,
        [pltpu.VMEM((TALL, WIDE), LOW)] * 2 + [pltpu.VMEM((WIDE, TILE), LOW)],
        4 * batch * TALL * TALL,
        features, *one, *two,
    )


def deep(spread, index, layer_low, examples, matrix_one, tail, matrix, lines, inverse):
    batch = layer_low.shape[1]
    days = inverse.shape[0]

    def kernel(k_ref, l_ref, x_ref, w_one_ref, t_ref, w_ref, n_ref, i_ref, *refs):
        logit_ref, back_ref, line_ref, sum_ref = refs[:4]
        out_refs = refs[4:-8]
        turned_one, turned, acc_ref, hidden_ref, slope_ref, low_ref, part_ref, wide_ref = refs[-8:]

        @first_step()
        def _():
            turn(turned_one, w_one_ref, t_ref)
            turn(turned, w_ref)
            acc_ref[...] = jnp.zeros_like(acc_ref)
            sum_ref[...] = jnp.zeros_like(sum_ref)
            part_ref[...] = jnp.zeros_like(part_ref)
            row = lax.broadcasted_iota(jnp.int32, (REST, TILE), 0)
            hidden_ref[H:] = jnp.where(row == 0, 1.0, 0.0).astype(LOW)

        widen(wide_ref, l_ref)
        for a, b in pieces_of(TILE):
            hidden, slope = gelu_both(product(turned_one[...], wide_ref[:, a:b]))
            hidden_ref[:H, a:b] = hidden.astype(LOW)
            slope_ref[:, a:b] = slope
        head = n_ref[:, 1:2]
        for a, b in pieces_of(TILE):
            two, slope = gelu_both(product(turned[...], hidden_ref[:H, a:b]) + n_ref[:, 0:1])
            two = two.astype(LOW).astype(F32)
            logits = n_ref[0:1, 2:3] + jnp.sum(two * head, axis=0, keepdims=True)
            label = x_ref[0:1, a:b]
            day = x_ref[1:2, a:b].astype(jnp.int32)
            row = lax.broadcasted_iota(jnp.int32, (days, b - a), 0)
            weight = jnp.sum(jnp.where(row == day, i_ref[:, 0:1], 0.0), axis=0, keepdims=True)
            decay = jnp.exp(-jnp.abs(logits))
            entropy = jnp.maximum(logits, 0.0) + jnp.log1p(decay) - label * logits
            chance = jnp.where(logits >= 0.0, 1.0, decay) / (1.0 + decay)
            logit_grad = (chance - label) * weight
            logit_ref[:, a:b] = logits
            sum_ref[0:1, a:b] += logit_grad
            sum_ref[1:2, a:b] += entropy * weight
            low_ref[:, a:b] = ((logit_grad * head) * slope).astype(LOW)
            one = logit_grad * two
            part = one[:, :LANES]
            for at in range(LANES, b - a, LANES):
                part = part + one[:, at : at + LANES]
            part_ref[...] += part
        for a, b in pieces_of(TILE):
            back_ref[:, a:b] = (product(w_ref[...], low_ref[:, a:b]) * slope_ref[:, a:b]).astype(LOW)
        for a, b in pieces_of(H):
            acc_ref[:, a:b] += outer(hidden_ref[...], low_ref[a:b])

        @last_step()
        def _():
            line_ref[0:8] = jnp.broadcast_to(
                jnp.sum(part_ref[...].T, axis=0, keepdims=True), (8, H)
            )
            line_ref[8:16] = acc_ref[H : H + 8]
            spread.write([acc_ref], k_ref, out_refs)

    return run(
        "deep",
        kernel,
        batch,
        [
            SMEM,
            columns(TALL),
            columns(2),
            once(H, H),
            once(LANES, H),
            once(H, H),
            whole(H, LANES),
            whole(days, LANES),
        ],
        [columns(1), columns(H), whole(16, H), whole(8, TILE)] + spread.specs(),
        [
            shaped(F32, 1, batch),
            shaped(LOW, H, batch),
            shaped(F32, 16, H),
            shaped(F32, 8, TILE),
        ]
        + spread.shapes(),
        [
            pltpu.VMEM((H, WIDE), LOW),
            pltpu.VMEM((H, H), LOW),
            pltpu.VMEM((TALL, H), F32),
            pltpu.VMEM((TALL, TILE), LOW),
            pltpu.VMEM((H, TILE), F32),
            pltpu.VMEM((H, TILE), LOW),
            pltpu.VMEM((H, LANES), F32),
            pltpu.VMEM((WIDE, TILE), LOW),
        ],
        8 * batch * H * H,
        index, layer_low, examples, matrix_one, tail, matrix, lines, inverse,
    )


def back_deep(spread, index, grad_low, layer_low, features, matrix, tail, after):
    batch = features.shape[1]

    def kernel(k_ref, g_ref, l_ref, x_ref, w_ref, t_ref, *refs):
        refs = refs[len(after) :]
        layer_ref, mixer_ref, line_ref = refs[:3]
        out_refs = refs[3:-2]
        held, acc_ref = refs[-2:]

        @first_step()
        def _():
            straight(held, w_ref, t_ref)
            acc_ref[...] = jnp.zeros_like(acc_ref)

        for a, b in pieces_of(TILE):
            layer = product(held[...], g_ref[:, a:b])
            layer_ref[:, a:b] = layer
            mixer_ref[:, a:b] = (layer * x_ref[:, a:b].astype(F32)).astype(LOW)
        for a, b in pieces_of(H):
            acc_ref[:, a:b] += outer(l_ref[...], g_ref[a:b])

        @last_step()
        def _():
            line_ref[...] = acc_ref[H:]
            spread.write([acc_ref], k_ref, out_refs)

    return run(
        "back_deep",
        kernel,
        batch,
        [SMEM, columns(H), columns(TALL), columns(TALL), once(H, H), once(LANES, H)]
        + [ANY] * len(after),
        [columns(TALL), columns(TALL), whole(REST, H)] + spread.specs(),
        [shaped(F32, TALL, batch), shaped(LOW, TALL, batch), shaped(F32, REST, H)]
        + spread.shapes(),
        [pltpu.VMEM((TALL, H), LOW), pltpu.VMEM((TALL, H), F32)],
        4 * batch * TALL * H,
        index, grad_low, layer_low, features, matrix, tail, *after,
    )


def back_two(
    spread, index, mixer_low, layer_low, layer_grad, features, mixer_one, mixer_two, matrix, tail,
    edge, lines, after,
):
    batch = features.shape[1]

    def kernel(k_ref, g_ref, l_ref, d_ref, x_ref, one_ref, two_ref, w_ref, t_ref, e_ref, *refs):
        top_ref, deep_ref, sums_ref = refs[:3]
        refs = refs[3 + len(after) :]
        part_ref, mixer_ref, vector_ref = refs[:3]
        out_refs = refs[3:-6]
        held, acc_ref, wide_ref, sum_ref, side_ref, next_side_ref = refs[-6:]

        @first_step()
        def _():
            straight(held, w_ref, t_ref, e_ref)
            acc_ref[...] = jnp.zeros_like(acc_ref)
            side_ref[...] = jnp.zeros_like(side_ref)
            next_side_ref[...] = jnp.zeros_like(next_side_ref)
            sum_ref[...] = jnp.zeros_like(sum_ref)

        widen(wide_ref, g_ref)
        for a, b in pieces_of(TILE):
            above = d_ref[:, a:b]
            layer = product(held[...], wide_ref[:, a:b]) + above
            mixer = (layer * x_ref[:, a:b].astype(F32)).astype(LOW)
            mixer_ref[:, a:b] = mixer
            mixer = mixer[:H].astype(F32)
            total = mixer[:, :LANES]
            for at in range(LANES, b - a, LANES):
                total = total + mixer[:, at : at + LANES]
            sum_ref[...] += total
            part = above * two_ref[:, a:b].astype(F32)
            part = part + layer * (one_ref[:, a:b].astype(F32) + 1.0)
            part_ref[:, a:b] = part.astype(LOW)
        for a, b in pieces_of(H):
            acc_ref[:, a:b] += outer(l_ref[...], g_ref[a:b])
        side_ref[...] += outer(g_ref[H:], l_ref[...])
        next_side_ref[...] += outer(mixer_ref[H:], x_ref[...])

        @last_step()
        def _():
            vector_ref[...] = jnp.zeros_like(vector_ref)
            vector_ref[0:1, :H] = jnp.sum(sum_ref[...].T, axis=0, keepdims=True)
            vector_ref[1:2, :H] = acc_ref[D : D + 1]
            vector_ref[2:3, :H] = deep_ref[EXTRA : EXTRA + 1]
            vector_ref[3:4, :H] = top_ref[8:9]
            vector_ref[4:5, :H] = top_ref[0:1]
            vector_ref[5:8, :TALL] = next_side_ref[:EXTRA]
            vector_ref[8:11, :TALL] = side_ref[:EXTRA]
            lane = lax.broadcasted_iota(jnp.int32, (1, LANES), 1)
            bias = jnp.sum(sums_ref[0:1], axis=1, keepdims=True)
            loss = jnp.sum(sums_ref[1:2], axis=1, keepdims=True)
            vector_ref[11:12, :LANES] = jnp.where(lane == 0, bias, jnp.where(lane == 1, loss, 0.0))
            spread.write([acc_ref], k_ref, out_refs)

    return run(
        "back_two",
        kernel,
        batch,
        [SMEM]
        + [columns(TALL)] * 6
        + [once(H, H), once(LANES, H), once(REST, WIDE)]
        + [whole(*v.shape) for v in lines]
        + [ANY] * len(after),
        [columns(TALL), columns(TALL)]
        + [whole(16, WIDE)]
        + spread.specs(),
        [
            shaped(LOW, TALL, batch),
            shaped(LOW, TALL, batch),
            shaped(F32, 16, WIDE),
        ]
        + spread.shapes(),
        [
            pltpu.VMEM((TALL, WIDE), LOW),
            pltpu.VMEM((TALL, H), F32),
            pltpu.VMEM((WIDE, TILE), LOW),
            pltpu.VMEM((H, LANES), F32),
            pltpu.VMEM((REST, TALL), F32),
            pltpu.VMEM((REST, TALL), F32),
        ],
        4 * batch * TALL * TALL,
        index, mixer_low, layer_low, layer_grad, features, mixer_one, mixer_two, matrix, tail,
        edge, *lines, *after,
    )


def grad_one(spread, index, mixer_low, features, overs, after):
    batch = features.shape[1]

    def kernel(k_ref, g_ref, x_ref, *refs):
        over_refs = refs[: len(overs)]
        out_refs = refs[len(overs) + len(after) : -1]
        acc_ref = refs[-1]

        @first_step()
        def _():
            acc_ref[...] = jnp.zeros_like(acc_ref)

        for a, b in pieces_of(H):
            acc_ref[:, a:b] += outer(x_ref[...], g_ref[a:b])

        @last_step()
        def _():
            spread.write([acc_ref], k_ref, out_refs, over_refs)

    return run(
        "grad_one",
        kernel,
        batch,
        [SMEM, columns(TALL), columns(TALL)]
        + [once(*v.shape) for v in overs]
        + [ANY] * len(after),
        spread.specs(),
        spread.shapes(),
        [pltpu.VMEM((TALL, H), F32)],
        2 * batch * TALL * TALL,
        index, mixer_low, features, *overs, *after,
    )


def back_one(mixer_low, part, matrix, tail, edge, after):
    batch = part.shape[1]

    def kernel(g_ref, p_ref, w_ref, t_ref, e_ref, *refs):
        out_ref, held, wide_ref = refs[len(after) :]

        @first_step()
        def _():
            straight(held, w_ref, t_ref, e_ref)

        widen(wide_ref, g_ref)
        for a, b in [(0, TILE)]:
            value = p_ref[:, a:b].astype(F32) + product(held[...], wide_ref[:, a:b])
            out_ref[:H, a:b] = value[:H]
            out_ref[H:, a:b] = value[H:D]

    return run(
        "back_one",
        kernel,
        batch,
        [columns(TALL), columns(TALL), whole(H, H), whole(LANES, H), whole(REST, WIDE)]
        + [ANY] * len(after),
        [columns(D)],
        [shaped(F32, D, batch)],
        [pltpu.VMEM((TALL, WIDE), LOW), pltpu.VMEM((WIDE, TILE), LOW)],
        2 * batch * TALL * TALL,
        mixer_low, part, matrix, tail, edge, *after,
    )[0]


def local(groups, features, labels, days, master, moment_one, moment_two):
    count = lax.axis_size(AXES)
    index = lax.axis_index(AXES)
    slot = index[None].astype(jnp.int32)
    rows = H // count
    starts = starts_of(count)
    sizes = piece_sizes(count)
    wide_piece = sizes[1]
    piece = [master[a : a + l] for a, l in zip(starts, sizes)]
    block_one = to_block(piece[0], index, D, rows, count)
    block_two = to_block(piece[2], index, D, rows, count)
    block_deep = to_block(piece[4], index, H, rows, count)

    day_hot = (days[:, None] == jnp.arange(DAYS, dtype=jnp.int32)[None, :]).astype(F32)
    own_counts = jnp.sum(day_hot, axis=0)
    counts_high = jnp.floor(own_counts / 64.0)
    counts_low = own_counts - 64.0 * counts_high

    def spill_side(block):
        side = block[rows:, H:].T
        return jnp.pad(side, ((0, 0), (0, rows - SPILL_ROWS)))

    misc = [
        piece[5],
        piece[7],
        piece[8],
        block_one[:rows, H:].T,
        block_two[:rows, H:].T,
        spill_side(block_one),
        spill_side(block_two),
        piece[1],
        piece[3],
        piece[9],
        counts_high,
        counts_low,
    ]
    misc = jnp.concatenate([part.reshape(-1) for part in misc])
    misc = jnp.pad(misc, (0, (AUX_ROWS - MISC_ROW) * H - misc.shape[0])).reshape(-1, H)
    first = jnp.concatenate(
        [
            block_one[:rows, :H],
            block_two[:rows, :H],
            block_one[rows:, :H],
            block_two[rows:, :H],
            block_deep[rows:],
            misc,
        ]
    ).astype(LOW)
    stacks_cross = gather(first, groups, count)
    rest = jnp.concatenate([block_deep[:rows], piece[6].reshape(rows, H)]).astype(LOW)
    crossed = [value for value, _ in stacks_cross[3:5]]
    stacks_rest = gather(rest, groups, count, direct=True, after=crossed)
    examples = jnp.stack([labels.astype(F32), days.astype(F32)])

    matrix_one, matrix_two, aux = place(slot, stacks_cross, rows, count, [0, SPILL_ROWS])
    matrix_deep, matrix_top = place(slot, stacks_rest, rows, count, [2 * SPILL_ROWS, None], aux)

    line = aux[:, MISC_ROW]
    at = UNIT_LINES * rows
    units = line[:, :at].reshape(count, UNIT_LINES, rows).transpose(1, 0, 2).reshape(UNIT_LINES, H)
    biases = line[:, at : at + 2 * wide_piece].reshape(count, 2, wide_piece)
    biases = biases.transpose(1, 0, 2).reshape(2, count * wide_piece)
    at += 2 * wide_piece
    head_bias = line[0, at]
    both_counts = jnp.sum(line[:, at + 1 : at + 1 + 2 * DAYS].astype(F32), axis=0)
    counts = 64.0 * both_counts[:DAYS] + both_counts[DAYS:]
    inverse = jnp.broadcast_to((1.0 / counts)[:, None], (DAYS, LANES))
    sides = jnp.pad(units[3:9], ((0, 0), (0, LANES))) + jnp.pad(
        units[9:15], ((0, 0), (rows, LANES - rows))
    )

    def tail_of(at, bias):
        return jnp.concatenate(
            [aux[count - 1, at : at + EXTRA], bias[None, :H], jnp.zeros((LANES - EXTRA - 1, H), LOW)]
        )

    def edge_of(side, bias):
        lane = lax.broadcasted_iota(jnp.int32, side.shape, 1)
        side = jnp.where(lane == D, bias[H:D, None], side)
        return jnp.pad(side, ((0, TALL - H - EXTRA), (0, 0)))

    tail_one, edge_one = tail_of(0, biases[0]), edge_of(sides[:3], biases[0])
    tail_two, edge_two = tail_of(SPILL_ROWS, biases[1]), edge_of(sides[3:], biases[1])
    tail_deep = tail_of(2 * SPILL_ROWS, units[0])
    lines = jnp.concatenate(
        [units[1:3], jnp.full((1, H), head_bias), jnp.zeros((LANES - 3, H), LOW)]
    )
    lines = lines.astype(F32).T
    spread_fixed = Spread(groups, rows, count, fixed=("plane", "z"))
    spread = Spread(groups, rows, count)
    spread_last = Spread(groups, rows, count, below=True)

    wide_features, mixer_one, mixer_two, low_one, low_two = forward_cross(
        features.T, (matrix_one, tail_one, edge_one), (matrix_two, tail_two, edge_two)
    )
    logits, pre_one_low, top_lines, sums, *outs = deep(
        spread_fixed, slot, low_two, examples, matrix_deep, tail_deep, matrix_top, lines, inverse
    )
    *top_stacks, _ = spread_fixed.finish(outs, slot)
    layer_grad, mixer_two_low, deep_lines, *outs = back_deep(
        spread, slot, pre_one_low, low_two, wide_features, matrix_deep, tail_deep, []
    )
    *deep_stacks, deep_over = spread.finish(outs, slot)
    top_sum = core_stage_whole(top_stacks, groups, count, [mixer_two_low])
    part, mixer_one_low, vectors, *outs = back_two(
        spread, slot, mixer_two_low, low_one, layer_grad, wide_features, mixer_one, mixer_two,
        matrix_two, tail_two, edge_two, (top_lines, deep_lines, sums), [top_sum],
    )
    *two_stacks, two_over = spread.finish(outs, slot)
    top_total = team_scatter(top_sum, groups["plane"], count)
    deep_plane = core_stage(deep_stacks, groups, count, [mixer_one_low])
    overs = (two_over, deep_over)
    outs = grad_one(
        spread_last, slot, mixer_one_low, wide_features, overs,
        deep_plane[1:],
    )
    last_stacks = spread_last.finish(outs, slot, overs)
    deep_z = plane_stage_z(deep_plane, groups, count, last_stacks[:1])
    last_plane = core_stage(last_stacks, groups, count)
    two_plane = core_stage(two_stacks, groups, count, last_stacks[:1])
    feature_grad = back_one(
        mixer_one_low, part, matrix_one, tail_one, edge_one,
        last_plane[1:] + deep_z[1:] + two_plane[1:],
    )

    vectors = jnp.sum(lax.all_gather(vectors, AXES, axis=0), axis=0)
    loss = vectors[11, 1]
    side_sums = vectors[5:11]

    own_top = team_scatter(top_total, groups["z"], count).astype(F32)
    own_deep = z_stage(deep_z, groups, count)
    joint = plane_stage_joint(two_plane, last_plane, groups, count, [feature_grad])
    joint = z_stage(joint, groups, count)
    own_two, own_last = joint[:rows], joint[rows:]
    own_one = own_last[:rows]
    spills = own_last[rows : rows + MISC_ROW]
    row = lax.broadcasted_iota(jnp.int32, spills.shape, 0)
    beyond = (row % SPILL_ROWS >= EXTRA) & (index == count - 1)
    spills = jnp.where(beyond, 0.0, spills)
    wide_biases = jnp.concatenate(
        [vectors[:2, :H], side_sums[:, D].reshape(2, EXTRA)], axis=1
    )
    wide_biases = jnp.pad(wide_biases, ((0, 0), (0, count * wide_piece - D)))
    wide_biases = lax.dynamic_slice(wide_biases, (0, index * wide_piece), (2, wide_piece))
    units = lax.dynamic_slice(vectors[2:5], (0, index * rows), (3, rows))
    side_sums = jnp.pad(side_sums[:, :D], ((0, 0), (0, WIDE - D)))
    side_sums = lax.dynamic_slice(side_sums, (0, index * rows), (6, rows + SPILL_ROWS)).T

    def whole_block(main, number):
        low = number * SPILL_ROWS
        body = jnp.concatenate([main, spills[low : low + SPILL_ROWS]])
        if number == 2:
            return body
        return jnp.concatenate([body, side_sums[:, 3 * number : 3 * number + 3]], axis=1)

    flat_grad = jnp.concatenate(
        [
            from_block(whole_block(own_one, 0), index, sizes[0], rows, count),
            wide_biases[0],
            from_block(whole_block(own_two, 1), index, sizes[2], rows, count),
            wide_biases[1],
            from_block(whole_block(own_deep, 2), index, sizes[4], rows, count),
            units[0],
            own_top.reshape(-1),
            units[1],
            units[2],
            jnp.where(index == 0, vectors[11, :1], 0.0),
        ]
    )
    new_moment_one = 0.9 * moment_one + 0.1 * flat_grad
    new_moment_two = 0.999 * moment_two + 0.001 * flat_grad * flat_grad
    corrected_one = new_moment_one / (1.0 - 0.9**STEP)
    corrected_two = new_moment_two / (1.0 - 0.999**STEP)
    new_master = master - 0.03 * (corrected_one / (jnp.sqrt(corrected_two) + 1e-08) + 0.01 * master)
    new_bias = jnp.concatenate(
        [new_master[starts[i] : starts[i] + sizes[i]] for i in (1, 3, 5, 7, 9)]
    )
    return (
        logits.reshape(-1),
        loss,
        feature_grad.T,
        flat_grad,
        new_moment_one,
        new_moment_two,
        new_master,
        new_bias,
    )


def solution(mesh):
    line = P(AXES)
    table = P(AXES, None)
    groups = bit_groups(mesh)
    return jax.shard_map(
        functools.partial(local, groups),
        mesh=mesh,
        in_specs=(table, line, line, line, line, line),
        out_specs=(line, P(), table, line, line, line, line, line),
        check_vma=False,
    )
```

```python
import functools
import math

import jax
import jax.numpy as jnp
from jax import lax
from jax.experimental import pallas as pl
from jax.experimental.pallas import tpu as pltpu
from jax.sharding import PartitionSpec as P

D = 1027
H = 1024
DAYS = 24
STEP = 10
AXES = ("dp", "cores")
EXTRA = D - H
LANES = 128
WIDE = H + LANES
AUX_ROWS = 16
SPILL_ROWS = 4
MISC_ROW = 12
UNIT_LINES = 15
TILE = 512
TALL = H + 16
MIB = 1024 * 1024
F32 = jnp.float32
LOW = jnp.bfloat16
SMEM = pl.BlockSpec(memory_space=pltpu.SMEM)
VMEM = pl.BlockSpec(memory_space=pltpu.VMEM)
PARAMS = pltpu.CompilerParams(vmem_limit_bytes=56 * MIB)


def shapes():
    return [(D, D), (D,), (D, D), (D,), (D, H), (H,), (H, H), (H,), (H,), (1,)]


def piece_sizes(count):
    return [(math.prod(shape) + count - 1) // count for shape in shapes()[:-1]] + [1]


def starts_of(count):
    starts = []
    position = 0
    for piece in piece_sizes(count):
        starts.append(position)
        position += piece
    return starts


def to_block(piece, index, width, rows, count):
    excess = piece.shape[0] - rows * width
    size = (rows + SPILL_ROWS) * width
    lead = (count - 1) * excess
    padded = jnp.pad(piece, (lead, max(0, size - piece.shape[0])))
    line = lax.dynamic_slice(padded, (lead - index * excess,), (size,))
    return line.reshape(rows + SPILL_ROWS, width)


def from_block(block, index, piece, rows, count):
    width = block.shape[1]
    excess = piece - rows * width
    last = (count - 1) * excess
    line = jnp.pad(block.reshape(-1), (0, max(0, last + piece - block.size)))
    return lax.dynamic_slice(line, (index * excess,), (piece,))


def bit_groups(mesh):
    devices = mesh.devices.reshape(-1)
    groups = {"z": [], "plane": [], "core": []}
    bit = 1
    while bit < devices.size:
        here = getattr(devices[0], "coords", None)
        there = getattr(devices[bit], "coords", None)
        if here is None or there is None:
            name = "core" if bit == 1 else "plane" if bit <= 4 else "z"
        elif tuple(here) == tuple(there):
            name = "core"
        elif here[2] != there[2]:
            name = "z"
        else:
            name = "plane"
        groups[name].append(bit)
        bit *= 2
    return groups


def masks_of(bits):
    masks = [0]
    for bit in bits:
        masks = masks + [mask | bit for mask in masks]
    return masks


def teams(bits, count):
    masks = masks_of(bits)
    return [[k | mask for mask in masks] for k in range(count) if not k & masks[-1]]


def owner(index, mask, groups, by_z):
    if by_z:
        index = jnp.bitwise_and(index, ~masks_of(groups["z"])[-1])
    return jnp.bitwise_xor(index, mask)


def swap(value, mask, count):
    return lax.ppermute(value, AXES, [(k, k ^ mask) for k in range(count)])


def join(parts, after):
    def kernel(*refs):
        for j in range(len(parts)):
            refs[-1][j] = refs[j][...]

    return pl.pallas_call(
        kernel,
        out_shape=jax.ShapeDtypeStruct((len(parts),) + parts[0].shape, parts[0].dtype),
        in_specs=[VMEM] * len(parts) + [pl.BlockSpec(memory_space=pl.ANY)] * len(after),
        out_specs=VMEM,
        compiler_params=PARAMS,
        name="join",
    )(*parts, *after)


def gather(block, groups, count, direct=False, after=()):
    z_masks = masks_of(groups["z"])
    core_masks = masks_of(groups["core"])
    line = [block] + [swap(block, mask, count) for mask in z_masks[1:]]
    line = join(line, after) if after else jnp.stack(line)
    plane = [(line, z_masks)]
    if len(groups["plane"]) == 2 and len(z_masks) > 1 and not direct:
        one, two = groups["plane"]
        half = len(z_masks) // 2
        by_one = swap(line, one, count)
        by_two = swap(line, two, count)
        plane.append((by_one, [one ^ z for z in z_masks]))
        plane.append((by_two, [two ^ z for z in z_masks]))
        both = one ^ two
        plane.append((swap(by_one[:half], two, count), [both ^ z for z in z_masks[:half]]))
        plane.append((swap(by_two[half:], one, count), [both ^ z for z in z_masks[half:]]))
    else:
        for mask in masks_of(groups["plane"])[1:]:
            plane.append((swap(line, mask, count), [mask ^ z for z in z_masks]))
    result = list(plane)
    for core in core_masks[1:]:
        result += [(swap(value, core, count), [core ^ m for m in row]) for value, row in plane]
    return result


def place(index, stacks, rows, count, parts, aux=None):
    sources = [value for value, _ in stacks]
    masks = [row for _, row in stacks]
    carries = aux is None
    top = min(16, rows)

    def kernel(index_ref, *refs):
        refs = list(refs)
        aux_ref = refs.pop() if carries else refs.pop(0)
        outs = refs[len(sources) :]
        for ref, row in zip(refs, masks):
            for j, mask in enumerate(row):
                at = jnp.bitwise_xor(index_ref[0], mask)
                for i, out_ref in enumerate(outs):
                    out_ref[at] = ref[j, i * rows : (i + 1) * rows]
                if carries:
                    aux_ref[at] = ref[j, len(outs) * rows :]
        for spill_at, out_ref in zip(parts, outs):
            if spill_at is None:
                continue
            for k in range(1, count):
                spill = aux_ref[k - 1].astype(F32)[spill_at : spill_at + SPILL_ROWS]
                old = out_ref[k, :top].astype(F32)
                new = old[:SPILL_ROWS] + spill
                if top > SPILL_ROWS:
                    new = jnp.concatenate([new, old[SPILL_ROWS:]], axis=0)
                out_ref[k, :top] = new.astype(LOW)

    out_shape = [jax.ShapeDtypeStruct((count, rows, H), LOW)] * len(parts)
    if carries:
        out_shape.append(jax.ShapeDtypeStruct((count, AUX_ROWS, H), LOW))
    extra = [] if carries else [aux]
    result = pl.pallas_call(
        kernel,
        out_shape=out_shape,
        in_specs=[SMEM] + [VMEM] * (len(extra) + len(sources)),
        out_specs=[VMEM] * len(out_shape),
        compiler_params=PARAMS,
        name="place",
    )(index, *extra, *sources)
    return [value.reshape(H, H) for value in result[: len(parts)]] + list(result[len(parts) :])


def split(index, value, masks, kinds, groups, by_z):
    def kernel(index_ref, value_ref, *out_refs):
        for ref, row, kind in zip(out_refs, masks, kinds):
            for j, mask in enumerate(row):
                ref[j] = value_ref[owner(index_ref[0], mask, groups, by_z)].astype(kind)

    shape = value.shape[1:]
    return pl.pallas_call(
        kernel,
        out_shape=[
            jax.ShapeDtypeStruct((len(row),) + shape, kind) for row, kind in zip(masks, kinds)
        ],
        in_specs=[SMEM, VMEM],
        out_specs=[VMEM] * len(masks),
        compiler_params=PARAMS,
        name="split",
    )(index, value)


def halves(groups):
    z_masks, plane_masks, core_masks = (masks_of(groups[g]) for g in ("z", "plane", "core"))
    inner = [p ^ z for p in plane_masks for z in z_masks]
    return [[core ^ m for m in inner] for core in core_masks]


def kinds_of(groups):
    return [F32] + [LOW] * (len(halves(groups)) - 1)


def adder(name, body, ins, outs, after):
    def kernel(*refs):
        body(refs[: len(ins)], refs[len(ins) + len(after) :])

    result = pl.pallas_call(
        kernel,
        out_shape=outs,
        in_specs=[VMEM] * len(ins) + [pl.BlockSpec(memory_space=pl.ANY)] * len(after),
        out_specs=[VMEM] * len(outs),
        compiler_params=PARAMS,
        name=name,
    )(*ins, *after)
    return list(result)


def core_stage(stacks, groups, count, after=()):
    z_count, plane_count = len(masks_of(groups["z"])), len(masks_of(groups["plane"]))
    cores = masks_of(groups["core"])[1:]
    gotten = [swap(stack, core, count) for core, stack in zip(cores, stacks[1:])]
    shape = (z_count,) + stacks[0].shape[1:]

    def body(ins, outs):
        for p, out_ref in enumerate(outs):
            for z in range(z_count):
                total = ins[0][p * z_count + z]
                for ref in ins[1:]:
                    total = total + ref[p * z_count + z].astype(F32)
                out_ref[z] = total.astype(out_ref.dtype)

    outs = [jax.ShapeDtypeStruct(shape, F32 if p == 0 else LOW) for p in range(plane_count)]
    return adder("core_sum", body, [stacks[0]] + gotten, outs, after)


def plane_swaps(parts, groups, count):
    masks = masks_of(groups["plane"])[1:]
    return [parts[0]] + [swap(part, mask, count) for mask, part in zip(masks, parts[1:])]


def plane_stage(parts, groups, count, after=()):
    def body(ins, outs):
        for z in range(ins[0].shape[0]):
            total = ins[0][z]
            for ref in ins[1:]:
                total = total + ref[z].astype(F32)
            outs[0][z] = total

    outs = [jax.ShapeDtypeStruct(parts[0].shape, F32)]
    return adder("plane_sum", body, plane_swaps(parts, groups, count), outs, after)[0]


def plane_stage_z(parts, groups, count, after=()):
    def body(ins, outs):
        for z, out_ref in enumerate(outs):
            total = ins[0][z]
            for ref in ins[1:]:
                total = total + ref[z].astype(F32)
            out_ref[...] = total.astype(out_ref.dtype)

    many, rows, width = parts[0].shape
    outs = [jax.ShapeDtypeStruct((rows, width), F32 if z == 0 else LOW) for z in range(many)]
    return adder("plane_sum", body, plane_swaps(parts, groups, count), outs, after)


def z_stage(parts, groups, count):
    own = parts[0]
    for mask, part in zip(masks_of(groups["z"])[1:], parts[1:]):
        own = own + swap(part, mask, count).astype(F32)
    return own


def z_scatter(total, groups, count):
    if not groups["z"]:
        return total[0]
    return lax.psum_scatter(
        total, AXES, scatter_dimension=0, axis_index_groups=teams(groups["z"], count)
    )


def product(left, right):
    return lax.dot_general(left, right, (((1,), (0,)), ((), ())), preferred_element_type=F32)


def outer(left, right):
    return lax.dot_general(left, right, (((1,), (1,)), ((), ())), preferred_element_type=F32)


def gelu_both(value):
    scale = math.sqrt(2.0 / math.pi)
    square = value * value
    share = 0.5 + 0.5 * jnp.tanh(value * (scale + scale * 0.044715 * square))
    result = value * share
    slope = share + result * (1.0 - share) * (2.0 * scale + 6.0 * scale * 0.044715 * square)
    return result, slope


def columns(height, tile=TILE):
    return pl.BlockSpec((height, tile), lambda i: (0, i))


def whole(*shape):
    return pl.BlockSpec(shape, lambda i: (0,) * len(shape))


def once(*shape):
    return pl.BlockSpec(shape, lambda i: (0,) * len(shape), pipeline_mode=pl.Buffered(1))


def shaped(kind, *shape):
    return jax.ShapeDtypeStruct(shape, kind)


def pieces_of(width):
    return [(a, a + 256) for a in range(0, width, 256)]


def run(name, kernel, batch, in_specs, out_specs, out_shape, scratch, flops, *args, tile=TILE):
    moved = sum(a.size * a.dtype.itemsize for a in args)
    moved += sum(math.prod(o.shape) * o.dtype.itemsize for o in out_shape)
    return pl.pallas_call(
        kernel,
        grid=(batch // tile,),
        in_specs=in_specs,
        out_specs=out_specs,
        out_shape=out_shape,
        scratch_shapes=scratch,
        compiler_params=PARAMS,
        cost_estimate=pl.CostEstimate(flops=flops, bytes_accessed=moved, transcendentals=0),
        name=name,
    )(*args)


def first_step():
    return pl.when(pl.program_id(0) == 0)


def last_step():
    return pl.when(pl.program_id(0) == pl.num_programs(0) - 1)


def turn(out_ref, matrix_ref, tail_ref=None, edge_ref=None):
    for a, b in pieces_of(H):
        out_ref[a:b, :H] = matrix_ref[:, a:b].T
    if tail_ref is not None:
        out_ref[:H, H:] = tail_ref[...].T
    if edge_ref is not None:
        out_ref[H:, :] = edge_ref[...]


def straight(out_ref, matrix_ref, tail_ref, edge_ref=None):
    out_ref[:H, :H] = matrix_ref[...]
    row = lax.broadcasted_iota(jnp.int32, (TALL - H, H), 0)
    tail = tail_ref[: TALL - H, :].astype(F32)
    out_ref[H:, :H] = jnp.where(row < EXTRA, tail, 0.0).astype(LOW)
    if edge_ref is not None:
        lane = lax.broadcasted_iota(jnp.int32, (TALL - H, WIDE), 1)
        edge = jnp.where(lane < D, edge_ref[...].astype(F32), 0.0)
        edge = jnp.concatenate([edge, jnp.zeros((LANES - (TALL - H), WIDE), F32)])
        out_ref[:, H:] = edge.T[:TALL].astype(LOW)


def widen(out_ref, value_ref):
    @first_step()
    def _():
        out_ref[TALL:] = jnp.zeros((WIDE - TALL, out_ref.shape[1]), LOW)

    out_ref[:TALL] = value_ref[...]


class Spread:
    def __init__(self, groups, rows, count, parts=1, below=False, by_z=False):
        self.groups, self.by_z = groups, by_z
        self.masks = halves(groups)
        self.kinds = kinds_of(groups)
        self.rows, self.count, self.parts, self.below = rows, count, parts, below
        self.direct = rows % 16 == 0

    def shapes(self):
        if not self.direct:
            return [shaped(F32, TALL, H)] * self.parts
        height = self.rows * self.parts + (AUX_ROWS if self.below else 0)
        outs = [shaped(kind, len(row), height, H) for row, kind in zip(self.masks, self.kinds)]
        overs = 0 if self.below else self.parts
        return outs + [shaped(F32, self.count, 8, H)] * overs

    def specs(self):
        return [whole(*s.shape) for s in self.shapes()]

    def write(self, acc_refs, index_ref, out_refs, over_refs=None):
        if not self.direct:
            for acc_ref, ref in zip(acc_refs, out_refs):
                ref[...] = acc_ref[...]
            return
        rows = self.rows
        for ref, row, kind in zip(out_refs, self.masks, self.kinds):
            for j, mask in enumerate(row):
                at = owner(index_ref[0], mask, self.groups, self.by_z)
                start = pl.multiple_of(at * rows, rows)
                for i, acc_ref in enumerate(acc_refs):
                    block = acc_ref[pl.ds(start, rows), :]
                    ref[j, i * rows : (i + 1) * rows] = block.astype(kind)
                if self.below:
                    mine = acc_ref[pl.ds(pl.multiple_of(start + rows, 8), 8), :]
                    parts = [mine[:SPILL_ROWS]] + [v[at][:SPILL_ROWS] for v in over_refs]
                    parts.append(jnp.zeros((AUX_ROWS - MISC_ROW, H), F32))
                    ref[j, rows:] = jnp.concatenate(parts).astype(kind)
        if not self.below:
            for acc_ref, ref in zip(acc_refs, out_refs[len(self.masks) :]):
                for k in range(self.count):
                    ref[k] = acc_ref[(k + 1) * rows : (k + 1) * rows + 8, :]

    def finish(self, outs, index, overs=None):
        if self.direct:
            return list(outs)
        rows, count = self.rows, self.count
        blocks = [grad[:H].reshape(count, rows, H) for grad in outs]
        own = [
            jnp.stack([grad[(k + 1) * rows : (k + 1) * rows + 8] for k in range(count)])
            for grad in outs
        ]
        if self.below:
            blocks += [v[:, :SPILL_ROWS] for v in own + list(overs)]
            blocks.append(jnp.zeros((count, AUX_ROWS - MISC_ROW, H), F32))
        stacks = split(
            index, jnp.concatenate(blocks, axis=1), self.masks, self.kinds, self.groups, self.by_z
        )
        stacks = list(stacks)
        return stacks if self.below else stacks + own


ANY = pl.BlockSpec(memory_space=pl.ANY)
REST = TALL - H


def forward_cross(features, one, two):
    batch = features.shape[1]

    def kernel(f_ref, *refs):
        x_ref, mixer_one_ref, mixer_two_ref, one_ref, two_ref = refs[6:11]
        turned_one, turned_two, wide_ref = refs[11:]

        @first_step()
        def _():
            turn(turned_one, *refs[:3])
            turn(turned_two, *refs[3:6])

        x_ref[:H] = f_ref[:H]
        last = f_ref[H:].astype(F32)
        last = jnp.concatenate([last, jnp.ones((1, TILE), F32), jnp.zeros((TALL - D - 1, TILE), F32)])
        x_ref[H:] = last.astype(LOW)
        widen(wide_ref, x_ref)
        layers = []
        for a, b in [(0, TILE)]:
            mixer = product(turned_one[...], wide_ref[:, a:b])
            mixer_one_ref[:, a:b] = mixer.astype(LOW)
            part = x_ref[:, a:b].astype(F32)
            layer = part * mixer + part
            layers.append(layer)
            one_ref[:, a:b] = layer.astype(LOW)
        wide_ref[:TALL] = one_ref[...]
        for (a, b), layer in zip([(0, TILE)], layers):
            mixer = product(turned_two[...], wide_ref[:, a:b])
            mixer_two_ref[:, a:b] = mixer.astype(LOW)
            two_ref[:, a:b] = (x_ref[:, a:b].astype(F32) * mixer + layer).astype(LOW)

    return run(
        "forward_cross",
        kernel,
        batch,
        [columns(D)] + [once(H, H), once(LANES, H), once(REST, WIDE)] * 2,
        [columns(TALL)] * 5,
        [shaped(LOW, TALL, batch)] * 5,
        [pltpu.VMEM((TALL, WIDE), LOW)] * 2 + [pltpu.VMEM((WIDE, TILE), LOW)],
        4 * batch * TALL * TALL,
        features, *one, *two,
    )


def deep(spread, index, layer_low, examples, matrix_one, tail, matrix, lines, inverse):
    batch = layer_low.shape[1]
    days = inverse.shape[0]

    def kernel(k_ref, l_ref, x_ref, w_one_ref, t_ref, w_ref, n_ref, i_ref, *refs):
        logit_ref, back_ref, line_ref, sum_ref = refs[:4]
        out_refs = refs[4:-8]
        turned_one, turned, acc_ref, hidden_ref, slope_ref, low_ref, part_ref, wide_ref = refs[-8:]

        @first_step()
        def _():
            turn(turned_one, w_one_ref, t_ref)
            turn(turned, w_ref)
            acc_ref[...] = jnp.zeros_like(acc_ref)
            sum_ref[...] = jnp.zeros_like(sum_ref)
            part_ref[...] = jnp.zeros_like(part_ref)
            row = lax.broadcasted_iota(jnp.int32, (REST, TILE), 0)
            hidden_ref[H:] = jnp.where(row == 0, 1.0, 0.0).astype(LOW)

        widen(wide_ref, l_ref)
        for a, b in pieces_of(TILE):
            hidden, slope = gelu_both(product(turned_one[...], wide_ref[:, a:b]))
            hidden_ref[:H, a:b] = hidden.astype(LOW)
            slope_ref[:, a:b] = slope
        head = n_ref[:, 1:2]
        for a, b in pieces_of(TILE):
            two, slope = gelu_both(product(turned[...], hidden_ref[:H, a:b]) + n_ref[:, 0:1])
            two = two.astype(LOW).astype(F32)
            logits = n_ref[0:1, 2:3] + jnp.sum(two * head, axis=0, keepdims=True)
            label = x_ref[0:1, a:b]
            day = x_ref[1:2, a:b].astype(jnp.int32)
            row = lax.broadcasted_iota(jnp.int32, (days, b - a), 0)
            weight = jnp.sum(jnp.where(row == day, i_ref[:, 0:1], 0.0), axis=0, keepdims=True)
            decay = jnp.exp(-jnp.abs(logits))
            entropy = jnp.maximum(logits, 0.0) + jnp.log1p(decay) - label * logits
            chance = jnp.where(logits >= 0.0, 1.0, decay) / (1.0 + decay)
            logit_grad = (chance - label) * weight
            logit_ref[:, a:b] = logits
            sum_ref[0:1, a:b] += logit_grad
            sum_ref[1:2, a:b] += entropy * weight
            low_ref[:, a:b] = ((logit_grad * head) * slope).astype(LOW)
            one = logit_grad * two
            part = one[:, :LANES]
            for at in range(LANES, b - a, LANES):
                part = part + one[:, at : at + LANES]
            part_ref[...] += part
        for a, b in pieces_of(TILE):
            back_ref[:, a:b] = (product(w_ref[...], low_ref[:, a:b]) * slope_ref[:, a:b]).astype(LOW)
        for a, b in pieces_of(H):
            acc_ref[:, a:b] += outer(hidden_ref[...], low_ref[a:b])

        @last_step()
        def _():
            line_ref[0:8] = jnp.broadcast_to(
                jnp.sum(part_ref[...].T, axis=0, keepdims=True), (8, H)
            )
            line_ref[8:16] = acc_ref[H : H + 8]
            spread.write([acc_ref], k_ref, out_refs)

    return run(
        "deep",
        kernel,
        batch,
        [
            SMEM,
            columns(TALL),
            columns(2),
            once(H, H),
            once(LANES, H),
            once(H, H),
            whole(H, LANES),
            whole(days, LANES),
        ],
        [columns(1), columns(H), whole(16, H), whole(8, TILE)] + spread.specs(),
        [
            shaped(F32, 1, batch),
            shaped(LOW, H, batch),
            shaped(F32, 16, H),
            shaped(F32, 8, TILE),
        ]
        + spread.shapes(),
        [
            pltpu.VMEM((H, WIDE), LOW),
            pltpu.VMEM((H, H), LOW),
            pltpu.VMEM((TALL, H), F32),
            pltpu.VMEM((TALL, TILE), LOW),
            pltpu.VMEM((H, TILE), F32),
            pltpu.VMEM((H, TILE), LOW),
            pltpu.VMEM((H, LANES), F32),
            pltpu.VMEM((WIDE, TILE), LOW),
        ],
        8 * batch * H * H,
        index, layer_low, examples, matrix_one, tail, matrix, lines, inverse,
    )


def back_deep(spread, index, grad_low, layer_low, features, matrix, tail, after):
    batch = features.shape[1]

    def kernel(k_ref, g_ref, l_ref, x_ref, w_ref, t_ref, *refs):
        refs = refs[len(after) :]
        layer_ref, mixer_ref, line_ref = refs[:3]
        out_refs = refs[3:-2]
        held, acc_ref = refs[-2:]

        @first_step()
        def _():
            straight(held, w_ref, t_ref)
            acc_ref[...] = jnp.zeros_like(acc_ref)

        for a, b in pieces_of(TILE):
            layer = product(held[...], g_ref[:, a:b])
            layer_ref[:, a:b] = layer
            mixer_ref[:, a:b] = (layer * x_ref[:, a:b].astype(F32)).astype(LOW)
        for a, b in pieces_of(H):
            acc_ref[:, a:b] += outer(l_ref[...], g_ref[a:b])

        @last_step()
        def _():
            line_ref[...] = acc_ref[H:]
            spread.write([acc_ref], k_ref, out_refs)

    return run(
        "back_deep",
        kernel,
        batch,
        [SMEM, columns(H), columns(TALL), columns(TALL), once(H, H), once(LANES, H)]
        + [ANY] * len(after),
        [columns(TALL), columns(TALL), whole(REST, H)] + spread.specs(),
        [shaped(F32, TALL, batch), shaped(LOW, TALL, batch), shaped(F32, REST, H)]
        + spread.shapes(),
        [pltpu.VMEM((TALL, H), LOW), pltpu.VMEM((TALL, H), F32)],
        4 * batch * TALL * H,
        index, grad_low, layer_low, features, matrix, tail, *after,
    )


def back_two(
    spread, index, mixer_low, layer_low, layer_grad, features, mixer_one, mixer_two, matrix, tail,
    edge, lines, after,
):
    batch = features.shape[1]

    def kernel(k_ref, g_ref, l_ref, d_ref, x_ref, one_ref, two_ref, w_ref, t_ref, e_ref, *refs):
        top_ref, deep_ref, sums_ref = refs[:3]
        refs = refs[3 + len(after) :]
        part_ref, mixer_ref, vector_ref = refs[:3]
        out_refs = refs[3:-6]
        held, acc_ref, wide_ref, sum_ref, side_ref, next_side_ref = refs[-6:]

        @first_step()
        def _():
            straight(held, w_ref, t_ref, e_ref)
            acc_ref[...] = jnp.zeros_like(acc_ref)
            side_ref[...] = jnp.zeros_like(side_ref)
            next_side_ref[...] = jnp.zeros_like(next_side_ref)
            sum_ref[...] = jnp.zeros_like(sum_ref)

        widen(wide_ref, g_ref)
        for a, b in pieces_of(TILE):
            above = d_ref[:, a:b]
            layer = product(held[...], wide_ref[:, a:b]) + above
            mixer = (layer * x_ref[:, a:b].astype(F32)).astype(LOW)
            mixer_ref[:, a:b] = mixer
            mixer = mixer[:H].astype(F32)
            total = mixer[:, :LANES]
            for at in range(LANES, b - a, LANES):
                total = total + mixer[:, at : at + LANES]
            sum_ref[...] += total
            part = above * two_ref[:, a:b].astype(F32)
            part = part + layer * (one_ref[:, a:b].astype(F32) + 1.0)
            part_ref[:, a:b] = part.astype(LOW)
        for a, b in pieces_of(H):
            acc_ref[:, a:b] += outer(l_ref[...], g_ref[a:b])
        side_ref[...] += outer(g_ref[H:], l_ref[...])
        next_side_ref[...] += outer(mixer_ref[H:], x_ref[...])

        @last_step()
        def _():
            vector_ref[...] = jnp.zeros_like(vector_ref)
            vector_ref[0:1, :H] = jnp.sum(sum_ref[...].T, axis=0, keepdims=True)
            vector_ref[1:2, :H] = acc_ref[D : D + 1]
            vector_ref[2:3, :H] = deep_ref[EXTRA : EXTRA + 1]
            vector_ref[3:4, :H] = top_ref[8:9]
            vector_ref[4:5, :H] = top_ref[0:1]
            vector_ref[5:8, :TALL] = next_side_ref[:EXTRA]
            vector_ref[8:11, :TALL] = side_ref[:EXTRA]
            lane = lax.broadcasted_iota(jnp.int32, (1, LANES), 1)
            bias = jnp.sum(sums_ref[0:1], axis=1, keepdims=True)
            loss = jnp.sum(sums_ref[1:2], axis=1, keepdims=True)
            vector_ref[11:12, :LANES] = jnp.where(lane == 0, bias, jnp.where(lane == 1, loss, 0.0))
            spread.write([acc_ref], k_ref, out_refs)

    return run(
        "back_two",
        kernel,
        batch,
        [SMEM]
        + [columns(TALL)] * 6
        + [once(H, H), once(LANES, H), once(REST, WIDE)]
        + [whole(*v.shape) for v in lines]
        + [ANY] * len(after),
        [columns(TALL), columns(TALL)]
        + [whole(16, WIDE)]
        + spread.specs(),
        [
            shaped(LOW, TALL, batch),
            shaped(LOW, TALL, batch),
            shaped(F32, 16, WIDE),
        ]
        + spread.shapes(),
        [
            pltpu.VMEM((TALL, WIDE), LOW),
            pltpu.VMEM((TALL, H), F32),
            pltpu.VMEM((WIDE, TILE), LOW),
            pltpu.VMEM((H, LANES), F32),
            pltpu.VMEM((REST, TALL), F32),
            pltpu.VMEM((REST, TALL), F32),
        ],
        4 * batch * TALL * TALL,
        index, mixer_low, layer_low, layer_grad, features, mixer_one, mixer_two, matrix, tail,
        edge, *lines, *after,
    )


def grad_one(spread, index, mixer_low, features, overs, after):
    batch = features.shape[1]

    def kernel(k_ref, g_ref, x_ref, *refs):
        over_refs = refs[: len(overs)]
        out_refs = refs[len(overs) + len(after) : -1]
        acc_ref = refs[-1]

        @first_step()
        def _():
            acc_ref[...] = jnp.zeros_like(acc_ref)

        for a, b in pieces_of(H):
            acc_ref[:, a:b] += outer(x_ref[...], g_ref[a:b])

        @last_step()
        def _():
            spread.write([acc_ref], k_ref, out_refs, over_refs)

    return run(
        "grad_one",
        kernel,
        batch,
        [SMEM, columns(TALL), columns(TALL)]
        + [once(*v.shape) for v in overs]
        + [ANY] * len(after),
        spread.specs(),
        spread.shapes(),
        [pltpu.VMEM((TALL, H), F32)],
        2 * batch * TALL * TALL,
        index, mixer_low, features, *overs, *after,
    )


def back_one(mixer_low, part, matrix, tail, edge, after):
    batch = part.shape[1]

    def kernel(g_ref, p_ref, w_ref, t_ref, e_ref, *refs):
        out_ref, held, wide_ref = refs[len(after) :]

        @first_step()
        def _():
            straight(held, w_ref, t_ref, e_ref)

        widen(wide_ref, g_ref)
        for a, b in [(0, TILE)]:
            value = p_ref[:, a:b].astype(F32) + product(held[...], wide_ref[:, a:b])
            out_ref[:H, a:b] = value[:H]
            out_ref[H:, a:b] = value[H:D]

    return run(
        "back_one",
        kernel,
        batch,
        [columns(TALL), columns(TALL), whole(H, H), whole(LANES, H), whole(REST, WIDE)]
        + [ANY] * len(after),
        [columns(D)],
        [shaped(F32, D, batch)],
        [pltpu.VMEM((TALL, WIDE), LOW), pltpu.VMEM((WIDE, TILE), LOW)],
        2 * batch * TALL * TALL,
        mixer_low, part, matrix, tail, edge, *after,
    )[0]


def local(groups, features, labels, days, master, moment_one, moment_two):
    count = lax.axis_size(AXES)
    index = lax.axis_index(AXES)
    slot = index[None].astype(jnp.int32)
    rows = H // count
    starts = starts_of(count)
    sizes = piece_sizes(count)
    wide_piece = sizes[1]
    piece = [master[a : a + l] for a, l in zip(starts, sizes)]
    block_one = to_block(piece[0], index, D, rows, count)
    block_two = to_block(piece[2], index, D, rows, count)
    block_deep = to_block(piece[4], index, H, rows, count)

    day_hot = (days[:, None] == jnp.arange(DAYS, dtype=jnp.int32)[None, :]).astype(F32)
    own_counts = jnp.sum(day_hot, axis=0)
    counts_high = jnp.floor(own_counts / 64.0)
    counts_low = own_counts - 64.0 * counts_high

    def spill_side(block):
        side = block[rows:, H:].T
        return jnp.pad(side, ((0, 0), (0, rows - SPILL_ROWS)))

    misc = [
        piece[5],
        piece[7],
        piece[8],
        block_one[:rows, H:].T,
        block_two[:rows, H:].T,
        spill_side(block_one),
        spill_side(block_two),
        piece[1],
        piece[3],
        piece[9],
        counts_high,
        counts_low,
    ]
    misc = jnp.concatenate([part.reshape(-1) for part in misc])
    misc = jnp.pad(misc, (0, (AUX_ROWS - MISC_ROW) * H - misc.shape[0])).reshape(-1, H)
    first = jnp.concatenate(
        [
            block_one[:rows, :H],
            block_two[:rows, :H],
            block_one[rows:, :H],
            block_two[rows:, :H],
            block_deep[rows:],
            misc,
        ]
    ).astype(LOW)
    stacks_cross = gather(first, groups, count)
    rest = jnp.concatenate([block_deep[:rows], piece[6].reshape(rows, H)]).astype(LOW)
    crossed = [value for value, _ in stacks_cross[3:5]]
    stacks_rest = gather(rest, groups, count, direct=True, after=crossed)
    examples = jnp.stack([labels.astype(F32), days.astype(F32)])

    matrix_one, matrix_two, aux = place(slot, stacks_cross, rows, count, [0, SPILL_ROWS])
    matrix_deep, matrix_top = place(slot, stacks_rest, rows, count, [2 * SPILL_ROWS, None], aux)

    line = aux[:, MISC_ROW]
    at = UNIT_LINES * rows
    units = line[:, :at].reshape(count, UNIT_LINES, rows).transpose(1, 0, 2).reshape(UNIT_LINES, H)
    biases = line[:, at : at + 2 * wide_piece].reshape(count, 2, wide_piece)
    biases = biases.transpose(1, 0, 2).reshape(2, count * wide_piece)
    at += 2 * wide_piece
    head_bias = line[0, at]
    both_counts = jnp.sum(line[:, at + 1 : at + 1 + 2 * DAYS].astype(F32), axis=0)
    counts = 64.0 * both_counts[:DAYS] + both_counts[DAYS:]
    inverse = jnp.broadcast_to((1.0 / counts)[:, None], (DAYS, LANES))
    sides = jnp.pad(units[3:9], ((0, 0), (0, LANES))) + jnp.pad(
        units[9:15], ((0, 0), (rows, LANES - rows))
    )

    def tail_of(at, bias):
        return jnp.concatenate(
            [aux[count - 1, at : at + EXTRA], bias[None, :H], jnp.zeros((LANES - EXTRA - 1, H), LOW)]
        )

    def edge_of(side, bias):
        lane = lax.broadcasted_iota(jnp.int32, side.shape, 1)
        side = jnp.where(lane == D, bias[H:D, None], side)
        return jnp.pad(side, ((0, TALL - H - EXTRA), (0, 0)))

    tail_one, edge_one = tail_of(0, biases[0]), edge_of(sides[:3], biases[0])
    tail_two, edge_two = tail_of(SPILL_ROWS, biases[1]), edge_of(sides[3:], biases[1])
    tail_deep = tail_of(2 * SPILL_ROWS, units[0])
    lines = jnp.concatenate(
        [units[1:3], jnp.full((1, H), head_bias), jnp.zeros((LANES - 3, H), LOW)]
    )
    lines = lines.astype(F32).T
    spread = Spread(groups, rows, count, by_z=True)
    spread_last = Spread(groups, rows, count, below=True)

    wide_features, mixer_one, mixer_two, low_one, low_two = forward_cross(
        features.T, (matrix_one, tail_one, edge_one), (matrix_two, tail_two, edge_two)
    )
    logits, pre_one_low, top_lines, sums, *outs = deep(
        spread, slot, low_two, examples, matrix_deep, tail_deep, matrix_top, lines, inverse
    )
    *top_stacks, _ = spread.finish(outs, slot)
    layer_grad, mixer_two_low, deep_lines, *outs = back_deep(
        spread, slot, pre_one_low, low_two, wide_features, matrix_deep, tail_deep, []
    )
    *deep_stacks, deep_over = spread.finish(outs, slot)
    top_plane = core_stage(top_stacks, groups, count, [mixer_two_low])
    part, mixer_one_low, vectors, *outs = back_two(
        spread, slot, mixer_two_low, low_one, layer_grad, wide_features, mixer_one, mixer_two,
        matrix_two, tail_two, edge_two, (top_lines, deep_lines, sums), top_plane[1:],
    )
    *two_stacks, two_over = spread.finish(outs, slot)
    top_total = plane_stage(top_plane, groups, count, [mixer_one_low])
    deep_plane = core_stage(deep_stacks, groups, count, [mixer_one_low])
    overs = (two_over, deep_over)
    outs = grad_one(
        spread_last, slot, mixer_one_low, wide_features, overs,
        deep_plane[1:] + [top_total],
    )
    last_stacks = spread_last.finish(outs, slot, overs)
    deep_total = plane_stage(deep_plane, groups, count, last_stacks[:1])
    two_plane = core_stage(two_stacks, groups, count, last_stacks[:1])
    last_plane = core_stage(last_stacks, groups, count)
    feature_grad = back_one(
        mixer_one_low, part, matrix_one, tail_one, edge_one,
        last_plane[1:] + two_plane[1:] + [deep_total],
    )

    vectors = jnp.sum(lax.all_gather(vectors, AXES, axis=0), axis=0)
    loss = vectors[11, 1]
    side_sums = vectors[5:11]

    own_top = z_scatter(top_total, groups, count)
    own_deep = z_scatter(deep_total, groups, count)
    two_total = plane_stage(two_plane, groups, count, [feature_grad])
    own_two = z_scatter(two_total, groups, count)
    own_last = z_stage(plane_stage_z(last_plane, groups, count, [feature_grad, two_total]), groups, count)
    own_one = own_last[:rows]
    spills = own_last[rows : rows + MISC_ROW]
    row = lax.broadcasted_iota(jnp.int32, spills.shape, 0)
    beyond = (row % SPILL_ROWS >= EXTRA) & (index == count - 1)
    spills = jnp.where(beyond, 0.0, spills)
    wide_biases = jnp.concatenate(
        [vectors[:2, :H], side_sums[:, D].reshape(2, EXTRA)], axis=1
    )
    wide_biases = jnp.pad(wide_biases, ((0, 0), (0, count * wide_piece - D)))
    wide_biases = lax.dynamic_slice(wide_biases, (0, index * wide_piece), (2, wide_piece))
    units = lax.dynamic_slice(vectors[2:5], (0, index * rows), (3, rows))
    side_sums = jnp.pad(side_sums[:, :D], ((0, 0), (0, WIDE - D)))
    side_sums = lax.dynamic_slice(side_sums, (0, index * rows), (6, rows + SPILL_ROWS)).T

    def whole_block(main, number):
        low = number * SPILL_ROWS
        body = jnp.concatenate([main, spills[low : low + SPILL_ROWS]])
        if number == 2:
            return body
        return jnp.concatenate([body, side_sums[:, 3 * number : 3 * number + 3]], axis=1)

    flat_grad = jnp.concatenate(
        [
            from_block(whole_block(own_one, 0), index, sizes[0], rows, count),
            wide_biases[0],
            from_block(whole_block(own_two, 1), index, sizes[2], rows, count),
            wide_biases[1],
            from_block(whole_block(own_deep, 2), index, sizes[4], rows, count),
            units[0],
            own_top.reshape(-1),
            units[1],
            units[2],
            jnp.where(index == 0, vectors[11, :1], 0.0),
        ]
    )
    new_moment_one = 0.9 * moment_one + 0.1 * flat_grad
    new_moment_two = 0.999 * moment_two + 0.001 * flat_grad * flat_grad
    corrected_one = new_moment_one / (1.0 - 0.9**STEP)
    corrected_two = new_moment_two / (1.0 - 0.999**STEP)
    new_master = master - 0.03 * (corrected_one / (jnp.sqrt(corrected_two) + 1e-08) + 0.01 * master)
    new_bias = jnp.concatenate(
        [new_master[starts[i] : starts[i] + sizes[i]] for i in (1, 3, 5, 7, 9)]
    )
    return (
        logits.reshape(-1),
        loss,
        feature_grad.T,
        flat_grad,
        new_moment_one,
        new_moment_two,
        new_master,
        new_bias,
    )


def solution(mesh):
    line = P(AXES)
    table = P(AXES, None)
    groups = bit_groups(mesh)
    return jax.shard_map(
        functools.partial(local, groups),
        mesh=mesh,
        in_specs=(table, line, line, line, line, line),
        out_specs=(line, P(), table, line, line, line, line, line),
        check_vma=False,
    )
```

```python
import functools
import math

import jax
import jax.numpy as jnp
from jax import lax
from jax.experimental import pallas as pl
from jax.experimental.pallas import tpu as pltpu
from jax.sharding import PartitionSpec as P

D = 1027
H = 1024
DAYS = 24
STEP = 10
AXES = ("dp", "cores")
EXTRA = D - H
LANES = 128
WIDE = H + LANES
AUX_ROWS = 16
SPILL_ROWS = 4
MISC_ROW = 12
UNIT_LINES = 15
TILE = 512
TALL = H + 16
MIB = 1024 * 1024
F32 = jnp.float32
LOW = jnp.bfloat16
SMEM = pl.BlockSpec(memory_space=pltpu.SMEM)
VMEM = pl.BlockSpec(memory_space=pltpu.VMEM)
PARAMS = pltpu.CompilerParams(vmem_limit_bytes=56 * MIB)


def shapes():
    return [(D, D), (D,), (D, D), (D,), (D, H), (H,), (H, H), (H,), (H,), (1,)]


def piece_sizes(count):
    return [(math.prod(shape) + count - 1) // count for shape in shapes()[:-1]] + [1]


def starts_of(count):
    starts = []
    position = 0
    for piece in piece_sizes(count):
        starts.append(position)
        position += piece
    return starts


def to_block(piece, index, width, rows, count):
    excess = piece.shape[0] - rows * width
    size = (rows + SPILL_ROWS) * width
    lead = (count - 1) * excess
    padded = jnp.pad(piece, (lead, max(0, size - piece.shape[0])))
    line = lax.dynamic_slice(padded, (lead - index * excess,), (size,))
    return line.reshape(rows + SPILL_ROWS, width)


def from_block(block, index, piece, rows, count):
    width = block.shape[1]
    excess = piece - rows * width
    last = (count - 1) * excess
    line = jnp.pad(block.reshape(-1), (0, max(0, last + piece - block.size)))
    return lax.dynamic_slice(line, (index * excess,), (piece,))


def bit_groups(mesh):
    devices = mesh.devices.reshape(-1)
    groups = {"z": [], "plane": [], "core": []}
    bit = 1
    while bit < devices.size:
        here = getattr(devices[0], "coords", None)
        there = getattr(devices[bit], "coords", None)
        if here is None or there is None:
            name = "core" if bit == 1 else "plane" if bit <= 4 else "z"
        elif tuple(here) == tuple(there):
            name = "core"
        elif here[2] != there[2]:
            name = "z"
        else:
            name = "plane"
        groups[name].append(bit)
        bit *= 2
    return groups


def masks_of(bits):
    masks = [0]
    for bit in bits:
        masks = masks + [mask | bit for mask in masks]
    return masks


def teams(bits, count):
    masks = masks_of(bits)
    return [[k | mask for mask in masks] for k in range(count) if not k & masks[-1]]


def owner(index, mask, groups, by_z):
    if by_z:
        index = jnp.bitwise_and(index, ~masks_of(groups["z"])[-1])
    return jnp.bitwise_xor(index, mask)


def swap(value, mask, count):
    return lax.ppermute(value, AXES, [(k, k ^ mask) for k in range(count)])


def join(parts, after):
    def kernel(*refs):
        for j in range(len(parts)):
            refs[-1][j] = refs[j][...]

    return pl.pallas_call(
        kernel,
        out_shape=jax.ShapeDtypeStruct((len(parts),) + parts[0].shape, parts[0].dtype),
        in_specs=[VMEM] * len(parts) + [pl.BlockSpec(memory_space=pl.ANY)] * len(after),
        out_specs=VMEM,
        compiler_params=PARAMS,
        name="join",
    )(*parts, *after)


def gather(block, groups, count, direct=False, after=()):
    z_masks = masks_of(groups["z"])
    core_masks = masks_of(groups["core"])
    line = [block] + [swap(block, mask, count) for mask in z_masks[1:]]
    line = join(line, after) if after else jnp.stack(line)
    plane = [(line, z_masks)]
    if len(groups["plane"]) == 2 and len(z_masks) > 1 and not direct:
        one, two = groups["plane"]
        half = len(z_masks) // 2
        by_one = swap(line, one, count)
        by_two = swap(line, two, count)
        plane.append((by_one, [one ^ z for z in z_masks]))
        plane.append((by_two, [two ^ z for z in z_masks]))
        both = one ^ two
        plane.append((swap(by_one[:half], two, count), [both ^ z for z in z_masks[:half]]))
        plane.append((swap(by_two[half:], one, count), [both ^ z for z in z_masks[half:]]))
    else:
        for mask in masks_of(groups["plane"])[1:]:
            plane.append((swap(line, mask, count), [mask ^ z for z in z_masks]))
    result = list(plane)
    for core in core_masks[1:]:
        result += [(swap(value, core, count), [core ^ m for m in row]) for value, row in plane]
    return result


def place(index, stacks, rows, count, parts, aux=None):
    sources = [value for value, _ in stacks]
    masks = [row for _, row in stacks]
    carries = aux is None
    top = min(16, rows)

    def kernel(index_ref, *refs):
        refs = list(refs)
        aux_ref = refs.pop() if carries else refs.pop(0)
        outs = refs[len(sources) :]
        for ref, row in zip(refs, masks):
            for j, mask in enumerate(row):
                at = jnp.bitwise_xor(index_ref[0], mask)
                for i, out_ref in enumerate(outs):
                    out_ref[at] = ref[j, i * rows : (i + 1) * rows]
                if carries:
                    aux_ref[at] = ref[j, len(outs) * rows :]
        for spill_at, out_ref in zip(parts, outs):
            if spill_at is None:
                continue
            for k in range(1, count):
                spill = aux_ref[k - 1].astype(F32)[spill_at : spill_at + SPILL_ROWS]
                old = out_ref[k, :top].astype(F32)
                new = old[:SPILL_ROWS] + spill
                if top > SPILL_ROWS:
                    new = jnp.concatenate([new, old[SPILL_ROWS:]], axis=0)
                out_ref[k, :top] = new.astype(LOW)

    out_shape = [jax.ShapeDtypeStruct((count, rows, H), LOW)] * len(parts)
    if carries:
        out_shape.append(jax.ShapeDtypeStruct((count, AUX_ROWS, H), LOW))
    extra = [] if carries else [aux]
    result = pl.pallas_call(
        kernel,
        out_shape=out_shape,
        in_specs=[SMEM] + [VMEM] * (len(extra) + len(sources)),
        out_specs=[VMEM] * len(out_shape),
        compiler_params=PARAMS,
        name="place",
    )(index, *extra, *sources)
    return [value.reshape(H, H) for value in result[: len(parts)]] + list(result[len(parts) :])


def split(index, value, masks, kinds, groups, by_z):
    def kernel(index_ref, value_ref, *out_refs):
        for ref, row, kind in zip(out_refs, masks, kinds):
            for j, mask in enumerate(row):
                ref[j] = value_ref[owner(index_ref[0], mask, groups, by_z)].astype(kind)

    shape = value.shape[1:]
    return pl.pallas_call(
        kernel,
        out_shape=[
            jax.ShapeDtypeStruct((len(row),) + shape, kind) for row, kind in zip(masks, kinds)
        ],
        in_specs=[SMEM, VMEM],
        out_specs=[VMEM] * len(masks),
        compiler_params=PARAMS,
        name="split",
    )(index, value)


def halves(groups):
    z_masks, plane_masks, core_masks = (masks_of(groups[g]) for g in ("z", "plane", "core"))
    inner = [p ^ z for p in plane_masks for z in z_masks]
    return [[core ^ m for m in inner] for core in core_masks]


def kinds_of(groups):
    return [F32] + [LOW] * (len(halves(groups)) - 1)


def adder(name, body, ins, outs, after):
    def kernel(*refs):
        body(refs[: len(ins)], refs[len(ins) + len(after) :])

    result = pl.pallas_call(
        kernel,
        out_shape=outs,
        in_specs=[VMEM] * len(ins) + [pl.BlockSpec(memory_space=pl.ANY)] * len(after),
        out_specs=[VMEM] * len(outs),
        compiler_params=PARAMS,
        name=name,
    )(*ins, *after)
    return list(result)


def core_stage(stacks, groups, count, after=()):
    z_count, plane_count = len(masks_of(groups["z"])), len(masks_of(groups["plane"]))
    cores = masks_of(groups["core"])[1:]
    gotten = [swap(stack, core, count) for core, stack in zip(cores, stacks[1:])]
    shape = (z_count,) + stacks[0].shape[1:]

    def body(ins, outs):
        for p, out_ref in enumerate(outs):
            for z in range(z_count):
                total = ins[0][p * z_count + z]
                for ref in ins[1:]:
                    total = total + ref[p * z_count + z].astype(F32)
                out_ref[z] = total.astype(out_ref.dtype)

    outs = [jax.ShapeDtypeStruct(shape, F32 if p == 0 else LOW) for p in range(plane_count)]
    return adder("core_sum", body, [stacks[0]] + gotten, outs, after)


def plane_swaps(parts, groups, count):
    masks = masks_of(groups["plane"])[1:]
    return [parts[0]] + [swap(part, mask, count) for mask, part in zip(masks, parts[1:])]


def plane_stage(parts, groups, count, after=()):
    def body(ins, outs):
        for z in range(ins[0].shape[0]):
            total = ins[0][z]
            for ref in ins[1:]:
                total = total + ref[z].astype(F32)
            outs[0][z] = total

    outs = [jax.ShapeDtypeStruct(parts[0].shape, F32)]
    return adder("plane_sum", body, plane_swaps(parts, groups, count), outs, after)[0]


def plane_stage_z(parts, groups, count, after=()):
    def body(ins, outs):
        for z, out_ref in enumerate(outs):
            total = ins[0][z]
            for ref in ins[1:]:
                total = total + ref[z].astype(F32)
            out_ref[...] = total.astype(out_ref.dtype)

    many, rows, width = parts[0].shape
    outs = [jax.ShapeDtypeStruct((rows, width), F32 if z == 0 else LOW) for z in range(many)]
    return adder("plane_sum", body, plane_swaps(parts, groups, count), outs, after)


def z_stage(parts, groups, count):
    own = parts[0]
    for mask, part in zip(masks_of(groups["z"])[1:], parts[1:]):
        own = own + swap(part, mask, count).astype(F32)
    return own


def z_scatter(total, groups, count):
    if not groups["z"]:
        return total[0]
    return lax.psum_scatter(
        total, AXES, scatter_dimension=0, axis_index_groups=teams(groups["z"], count)
    )


def product(left, right):
    return lax.dot_general(left, right, (((1,), (0,)), ((), ())), preferred_element_type=F32)


def outer(left, right):
    return lax.dot_general(left, right, (((1,), (1,)), ((), ())), preferred_element_type=F32)


def gelu_both(value):
    scale = math.sqrt(2.0 / math.pi)
    square = value * value
    share = 0.5 + 0.5 * jnp.tanh(value * (scale + scale * 0.044715 * square))
    result = value * share
    slope = share + result * (1.0 - share) * (2.0 * scale + 6.0 * scale * 0.044715 * square)
    return result, slope


def columns(height, tile=TILE):
    return pl.BlockSpec((height, tile), lambda i: (0, i))


def whole(*shape):
    return pl.BlockSpec(shape, lambda i: (0,) * len(shape))


def once(*shape):
    return pl.BlockSpec(shape, lambda i: (0,) * len(shape), pipeline_mode=pl.Buffered(1))


def shaped(kind, *shape):
    return jax.ShapeDtypeStruct(shape, kind)


def pieces_of(width):
    return [(a, a + 256) for a in range(0, width, 256)]


def run(name, kernel, batch, in_specs, out_specs, out_shape, scratch, flops, *args, tile=TILE):
    moved = sum(a.size * a.dtype.itemsize for a in args)
    moved += sum(math.prod(o.shape) * o.dtype.itemsize for o in out_shape)
    return pl.pallas_call(
        kernel,
        grid=(batch // tile,),
        in_specs=in_specs,
        out_specs=out_specs,
        out_shape=out_shape,
        scratch_shapes=scratch,
        compiler_params=PARAMS,
        cost_estimate=pl.CostEstimate(flops=flops, bytes_accessed=moved, transcendentals=0),
        name=name,
    )(*args)


def first_step():
    return pl.when(pl.program_id(0) == 0)


def last_step():
    return pl.when(pl.program_id(0) == pl.num_programs(0) - 1)


def turn(out_ref, matrix_ref, tail_ref=None, edge_ref=None):
    for a, b in pieces_of(H):
        out_ref[a:b, :H] = matrix_ref[:, a:b].T
    if tail_ref is not None:
        out_ref[:H, H:] = tail_ref[...].T
    if edge_ref is not None:
        out_ref[H:, :] = edge_ref[...]


def straight(out_ref, matrix_ref, tail_ref, edge_ref=None):
    out_ref[:H, :H] = matrix_ref[...]
    row = lax.broadcasted_iota(jnp.int32, (TALL - H, H), 0)
    tail = tail_ref[: TALL - H, :].astype(F32)
    out_ref[H:, :H] = jnp.where(row < EXTRA, tail, 0.0).astype(LOW)
    if edge_ref is not None:
        lane = lax.broadcasted_iota(jnp.int32, (TALL - H, WIDE), 1)
        edge = jnp.where(lane < D, edge_ref[...].astype(F32), 0.0)
        edge = jnp.concatenate([edge, jnp.zeros((LANES - (TALL - H), WIDE), F32)])
        out_ref[:, H:] = edge.T[:TALL].astype(LOW)


def widen(out_ref, value_ref):
    @first_step()
    def _():
        out_ref[TALL:] = jnp.zeros((WIDE - TALL, out_ref.shape[1]), LOW)

    out_ref[:TALL] = value_ref[...]


class Spread:
    def __init__(self, groups, rows, count, parts=1, below=False, by_z=False):
        self.groups, self.by_z = groups, by_z
        self.masks = halves(groups)
        self.kinds = kinds_of(groups)
        self.rows, self.count, self.parts, self.below = rows, count, parts, below
        self.direct = rows % 16 == 0

    def shapes(self):
        if not self.direct:
            return [shaped(F32, TALL, H)] * self.parts
        height = self.rows * self.parts + (AUX_ROWS if self.below else 0)
        outs = [shaped(kind, len(row), height, H) for row, kind in zip(self.masks, self.kinds)]
        overs = 0 if self.below else self.parts
        return outs + [shaped(F32, self.count, 8, H)] * overs

    def specs(self):
        return [whole(*s.shape) for s in self.shapes()]

    def write(self, acc_refs, index_ref, out_refs, over_refs=None):
        if not self.direct:
            for acc_ref, ref in zip(acc_refs, out_refs):
                ref[...] = acc_ref[...]
            return
        rows = self.rows
        for ref, row, kind in zip(out_refs, self.masks, self.kinds):
            for j, mask in enumerate(row):
                at = owner(index_ref[0], mask, self.groups, self.by_z)
                start = pl.multiple_of(at * rows, rows)
                for i, acc_ref in enumerate(acc_refs):
                    block = acc_ref[pl.ds(start, rows), :]
                    ref[j, i * rows : (i + 1) * rows] = block.astype(kind)
                if self.below:
                    mine = acc_ref[pl.ds(pl.multiple_of(start + rows, 8), 8), :]
                    parts = [mine[:SPILL_ROWS]] + [v[at][:SPILL_ROWS] for v in over_refs]
                    parts.append(jnp.zeros((AUX_ROWS - MISC_ROW, H), F32))
                    ref[j, rows:] = jnp.concatenate(parts).astype(kind)
        if not self.below:
            for acc_ref, ref in zip(acc_refs, out_refs[len(self.masks) :]):
                for k in range(self.count):
                    ref[k] = acc_ref[(k + 1) * rows : (k + 1) * rows + 8, :]

    def finish(self, outs, index, overs=None):
        if self.direct:
            return list(outs)
        rows, count = self.rows, self.count
        blocks = [grad[:H].reshape(count, rows, H) for grad in outs]
        own = [
            jnp.stack([grad[(k + 1) * rows : (k + 1) * rows + 8] for k in range(count)])
            for grad in outs
        ]
        if self.below:
            blocks += [v[:, :SPILL_ROWS] for v in own + list(overs)]
            blocks.append(jnp.zeros((count, AUX_ROWS - MISC_ROW, H), F32))
        stacks = split(
            index, jnp.concatenate(blocks, axis=1), self.masks, self.kinds, self.groups, self.by_z
        )
        stacks = list(stacks)
        return stacks if self.below else stacks + own


ANY = pl.BlockSpec(memory_space=pl.ANY)
REST = TALL - H


def forward_cross(features, one, two):
    batch = features.shape[1]

    def kernel(f_ref, *refs):
        x_ref, mixer_one_ref, mixer_two_ref, one_ref, two_ref = refs[6:11]
        turned_one, turned_two, wide_ref = refs[11:]

        @first_step()
        def _():
            turn(turned_one, *refs[:3])
            turn(turned_two, *refs[3:6])

        x_ref[:H] = f_ref[:H]
        last = f_ref[H:].astype(F32)
        last = jnp.concatenate([last, jnp.ones((1, TILE), F32), jnp.zeros((TALL - D - 1, TILE), F32)])
        x_ref[H:] = last.astype(LOW)
        widen(wide_ref, x_ref)
        layers = []
        for a, b in [(0, TILE)]:
            mixer = product(turned_one[...], wide_ref[:, a:b])
            mixer_one_ref[:, a:b] = mixer.astype(LOW)
            part = x_ref[:, a:b].astype(F32)
            layer = part * mixer + part
            layers.append(layer)
            one_ref[:, a:b] = layer.astype(LOW)
        wide_ref[:TALL] = one_ref[...]
        for (a, b), layer in zip([(0, TILE)], layers):
            mixer = product(turned_two[...], wide_ref[:, a:b])
            mixer_two_ref[:, a:b] = mixer.astype(LOW)
            two_ref[:, a:b] = (x_ref[:, a:b].astype(F32) * mixer + layer).astype(LOW)

    return run(
        "forward_cross",
        kernel,
        batch,
        [columns(D)] + [once(H, H), once(LANES, H), once(REST, WIDE)] * 2,
        [columns(TALL)] * 5,
        [shaped(LOW, TALL, batch)] * 5,
        [pltpu.VMEM((TALL, WIDE), LOW)] * 2 + [pltpu.VMEM((WIDE, TILE), LOW)],
        4 * batch * TALL * TALL,
        features, *one, *two,
    )


def deep(spread, index, layer_low, examples, matrix_one, tail, matrix, lines, inverse):
    batch = layer_low.shape[1]
    days = inverse.shape[0]

    def kernel(k_ref, l_ref, x_ref, w_one_ref, t_ref, w_ref, n_ref, i_ref, *refs):
        logit_ref, back_ref, line_ref, sum_ref = refs[:4]
        out_refs = refs[4:-8]
        turned_one, turned, acc_ref, hidden_ref, slope_ref, low_ref, part_ref, wide_ref = refs[-8:]

        @first_step()
        def _():
            turn(turned_one, w_one_ref, t_ref)
            turn(turned, w_ref)
            acc_ref[...] = jnp.zeros_like(acc_ref)
            sum_ref[...] = jnp.zeros_like(sum_ref)
            part_ref[...] = jnp.zeros_like(part_ref)
            row = lax.broadcasted_iota(jnp.int32, (REST, TILE), 0)
            hidden_ref[H:] = jnp.where(row == 0, 1.0, 0.0).astype(LOW)

        widen(wide_ref, l_ref)
        for a, b in pieces_of(TILE):
            hidden, slope = gelu_both(product(turned_one[...], wide_ref[:, a:b]))
            hidden_ref[:H, a:b] = hidden.astype(LOW)
            slope_ref[:, a:b] = slope
        head = n_ref[:, 1:2]
        for a, b in pieces_of(TILE):
            two, slope = gelu_both(product(turned[...], hidden_ref[:H, a:b]) + n_ref[:, 0:1])
            two = two.astype(LOW).astype(F32)
            logits = n_ref[0:1, 2:3] + jnp.sum(two * head, axis=0, keepdims=True)
            label = x_ref[0:1, a:b]
            day = x_ref[1:2, a:b].astype(jnp.int32)
            row = lax.broadcasted_iota(jnp.int32, (days, b - a), 0)
            weight = jnp.sum(jnp.where(row == day, i_ref[:, 0:1], 0.0), axis=0, keepdims=True)
            decay = jnp.exp(-jnp.abs(logits))
            entropy = jnp.maximum(logits, 0.0) + jnp.log1p(decay) - label * logits
            chance = jnp.where(logits >= 0.0, 1.0, decay) / (1.0 + decay)
            logit_grad = (chance - label) * weight
            logit_ref[:, a:b] = logits
            sum_ref[0:1, a:b] += logit_grad
            sum_ref[1:2, a:b] += entropy * weight
            low_ref[:, a:b] = ((logit_grad * head) * slope).astype(LOW)
            one = logit_grad * two
            part = one[:, :LANES]
            for at in range(LANES, b - a, LANES):
                part = part + one[:, at : at + LANES]
            part_ref[...] += part
        for a, b in pieces_of(TILE):
            back_ref[:, a:b] = (product(w_ref[...], low_ref[:, a:b]) * slope_ref[:, a:b]).astype(LOW)
        for a, b in pieces_of(H):
            acc_ref[:, a:b] += outer(hidden_ref[...], low_ref[a:b])

        @last_step()
        def _():
            line_ref[0:8] = jnp.broadcast_to(
                jnp.sum(part_ref[...].T, axis=0, keepdims=True), (8, H)
            )
            line_ref[8:16] = acc_ref[H : H + 8]
            spread.write([acc_ref], k_ref, out_refs)

    return run(
        "deep",
        kernel,
        batch,
        [
            SMEM,
            columns(TALL),
            columns(2),
            once(H, H),
            once(LANES, H),
            once(H, H),
            whole(H, LANES),
            whole(days, LANES),
        ],
        [columns(1), columns(H), whole(16, H), whole(8, TILE)] + spread.specs(),
        [
            shaped(F32, 1, batch),
            shaped(LOW, H, batch),
            shaped(F32, 16, H),
            shaped(F32, 8, TILE),
        ]
        + spread.shapes(),
        [
            pltpu.VMEM((H, WIDE), LOW),
            pltpu.VMEM((H, H), LOW),
            pltpu.VMEM((TALL, H), F32),
            pltpu.VMEM((TALL, TILE), LOW),
            pltpu.VMEM((H, TILE), F32),
            pltpu.VMEM((H, TILE), LOW),
            pltpu.VMEM((H, LANES), F32),
            pltpu.VMEM((WIDE, TILE), LOW),
        ],
        8 * batch * H * H,
        index, layer_low, examples, matrix_one, tail, matrix, lines, inverse,
    )


def back_deep(spread, index, grad_low, layer_low, features, matrix, tail, after):
    batch = features.shape[1]

    def kernel(k_ref, g_ref, l_ref, x_ref, w_ref, t_ref, *refs):
        refs = refs[len(after) :]
        layer_ref, mixer_ref, line_ref = refs[:3]
        out_refs = refs[3:-2]
        held, acc_ref = refs[-2:]

        @first_step()
        def _():
            straight(held, w_ref, t_ref)
            acc_ref[...] = jnp.zeros_like(acc_ref)

        for a, b in pieces_of(TILE):
            layer = product(held[...], g_ref[:, a:b])
            layer_ref[:, a:b] = layer
            mixer_ref[:, a:b] = (layer * x_ref[:, a:b].astype(F32)).astype(LOW)
        for a, b in pieces_of(H):
            acc_ref[:, a:b] += outer(l_ref[...], g_ref[a:b])

        @last_step()
        def _():
            line_ref[...] = acc_ref[H:]
            spread.write([acc_ref], k_ref, out_refs)

    return run(
        "back_deep",
        kernel,
        batch,
        [SMEM, columns(H), columns(TALL), columns(TALL), once(H, H), once(LANES, H)]
        + [ANY] * len(after),
        [columns(TALL), columns(TALL), whole(REST, H)] + spread.specs(),
        [shaped(F32, TALL, batch), shaped(LOW, TALL, batch), shaped(F32, REST, H)]
        + spread.shapes(),
        [pltpu.VMEM((TALL, H), LOW), pltpu.VMEM((TALL, H), F32)],
        4 * batch * TALL * H,
        index, grad_low, layer_low, features, matrix, tail, *after,
    )


def back_two(
    spread, index, mixer_low, layer_low, layer_grad, features, mixer_one, mixer_two, matrix, tail,
    edge, lines, after,
):
    batch = features.shape[1]

    def kernel(k_ref, g_ref, l_ref, d_ref, x_ref, one_ref, two_ref, w_ref, t_ref, e_ref, *refs):
        top_ref, deep_ref, sums_ref = refs[:3]
        refs = refs[3 + len(after) :]
        part_ref, mixer_ref, vector_ref = refs[:3]
        out_refs = refs[3:-6]
        held, acc_ref, wide_ref, sum_ref, side_ref, next_side_ref = refs[-6:]

        @first_step()
        def _():
            straight(held, w_ref, t_ref, e_ref)
            acc_ref[...] = jnp.zeros_like(acc_ref)
            side_ref[...] = jnp.zeros_like(side_ref)
            next_side_ref[...] = jnp.zeros_like(next_side_ref)
            sum_ref[...] = jnp.zeros_like(sum_ref)

        widen(wide_ref, g_ref)
        for a, b in pieces_of(TILE):
            above = d_ref[:, a:b]
            layer = product(held[...], wide_ref[:, a:b]) + above
            mixer = (layer * x_ref[:, a:b].astype(F32)).astype(LOW)
            mixer_ref[:, a:b] = mixer
            mixer = mixer[:H].astype(F32)
            total = mixer[:, :LANES]
            for at in range(LANES, b - a, LANES):
                total = total + mixer[:, at : at + LANES]
            sum_ref[...] += total
            part = above * two_ref[:, a:b].astype(F32)
            part = part + layer * (one_ref[:, a:b].astype(F32) + 1.0)
            part_ref[:, a:b] = part.astype(LOW)
        for a, b in pieces_of(H):
            acc_ref[:, a:b] += outer(l_ref[...], g_ref[a:b])
        side_ref[...] += outer(g_ref[H:], l_ref[...])
        next_side_ref[...] += outer(mixer_ref[H:], x_ref[...])

        @last_step()
        def _():
            vector_ref[...] = jnp.zeros_like(vector_ref)
            vector_ref[0:1, :H] = jnp.sum(sum_ref[...].T, axis=0, keepdims=True)
            vector_ref[1:2, :H] = acc_ref[D : D + 1]
            vector_ref[2:3, :H] = deep_ref[EXTRA : EXTRA + 1]
            vector_ref[3:4, :H] = top_ref[8:9]
            vector_ref[4:5, :H] = top_ref[0:1]
            vector_ref[5:8, :TALL] = next_side_ref[:EXTRA]
            vector_ref[8:11, :TALL] = side_ref[:EXTRA]
            lane = lax.broadcasted_iota(jnp.int32, (1, LANES), 1)
            bias = jnp.sum(sums_ref[0:1], axis=1, keepdims=True)
            loss = jnp.sum(sums_ref[1:2], axis=1, keepdims=True)
            vector_ref[11:12, :LANES] = jnp.where(lane == 0, bias, jnp.where(lane == 1, loss, 0.0))
            spread.write([acc_ref], k_ref, out_refs)

    return run(
        "back_two",
        kernel,
        batch,
        [SMEM]
        + [columns(TALL)] * 6
        + [once(H, H), once(LANES, H), once(REST, WIDE)]
        + [whole(*v.shape) for v in lines]
        + [ANY] * len(after),
        [columns(TALL), columns(TALL)]
        + [whole(16, WIDE)]
        + spread.specs(),
        [
            shaped(LOW, TALL, batch),
            shaped(LOW, TALL, batch),
            shaped(F32, 16, WIDE),
        ]
        + spread.shapes(),
        [
            pltpu.VMEM((TALL, WIDE), LOW),
            pltpu.VMEM((TALL, H), F32),
            pltpu.VMEM((WIDE, TILE), LOW),
            pltpu.VMEM((H, LANES), F32),
            pltpu.VMEM((REST, TALL), F32),
            pltpu.VMEM((REST, TALL), F32),
        ],
        4 * batch * TALL * TALL,
        index, mixer_low, layer_low, layer_grad, features, mixer_one, mixer_two, matrix, tail,
        edge, *lines, *after,
    )


def grad_one(spread, index, mixer_low, features, overs, after):
    batch = features.shape[1]

    def kernel(k_ref, g_ref, x_ref, *refs):
        over_refs = refs[: len(overs)]
        out_refs = refs[len(overs) + len(after) : -1]
        acc_ref = refs[-1]

        @first_step()
        def _():
            acc_ref[...] = jnp.zeros_like(acc_ref)

        for a, b in pieces_of(H):
            acc_ref[:, a:b] += outer(x_ref[...], g_ref[a:b])

        @last_step()
        def _():
            spread.write([acc_ref], k_ref, out_refs, over_refs)

    return run(
        "grad_one",
        kernel,
        batch,
        [SMEM, columns(TALL), columns(TALL)]
        + [once(*v.shape) for v in overs]
        + [ANY] * len(after),
        spread.specs(),
        spread.shapes(),
        [pltpu.VMEM((TALL, H), F32)],
        2 * batch * TALL * TALL,
        index, mixer_low, features, *overs, *after,
    )


def back_one(mixer_low, part, matrix, tail, edge, after):
    batch = part.shape[1]

    def kernel(g_ref, p_ref, w_ref, t_ref, e_ref, *refs):
        out_ref, held, wide_ref = refs[len(after) :]

        @first_step()
        def _():
            straight(held, w_ref, t_ref, e_ref)

        widen(wide_ref, g_ref)
        for a, b in [(0, TILE)]:
            value = p_ref[:, a:b].astype(F32) + product(held[...], wide_ref[:, a:b])
            out_ref[:H, a:b] = value[:H]
            out_ref[H:, a:b] = value[H:D]

    return run(
        "back_one",
        kernel,
        batch,
        [columns(TALL), columns(TALL), whole(H, H), whole(LANES, H), whole(REST, WIDE)]
        + [ANY] * len(after),
        [columns(D)],
        [shaped(F32, D, batch)],
        [pltpu.VMEM((TALL, WIDE), LOW), pltpu.VMEM((WIDE, TILE), LOW)],
        2 * batch * TALL * TALL,
        mixer_low, part, matrix, tail, edge, *after,
    )[0]


def local(groups, features, labels, days, master, moment_one, moment_two):
    count = lax.axis_size(AXES)
    index = lax.axis_index(AXES)
    slot = index[None].astype(jnp.int32)
    rows = H // count
    starts = starts_of(count)
    sizes = piece_sizes(count)
    wide_piece = sizes[1]
    piece = [master[a : a + l] for a, l in zip(starts, sizes)]
    block_one = to_block(piece[0], index, D, rows, count)
    block_two = to_block(piece[2], index, D, rows, count)
    block_deep = to_block(piece[4], index, H, rows, count)

    day_hot = (days[:, None] == jnp.arange(DAYS, dtype=jnp.int32)[None, :]).astype(F32)
    own_counts = jnp.sum(day_hot, axis=0)
    counts_high = jnp.floor(own_counts / 64.0)
    counts_low = own_counts - 64.0 * counts_high

    def spill_side(block):
        side = block[rows:, H:].T
        return jnp.pad(side, ((0, 0), (0, rows - SPILL_ROWS)))

    misc = [
        piece[5],
        piece[7],
        piece[8],
        block_one[:rows, H:].T,
        block_two[:rows, H:].T,
        spill_side(block_one),
        spill_side(block_two),
        piece[1],
        piece[3],
        piece[9],
        counts_high,
        counts_low,
    ]
    misc = jnp.concatenate([part.reshape(-1) for part in misc])
    misc = jnp.pad(misc, (0, (AUX_ROWS - MISC_ROW) * H - misc.shape[0])).reshape(-1, H)
    first = jnp.concatenate(
        [
            block_one[:rows, :H],
            block_two[:rows, :H],
            block_one[rows:, :H],
            block_two[rows:, :H],
            block_deep[rows:],
            misc,
        ]
    ).astype(LOW)
    stacks_cross = gather(first, groups, count)
    rest = jnp.concatenate([block_deep[:rows], piece[6].reshape(rows, H)]).astype(LOW)
    crossed = [value for value, _ in stacks_cross[3:5]]
    stacks_rest = gather(rest, groups, count, direct=True, after=crossed)
    examples = jnp.stack([labels.astype(F32), days.astype(F32)])

    matrix_one, matrix_two, aux = place(slot, stacks_cross, rows, count, [0, SPILL_ROWS])
    matrix_deep, matrix_top = place(slot, stacks_rest, rows, count, [2 * SPILL_ROWS, None], aux)

    line = aux[:, MISC_ROW]
    at = UNIT_LINES * rows
    units = line[:, :at].reshape(count, UNIT_LINES, rows).transpose(1, 0, 2).reshape(UNIT_LINES, H)
    biases = line[:, at : at + 2 * wide_piece].reshape(count, 2, wide_piece)
    biases = biases.transpose(1, 0, 2).reshape(2, count * wide_piece)
    at += 2 * wide_piece
    head_bias = line[0, at]
    both_counts = jnp.sum(line[:, at + 1 : at + 1 + 2 * DAYS].astype(F32), axis=0)
    counts = 64.0 * both_counts[:DAYS] + both_counts[DAYS:]
    inverse = jnp.broadcast_to((1.0 / counts)[:, None], (DAYS, LANES))
    sides = jnp.pad(units[3:9], ((0, 0), (0, LANES))) + jnp.pad(
        units[9:15], ((0, 0), (rows, LANES - rows))
    )

    def tail_of(at, bias):
        return jnp.concatenate(
            [aux[count - 1, at : at + EXTRA], bias[None, :H], jnp.zeros((LANES - EXTRA - 1, H), LOW)]
        )

    def edge_of(side, bias):
        lane = lax.broadcasted_iota(jnp.int32, side.shape, 1)
        side = jnp.where(lane == D, bias[H:D, None], side)
        return jnp.pad(side, ((0, TALL - H - EXTRA), (0, 0)))

    tail_one, edge_one = tail_of(0, biases[0]), edge_of(sides[:3], biases[0])
    tail_two, edge_two = tail_of(SPILL_ROWS, biases[1]), edge_of(sides[3:], biases[1])
    tail_deep = tail_of(2 * SPILL_ROWS, units[0])
    lines = jnp.concatenate(
        [units[1:3], jnp.full((1, H), head_bias), jnp.zeros((LANES - 3, H), LOW)]
    )
    lines = lines.astype(F32).T
    spread = Spread(groups, rows, count, by_z=True)
    spread_two = Spread(groups, rows, count)
    spread_last = Spread(groups, rows, count, below=True)

    wide_features, mixer_one, mixer_two, low_one, low_two = forward_cross(
        features.T, (matrix_one, tail_one, edge_one), (matrix_two, tail_two, edge_two)
    )
    logits, pre_one_low, top_lines, sums, *outs = deep(
        spread, slot, low_two, examples, matrix_deep, tail_deep, matrix_top, lines, inverse
    )
    *top_stacks, _ = spread.finish(outs, slot)
    layer_grad, mixer_two_low, deep_lines, *outs = back_deep(
        spread, slot, pre_one_low, low_two, wide_features, matrix_deep, tail_deep, []
    )
    *deep_stacks, deep_over = spread.finish(outs, slot)
    top_plane = core_stage(top_stacks, groups, count, [mixer_two_low])
    part, mixer_one_low, vectors, *outs = back_two(
        spread_two, slot, mixer_two_low, low_one, layer_grad, wide_features, mixer_one, mixer_two,
        matrix_two, tail_two, edge_two, (top_lines, deep_lines, sums), top_plane[1:],
    )
    *two_stacks, two_over = spread_two.finish(outs, slot)
    top_total = plane_stage(top_plane, groups, count, [mixer_one_low])
    deep_plane = core_stage(deep_stacks, groups, count, [mixer_one_low])
    overs = (two_over, deep_over)
    outs = grad_one(
        spread_last, slot, mixer_one_low, wide_features, overs,
        deep_plane[1:] + [top_total],
    )
    last_stacks = spread_last.finish(outs, slot, overs)
    deep_total = plane_stage(deep_plane, groups, count, last_stacks[:1])
    two_plane = core_stage(two_stacks, groups, count, last_stacks[:1])
    last_plane = core_stage(last_stacks, groups, count)
    feature_grad = back_one(
        mixer_one_low, part, matrix_one, tail_one, edge_one,
        last_plane[1:] + two_plane[1:] + [deep_total],
    )

    vectors = jnp.sum(lax.all_gather(vectors, AXES, axis=0), axis=0)
    loss = vectors[11, 1]
    side_sums = vectors[5:11]

    own_top = z_scatter(top_total, groups, count)
    own_deep = z_scatter(deep_total, groups, count)
    own_two = z_stage(plane_stage_z(two_plane, groups, count, [feature_grad]), groups, count)
    own_last = z_stage(plane_stage_z(last_plane, groups, count, [feature_grad, own_two]), groups, count)
    own_one = own_last[:rows]
    spills = own_last[rows : rows + MISC_ROW]
    row = lax.broadcasted_iota(jnp.int32, spills.shape, 0)
    beyond = (row % SPILL_ROWS >= EXTRA) & (index == count - 1)
    spills = jnp.where(beyond, 0.0, spills)
    wide_biases = jnp.concatenate(
        [vectors[:2, :H], side_sums[:, D].reshape(2, EXTRA)], axis=1
    )
    wide_biases = jnp.pad(wide_biases, ((0, 0), (0, count * wide_piece - D)))
    wide_biases = lax.dynamic_slice(wide_biases, (0, index * wide_piece), (2, wide_piece))
    units = lax.dynamic_slice(vectors[2:5], (0, index * rows), (3, rows))
    side_sums = jnp.pad(side_sums[:, :D], ((0, 0), (0, WIDE - D)))
    side_sums = lax.dynamic_slice(side_sums, (0, index * rows), (6, rows + SPILL_ROWS)).T

    def whole_block(main, number):
        low = number * SPILL_ROWS
        body = jnp.concatenate([main, spills[low : low + SPILL_ROWS]])
        if number == 2:
            return body
        return jnp.concatenate([body, side_sums[:, 3 * number : 3 * number + 3]], axis=1)

    flat_grad = jnp.concatenate(
        [
            from_block(whole_block(own_one, 0), index, sizes[0], rows, count),
            wide_biases[0],
            from_block(whole_block(own_two, 1), index, sizes[2], rows, count),
            wide_biases[1],
            from_block(whole_block(own_deep, 2), index, sizes[4], rows, count),
            units[0],
            own_top.reshape(-1),
            units[1],
            units[2],
            jnp.where(index == 0, vectors[11, :1], 0.0),
        ]
    )
    new_moment_one = 0.9 * moment_one + 0.1 * flat_grad
    new_moment_two = 0.999 * moment_two + 0.001 * flat_grad * flat_grad
    corrected_one = new_moment_one / (1.0 - 0.9**STEP)
    corrected_two = new_moment_two / (1.0 - 0.999**STEP)
    new_master = master - 0.03 * (corrected_one / (jnp.sqrt(corrected_two) + 1e-08) + 0.01 * master)
    new_bias = jnp.concatenate(
        [new_master[starts[i] : starts[i] + sizes[i]] for i in (1, 3, 5, 7, 9)]
    )
    return (
        logits.reshape(-1),
        loss,
        feature_grad.T,
        flat_grad,
        new_moment_one,
        new_moment_two,
        new_master,
        new_bias,
    )


def solution(mesh):
    line = P(AXES)
    table = P(AXES, None)
    groups = bit_groups(mesh)
    return jax.shard_map(
        functools.partial(local, groups),
        mesh=mesh,
        in_specs=(table, line, line, line, line, line),
        out_specs=(line, P(), table, line, line, line, line, line),
        check_vma=False,
    )
```

```python
import functools
import math

import jax
import jax.numpy as jnp
from jax import lax
from jax.experimental import pallas as pl
from jax.experimental.pallas import tpu as pltpu
from jax.sharding import PartitionSpec as P

D = 1027
H = 1024
DAYS = 24
STEP = 10
AXES = ("dp", "cores")
EXTRA = D - H
LANES = 128
WIDE = H + LANES
AUX_ROWS = 16
SPILL_ROWS = 4
MISC_ROW = 12
UNIT_LINES = 15
TILE = 512
TALL = H + 16
MIB = 1024 * 1024
F32 = jnp.float32
LOW = jnp.bfloat16
SMEM = pl.BlockSpec(memory_space=pltpu.SMEM)
VMEM = pl.BlockSpec(memory_space=pltpu.VMEM)
PARAMS = pltpu.CompilerParams(vmem_limit_bytes=56 * MIB)


def shapes():
    return [(D, D), (D,), (D, D), (D,), (D, H), (H,), (H, H), (H,), (H,), (1,)]


def piece_sizes(count):
    return [(math.prod(shape) + count - 1) // count for shape in shapes()[:-1]] + [1]


def starts_of(count):
    starts = []
    position = 0
    for piece in piece_sizes(count):
        starts.append(position)
        position += piece
    return starts


def to_block(piece, index, width, rows, count):
    excess = piece.shape[0] - rows * width
    size = (rows + SPILL_ROWS) * width
    lead = (count - 1) * excess
    padded = jnp.pad(piece, (lead, max(0, size - piece.shape[0])))
    line = lax.dynamic_slice(padded, (lead - index * excess,), (size,))
    return line.reshape(rows + SPILL_ROWS, width)


def from_block(block, index, piece, rows, count):
    width = block.shape[1]
    excess = piece - rows * width
    last = (count - 1) * excess
    line = jnp.pad(block.reshape(-1), (0, max(0, last + piece - block.size)))
    return lax.dynamic_slice(line, (index * excess,), (piece,))


def bit_groups(mesh):
    devices = mesh.devices.reshape(-1)
    groups = {"z": [], "plane": [], "core": []}
    bit = 1
    while bit < devices.size:
        here = getattr(devices[0], "coords", None)
        there = getattr(devices[bit], "coords", None)
        if here is None or there is None:
            name = "core" if bit == 1 else "plane" if bit <= 4 else "z"
        elif tuple(here) == tuple(there):
            name = "core"
        elif here[2] != there[2]:
            name = "z"
        else:
            name = "plane"
        groups[name].append(bit)
        bit *= 2
    return groups


def masks_of(bits):
    masks = [0]
    for bit in bits:
        masks = masks + [mask | bit for mask in masks]
    return masks


def teams(bits, count):
    masks = masks_of(bits)
    return [[k | mask for mask in masks] for k in range(count) if not k & masks[-1]]


def owner(index, mask, groups, by_z):
    if by_z:
        index = jnp.bitwise_and(index, ~masks_of(groups["z"])[-1])
    return jnp.bitwise_xor(index, mask)


def swap(value, mask, count):
    return lax.ppermute(value, AXES, [(k, k ^ mask) for k in range(count)])


def join(parts, after):
    def kernel(*refs):
        for j in range(len(parts)):
            refs[-1][j] = refs[j][...]

    return pl.pallas_call(
        kernel,
        out_shape=jax.ShapeDtypeStruct((len(parts),) + parts[0].shape, parts[0].dtype),
        in_specs=[VMEM] * len(parts) + [pl.BlockSpec(memory_space=pl.ANY)] * len(after),
        out_specs=VMEM,
        compiler_params=PARAMS,
        name="join",
    )(*parts, *after)


def gather(block, groups, count, direct=False, after=()):
    z_masks = masks_of(groups["z"])
    core_masks = masks_of(groups["core"])
    line = [block] + [swap(block, mask, count) for mask in z_masks[1:]]
    line = join(line, after) if after else jnp.stack(line)
    plane = [(line, z_masks)]
    if len(groups["plane"]) == 2 and len(z_masks) > 1 and not direct:
        one, two = groups["plane"]
        half = len(z_masks) // 2
        by_one = swap(line, one, count)
        by_two = swap(line, two, count)
        plane.append((by_one, [one ^ z for z in z_masks]))
        plane.append((by_two, [two ^ z for z in z_masks]))
        both = one ^ two
        plane.append((swap(by_one[:half], two, count), [both ^ z for z in z_masks[:half]]))
        plane.append((swap(by_two[half:], one, count), [both ^ z for z in z_masks[half:]]))
    else:
        for mask in masks_of(groups["plane"])[1:]:
            plane.append((swap(line, mask, count), [mask ^ z for z in z_masks]))
    result = list(plane)
    for core in core_masks[1:]:
        result += [(swap(value, core, count), [core ^ m for m in row]) for value, row in plane]
    return result


def place(index, stacks, rows, count, parts, aux=None):
    sources = [value for value, _ in stacks]
    masks = [row for _, row in stacks]
    carries = aux is None
    top = min(16, rows)

    def kernel(index_ref, *refs):
        refs = list(refs)
        aux_ref = refs.pop() if carries else refs.pop(0)
        outs = refs[len(sources) :]
        for ref, row in zip(refs, masks):
            for j, mask in enumerate(row):
                at = jnp.bitwise_xor(index_ref[0], mask)
                for i, out_ref in enumerate(outs):
                    out_ref[at] = ref[j, i * rows : (i + 1) * rows]
                if carries:
                    aux_ref[at] = ref[j, len(outs) * rows :]
        for spill_at, out_ref in zip(parts, outs):
            if spill_at is None:
                continue
            for k in range(1, count):
                spill = aux_ref[k - 1].astype(F32)[spill_at : spill_at + SPILL_ROWS]
                old = out_ref[k, :top].astype(F32)
                new = old[:SPILL_ROWS] + spill
                if top > SPILL_ROWS:
                    new = jnp.concatenate([new, old[SPILL_ROWS:]], axis=0)
                out_ref[k, :top] = new.astype(LOW)

    out_shape = [jax.ShapeDtypeStruct((count, rows, H), LOW)] * len(parts)
    if carries:
        out_shape.append(jax.ShapeDtypeStruct((count, AUX_ROWS, H), LOW))
    extra = [] if carries else [aux]
    result = pl.pallas_call(
        kernel,
        out_shape=out_shape,
        in_specs=[SMEM] + [VMEM] * (len(extra) + len(sources)),
        out_specs=[VMEM] * len(out_shape),
        compiler_params=PARAMS,
        name="place",
    )(index, *extra, *sources)
    return [value.reshape(H, H) for value in result[: len(parts)]] + list(result[len(parts) :])


def split(index, value, masks, kinds, groups, by_z):
    def kernel(index_ref, value_ref, *out_refs):
        for ref, row, kind in zip(out_refs, masks, kinds):
            for j, mask in enumerate(row):
                ref[j] = value_ref[owner(index_ref[0], mask, groups, by_z)].astype(kind)

    shape = value.shape[1:]
    return pl.pallas_call(
        kernel,
        out_shape=[
            jax.ShapeDtypeStruct((len(row),) + shape, kind) for row, kind in zip(masks, kinds)
        ],
        in_specs=[SMEM, VMEM],
        out_specs=[VMEM] * len(masks),
        compiler_params=PARAMS,
        name="split",
    )(index, value)


def halves(groups):
    z_masks, plane_masks, core_masks = (masks_of(groups[g]) for g in ("z", "plane", "core"))
    inner = [p ^ z for p in plane_masks for z in z_masks]
    return [[core ^ m for m in inner] for core in core_masks]


def kinds_of(groups):
    return [F32] + [LOW] * (len(halves(groups)) - 1)


def adder(name, body, ins, outs, after):
    def kernel(*refs):
        body(refs[: len(ins)], refs[len(ins) + len(after) :])

    result = pl.pallas_call(
        kernel,
        out_shape=outs,
        in_specs=[VMEM] * len(ins) + [pl.BlockSpec(memory_space=pl.ANY)] * len(after),
        out_specs=[VMEM] * len(outs),
        compiler_params=PARAMS,
        name=name,
    )(*ins, *after)
    return list(result)


def core_stage(stacks, groups, count, after=()):
    z_count, plane_count = len(masks_of(groups["z"])), len(masks_of(groups["plane"]))
    cores = masks_of(groups["core"])[1:]
    gotten = [swap(stack, core, count) for core, stack in zip(cores, stacks[1:])]
    shape = (z_count,) + stacks[0].shape[1:]

    def body(ins, outs):
        for p, out_ref in enumerate(outs):
            for z in range(z_count):
                total = ins[0][p * z_count + z]
                for ref in ins[1:]:
                    total = total + ref[p * z_count + z].astype(F32)
                out_ref[z] = total.astype(out_ref.dtype)

    outs = [jax.ShapeDtypeStruct(shape, F32 if p == 0 else LOW) for p in range(plane_count)]
    return adder("core_sum", body, [stacks[0]] + gotten, outs, after)


def plane_swaps(parts, groups, count):
    masks = masks_of(groups["plane"])[1:]
    return [parts[0]] + [swap(part, mask, count) for mask, part in zip(masks, parts[1:])]


def plane_stage(parts, groups, count, after=()):
    def body(ins, outs):
        for z in range(ins[0].shape[0]):
            total = ins[0][z]
            for ref in ins[1:]:
                total = total + ref[z].astype(F32)
            outs[0][z] = total

    outs = [jax.ShapeDtypeStruct(parts[0].shape, F32)]
    return adder("plane_sum", body, plane_swaps(parts, groups, count), outs, after)[0]


def plane_stage_z(parts, groups, count, after=()):
    def body(ins, outs):
        for z, out_ref in enumerate(outs):
            total = ins[0][z]
            for ref in ins[1:]:
                total = total + ref[z].astype(F32)
            out_ref[...] = total.astype(out_ref.dtype)

    many, rows, width = parts[0].shape
    outs = [jax.ShapeDtypeStruct((rows, width), F32 if z == 0 else LOW) for z in range(many)]
    return adder("plane_sum", body, plane_swaps(parts, groups, count), outs, after)


def z_stage(parts, groups, count):
    own = parts[0]
    for mask, part in zip(masks_of(groups["z"])[1:], parts[1:]):
        own = own + swap(part, mask, count).astype(F32)
    return own


def z_scatter(total, groups, count):
    if not groups["z"]:
        return total[0]
    return lax.psum_scatter(
        total, AXES, scatter_dimension=0, axis_index_groups=teams(groups["z"], count)
    )


def product(left, right):
    return lax.dot_general(left, right, (((1,), (0,)), ((), ())), preferred_element_type=F32)


def outer(left, right):
    return lax.dot_general(left, right, (((1,), (1,)), ((), ())), preferred_element_type=F32)


def gelu_both(value):
    scale = math.sqrt(2.0 / math.pi)
    square = value * value
    share = 0.5 + 0.5 * jnp.tanh(value * (scale + scale * 0.044715 * square))
    result = value * share
    slope = share + result * (1.0 - share) * (2.0 * scale + 6.0 * scale * 0.044715 * square)
    return result, slope


def columns(height, tile=TILE):
    return pl.BlockSpec((height, tile), lambda i: (0, i))


def whole(*shape):
    return pl.BlockSpec(shape, lambda i: (0,) * len(shape))


def once(*shape):
    return pl.BlockSpec(shape, lambda i: (0,) * len(shape), pipeline_mode=pl.Buffered(1))


def shaped(kind, *shape):
    return jax.ShapeDtypeStruct(shape, kind)


def pieces_of(width):
    return [(a, a + 256) for a in range(0, width, 256)]


def run(name, kernel, batch, in_specs, out_specs, out_shape, scratch, flops, *args, tile=TILE):
    moved = sum(a.size * a.dtype.itemsize for a in args)
    moved += sum(math.prod(o.shape) * o.dtype.itemsize for o in out_shape)
    return pl.pallas_call(
        kernel,
        grid=(batch // tile,),
        in_specs=in_specs,
        out_specs=out_specs,
        out_shape=out_shape,
        scratch_shapes=scratch,
        compiler_params=PARAMS,
        cost_estimate=pl.CostEstimate(flops=flops, bytes_accessed=moved, transcendentals=0),
        name=name,
    )(*args)


def first_step():
    return pl.when(pl.program_id(0) == 0)


def last_step():
    return pl.when(pl.program_id(0) == pl.num_programs(0) - 1)


def turn(out_ref, matrix_ref, tail_ref=None, edge_ref=None):
    for a, b in pieces_of(H):
        out_ref[a:b, :H] = matrix_ref[:, a:b].T
    if tail_ref is not None:
        out_ref[:H, H:] = tail_ref[...].T
    if edge_ref is not None:
        out_ref[H:, :] = edge_ref[...]


def straight(out_ref, matrix_ref, tail_ref, edge_ref=None):
    out_ref[:H, :H] = matrix_ref[...]
    row = lax.broadcasted_iota(jnp.int32, (TALL - H, H), 0)
    tail = tail_ref[: TALL - H, :].astype(F32)
    out_ref[H:, :H] = jnp.where(row < EXTRA, tail, 0.0).astype(LOW)
    if edge_ref is not None:
        lane = lax.broadcasted_iota(jnp.int32, (TALL - H, WIDE), 1)
        edge = jnp.where(lane < D, edge_ref[...].astype(F32), 0.0)
        edge = jnp.concatenate([edge, jnp.zeros((LANES - (TALL - H), WIDE), F32)])
        out_ref[:, H:] = edge.T[:TALL].astype(LOW)


def widen(out_ref, value_ref):
    @first_step()
    def _():
        out_ref[TALL:] = jnp.zeros((WIDE - TALL, out_ref.shape[1]), LOW)

    out_ref[:TALL] = value_ref[...]


class Spread:
    def __init__(self, groups, rows, count, parts=1, below=False, by_z=False):
        self.groups, self.by_z = groups, by_z
        self.masks = halves(groups)
        self.kinds = kinds_of(groups)
        self.rows, self.count, self.parts, self.below = rows, count, parts, below
        self.direct = rows % 16 == 0

    def shapes(self):
        if not self.direct:
            return [shaped(F32, TALL, H)] * self.parts
        height = self.rows * self.parts + (AUX_ROWS if self.below else 0)
        outs = [shaped(kind, len(row), height, H) for row, kind in zip(self.masks, self.kinds)]
        overs = 0 if self.below else self.parts
        return outs + [shaped(F32, self.count, 8, H)] * overs

    def specs(self):
        return [whole(*s.shape) for s in self.shapes()]

    def write(self, acc_refs, index_ref, out_refs, over_refs=None):
        if not self.direct:
            for acc_ref, ref in zip(acc_refs, out_refs):
                ref[...] = acc_ref[...]
            return
        rows = self.rows
        for ref, row, kind in zip(out_refs, self.masks, self.kinds):
            for j, mask in enumerate(row):
                at = owner(index_ref[0], mask, self.groups, self.by_z)
                start = pl.multiple_of(at * rows, rows)
                for i, acc_ref in enumerate(acc_refs):
                    block = acc_ref[pl.ds(start, rows), :]
                    ref[j, i * rows : (i + 1) * rows] = block.astype(kind)
                if self.below:
                    mine = acc_ref[pl.ds(pl.multiple_of(start + rows, 8), 8), :]
                    parts = [mine[:SPILL_ROWS]] + [v[at][:SPILL_ROWS] for v in over_refs]
                    parts.append(jnp.zeros((AUX_ROWS - MISC_ROW, H), F32))
                    ref[j, rows:] = jnp.concatenate(parts).astype(kind)
        if not self.below:
            for acc_ref, ref in zip(acc_refs, out_refs[len(self.masks) :]):
                for k in range(self.count):
                    ref[k] = acc_ref[(k + 1) * rows : (k + 1) * rows + 8, :]

    def finish(self, outs, index, overs=None):
        if self.direct:
            return list(outs)
        rows, count = self.rows, self.count
        blocks = [grad[:H].reshape(count, rows, H) for grad in outs]
        own = [
            jnp.stack([grad[(k + 1) * rows : (k + 1) * rows + 8] for k in range(count)])
            for grad in outs
        ]
        if self.below:
            blocks += [v[:, :SPILL_ROWS] for v in own + list(overs)]
            blocks.append(jnp.zeros((count, AUX_ROWS - MISC_ROW, H), F32))
        stacks = split(
            index, jnp.concatenate(blocks, axis=1), self.masks, self.kinds, self.groups, self.by_z
        )
        stacks = list(stacks)
        return stacks if self.below else stacks + own


ANY = pl.BlockSpec(memory_space=pl.ANY)
REST = TALL - H


def forward_cross(features, one, two):
    batch = features.shape[1]

    def kernel(f_ref, *refs):
        x_ref, mixer_one_ref, mixer_two_ref, one_ref, two_ref = refs[6:11]
        turned_one, turned_two, wide_ref = refs[11:]

        @first_step()
        def _():
            turn(turned_one, *refs[:3])
            turn(turned_two, *refs[3:6])

        x_ref[:H] = f_ref[:H]
        last = f_ref[H:].astype(F32)
        last = jnp.concatenate([last, jnp.ones((1, TILE), F32), jnp.zeros((TALL - D - 1, TILE), F32)])
        x_ref[H:] = last.astype(LOW)
        widen(wide_ref, x_ref)
        layers = []
        for a, b in [(0, TILE)]:
            mixer = product(turned_one[...], wide_ref[:, a:b])
            mixer_one_ref[:, a:b] = mixer.astype(LOW)
            part = x_ref[:, a:b].astype(F32)
            layer = part * mixer + part
            layers.append(layer)
            one_ref[:, a:b] = layer.astype(LOW)
        wide_ref[:TALL] = one_ref[...]
        for (a, b), layer in zip([(0, TILE)], layers):
            mixer = product(turned_two[...], wide_ref[:, a:b])
            mixer_two_ref[:, a:b] = mixer.astype(LOW)
            two_ref[:, a:b] = (x_ref[:, a:b].astype(F32) * mixer + layer).astype(LOW)

    return run(
        "forward_cross",
        kernel,
        batch,
        [columns(D)] + [once(H, H), once(LANES, H), once(REST, WIDE)] * 2,
        [columns(TALL)] * 5,
        [shaped(LOW, TALL, batch)] * 5,
        [pltpu.VMEM((TALL, WIDE), LOW)] * 2 + [pltpu.VMEM((WIDE, TILE), LOW)],
        4 * batch * TALL * TALL,
        features, *one, *two,
    )


def deep(spread, index, layer_low, examples, matrix_one, tail, matrix, lines, inverse):
    batch = layer_low.shape[1]
    days = inverse.shape[0]

    def kernel(k_ref, l_ref, x_ref, w_one_ref, t_ref, w_ref, n_ref, i_ref, *refs):
        logit_ref, back_ref, line_ref, sum_ref = refs[:4]
        out_refs = refs[4:-8]
        turned_one, turned, acc_ref, hidden_ref, slope_ref, low_ref, part_ref, wide_ref = refs[-8:]

        @first_step()
        def _():
            turn(turned_one, w_one_ref, t_ref)
            turn(turned, w_ref)
            acc_ref[...] = jnp.zeros_like(acc_ref)
            sum_ref[...] = jnp.zeros_like(sum_ref)
            part_ref[...] = jnp.zeros_like(part_ref)
            row = lax.broadcasted_iota(jnp.int32, (REST, TILE), 0)
            hidden_ref[H:] = jnp.where(row == 0, 1.0, 0.0).astype(LOW)

        widen(wide_ref, l_ref)
        for a, b in pieces_of(TILE):
            hidden, slope = gelu_both(product(turned_one[...], wide_ref[:, a:b]))
            hidden_ref[:H, a:b] = hidden.astype(LOW)
            slope_ref[:, a:b] = slope
        head = n_ref[:, 1:2]
        for a, b in pieces_of(TILE):
            two, slope = gelu_both(product(turned[...], hidden_ref[:H, a:b]) + n_ref[:, 0:1])
            two = two.astype(LOW).astype(F32)
            logits = n_ref[0:1, 2:3] + jnp.sum(two * head, axis=0, keepdims=True)
            label = x_ref[0:1, a:b]
            day = x_ref[1:2, a:b].astype(jnp.int32)
            row = lax.broadcasted_iota(jnp.int32, (days, b - a), 0)
            weight = jnp.sum(jnp.where(row == day, i_ref[:, 0:1], 0.0), axis=0, keepdims=True)
            decay = jnp.exp(-jnp.abs(logits))
            entropy = jnp.maximum(logits, 0.0) + jnp.log1p(decay) - label * logits
            chance = jnp.where(logits >= 0.0, 1.0, decay) / (1.0 + decay)
            logit_grad = (chance - label) * weight
            logit_ref[:, a:b] = logits
            sum_ref[0:1, a:b] += logit_grad
            sum_ref[1:2, a:b] += entropy * weight
            low_ref[:, a:b] = ((logit_grad * head) * slope).astype(LOW)
            one = logit_grad * two
            part = one[:, :LANES]
            for at in range(LANES, b - a, LANES):
                part = part + one[:, at : at + LANES]
            part_ref[...] += part
        for a, b in pieces_of(TILE):
            back_ref[:, a:b] = (product(w_ref[...], low_ref[:, a:b]) * slope_ref[:, a:b]).astype(LOW)
        for a, b in pieces_of(H):
            acc_ref[:, a:b] += outer(hidden_ref[...], low_ref[a:b])

        @last_step()
        def _():
            line_ref[0:8] = jnp.broadcast_to(
                jnp.sum(part_ref[...].T, axis=0, keepdims=True), (8, H)
            )
            line_ref[8:16] = acc_ref[H : H + 8]
            spread.write([acc_ref], k_ref, out_refs)

    return run(
        "deep",
        kernel,
        batch,
        [
            SMEM,
            columns(TALL),
            columns(2),
            once(H, H),
            once(LANES, H),
            once(H, H),
            whole(H, LANES),
            whole(days, LANES),
        ],
        [columns(1), columns(H), whole(16, H), whole(8, TILE)] + spread.specs(),
        [
            shaped(F32, 1, batch),
            shaped(LOW, H, batch),
            shaped(F32, 16, H),
            shaped(F32, 8, TILE),
        ]
        + spread.shapes(),
        [
            pltpu.VMEM((H, WIDE), LOW),
            pltpu.VMEM((H, H), LOW),
            pltpu.VMEM((TALL, H), F32),
            pltpu.VMEM((TALL, TILE), LOW),
            pltpu.VMEM((H, TILE), F32),
            pltpu.VMEM((H, TILE), LOW),
            pltpu.VMEM((H, LANES), F32),
            pltpu.VMEM((WIDE, TILE), LOW),
        ],
        8 * batch * H * H,
        index, layer_low, examples, matrix_one, tail, matrix, lines, inverse,
    )


def back_deep(spread, index, grad_low, layer_low, features, matrix, tail, after):
    batch = features.shape[1]

    def kernel(k_ref, g_ref, l_ref, x_ref, w_ref, t_ref, *refs):
        refs = refs[len(after) :]
        layer_ref, mixer_ref, line_ref = refs[:3]
        out_refs = refs[3:-2]
        held, acc_ref = refs[-2:]

        @first_step()
        def _():
            straight(held, w_ref, t_ref)
            acc_ref[...] = jnp.zeros_like(acc_ref)

        for a, b in pieces_of(TILE):
            layer = product(held[...], g_ref[:, a:b])
            layer_ref[:, a:b] = layer
            mixer_ref[:, a:b] = (layer * x_ref[:, a:b].astype(F32)).astype(LOW)
        for a, b in pieces_of(H):
            acc_ref[:, a:b] += outer(l_ref[...], g_ref[a:b])

        @last_step()
        def _():
            line_ref[...] = acc_ref[H:]
            spread.write([acc_ref], k_ref, out_refs)

    return run(
        "back_deep",
        kernel,
        batch,
        [SMEM, columns(H), columns(TALL), columns(TALL), once(H, H), once(LANES, H)]
        + [ANY] * len(after),
        [columns(TALL), columns(TALL), whole(REST, H)] + spread.specs(),
        [shaped(F32, TALL, batch), shaped(LOW, TALL, batch), shaped(F32, REST, H)]
        + spread.shapes(),
        [pltpu.VMEM((TALL, H), LOW), pltpu.VMEM((TALL, H), F32)],
        4 * batch * TALL * H,
        index, grad_low, layer_low, features, matrix, tail, *after,
    )


def back_two(
    spread, index, mixer_low, layer_low, layer_grad, features, mixer_one, mixer_two, matrix, tail,
    edge, lines, after,
):
    batch = features.shape[1]

    def kernel(k_ref, g_ref, l_ref, d_ref, x_ref, one_ref, two_ref, w_ref, t_ref, e_ref, *refs):
        top_ref, deep_ref, sums_ref = refs[:3]
        refs = refs[3 + len(after) :]
        part_ref, mixer_ref, vector_ref = refs[:3]
        out_refs = refs[3:-6]
        held, acc_ref, wide_ref, sum_ref, side_ref, next_side_ref = refs[-6:]

        @first_step()
        def _():
            straight(held, w_ref, t_ref, e_ref)
            acc_ref[...] = jnp.zeros_like(acc_ref)
            side_ref[...] = jnp.zeros_like(side_ref)
            next_side_ref[...] = jnp.zeros_like(next_side_ref)
            sum_ref[...] = jnp.zeros_like(sum_ref)

        widen(wide_ref, g_ref)
        for a, b in pieces_of(TILE):
            above = d_ref[:, a:b]
            layer = product(held[...], wide_ref[:, a:b]) + above
            mixer = (layer * x_ref[:, a:b].astype(F32)).astype(LOW)
            mixer_ref[:, a:b] = mixer
            mixer = mixer[:H].astype(F32)
            total = mixer[:, :LANES]
            for at in range(LANES, b - a, LANES):
                total = total + mixer[:, at : at + LANES]
            sum_ref[...] += total
            part = above * two_ref[:, a:b].astype(F32)
            part = part + layer * (one_ref[:, a:b].astype(F32) + 1.0)
            part_ref[:, a:b] = part.astype(LOW)
        for a, b in pieces_of(H):
            acc_ref[:, a:b] += outer(l_ref[...], g_ref[a:b])
        side_ref[...] += outer(g_ref[H:], l_ref[...])
        next_side_ref[...] += outer(mixer_ref[H:], x_ref[...])

        @last_step()
        def _():
            vector_ref[...] = jnp.zeros_like(vector_ref)
            vector_ref[0:1, :H] = jnp.sum(sum_ref[...].T, axis=0, keepdims=True)
            vector_ref[1:2, :H] = acc_ref[D : D + 1]
            vector_ref[2:3, :H] = deep_ref[EXTRA : EXTRA + 1]
            vector_ref[3:4, :H] = top_ref[8:9]
            vector_ref[4:5, :H] = top_ref[0:1]
            vector_ref[5:8, :TALL] = next_side_ref[:EXTRA]
            vector_ref[8:11, :TALL] = side_ref[:EXTRA]
            lane = lax.broadcasted_iota(jnp.int32, (1, LANES), 1)
            bias = jnp.sum(sums_ref[0:1], axis=1, keepdims=True)
            loss = jnp.sum(sums_ref[1:2], axis=1, keepdims=True)
            vector_ref[11:12, :LANES] = jnp.where(lane == 0, bias, jnp.where(lane == 1, loss, 0.0))
            spread.write([acc_ref], k_ref, out_refs)

    return run(
        "back_two",
        kernel,
        batch,
        [SMEM]
        + [columns(TALL)] * 6
        + [once(H, H), once(LANES, H), once(REST, WIDE)]
        + [whole(*v.shape) for v in lines]
        + [ANY] * len(after),
        [columns(TALL), columns(TALL)]
        + [whole(16, WIDE)]
        + spread.specs(),
        [
            shaped(LOW, TALL, batch),
            shaped(LOW, TALL, batch),
            shaped(F32, 16, WIDE),
        ]
        + spread.shapes(),
        [
            pltpu.VMEM((TALL, WIDE), LOW),
            pltpu.VMEM((TALL, H), F32),
            pltpu.VMEM((WIDE, TILE), LOW),
            pltpu.VMEM((H, LANES), F32),
            pltpu.VMEM((REST, TALL), F32),
            pltpu.VMEM((REST, TALL), F32),
        ],
        4 * batch * TALL * TALL,
        index, mixer_low, layer_low, layer_grad, features, mixer_one, mixer_two, matrix, tail,
        edge, *lines, *after,
    )


def grad_one(spread, index, mixer_low, features, overs, after):
    batch = features.shape[1]

    def kernel(k_ref, g_ref, x_ref, *refs):
        over_refs = refs[: len(overs)]
        out_refs = refs[len(overs) + len(after) : -1]
        acc_ref = refs[-1]

        @first_step()
        def _():
            acc_ref[...] = jnp.zeros_like(acc_ref)

        for a, b in pieces_of(H):
            acc_ref[:, a:b] += outer(x_ref[...], g_ref[a:b])

        @last_step()
        def _():
            spread.write([acc_ref], k_ref, out_refs, over_refs)

    return run(
        "grad_one",
        kernel,
        batch,
        [SMEM, columns(TALL), columns(TALL)]
        + [once(*v.shape) for v in overs]
        + [ANY] * len(after),
        spread.specs(),
        spread.shapes(),
        [pltpu.VMEM((TALL, H), F32)],
        2 * batch * TALL * TALL,
        index, mixer_low, features, *overs, *after,
    )


def back_one(mixer_low, part, matrix, tail, edge, after):
    batch = part.shape[1]

    def kernel(g_ref, p_ref, w_ref, t_ref, e_ref, *refs):
        out_ref, held, wide_ref = refs[len(after) :]

        @first_step()
        def _():
            straight(held, w_ref, t_ref, e_ref)

        widen(wide_ref, g_ref)
        for a, b in [(0, TILE)]:
            value = p_ref[:, a:b].astype(F32) + product(held[...], wide_ref[:, a:b])
            out_ref[:H, a:b] = value[:H]
            out_ref[H:, a:b] = value[H:D]

    return run(
        "back_one",
        kernel,
        batch,
        [columns(TALL), columns(TALL), whole(H, H), whole(LANES, H), whole(REST, WIDE)]
        + [ANY] * len(after),
        [columns(D)],
        [shaped(F32, D, batch)],
        [pltpu.VMEM((TALL, WIDE), LOW), pltpu.VMEM((WIDE, TILE), LOW)],
        2 * batch * TALL * TALL,
        mixer_low, part, matrix, tail, edge, *after,
    )[0]


def local(groups, features, labels, days, master, moment_one, moment_two):
    count = lax.axis_size(AXES)
    index = lax.axis_index(AXES)
    slot = index[None].astype(jnp.int32)
    rows = H // count
    starts = starts_of(count)
    sizes = piece_sizes(count)
    wide_piece = sizes[1]
    piece = [master[a : a + l] for a, l in zip(starts, sizes)]
    block_one = to_block(piece[0], index, D, rows, count)
    block_two = to_block(piece[2], index, D, rows, count)
    block_deep = to_block(piece[4], index, H, rows, count)

    day_hot = (days[:, None] == jnp.arange(DAYS, dtype=jnp.int32)[None, :]).astype(F32)
    own_counts = jnp.sum(day_hot, axis=0)
    counts_high = jnp.floor(own_counts / 64.0)
    counts_low = own_counts - 64.0 * counts_high

    def spill_side(block):
        side = block[rows:, H:].T
        return jnp.pad(side, ((0, 0), (0, rows - SPILL_ROWS)))

    misc = [
        piece[5],
        piece[7],
        piece[8],
        block_one[:rows, H:].T,
        block_two[:rows, H:].T,
        spill_side(block_one),
        spill_side(block_two),
        piece[1],
        piece[3],
        piece[9],
        counts_high,
        counts_low,
    ]
    misc = jnp.concatenate([part.reshape(-1) for part in misc])
    misc = jnp.pad(misc, (0, (AUX_ROWS - MISC_ROW) * H - misc.shape[0])).reshape(-1, H)
    first = jnp.concatenate(
        [
            block_one[:rows, :H],
            block_two[:rows, :H],
            block_one[rows:, :H],
            block_two[rows:, :H],
            block_deep[rows:],
            misc,
        ]
    ).astype(LOW)
    stacks_cross = gather(first, groups, count)
    rest = jnp.concatenate([block_deep[:rows], piece[6].reshape(rows, H)]).astype(LOW)
    crossed = [value for value, _ in stacks_cross[3:5]]
    stacks_rest = gather(rest, groups, count, direct=True, after=crossed)
    examples = jnp.stack([labels.astype(F32), days.astype(F32)])

    matrix_one, matrix_two, aux = place(slot, stacks_cross, rows, count, [0, SPILL_ROWS])
    matrix_deep, matrix_top = place(slot, stacks_rest, rows, count, [2 * SPILL_ROWS, None], aux)

    line = aux[:, MISC_ROW]
    at = UNIT_LINES * rows
    units = line[:, :at].reshape(count, UNIT_LINES, rows).transpose(1, 0, 2).reshape(UNIT_LINES, H)
    biases = line[:, at : at + 2 * wide_piece].reshape(count, 2, wide_piece)
    biases = biases.transpose(1, 0, 2).reshape(2, count * wide_piece)
    at += 2 * wide_piece
    head_bias = line[0, at]
    both_counts = jnp.sum(line[:, at + 1 : at + 1 + 2 * DAYS].astype(F32), axis=0)
    counts = 64.0 * both_counts[:DAYS] + both_counts[DAYS:]
    inverse = jnp.broadcast_to((1.0 / counts)[:, None], (DAYS, LANES))
    sides = jnp.pad(units[3:9], ((0, 0), (0, LANES))) + jnp.pad(
        units[9:15], ((0, 0), (rows, LANES - rows))
    )

    def tail_of(at, bias):
        return jnp.concatenate(
            [aux[count - 1, at : at + EXTRA], bias[None, :H], jnp.zeros((LANES - EXTRA - 1, H), LOW)]
        )

    def edge_of(side, bias):
        lane = lax.broadcasted_iota(jnp.int32, side.shape, 1)
        side = jnp.where(lane == D, bias[H:D, None], side)
        return jnp.pad(side, ((0, TALL - H - EXTRA), (0, 0)))

    tail_one, edge_one = tail_of(0, biases[0]), edge_of(sides[:3], biases[0])
    tail_two, edge_two = tail_of(SPILL_ROWS, biases[1]), edge_of(sides[3:], biases[1])
    tail_deep = tail_of(2 * SPILL_ROWS, units[0])
    lines = jnp.concatenate(
        [units[1:3], jnp.full((1, H), head_bias), jnp.zeros((LANES - 3, H), LOW)]
    )
    lines = lines.astype(F32).T
    spread = Spread(groups, rows, count, by_z=True)
    spread_two = Spread(groups, rows, count)
    spread_last = Spread(groups, rows, count, below=True)

    wide_features, mixer_one, mixer_two, low_one, low_two = forward_cross(
        features.T, (matrix_one, tail_one, edge_one), (matrix_two, tail_two, edge_two)
    )
    logits, pre_one_low, top_lines, sums, *outs = deep(
        spread, slot, low_two, examples, matrix_deep, tail_deep, matrix_top, lines, inverse
    )
    *top_stacks, _ = spread.finish(outs, slot)
    layer_grad, mixer_two_low, deep_lines, *outs = back_deep(
        spread, slot, pre_one_low, low_two, wide_features, matrix_deep, tail_deep, []
    )
    *deep_stacks, deep_over = spread.finish(outs, slot)
    top_plane = core_stage(top_stacks, groups, count, [mixer_two_low])
    part, mixer_one_low, vectors, *outs = back_two(
        spread_two, slot, mixer_two_low, low_one, layer_grad, wide_features, mixer_one, mixer_two,
        matrix_two, tail_two, edge_two, (top_lines, deep_lines, sums), top_plane[1:],
    )
    *two_stacks, two_over = spread_two.finish(outs, slot)
    top_total = plane_stage(top_plane, groups, count, [mixer_one_low])
    deep_plane = core_stage(deep_stacks, groups, count, [mixer_one_low])
    overs = (two_over, deep_over)
    outs = grad_one(
        spread_last, slot, mixer_one_low, wide_features, overs,
        deep_plane[1:] + [top_total],
    )
    last_stacks = spread_last.finish(outs, slot, overs)
    deep_total = plane_stage(deep_plane, groups, count, last_stacks[:1])
    two_plane = core_stage(two_stacks, groups, count, last_stacks[:1])
    last_plane = core_stage(last_stacks, groups, count)
    feature_grad = back_one(
        mixer_one_low, part, matrix_one, tail_one, edge_one,
        last_plane[1:] + two_plane[1:] + [deep_total],
    )

    vectors = jnp.sum(lax.all_gather(vectors, AXES, axis=0), axis=0)
    loss = vectors[11, 1]
    side_sums = vectors[5:11]

    own_top = z_scatter(top_total, groups, count)
    own_deep = z_scatter(deep_total, groups, count)
    two_z = plane_stage_z(two_plane, groups, count, [feature_grad])
    own_two = z_stage(two_z, groups, count)
    own_last = z_stage(plane_stage_z(last_plane, groups, count, [feature_grad] + two_z[1:]), groups, count)
    own_one = own_last[:rows]
    spills = own_last[rows : rows + MISC_ROW]
    row = lax.broadcasted_iota(jnp.int32, spills.shape, 0)
    beyond = (row % SPILL_ROWS >= EXTRA) & (index == count - 1)
    spills = jnp.where(beyond, 0.0, spills)
    wide_biases = jnp.concatenate(
        [vectors[:2, :H], side_sums[:, D].reshape(2, EXTRA)], axis=1
    )
    wide_biases = jnp.pad(wide_biases, ((0, 0), (0, count * wide_piece - D)))
    wide_biases = lax.dynamic_slice(wide_biases, (0, index * wide_piece), (2, wide_piece))
    units = lax.dynamic_slice(vectors[2:5], (0, index * rows), (3, rows))
    side_sums = jnp.pad(side_sums[:, :D], ((0, 0), (0, WIDE - D)))
    side_sums = lax.dynamic_slice(side_sums, (0, index * rows), (6, rows + SPILL_ROWS)).T

    def whole_block(main, number):
        low = number * SPILL_ROWS
        body = jnp.concatenate([main, spills[low : low + SPILL_ROWS]])
        if number == 2:
            return body
        return jnp.concatenate([body, side_sums[:, 3 * number : 3 * number + 3]], axis=1)

    flat_grad = jnp.concatenate(
        [
            from_block(whole_block(own_one, 0), index, sizes[0], rows, count),
            wide_biases[0],
            from_block(whole_block(own_two, 1), index, sizes[2], rows, count),
            wide_biases[1],
            from_block(whole_block(own_deep, 2), index, sizes[4], rows, count),
            units[0],
            own_top.reshape(-1),
            units[1],
            units[2],
            jnp.where(index == 0, vectors[11, :1], 0.0),
        ]
    )
    new_moment_one = 0.9 * moment_one + 0.1 * flat_grad
    new_moment_two = 0.999 * moment_two + 0.001 * flat_grad * flat_grad
    corrected_one = new_moment_one / (1.0 - 0.9**STEP)
    corrected_two = new_moment_two / (1.0 - 0.999**STEP)
    new_master = master - 0.03 * (corrected_one / (jnp.sqrt(corrected_two) + 1e-08) + 0.01 * master)
    new_bias = jnp.concatenate(
        [new_master[starts[i] : starts[i] + sizes[i]] for i in (1, 3, 5, 7, 9)]
    )
    return (
        logits.reshape(-1),
        loss,
        feature_grad.T,
        flat_grad,
        new_moment_one,
        new_moment_two,
        new_master,
        new_bias,
    )


def solution(mesh):
    line = P(AXES)
    table = P(AXES, None)
    groups = bit_groups(mesh)
    return jax.shard_map(
        functools.partial(local, groups),
        mesh=mesh,
        in_specs=(table, line, line, line, line, line),
        out_specs=(line, P(), table, line, line, line, line, line),
        check_vma=False,
    )
```
